32 devices in a mesh: dp: 8 (over z, y), fsdp: 4 (over x, core).
Axes of the slice: x: 2, y: 2, z: 4, core: 2. Of those that a mesh axis runs over, the one named last changes fastest.
Arguments:
- features: bfloat16 [8, 4, 18, 180, 300], P('dp', 'fsdp'), may hold values from -8 to 8
- land_mask: int32 [144, 180], replicated, may hold values from 0 to 1, as said below
- cotangent: bfloat16 [8, 4, 18, 180, 300], P('dp', 'fsdp'), may hold values from -6 to 6
- kernel: bfloat16 [300, 49], P('fsdp'), may hold values from -0.875 to 0.875
- norm_gain: bfloat16 [300], P('fsdp'), may hold values from 0.099609375 to 1.8984375
- norm_shift: bfloat16 [300], P('fsdp'), may hold values from -3 to 3
- in_proj: bfloat16 [300, 1200], P('fsdp'), may hold values from -0.375 to 0.375
- in_bias: bfloat16 [1200], P('fsdp'), may hold values from -3 to 3
- out_proj: bfloat16 [1200, 300], P('fsdp'), may hold values from -0.1875 to 0.1875
- out_bias: bfloat16 [300], P('fsdp'), may hold values from -3 to 3
Outputs:
- output: bfloat16 [8, 4, 18, 180, 300], P('dp', 'fsdp')
- grad_features: bfloat16 [8, 4, 18, 180, 300], P('dp', 'fsdp')
- grad_kernel: float32 [300, 49], P('fsdp')
- grad_gain: float32 [300], P('fsdp')
- grad_shift: float32 [300], P('fsdp')
- grad_in_proj: float32 [300, 1200], P('fsdp')
- grad_in_bias: float32 [1200], P('fsdp')
- grad_out_proj: float32 [1200, 300], P('fsdp')
- grad_out_bias: float32 [300], P('fsdp')
The draws below stay inside these ranges and needn't reach their ends.
Inputs may be any that keep to these rules, and one draw needn't show every extreme that they name: `land_mask`: 1 marks an ocean cell; every latitude row has ocean cells.
All inputs are finite; a program needn't handle non-finite values.
Results may differ from the reference program's by a relative error of at most 0.0059.
Values may be sent and summed in bfloat16 or wider, within the bound.
No kernel may reach another device: no remote copies, remote signals or barrier semaphores. Data moves between devices by JAX's collectives and lax.ppermute only.
A program may use at most 320 MiB of HBM per device.

```python
import math
import jax
import jax.numpy as jnp
from jax import lax

C = 300
F = 1200
KW = 7
TILES = 8
ROWS = 18
W = 180
SAMPLES = 4
GROUPS = 1
NH = 144
N_DP = 8


def draw_features(key, part):
    key = jax.random.fold_in(key, 11)
    first = jax.random.fold_in(key, 0)
    third = jax.random.fold_in(key, 2)
    fourth = jax.random.fold_in(key, 3)
    fifth = jax.random.fold_in(key, 4)
    sixth = jax.random.fold_in(key, 5)
    blockidx = jnp.arange(N_DP, dtype=jnp.int32)
    tileidx = blockidx % TILES
    groupidx = blockidx // TILES
    rowidx = tileidx[:, None] * ROWS + jnp.arange(ROWS, dtype=jnp.int32)[None, :]
    rowpos = rowidx.astype(jnp.float32) / max(NH - 1, 1)
    rowscale = (0.6 + 1.2 * rowpos)[:, None, :, None, None]
    latitude = (rowidx.astype(jnp.float32) + 0.5) * (math.pi / NH)
    longitude = jnp.arange(W, dtype=jnp.int32).astype(jnp.float32) * (2.0 * math.pi / W)
    freq_lon = jax.random.randint(third, (C,), 1, 3).astype(jnp.float32)
    freq_lat = jax.random.randint(fourth, (C,), 1, 4).astype(jnp.float32)
    phases = jax.random.uniform(fifth, (2, GROUPS, SAMPLES, C), jnp.float32, 0.0, 2.0 * math.pi)
    amplitude = jax.random.uniform(sixth, (GROUPS, SAMPLES, C), jnp.float32, 0.8, 1.2)
    phase_lon = phases[0][groupidx][:, :, None, None, :]
    phase_lat = phases[1][groupidx][:, :, None, None, :]
    wave_lon = jnp.sin(longitude[None, None, None, :, None] * freq_lon + phase_lon)
    wave_lat = jnp.cos(latitude[:, None, :, None, None] * freq_lat + phase_lat)
    smooth = amplitude[groupidx][:, :, None, None, :] * wave_lon * wave_lat
    base = 0.7 * jnp.clip(jax.random.normal(first, (N_DP, SAMPLES, ROWS, W, C), jnp.float32), -3.0, 3.0)
    values = (base + 1.9 * smooth) * rowscale
    return values.astype(jnp.bfloat16)


def draw_land_mask(key, part):
    key = jax.random.fold_in(key, 23)
    rowidx = jnp.arange(NH, dtype=jnp.int32)
    limit = 250 + 650 * rowidx // max(NH - 1, 1)
    picks = jax.random.randint(key, (NH, W), 0, 1000)
    return (picks < limit[:, None]).astype(jnp.int32)


def shard_levels(rng, dims, pieces, least, largest):
    gain, own = 1.0, jax.random.fold_in(rng, 6)
    for axis_at, blocks in pieces:
        heights = jnp.exp(jax.random.uniform(jax.random.fold_in(own, axis_at), (blocks,), jnp.float32, least / len(pieces), largest / len(pieces)))
        gain = gain * jnp.repeat(heights, dims[axis_at] // blocks).reshape([-1 if axis == axis_at else 1 for axis in range(len(dims))])
    return gain


def centred(rng, shape, spread, reach, cuts=(), kind=jnp.bfloat16):
    level = shard_levels(rng, shape, cuts, -0.22, 0.18) if cuts else 1.0
    values = jax.random.normal(rng, shape, jnp.float32) * spread * level
    return jnp.minimum(jnp.maximum(values, -reach), reach).astype(kind)


def setup_inputs(seed: int = 0) -> dict:
    arg_keys = jax.random.split(jax.random.key(seed), 11)
    return {
        "features": draw_features(jax.random.fold_in(arg_keys[10], 71), 0),
        "land_mask": draw_land_mask(jax.random.fold_in(arg_keys[10], 71), 0),
        "cotangent": centred(arg_keys[2], (N_DP, SAMPLES, ROWS, W, C), 1.0, 6.0, ((0, 8), (1, 4))),
        "kernel": centred(arg_keys[3], (C, KW * KW), (KW * KW) ** -0.5, 0.875, ((0, 4),)),
        "norm_gain": jnp.clip(1.0 + 0.18 * jax.random.normal(arg_keys[4], (C,), jnp.float32), 0.099609375, 1.8984375).astype(jnp.bfloat16),
        "norm_shift": centred(arg_keys[5], (C,), 0.5, 3.0, ((0, 4),)),
        "in_proj": centred(arg_keys[6], (C, F), C ** -0.5, 0.375, ((0, 4),)),
        "in_bias": centred(arg_keys[7], (F,), 0.5, 3.0, ((0, 4),)),
        "out_proj": centred(arg_keys[8], (F, C), F ** -0.5, 0.1875, ((0, 4),)),
        "out_bias": centred(arg_keys[9], (C,), 0.4, 3.0, ((0, 4),)),
    }


EPSILON = 1e-05
HIGH = lax.Precision.HIGHEST

@jax.custom_vjp
def low(v):
    return lax.optimization_barrier(v.astype(jnp.bfloat16)).astype(jnp.float32)

@jax.custom_vjp
def low_back(v):
    return v

def low_keep(v):
    return (low(v), None)

def low_pass(kept, grad):
    return (grad,)

def back_keep(v):
    return (v, None)

def back_low(kept, grad):
    return (low(grad),)
low.defvjp(low_keep, low_pass)
low_back.defvjp(back_keep, back_low)

def to_grids(blocks):
    groups = blocks.shape[0] // TILES
    sectioned = blocks.reshape(groups, TILES, SAMPLES, ROWS, W, blocks.shape[-1])
    sectioned = jnp.transpose(sectioned, (0, 2, 1, 3, 4, 5))
    return sectioned.reshape(groups * SAMPLES, TILES * ROWS, W, blocks.shape[-1])

def to_blocks(grids):
    groups = grids.shape[0] // SAMPLES
    sectioned = grids.reshape(groups, SAMPLES, TILES, ROWS, W, grids.shape[-1])
    sectioned = jnp.transpose(sectioned, (0, 2, 1, 3, 4, 5))
    return sectioned.reshape(groups * TILES, SAMPLES, ROWS, W, grids.shape[-1])

def convolve(field, taps):
    span = KW // 2
    height = field.shape[0]
    padded = jnp.pad(field, ((span, span), (0, 0), (0, 0)))
    total = jnp.zeros_like(field)
    for row_tap in range(KW):
        for col_tap in range(KW):
            total = total + taps[:, row_tap * KW + col_tap] * jnp.roll(padded[row_tap:row_tap + height], span - col_tap, axis=1)
    return total

def forward(maskf, blocks, taps, gamma, betas, in_w, in_b, out_w, out_b):
    feats = to_grids(blocks)
    ocean = maskf[None, :, :, None]
    masked = feats * ocean
    conv_out = lax.map(jax.checkpoint(lambda one: convolve(one, taps)), masked)
    conv_out = low_back(conv_out)
    count = jnp.maximum(feats.shape[0] * jnp.sum(maskf), 1.0)
    mean = lax.optimization_barrier(jnp.sum(conv_out * ocean, axis=(0, 1, 2))) / count
    var = lax.optimization_barrier(jnp.sum(ocean * (conv_out - mean) ** 2, axis=(0, 1, 2))) / count
    normed = (conv_out - mean) * lax.rsqrt(var + EPSILON)
    zvals = low(gamma * normed + betas)

    def pointwise(zone):
        hidden = low_back(jnp.matmul(zone, in_w, precision=HIGH) + in_b)
        act = low(jax.nn.gelu(hidden))
        return low_back(jnp.matmul(act, out_w, precision=HIGH) + out_b)
    branch = lax.map(jax.checkpoint(pointwise), zvals)
    return to_blocks((feats + branch) * ocean)

def reference(features, land_mask, cotangent, kernel, norm_gain, norm_shift, in_proj, in_bias, out_proj, out_bias):
    maskf = land_mask.astype(jnp.float32)
    floats = [v.astype(jnp.float32) for v in (features, kernel, norm_gain, norm_shift, in_proj, in_bias, out_proj, out_bias)]
    result, pullback = jax.vjp(lambda *vals: forward(maskf, *vals), *floats)
    grads = pullback(cotangent.astype(jnp.float32))
    return (result.astype(jnp.bfloat16), grads[0].astype(jnp.bfloat16), grads[1], grads[2], grads[3], grads[4], grads[5], grads[6], grads[7])
```

```python
import functools

import jax
import jax.numpy as jnp
import numpy as np
from jax import lax
from jax.experimental import pallas as pl
from jax.experimental.pallas import tpu as pltpu
from jax.sharding import PartitionSpec as P

KW = 7
SPAN = KW // 2
TILES = 8
EPSILON = 1e-05

LANES = 128
HALF = 64
FINE = 12
PAD = 16
PASSES = (KW + 1) // 2
TAPS = KW * KW
BASE = 8

F32 = jnp.float32
BF16 = jnp.bfloat16
LIMIT = 60 * 2**20
WHOLE = pl.BlockSpec(memory_space=pltpu.VMEM)
HBM = pl.BlockSpec(memory_space=pl.ANY)


def round_up(value, step):
    return -(-value // step) * step


def call(kernel, outs, operands, in_specs, scratch=(), flops=0, moved=0, grid=None, out_specs=None, name=None):
    extra = {} if grid is None else {"grid": grid}
    return pl.pallas_call(
        kernel,
        out_shape=[jax.ShapeDtypeStruct(shape, dtype) for shape, dtype in outs],
        in_specs=in_specs,
        out_specs=[WHOLE] * len(outs) if out_specs is None else out_specs,
        scratch_shapes=list(scratch),
        compiler_params=pltpu.CompilerParams(vmem_limit_bytes=LIMIT),
        cost_estimate=pl.CostEstimate(flops=flops, bytes_accessed=moved, transcendentals=0),
        name=name,
        **extra,
    )(*operands)


def low_half(rows):
    return lax.broadcasted_iota(jnp.int32, (rows, LANES), 1) < HALF


def swap(value):
    return pltpu.roll(value, HALF, 1)


def tiles_of(channels):
    return [(t, min(LANES, channels - t * LANES)) for t in range(-(-channels // LANES))]


def mask_column(land_t, row):
    lane = lax.broadcasted_iota(jnp.int32, land_t.shape, 1)
    return jnp.sum(jnp.where(lane == row, land_t, 0.0), axis=1, keepdims=True)


def stage_row(stage, values, width):
    lanes = values.shape[1]
    stage[0, BASE : BASE + width, :lanes] = values
    stage[0, BASE - SPAN : BASE, :lanes] = values[width - SPAN :]
    stage[0, BASE + width : BASE + width + SPAN, :lanes] = values[:SPAN]
    stage[1] = swap(stage[0])


def plane(stage, which, start):
    return stage[which, pl.ds(start, PAD, stride=FINE), :]


def place_row(paired, stage, tile, blocks, pair, side):
    low = low_half(PAD)
    lanes = pl.ds(side * LANES, LANES)
    for k in range((FINE + 2 * SPAN) // 2):
        start = BASE - SPAN + 2 * k
        paired[2 * tile, pair, k, :, lanes] = jnp.where(
            low, plane(stage, 0, start), plane(stage, 1, start + 1)
        ).astype(BF16)
        if 2 * tile + 1 < blocks:
            paired[2 * tile + 1, pair, k, :, lanes] = jnp.where(
                low, plane(stage, 1, start), plane(stage, 0, start + 1)
            ).astype(BF16)


def place_natural(paired, stage, source, channels, width, blocks, pair, side, factor=None):
    for t, lanes in tiles_of(channels):
        values = source(t * LANES, t * LANES + lanes).astype(F32)
        if factor is not None:
            values = values * factor
        buffer = stage.at[side, t]
        stage_row(buffer, values, width)
        place_row(paired, buffer, t, blocks, pair, side)


def place_rims(paired, stage, top, bottom, channels, width, blocks, height):
    for index in range(SPAN):
        for source, row in ((top, index), (bottom, SPAN + height + index)):
            place_natural(
                paired,
                stage,
                lambda a, b, source=source, index=index: source[index, :, a:b],
                channels,
                width,
                blocks,
                row // 2,
                row % 2,
            )


def build_weights(weights, taps, block, flip):
    lane = lax.broadcasted_iota(jnp.int32, (HALF, LANES), 1)
    sub = lax.broadcasted_iota(jnp.int32, (HALF, LANES), 0)
    diagonal = lax.rem(lane, HALF) == sub
    low = low_half(1)
    zero = jnp.zeros((1, LANES), F32)

    def tap_row(a, b):
        if not (0 <= a < KW and 0 <= b < KW):
            return zero
        index = (KW - 1 - a) * KW + KW - 1 - b if flip else a * KW + b
        return taps[block, index : index + 1, :]

    for m in range(PASSES):
        for s in range(PASSES):
            for place in range(4):
                pr, pj = divmod(place, 2)
                for qr in range(2):
                    a, b = 2 * m + pr - qr, 2 * s + pj
                    row = jnp.where(low, tap_row(a, b), tap_row(a, b - 1))
                    weights[
                        (m * PASSES + s) * 4 * HALF + place * HALF : (m * PASSES + s) * 4 * HALF + (place + 1) * HALF,
                        qr * LANES : (qr + 1) * LANES,
                    ] = jnp.where(diagonal, row, 0.0).astype(BF16)


def pass_rows(paired, block, m, s, pairs):
    piece = paired[block, m : m + pairs, s : s + FINE // 2]
    return piece.reshape(pairs * (FINE // 2) * PAD, 4 * HALF)


def convolve_block(paired, weights, block, pairs):
    rows = jnp.concatenate(
        [pass_rows(paired, block, m, s, pairs) for m in range(PASSES) for s in range(PASSES)], axis=1
    )
    return jnp.dot(rows, weights[...], preferred_element_type=F32)


def split_blocks(lower, upper, start, side):
    low = low_half(PAD)
    rows, lanes = pl.ds(start, PAD), pl.ds(side * LANES, LANES)
    first = lower[rows, lanes]
    if upper is None:
        return first, swap(first)
    second = upper[rows, lanes]
    return jnp.where(low, first, swap(second)), jnp.where(low, swap(first), second)


def prepare_kernel(feats, cot, land_t, paired, gbranch, mask, stage, plain):
    height, width, channels = feats.shape
    blocks = paired.shape[0]
    stage[...] = jnp.zeros_like(stage)
    plain[...] = jnp.zeros_like(plain)

    def one(row, pair, side):
        factor = mask_column(land_t[...], row)
        place_natural(
            paired, stage, lambda a, b: feats[row, :, a:b], channels, width, blocks, pair, side, factor
        )
        rows = pl.ds(BASE, width)
        plain[side, 0, rows, :] = jnp.broadcast_to(factor, (width, LANES))
        for t, lanes in tiles_of(channels):
            plain[side, 1 + t, rows, :lanes] = cot[row, :, t * LANES : t * LANES + lanes].astype(F32) * factor
        for r in range(FINE):
            mask[row, r] = plain[side, 0, pl.ds(BASE + r, PAD, stride=FINE), :]
            for t, _ in tiles_of(channels):
                gbranch[row, r, :, t * LANES : (t + 1) * LANES] = plain[
                    side, 1 + t, pl.ds(BASE + r, PAD, stride=FINE), :
                ].astype(BF16)

    one(0, SPAN // 2, SPAN % 2)

    def step(pair, _):
        one(2 * pair - SPAN, pair, 0)
        one(2 * pair + 1 - SPAN, pair, 1)
        return 0

    lax.fori_loop(SPAN // 2 + 1, (SPAN + height) // 2, step, 0)
    one(height - 1, (SPAN + height - 1) // 2, (SPAN + height - 1) % 2)


def forward_kernel(channels, paired_hbm, top, bottom, taps, mask, conv, stats, paired, weights, accs, stage, sem):
    height = conv.shape[0]
    blocks, pairs = paired.shape[0], height // 2
    width = top.shape[1]
    copy = pltpu.make_async_copy(paired_hbm, paired, sem)
    copy.start()
    stage[...] = jnp.zeros_like(stage)
    copy.wait()
    place_rims(paired, stage, top, bottom, channels, width, blocks, height)
    conv[...] = jnp.zeros_like(conv)
    for t, _ in tiles_of(channels):
        lanes = pl.ds(t * LANES, LANES)
        has_upper = 2 * t + 1 < blocks
        for half in range(1 + has_upper):
            build_weights(weights, taps, 2 * t + half, False)
            accs[half] = convolve_block(paired, weights, 2 * t + half, pairs)

        def spread(h, sums, t=t, lanes=lanes, has_upper=has_upper):
            total, count = sums
            for k in range(FINE // 2):
                for side in range(2):
                    even, odd = split_blocks(
                        accs.at[0], accs.at[1] if has_upper else None, (h * (FINE // 2) + k) * PAD, side
                    )
                    row = 2 * h + side
                    conv[row, 2 * k, :, lanes] = even
                    conv[row, 2 * k + 1, :, lanes] = odd
                    first, second = mask[row, 2 * k], mask[row, 2 * k + 1]
                    total = total + first * even + second * odd
                    count = count + first + second
            return total, count

        zero = jnp.zeros((PAD, LANES), F32)
        total, count = lax.fori_loop(0, pairs, spread, (zero, zero))
        total = jnp.sum(total, axis=0, keepdims=True)
        count = jnp.sum(count, axis=0, keepdims=True)
        mean = total / jnp.maximum(count, 1.0)

        def deviate(row, sums, lanes=lanes, mean=mean):
            for r in range(FINE):
                away = conv[row, r, :, lanes] - mean
                sums = sums + mask[row, r] * (away * away)
            return sums

        spread_sum = lax.fori_loop(0, height, deviate, zero)
        stats[0:1, lanes] = mean
        stats[1:2, lanes] = jnp.sum(spread_sum, axis=0, keepdims=True)


def pointwise_kernel(
    channels, real_units, conv, gbranch, feats, land_t, mask, vec, w_in, w_out, w_in_t, w_out_t,
    output, act_out, ghid_out, gz_out, z_out, sums, stage,
):
    rows, width = feats.shape[0], feats.shape[1]
    padded = conv.shape[-1]
    cells = rows * FINE * PAD
    hidden_units = act_out.shape[1]
    step = pl.program_id(0)

    @pl.when(step == 0)
    def _():
        sums[...] = jnp.zeros_like(sums)

    one_lane = lax.broadcasted_iota(jnp.int32, (1, padded), 1) == channels
    mean, inverse, gain, shift = (vec[i : i + 1, :] for i in range(4))
    normed = (conv[...].reshape(cells, padded) - mean) * inverse
    zvals = jnp.where(one_lane, 1.0, gain * normed + shift).astype(BF16)
    z_out[...] = zvals
    upstream = gbranch[...].reshape(cells, padded)
    branch = jnp.zeros((cells, padded), F32)
    gz = jnp.zeros((cells, padded), F32)
    chunk = 2 * LANES
    c0 = 0.7978845608028654
    c1 = 0.044715 * c0
    for start in range(0, hidden_units, chunk):
        span = pl.ds(start, chunk)
        hidden = jnp.dot(zvals, w_in[:, span], preferred_element_type=F32)
        gact = jnp.dot(upstream, w_out_t[:, span], preferred_element_type=F32)
        square = hidden * hidden
        bent = jnp.tanh(hidden * (c0 + c1 * square))
        half = 0.5 * hidden
        act = half + half * bent
        slope = (0.5 + 0.5 * bent) + half * (1.0 - bent * bent) * (c0 + (3.0 * c1) * square)
        ghid = (gact * slope).astype(BF16)
        act = act.astype(BF16)
        if start + chunk > real_units:
            lane = lax.broadcasted_iota(jnp.int32, (1, chunk), 1)
            act = jnp.where(lane == real_units - start, jnp.ones((), BF16), act)
        act_out[:, span] = act
        ghid_out[:, span] = ghid
        branch = branch + jnp.dot(act, w_out[span, :], preferred_element_type=F32)
        gz = gz + jnp.dot(ghid, w_in_t[span, :], preferred_element_type=F32)
    gz_out[...] = gz.reshape(gz_out.shape)
    sums[0:1, :] += jnp.sum(gz * normed, axis=0, keepdims=True)
    sums[1:2, :] += jnp.sum(gz, axis=0, keepdims=True)
    for row in range(rows):
        factor = mask_column(land_t[...], step * rows + row)
        for t, lanes in tiles_of(channels):
            for r in range(FINE):
                start = (row * FINE + r) * PAD
                stage[row, t, pl.ds(r, PAD, stride=FINE), :] = branch[start : start + PAD, t * LANES : (t + 1) * LANES]
            piece = pl.ds(t * LANES, lanes)
            values = feats[row, :, piece].astype(F32) + stage[row, t, 0:width, :lanes]
            output[row, :, piece] = (values * factor).astype(BF16)


def weight_kernel(zvals, ghid, gbranch, act, grad_in, grad_out):
    @pl.when(pl.program_id(0) == 0)
    def _():
        grad_in[...] = jnp.zeros_like(grad_in)
        grad_out[...] = jnp.zeros_like(grad_out)

    over_rows = (((0,), (0,)), ((), ()))
    rows = grad_in.shape[0]
    grad_in[...] += lax.dot_general(zvals[:, :rows], ghid[...], over_rows, preferred_element_type=F32)
    grad_out[...] += lax.dot_general(gbranch[:, :rows], act[...], over_rows, preferred_element_type=F32)


def gradient_kernel(
    channels, gz, conv, mask, vec, paired_hbm, top, bottom, select, gconv, grad_taps, paired, own, stage, sem
):
    height = gz.shape[0]
    blocks, pairs = paired.shape[0], height // 2
    width = top.shape[1]
    copy = pltpu.make_async_copy(paired_hbm, paired, sem)
    copy.start()
    stage[...] = jnp.zeros_like(stage)
    low = low_half(PAD)

    def arrange(h, _):
        for t, _unused in tiles_of(channels):
            lanes = pl.ds(t * LANES, LANES)
            mean, inverse, scaled, bias, slope = (vec[i : i + 1, lanes] for i in range(5))
            for k in range(FINE // 2):
                rows = pl.ds((h * (FINE // 2) + k) * PAD, PAD)
                for side in range(2):
                    both = []
                    for r in (2 * k, 2 * k + 1):
                        row = 2 * h + side
                        normed = (conv[row, r, :, lanes] - mean) * inverse
                        value = scaled * gz[row, r, :, lanes] - mask[row, r] * (bias + normed * slope)
                        gconv[row, r, :, lanes] = value.astype(BF16)
                        both.append(value)
                    out_lanes = pl.ds(side * LANES, LANES)
                    own[2 * t, rows, out_lanes] = jnp.where(low, both[0], swap(both[1])).astype(BF16)
                    if 2 * t + 1 < blocks:
                        own[2 * t + 1, rows, out_lanes] = jnp.where(low, swap(both[0]), both[1]).astype(BF16)
        return 0

    lax.fori_loop(0, pairs, arrange, 0)
    copy.wait()
    place_rims(paired, stage, top, bottom, channels, width, blocks, height)
    lane = lax.broadcasted_iota(jnp.int32, (HALF, 2 * LANES), 1)
    sub = lax.broadcasted_iota(jnp.int32, (HALF, 2 * LANES), 0)
    diagonal = lax.rem(lane, HALF) == sub

    def one_block(block, _):
        turned = own[block].T
        found = []
        for m in range(PASSES):
            for s in range(PASSES):
                product = jnp.dot(turned, pass_rows(paired, block, m, s, pairs), preferred_element_type=F32)
                for q in range(4):
                    part = product[q * HALF : (q + 1) * HALF]
                    found.append(jnp.sum(jnp.where(diagonal, part, 0.0), axis=0, keepdims=True))
        found = jnp.concatenate(found, axis=0)
        total = None
        for place in range(4):
            group = jnp.dot(
                select[place], found, preferred_element_type=F32, precision=lax.Precision.HIGHEST
            )
            group = group[:, (place // 2) * LANES : (place // 2 + 1) * LANES]
            if place % 2:
                group = swap(group)
            total = group if total is None else total + group
        grad_taps[block] = total
        return 0

    lax.fori_loop(0, blocks, one_block, 0)


def backward_kernel(channels, gconv, top, bottom, taps, mask, cot, land_t, result, paired, weights, accs, stage):
    height, width = cot.shape[0], cot.shape[1]
    blocks, pairs = paired.shape[0], height // 2
    real = width // FINE
    low = low_half(PAD)

    def planes(source, row, lanes):
        out = []
        for r in range(-SPAN, FINE + SPAN):
            value = source[row, r % FINE, :, lanes].astype(F32)
            if r < 0:
                value = jnp.concatenate([value[real - 1 : real], value[: PAD - 1]], axis=0)
            elif r >= FINE:
                value = jnp.concatenate([value[1:real], value[:1], value[: PAD - real]], axis=0)
            out.append(value)
        return out

    def place(source, row, pair, side):
        out_lanes = pl.ds(side * LANES, LANES)
        for t, _unused in tiles_of(channels):
            values = planes(source, row, pl.ds(t * LANES, LANES))
            for k in range((FINE + 2 * SPAN) // 2):
                first, second = values[2 * k], values[2 * k + 1]
                paired[2 * t, pair, k, :, out_lanes] = jnp.where(low, first, swap(second)).astype(BF16)
                if 2 * t + 1 < blocks:
                    paired[2 * t + 1, pair, k, :, out_lanes] = jnp.where(low, swap(first), second).astype(BF16)

    for index in range(SPAN):
        place(top, index, index // 2, index % 2)
        place(bottom, index, (SPAN + height + index) // 2, (SPAN + height + index) % 2)
    place(gconv, 0, SPAN // 2, SPAN % 2)
    place(gconv, height - 1, (SPAN + height - 1) // 2, (SPAN + height - 1) % 2)

    def body(pair, _):
        place(gconv, 2 * pair - SPAN, pair, 0)
        place(gconv, 2 * pair + 1 - SPAN, pair, 1)
        return 0

    lax.fori_loop(SPAN // 2 + 1, (SPAN + height) // 2, body, 0)
    for t, count in tiles_of(channels):
        has_upper = 2 * t + 1 < blocks
        for half in range(1 + has_upper):
            build_weights(weights, taps, 2 * t + half, True)
            accs[half] = convolve_block(paired, weights, 2 * t + half, pairs)

        def spread(h, _, t=t, count=count, has_upper=has_upper):
            for side in range(2):
                row = 2 * h + side
                for k in range(FINE // 2):
                    even, odd = split_blocks(
                        accs.at[0], accs.at[1] if has_upper else None, (h * (FINE // 2) + k) * PAD, side
                    )
                    stage[side, pl.ds(2 * k, PAD, stride=FINE), :] = even
                    stage[side, pl.ds(2 * k + 1, PAD, stride=FINE), :] = odd
                factor = mask_column(land_t[...], row)
                piece = pl.ds(t * LANES, count)
                values = cot[row, :, piece].astype(F32) + stage[side, 0:width, :count]
                result[row, :, piece] = (values * factor).astype(BF16)
            return 0

        lax.fori_loop(0, pairs, spread, 0)


def partners(size, bit):
    return [(i, i ^ bit) for i in range(size)]


def bits(size):
    bit = 1
    while bit < size:
        yield bit
        bit *= 2


def butterfly(values, merge, axes=("fsdp", "dp")):
    for axis in axes:
        size = lax.axis_size(axis)
        for bit in bits(size):
            values = merge(values, lax.ppermute(values, axis, partners(size, bit)))
    return values


def merge_stats(mine, other):
    count = mine[2:3] + other[2:3]
    safe = jnp.maximum(count, 1.0)
    mean = (mine[0:1] * mine[2:3] + other[0:1] * other[2:3]) / safe
    away = mine[0:1] - other[0:1]
    spread = mine[1:2] + other[1:2] + away * away * (mine[2:3] * other[2:3] / safe)
    return jnp.concatenate([mean, spread, count], axis=0)


def rims(array):
    size = lax.axis_size("dp")
    down = [(i, i + 1) for i in range(size - 1) if (i + 1) % TILES]
    up = [(j, i) for i, j in down]
    return lax.ppermute(array[-SPAN:], "dp", down), lax.ppermute(array[:SPAN], "dp", up)


def tap_selectors(rows):
    out = np.zeros((4, rows, PASSES * PASSES * 4), np.float32)
    for m in range(PASSES):
        for s in range(PASSES):
            for q in range(4):
                for p in range(4):
                    a = 2 * m + p // 2 - q // 2
                    b = 2 * s + p % 2 - q % 2
                    if 0 <= a < KW and 0 <= b < KW:
                        out[p, a * KW + b, (m * PASSES + s) * 4 + q] = 1.0
    return out


def own_share(value):
    share = value.shape[0] // lax.axis_size("fsdp")
    return lax.dynamic_slice_in_dim(value, lax.axis_index("fsdp") * share, share, 0)


def gather(value):
    return lax.all_gather(value, "fsdp", axis=0, tiled=True)


def local(features, land_mask, cotangent, kernel, norm_gain, norm_shift, in_proj, in_bias, out_proj, out_bias):
    feats, cot = features[0, 0], cotangent[0, 0]
    height, width, channels = feats.shape
    hidden = in_proj.shape[1]
    padded = round_up(channels + 1, LANES)
    hidden_pad = round_up(hidden + 1, 2 * LANES)
    blocks = -(-channels // HALF)
    pairs = height // 2
    planes_in = (FINE + 2 * SPAN) // 2
    row_pairs = (height + 2 * SPAN) // 2
    cells = height * FINE * PAD
    block_rows = pairs * (FINE // 2) * PAD
    stage_rows = round_up(BASE + SPAN + FINE * PAD, 8)
    tile_count = len(tiles_of(channels))

    tile_index = lax.axis_index("dp") % TILES
    land = lax.dynamic_slice_in_dim(land_mask, tile_index * height, height, 0)
    land_t = land.T.astype(F32)
    low_mask = land.astype(BF16)[:, :, None]
    edge = jnp.concatenate([feats[:SPAN] * low_mask[:SPAN], feats[-SPAN:] * low_mask[-SPAN:]], axis=0)
    top, bottom = rims(edge)

    paired_shape = (blocks, row_pairs, planes_in, PAD, 4 * HALF)
    plane_shape = (height, FINE, PAD, padded)
    mask_shape = (height, FINE, PAD, LANES)
    stage = pltpu.VMEM((2, tile_count, 2, stage_rows, LANES), F32)
    paired, gbranch, mask = call(
        prepare_kernel,
        [(paired_shape, BF16), (plane_shape, BF16), (mask_shape, F32)],
        (feats, cot, land_t),
        [WHOLE] * 3,
        [stage, pltpu.VMEM((2, 1 + tile_count, stage_rows, LANES), F32)],
        moved=20 * 2**20,
        name="prepare",
    )

    taps_full = gather(kernel)
    taps = jnp.pad(taps_full.astype(F32), ((0, blocks * HALF - channels), (0, 0)))
    taps = jnp.swapaxes(taps.reshape(blocks, HALF, TAPS), 1, 2)
    taps = jnp.concatenate([taps, taps], axis=2)
    accs = pltpu.VMEM((2, block_rows, 4 * HALF), F32)
    weights = pltpu.VMEM((PASSES * PASSES * 4 * HALF, 4 * HALF), BF16)
    conv, stats = call(
        functools.partial(forward_kernel, channels),
        [(plane_shape, F32), ((8, padded), F32)],
        (paired, top, bottom, taps, mask),
        [HBM] + [WHOLE] * 4,
        [pltpu.VMEM(paired_shape, BF16), weights, accs, stage, pltpu.SemaphoreType.DMA],
        flops=9 * 10**9,
        name="forward",
    )

    gain, shift = (jnp.pad(gather(v).astype(F32), (0, padded - channels)) for v in (norm_gain, norm_shift))
    in_full, in_b, out_full, out_b = gather(in_proj), gather(in_bias), gather(out_proj), gather(out_bias)
    w_in = jnp.concatenate([in_full, in_b[None]], axis=0)
    w_in = jnp.pad(w_in, ((0, padded - channels - 1), (0, hidden_pad - hidden)))
    w_out = jnp.concatenate([out_full, out_b[None]], axis=0)
    w_out = jnp.pad(w_out, ((0, hidden_pad - hidden - 1), (0, padded - channels)))
    w_in_t = jnp.pad(in_full, ((0, padded - channels), (0, hidden_pad - hidden))).T
    w_out_t = w_out.T

    own_count = jnp.sum(land.astype(F32))
    stats = jnp.concatenate([stats[:2], jnp.broadcast_to(own_count, (1, padded))], axis=0)
    stats = butterfly(stats, merge_stats)
    count = jnp.maximum(stats[2, 0], 1.0)
    mean = stats[0]
    inverse = lax.rsqrt(stats[1] / count + EPSILON)
    zero = jnp.zeros_like(gain)
    vec = jnp.stack([mean, inverse, gain, shift, zero, zero, zero, zero])

    rows = 3 if height % 3 == 0 else height
    steps = height // rows
    part = rows * FINE * PAD
    by_row = lambda *rest: pl.BlockSpec((rows, *rest), lambda i: (i,) + (0,) * len(rest))
    by_cell = lambda lanes: pl.BlockSpec((part, lanes), lambda i: (i, 0))
    fixed = lambda *shape: pl.BlockSpec(shape, lambda i: (0,) * len(shape))
    output, act, ghid, gz, zvals, sums = call(
        functools.partial(pointwise_kernel, channels, hidden),
        [
            ((height, width, channels), BF16),
            ((cells, hidden_pad), BF16),
            ((cells, hidden_pad), BF16),
            (plane_shape, F32),
            ((cells, padded), BF16),
            ((8, padded), F32),
        ],
        (conv, gbranch, feats, land_t, mask, vec, w_in, w_out, w_in_t, w_out_t),
        [
            by_row(FINE, PAD, padded),
            by_row(FINE, PAD, padded),
            by_row(width, channels),
            fixed(width, height),
            by_row(FINE, PAD, LANES),
            fixed(8, padded),
            fixed(padded, hidden_pad),
            fixed(hidden_pad, padded),
            fixed(hidden_pad, padded),
            fixed(padded, hidden_pad),
        ],
        [pltpu.VMEM((rows, tile_count, round_up(FINE * PAD, 8), LANES), F32)],
        flops=14 * 10**9,
        grid=(steps,),
        out_specs=[
            by_row(width, channels),
            by_cell(hidden_pad),
            by_cell(hidden_pad),
            by_row(FINE, PAD, padded),
            by_cell(padded),
            fixed(8, padded),
        ],
        name="pointwise",
    )

    sums = butterfly(sums[:2], lambda mine, other: mine + other)
    grad_rows = round_up(channels + 1, 16)
    big = 2 * part if steps % 2 == 0 else part
    by_big = lambda lanes: pl.BlockSpec((big, lanes), lambda i: (i, 0))
    grad_in, grad_out = call(
        weight_kernel,
        [((grad_rows, hidden_pad), F32), ((grad_rows, hidden_pad), F32)],
        (zvals, ghid, gbranch.reshape(cells, padded), act),
        [by_big(padded), by_big(hidden_pad), by_big(padded), by_big(hidden_pad)],
        flops=7 * 10**9,
        grid=(cells // big,),
        out_specs=[fixed(grad_rows, hidden_pad)] * 2,
        name="weight_grads",
    )

    grad_gain, grad_shift = sums[0], sums[1]
    scaled = inverse * gain
    gvec = jnp.stack([mean, inverse, scaled, scaled * grad_shift / count, scaled * grad_gain / count, zero, zero, zero])
    tap_rows = round_up(TAPS, 8)
    gconv, grad_taps = call(
        functools.partial(gradient_kernel, channels),
        [(plane_shape, BF16), ((blocks, tap_rows, LANES), F32)],
        (gz, conv, mask, gvec, paired, top, bottom, jnp.asarray(tap_selectors(tap_rows))),
        [WHOLE] * 4 + [HBM] + [WHOLE] * 3,
        [
            pltpu.VMEM(paired_shape, BF16),
            pltpu.VMEM((blocks, block_rows, 4 * HALF), BF16),
            stage,
            pltpu.SemaphoreType.DMA,
        ],
        flops=9 * 10**9,
        name="gradient",
    )
    gtop, gbottom = rims(gconv)
    (grad_features,) = call(
        functools.partial(backward_kernel, channels),
        [((height, width, channels), BF16)],
        (gconv, gtop, gbottom, taps, mask, cot, land_t),
        [WHOLE] * 7,
        [
            pltpu.VMEM(paired_shape, BF16),
            weights,
            accs,
            pltpu.VMEM((2, round_up(FINE * PAD, 8), LANES), F32),
        ],
        flops=9 * 10**9,
        name="backward",
    )

    grad_taps = jnp.swapaxes(grad_taps[:, :TAPS, :HALF], 1, 2).reshape(blocks * HALF, TAPS)[:channels]
    grad_taps, grad_in, grad_out = lax.psum((grad_taps, grad_in, grad_out), ("dp", "fsdp"))
    return (
        output[None, None],
        grad_features[None, None],
        own_share(grad_taps),
        own_share(grad_gain[:channels]),
        own_share(grad_shift[:channels]),
        own_share(grad_in[:channels, :hidden]),
        own_share(grad_in[channels, :hidden]),
        own_share(grad_out[:channels, :hidden].T),
        own_share(grad_out[:channels, hidden]),
    )


def solution(mesh):
    spread = P("dp", "fsdp", None, None, None)
    split = P("fsdp", None)
    line = P("fsdp")
    return jax.shard_map(
        local,
        mesh=mesh,
        in_specs=(spread, P(), spread, split, line, line, split, line, split, line),
        out_specs=(spread, spread, split, line, line, split, line, split, line),
        check_vma=False,
    )
```

```python
import functools

import jax
import jax.numpy as jnp
import numpy as np
from jax import lax
from jax.experimental import pallas as pl
from jax.experimental.pallas import tpu as pltpu
from jax.sharding import PartitionSpec as P

KW = 7
SPAN = KW // 2
TILES = 8
EPSILON = 1e-05

LANES = 128
HALF = 64
FINE = 12
PAD = 16
PASSES = (KW + 1) // 2
TAPS = KW * KW
RIM_PAIRS = 4
BASE = 8

F32 = jnp.float32
BF16 = jnp.bfloat16
MIB = 2**20
WHOLE = pl.BlockSpec(memory_space=pltpu.VMEM)
HBM = pl.BlockSpec(memory_space=pl.ANY)


def round_up(value, step):
    return -(-value // step) * step


def call(kernel, outs, operands, in_specs, scratch=(), flops=0, moved=0, grid=None, out_specs=None, limit=24, name=None):
    extra = {} if grid is None else {"grid": grid}
    return pl.pallas_call(
        kernel,
        out_shape=[jax.ShapeDtypeStruct(shape, dtype) for shape, dtype in outs],
        in_specs=in_specs,
        out_specs=[WHOLE] * len(outs) if out_specs is None else out_specs,
        scratch_shapes=list(scratch),
        compiler_params=pltpu.CompilerParams(vmem_limit_bytes=limit * MIB),
        cost_estimate=pl.CostEstimate(flops=flops, bytes_accessed=moved, transcendentals=0),
        name=name,
        **extra,
    )(*operands)


def low_half(rows):
    return lax.broadcasted_iota(jnp.int32, (rows, LANES), 1) < HALF


def swap(value):
    return pltpu.roll(value, HALF, 1)


def tiles_of(channels):
    return [(t, min(LANES, channels - t * LANES)) for t in range(-(-channels // LANES))]


def mask_of_row(turned, row):
    chosen = lax.broadcasted_iota(jnp.int32, (LANES, LANES), 0) == row
    return jnp.dot(turned, jnp.where(chosen, 1.0, 0.0).astype(BF16), preferred_element_type=F32)


def stage_row(stage, values, width):
    lanes = values.shape[1]
    stage[0, BASE : BASE + width, :lanes] = values
    stage[0, BASE - SPAN : BASE, :lanes] = values[width - SPAN :]
    stage[0, BASE + width : BASE + width + SPAN, :lanes] = values[:SPAN]
    stage[1] = swap(stage[0])


def plane(stage, which, start):
    return stage[which, pl.ds(start, PAD, stride=FINE), :]


def place_row(paired, stage, tile, blocks, pair, side):
    low = low_half(PAD)
    lanes = pl.ds(side * LANES, LANES)
    for k in range((FINE + 2 * SPAN) // 2):
        start = BASE - SPAN + 2 * k
        paired[2 * tile, pair, k, :, lanes] = jnp.where(
            low, plane(stage, 0, start), plane(stage, 1, start + 1)
        ).astype(BF16)
        if 2 * tile + 1 < blocks:
            paired[2 * tile + 1, pair, k, :, lanes] = jnp.where(
                low, plane(stage, 1, start), plane(stage, 0, start + 1)
            ).astype(BF16)


def place_natural(paired, stage, source, channels, width, blocks, pair, side, factor=None):
    for t, lanes in tiles_of(channels):
        values = source(t * LANES, t * LANES + lanes).astype(F32)
        if factor is not None:
            values = values * factor[:, :lanes]
        buffer = stage.at[side, t]
        stage_row(buffer, values, width)
        place_row(paired, buffer, t, blocks, pair, side)


def rim_rows(height):
    inner = (height + 2 * SPAN) // 2 - RIM_PAIRS // 2
    for index in range(SPAN):
        yield 0, index, index // 2, index % 2
    for index in range(SPAN):
        row = SPAN + height + index
        yield 1, index, row // 2 - inner + RIM_PAIRS // 2, row % 2


def build_weights(weights, taps, block, flip):
    lane = lax.broadcasted_iota(jnp.int32, (HALF, LANES), 1)
    sub = lax.broadcasted_iota(jnp.int32, (HALF, LANES), 0)
    diagonal = lax.rem(lane, HALF) == sub
    low = low_half(1)
    zero = jnp.zeros((1, LANES), F32)

    def tap_row(a, b):
        if not (0 <= a < KW and 0 <= b < KW):
            return zero
        index = (KW - 1 - a) * KW + KW - 1 - b if flip else a * KW + b
        return taps[block, index : index + 1, :]

    for m in range(PASSES):
        for s in range(PASSES):
            for place in range(4):
                pr, pj = divmod(place, 2)
                for qr in range(2):
                    a, b = 2 * m + pr - qr, 2 * s + pj
                    row = jnp.where(low, tap_row(a, b), tap_row(a, b - 1))
                    weights[
                        (m * PASSES + s) * 4 * HALF + place * HALF : (m * PASSES + s) * 4 * HALF + (place + 1) * HALF,
                        qr * LANES : (qr + 1) * LANES,
                    ] = jnp.where(diagonal, row, 0.0).astype(BF16)


def pass_rows(paired, rims, block, m, s, pairs):
    places = pl.ds(s, FINE // 2)
    inner = (RIM_PAIRS // 2, pairs + PASSES - 1 - RIM_PAIRS // 2)
    pieces = [rims[block, i, places] for i in range(m, inner[0])]
    pieces.append(paired[block, max(m, inner[0]) : min(m + pairs, inner[1]), places])
    pieces += [rims[block, i - inner[1] + RIM_PAIRS // 2, places] for i in range(inner[1], m + pairs)]
    return jnp.concatenate([piece.reshape(-1, 4 * HALF) for piece in pieces], axis=0)


def convolve_block(paired, rims, weights, block, pairs):
    rows = jnp.concatenate(
        [pass_rows(paired, rims, block, m, s, pairs) for m in range(PASSES) for s in range(PASSES)], axis=1
    )
    return jnp.dot(rows, weights[...], preferred_element_type=F32)


def split_blocks(lower, upper, start, side):
    low = low_half(PAD)
    rows, lanes = pl.ds(start, PAD), pl.ds(side * LANES, LANES)
    first = lower[rows, lanes]
    if upper is None:
        return first, swap(first)
    second = upper[rows, lanes]
    return jnp.where(low, first, swap(second)), jnp.where(low, swap(first), second)


def prepare_kernel(feats, cot, land, paired, gbranch, mask, masked, upstream, stage, plain, table):
    height, width, channels = feats.shape
    blocks = paired.shape[0]
    stage[...] = jnp.zeros_like(stage)
    plain[...] = jnp.zeros_like(plain)
    table[...] = jnp.zeros_like(table)
    table[:height, :width] = land[...].astype(F32)
    turned = table[...].T[:width].astype(BF16)

    def one(row, pair, side):
        factor = mask_of_row(turned, row)
        rows = pl.ds(BASE, width)
        plain[side, 0, rows, :] = factor
        for t, lanes in tiles_of(channels):
            piece = pl.ds(t * LANES, lanes)
            values = feats[row, :, piece].astype(F32) * factor[:, :lanes]
            masked[row, :, piece] = values.astype(BF16)
            buffer = stage.at[side, t]
            stage_row(buffer, values, width)
            place_row(paired, buffer, t, blocks, pair, side)
            values = cot[row, :, piece].astype(F32) * factor[:, :lanes]
            upstream[row, :, piece] = values.astype(BF16)
            plain[side, 1 + t, rows, :lanes] = values
        for r in range(FINE):
            mask[row, r] = plain[side, 0, pl.ds(BASE + r, PAD, stride=FINE), :]
            for t, _ in tiles_of(channels):
                gbranch[row, r, :, t * LANES : (t + 1) * LANES] = plain[
                    side, 1 + t, pl.ds(BASE + r, PAD, stride=FINE), :
                ].astype(BF16)

    one(0, SPAN // 2, SPAN % 2)

    def step(pair, _):
        one(2 * pair - SPAN, pair, 0)
        one(2 * pair + 1 - SPAN, pair, 1)
        return 0

    lax.fori_loop(SPAN // 2 + 1, (SPAN + height) // 2, step, 0)
    one(height - 1, (SPAN + height - 1) // 2, (SPAN + height - 1) % 2)


def forward_kernel(channels, paired, top, bottom, shards, mask, conv, stats, rims, taps, weights, accs, stage, table):
    height = conv.shape[0]
    blocks, pairs = paired.shape[0], height // 2
    width = top.shape[1]
    share = channels // shards.shape[0]
    stage[...] = jnp.zeros_like(stage)
    table[...] = jnp.zeros_like(table)
    for f in range(shards.shape[0]):
        table[f * share : (f + 1) * share] = shards[f].astype(F32)[:share]
    for block in range(blocks):
        piece = table[block * HALF : (block + 1) * HALF]
        taps[block] = jnp.concatenate([piece, piece], axis=0).T[: taps.shape[1]]
    last = pairs + PASSES - 1
    first_half = (SPAN % 2) * LANES
    last_half = ((SPAN + height - 1) % 2) * LANES
    rims[:, 1, :, :, first_half : first_half + LANES] = paired[:, 1, :, :, first_half : first_half + LANES]
    rims[:, 2, :, :, last_half : last_half + LANES] = paired[:, last - 2, :, :, last_half : last_half + LANES]
    for below, index, pair, side in rim_rows(height):
        source = bottom if below else top
        place_natural(
            rims, stage, lambda a, b, source=source, index=index: source[index, :, a:b], channels, width, blocks, pair, side
        )
    for t, _ in tiles_of(channels):
        lanes = pl.ds(t * LANES, LANES)
        has_upper = 2 * t + 1 < blocks
        for half in range(1 + has_upper):
            build_weights(weights, taps, 2 * t + half, False)
            accs[half] = convolve_block(paired, rims, weights, 2 * t + half, pairs)

        def planes(h, k, side, has_upper=has_upper):
            return split_blocks(accs.at[0], accs.at[1] if has_upper else None, (h * (FINE // 2) + k) * PAD, side)

        zero = jnp.zeros((PAD, LANES), F32)
        total, count = zero, zero
        for k in range(FINE // 2):
            even, odd = planes(0, k, 0)
            total = total + (mask[0, 2 * k] * even + mask[0, 2 * k + 1] * odd)
            count = count + (mask[0, 2 * k] + mask[0, 2 * k + 1])
        near = jnp.sum(total, axis=0, keepdims=True) / jnp.maximum(jnp.sum(count, axis=0, keepdims=True), 1.0)

        def spread(h, sums, lanes=lanes, planes=planes, near=near):
            sums = list(sums)
            for k in range(FINE // 2):
                for side in range(2):
                    row = 2 * h + side
                    for odd, value in enumerate(planes(h, k, side)):
                        r = 2 * k + odd
                        conv[row, r, :, lanes] = value
                        weight = mask[row, r]
                        away = value - near
                        part = weight * away
                        at = 3 * (2 * side + odd)
                        sums[at] = sums[at] + part
                        sums[at + 1] = sums[at + 1] + part * away
                        sums[at + 2] = sums[at + 2] + weight
            return tuple(sums)

        sums = lax.fori_loop(0, pairs, spread, (zero,) * 12)
        total, square, count = (
            jnp.sum(sums[i] + sums[i + 3] + sums[i + 6] + sums[i + 9], axis=0, keepdims=True) for i in range(3)
        )
        shift = total / jnp.maximum(count, 1.0)
        stats[0:1, lanes] = near + shift
        stats[1:2, lanes] = jnp.maximum(square - total * shift, 0.0)
        stats[2:3, lanes] = count


def pointwise_kernel(
    channels, real_units, conv, gbranch, feats, mask, vec, w_in, w_out,
    output, act_out, ghid_out, gz_out, z_out, sums, stage,
):
    rows, width = feats.shape[0], feats.shape[1]
    padded = conv.shape[-1]
    cells = rows * FINE * PAD
    hidden_units = act_out.shape[1]
    step = pl.program_id(0)

    @pl.when(step == 0)
    def _():
        sums[...] = jnp.zeros_like(sums)

    one_lane = lax.broadcasted_iota(jnp.int32, (1, padded), 1) == channels
    mean, inverse, gain, shift = (vec[i : i + 1, :] for i in range(4))
    normed = (conv[...].reshape(cells, padded) - mean) * inverse
    zvals = jnp.where(one_lane, 1.0, gain * normed + shift).astype(BF16)
    z_out[...] = zvals
    upstream = gbranch[...].reshape(cells, padded)
    branch = jnp.zeros((cells, padded), F32)
    gz = jnp.zeros((cells, padded), F32)
    chunk = 2 * LANES
    across = (((1,), (1,)), ((), ()))
    c0 = 0.7978845608028654
    c1 = 0.044715 * c0
    for start in range(0, hidden_units, chunk):
        span = pl.ds(start, chunk)
        hidden = jnp.dot(zvals, w_in[:, span], preferred_element_type=F32)
        gact = lax.dot_general(upstream, w_out[span, :], across, preferred_element_type=F32)
        square = hidden * hidden
        bent = jnp.tanh(hidden * (c0 + c1 * square))
        half = 0.5 * hidden
        act = half + half * bent
        slope = (0.5 + 0.5 * bent) + half * (1.0 - bent * bent) * (c0 + (3.0 * c1) * square)
        ghid = (gact * slope).astype(BF16)
        act = act.astype(BF16)
        if start + chunk > real_units:
            lane = lax.broadcasted_iota(jnp.int32, (1, chunk), 1)
            act = jnp.where(lane == real_units - start, jnp.ones((), BF16), act)
        act_out[:, span] = act
        ghid_out[:, span] = ghid
        branch = branch + jnp.dot(act, w_out[span, :], preferred_element_type=F32)
        gz = gz + lax.dot_general(ghid, w_in[:, span], across, preferred_element_type=F32)
    gz_out[...] = gz.reshape(gz_out.shape)
    sums[0:1, :] += jnp.sum(gz * normed, axis=0, keepdims=True)
    sums[1:2, :] += jnp.sum(gz, axis=0, keepdims=True)
    for row in range(rows):
        for t, lanes in tiles_of(channels):
            for r in range(FINE):
                start = (row * FINE + r) * PAD
                values = branch[start : start + PAD, t * LANES : (t + 1) * LANES] * mask[row, r]
                stage[row, t, pl.ds(r, PAD, stride=FINE), :] = values
            piece = pl.ds(t * LANES, lanes)
            values = feats[row, :, piece].astype(F32) + stage[row, t, 0:width, :lanes]
            output[row, :, piece] = values.astype(BF16)


def out_grads_kernel(gbranch, act, grad):
    grad[...] = turned_product(gbranch, act, grad.shape[0])


def turned_product(left, right, rows):
    return lax.dot_general(left[:, :rows], right[...], (((0,), (0,)), ((), ())), preferred_element_type=F32)


def in_grads_kernel(channels, hidden, zvals, ghid, grad_out, packed, grad_in):
    grad_in[...] = turned_product(zvals, ghid, grad_in.shape[0])
    shares, _, _ = packed.shape
    layout = Packing(channels, hidden, shares)
    last = layout.in_tiles - 1
    lane = lax.broadcasted_iota(jnp.int32, (1, LANES), 1)
    for j in range(shares):
        rows = slice(j * layout.in_rows, (j + 1) * layout.in_rows)
        fill = jnp.zeros((layout.in_pad - layout.in_rows, LANES), F32)
        for t in range(layout.in_tiles):
            lanes = slice(t * LANES, (t + 1) * LANES)
            tile = grad_in[rows, lanes]
            if t == last:
                tile = jnp.where(lane == hidden - t * LANES, grad_out[rows, lanes], tile)
            packed[j, t * layout.in_pad : (t + 1) * layout.in_pad] = jnp.concatenate([tile, fill], axis=0).astype(BF16)
        start = j * layout.out_rows
        aligned = start // LANES * LANES
        stop = min(aligned + (layout.out_tiles + 1) * LANES, grad_out.shape[1])
        spot = lax.broadcasted_iota(jnp.int32, (layout.out_pad, 1), 0)
        part = jnp.where(
            spot == channels, grad_in[: layout.out_pad, aligned:stop], grad_out[: layout.out_pad, aligned:stop]
        )
        if start != aligned:
            part = pltpu.roll(part, stop - start, 1)
        for u in range(layout.out_tiles):
            base = layout.out_base + u * layout.out_pad
            packed[j, base : base + layout.out_pad] = part[:, u * LANES : (u + 1) * LANES].astype(BF16)
        packed[j, layout.small_base :] = jnp.zeros((layout.rows - layout.small_base, LANES), BF16)


def finish_kernel(channels, hidden, packed, grad_in, grad_in_bias, grad_out, grad_out_bias):
    layout = Packing(channels, hidden, channels // grad_in.shape[0])
    for t in range(layout.in_tiles):
        stop = min((t + 1) * LANES, hidden)
        tile = packed[t * layout.in_pad : (t + 1) * layout.in_pad].astype(F32)
        grad_in[:, t * LANES : stop] = tile[: layout.in_rows, : stop - t * LANES]
    tall = jnp.concatenate([tile, jnp.zeros((LANES - layout.in_pad, LANES), F32)], axis=0).T
    at = hidden - (layout.in_tiles - 1) * LANES
    grad_out_bias[...] = tall[at : at + 1, : layout.in_rows]
    for u in range(layout.out_tiles):
        base = layout.out_base + u * layout.out_pad
        tile = packed[base : base + layout.out_pad].astype(F32)
        stop = min((u + 1) * LANES, layout.out_rows)
        count = stop - u * LANES
        grad_in_bias[:, u * LANES : stop] = tile[channels : channels + 1, :count]
        fill = jnp.zeros((round_up(layout.out_pad, LANES) - layout.out_pad, LANES), F32)
        grad_out[u * LANES : stop, :] = jnp.concatenate([tile, fill], axis=0).T[:count, :channels]


class Packing:
    def __init__(self, channels, hidden, shares):
        self.in_rows = channels // shares
        self.in_pad = round_up(self.in_rows, 16)
        self.in_tiles = -(-(hidden + 1) // LANES)
        self.out_rows = hidden // shares
        self.out_tiles = -(-self.out_rows // LANES)
        self.out_pad = round_up(max(channels + 1, self.out_rows), 16)
        self.out_base = self.in_pad * self.in_tiles
        self.small_base = self.out_base + self.out_pad * self.out_tiles
        self.small = self.out_tiles + 3
        self.rows = round_up(self.small_base + self.small, 32)


def pack_kernel(layout, in_proj, in_bias, out_proj, gain, shift, out_bias, packed, wide, tall):
    wide[...] = jnp.zeros_like(wide)
    tall[...] = jnp.zeros_like(tall)
    wide[: layout.in_rows, : in_proj.shape[1]] = in_proj[...].astype(F32)
    for t in range(layout.in_tiles):
        packed[t * layout.in_pad : (t + 1) * layout.in_pad] = wide[:, t * LANES : (t + 1) * LANES].astype(BF16)
    tall[: layout.out_rows, : out_proj.shape[1]] = out_proj[...].astype(F32)
    for u in range(layout.out_tiles):
        base = layout.out_base + u * layout.out_pad
        packed[base : base + layout.out_pad] = tall[:, u * LANES : (u + 1) * LANES].astype(BF16)
    wide[...] = jnp.zeros_like(wide)
    wide[0:1, : in_bias.shape[1]] = in_bias[...].astype(F32)
    for i, small in enumerate((gain, shift, out_bias)):
        wide[i + 1 : i + 2, : small.shape[1]] = small[...].astype(F32)
    rows = [wide[0:1, u * LANES : (u + 1) * LANES] for u in range(layout.out_tiles)]
    rows += [wide[i + 1 : i + 2, :LANES] for i in range(3)]
    rows.append(jnp.zeros((layout.rows - layout.small_base - layout.small, LANES), F32))
    packed[layout.small_base :] = jnp.concatenate(rows, axis=0).astype(BF16)


def assemble_kernel(layout, packed, w_in, w_out, vectors, wide, tall):
    wide[...] = jnp.zeros_like(wide)
    tall[...] = jnp.zeros_like(tall)
    shares = packed.shape[0]
    channels, hidden = layout.in_rows * shares, layout.out_rows * shares
    in_bias = jnp.zeros((8, wide.shape[1]), F32)
    smalls = [jnp.zeros((8, tall.shape[1]), F32)] * 3
    for f in range(shares):
        for t in range(layout.in_tiles):
            tile = packed[f, t * layout.in_pad : (t + 1) * layout.in_pad].astype(F32)
            wide[f * layout.in_rows : (f + 1) * layout.in_rows, t * LANES : (t + 1) * LANES] = tile[: layout.in_rows]
        for u in range(layout.out_tiles):
            base = layout.out_base + u * layout.out_pad
            tile = packed[f, base : base + layout.out_pad].astype(F32)
            tall[f * layout.out_rows : (f + 1) * layout.out_rows, u * LANES : (u + 1) * LANES] = tile[: layout.out_rows]
        small = packed[f, layout.small_base :].astype(F32)

        def spread(first, count, lanes, turn):
            pieces = [small[first + u : first + u + 1] for u in range(count)]
            pieces.append(jnp.zeros((1, lanes - count * LANES), F32))
            row = jnp.broadcast_to(jnp.concatenate(pieces, axis=1), (8, lanes))
            return pltpu.roll(row, turn, 1) if turn else row

        in_bias = in_bias + spread(0, layout.out_tiles, wide.shape[1], f * layout.out_rows)
        smalls = [
            total + spread(layout.out_tiles + i, 1, tall.shape[1], f * layout.in_rows)
            for i, total in enumerate(smalls)
        ]
    wide[channels : channels + 1] = in_bias[:1]
    tall[hidden : hidden + 1] = smalls[2][:1]
    w_in[...] = wide[...].astype(BF16)
    w_out[...] = tall[...].astype(BF16)
    vectors[...] = jnp.concatenate([smalls[0][:1], smalls[1][:1], jnp.zeros((6, tall.shape[1]), F32)], axis=0)


def shifted_planes(values, real):
    out = []
    for r in range(-SPAN, FINE + SPAN):
        value = values[r % FINE]
        if r < 0:
            value = jnp.concatenate([value[real - 1 : real], value[: PAD - 1]], axis=0)
        elif r >= FINE:
            value = jnp.concatenate([value[1:real], value[:1], value[: PAD - real]], axis=0)
        out.append(value)
    return out


def join_planes(first, second):
    low = low_half(PAD)
    return (
        jnp.where(low, first, swap(second)).astype(BF16),
        jnp.where(low, swap(first), second).astype(BF16),
    )


def place_planes(paired, planes, tile, blocks, pair, side):
    out_lanes = pl.ds(side * LANES, LANES)
    for k in range(len(planes) // 2):
        for half, value in enumerate(join_planes(planes[2 * k], planes[2 * k + 1])):
            if 2 * tile + half < blocks:
                paired[2 * tile + half, pair, k, :, out_lanes] = value


def gradient_kernel(
    channels, real, gz, conv, mask, vec, paired, rims, select, edges, gpaired, grad_taps, own
):
    height = gz.shape[0]
    blocks, pairs = paired.shape[0], height // 2

    def arrange(h, _):
        for t, _unused in tiles_of(channels):
            lanes = pl.ds(t * LANES, LANES)
            mean, inverse, scaled, bias, slope = (vec[i : i + 1, lanes] for i in range(5))
            for side in range(2):
                row = 2 * h + side
                values = []
                for r in range(FINE):
                    normed = (conv[row, r, :, lanes] - mean) * inverse
                    values.append(scaled * gz[row, r, :, lanes] - mask[row, r] * (bias + normed * slope))
                out_lanes = pl.ds(side * LANES, LANES)
                for k in range(FINE // 2):
                    rows = pl.ds((h * (FINE // 2) + k) * PAD, PAD)
                    for half, value in enumerate(join_planes(values[2 * k], values[2 * k + 1])):
                        if 2 * t + half < blocks:
                            own[2 * t + half, rows, out_lanes] = value
                place_planes(
                    gpaired, shifted_planes(values, real), t, blocks, h + (SPAN + side) // 2, (SPAN + side) % 2
                )
                for edge, near in ((0, row < SPAN), (1, row >= height - SPAN)):

                    @pl.when(near)
                    def _(edge=edge, row=row, values=values, lanes=lanes):
                        place = row - (height - SPAN) * edge
                        for r in range(FINE):
                            edges[edge, place, r, :, lanes] = values[r].astype(BF16)

        return 0

    lax.fori_loop(0, pairs, arrange, 0)
    lane = lax.broadcasted_iota(jnp.int32, (HALF, 2 * LANES), 1)
    sub = lax.broadcasted_iota(jnp.int32, (HALF, 2 * LANES), 0)
    diagonal = lax.rem(lane, HALF) == sub
    low = low_half(grad_taps.shape[1])
    totals = []
    for block in range(blocks):
        turned = own[block].T
        found = []
        for m in range(PASSES):
            for s in range(PASSES):
                product = jnp.dot(turned, pass_rows(paired, rims, block, m, s, pairs), preferred_element_type=F32)
                for q in range(4):
                    part = product[q * HALF : (q + 1) * HALF]
                    found.append(jnp.sum(jnp.where(diagonal, part, 0.0), axis=0, keepdims=True))
        found = jnp.concatenate(found, axis=0)
        total = None
        for place in range(4):
            group = jnp.dot(select[place], found, preferred_element_type=F32, precision=lax.Precision.HIGHEST)
            group = group[:, (place // 2) * LANES : (place // 2 + 1) * LANES]
            if place % 2:
                group = swap(group)
            total = group if total is None else total + group
        totals.append(total)
    for t, _ in tiles_of(channels):
        second = swap(totals[2 * t + 1]) if 2 * t + 1 < blocks else jnp.zeros_like(totals[0])
        grad_taps[t] = jnp.where(low, totals[2 * t], second)


def backward_kernel(tile, real, gpaired, top, bottom, taps, cot, mask, *rest):
    result, rims, weights, accs, stage = rest[-5:]
    height, width = cot.shape[0], cot.shape[1]
    blocks, pairs = gpaired.shape[0], height // 2
    last = pairs + PASSES - 1
    first_half = (SPAN % 2) * LANES
    last_half = ((SPAN + height - 1) % 2) * LANES
    has_upper = 2 * tile + 1 < blocks
    for half in range(1 + has_upper):
        source = gpaired.at[2 * tile + half]
        rims[half, 1, :, :, first_half : first_half + LANES] = source[1, :, :, first_half : first_half + LANES]
        rims[half, 2, :, :, last_half : last_half + LANES] = source[last - 2, :, :, last_half : last_half + LANES]
    for below, index, pair, side in rim_rows(height):
        source = bottom if below else top
        values = [source[index, r, :, tile * LANES : (tile + 1) * LANES].astype(F32) for r in range(FINE)]
        place_planes(rims, shifted_planes(values, real), 0, 1 + has_upper, pair, side)
    for half in range(1 + has_upper):
        block = 2 * tile + half
        build_weights(weights, taps, block, True)
        accs[half] = convolve_block(gpaired.at[block : block + 1], rims.at[half : half + 1], weights, 0, pairs)

    def spread(h, _):
        for side in range(2):
            row = 2 * h + side
            for k in range(FINE // 2):
                even, odd = split_blocks(
                    accs.at[0], accs.at[1] if has_upper else None, (h * (FINE // 2) + k) * PAD, side
                )
                stage[side, pl.ds(2 * k, PAD, stride=FINE), :] = even * mask[row, 2 * k]
                stage[side, pl.ds(2 * k + 1, PAD, stride=FINE), :] = odd * mask[row, 2 * k + 1]
            values = cot[row].astype(F32) + stage[side, 0:width]
            result[row] = values.astype(BF16)
        return 0

    lax.fori_loop(0, pairs, spread, 0)


def bits(size):
    bit = 1
    while bit < size:
        yield bit
        bit *= 2


def swapped(value, axis, bit):
    size = lax.axis_size(axis)
    return lax.ppermute(value, axis, [(i, i ^ bit) for i in range(size)])


def side_of(axis, bit):
    return lax.axis_index(axis) // bit % 2


def butterfly(values, merge, axes=("fsdp", "dp")):
    for axis in axes:
        for bit in bits(lax.axis_size(axis)):
            values = merge(values, swapped(values, axis, bit))
    return values


def add(mine, other):
    return (mine.astype(F32) + other.astype(F32)).astype(mine.dtype)


def merge_stats(mine, other):
    count = mine[2:3] + other[2:3]
    safe = jnp.maximum(count, 1.0)
    mean = (mine[0:1] * mine[2:3] + other[0:1] * other[2:3]) / safe
    away = mine[0:1] - other[0:1]
    spread = mine[1:2] + other[1:2] + away * away * (mine[2:3] * other[2:3] / safe)
    return jnp.concatenate([mean, spread, count], axis=0)


def gathered(value, axis):
    value = value[None]
    for bit in reversed(list(bits(lax.axis_size(axis)))):
        other = swapped(value, axis, bit)
        first = side_of(axis, bit) == 0
        pair = [jnp.where(first, value, other), jnp.where(first, other, value)]
        value = jnp.stack(pair, axis=1).reshape(-1, *value.shape[1:])
    return value


def keep_and_send(value, axis, bit, dim):
    side = side_of(axis, bit)
    return (
        lax.dynamic_index_in_dim(value, side, dim, keepdims=False),
        lax.dynamic_index_in_dim(value, 1 - side, dim, keepdims=False),
    )


def summed_share(value):
    for bit in bits(lax.axis_size("fsdp")):
        value = value.reshape(-1, 2, *value.shape[1:])
        keep, send = keep_and_send(value, "fsdp", bit, 1)
        value = add(keep, swapped(send, "fsdp", bit))
    value = value[0]
    rest = list(bits(lax.axis_size("dp")))
    if not rest:
        return value
    keep, send = keep_and_send(value.reshape(2, -1, value.shape[-1]), "dp", rest[0], 0)
    half = add(keep, swapped(send, "dp", rest[0]))
    for bit in rest[1:]:
        half = add(half, swapped(half, "dp", bit))
    other = swapped(half, "dp", rest[0])
    first = side_of("dp", rest[0]) == 0
    return jnp.concatenate([jnp.where(first, half, other), jnp.where(first, other, half)], axis=0)


def rims_of(top_rows, bottom_rows):
    size = lax.axis_size("dp")
    down = [(i, i + 1) for i in range(size - 1) if (i + 1) % TILES]
    up = [(j, i) for i, j in down]
    return lax.ppermute(bottom_rows, "dp", down), lax.ppermute(top_rows, "dp", up)


def tap_selectors(rows):
    out = np.zeros((4, rows, PASSES * PASSES * 4), np.float32)
    for m in range(PASSES):
        for s in range(PASSES):
            for q in range(4):
                for p in range(4):
                    a = 2 * m + p // 2 - q // 2
                    b = 2 * s + p % 2 - q % 2
                    if 0 <= a < KW and 0 <= b < KW:
                        out[p, a * KW + b, (m * PASSES + s) * 4 + q] = 1.0
    return out


def own_share(value):
    share = value.shape[0] // lax.axis_size("fsdp")
    return lax.dynamic_slice_in_dim(value, lax.axis_index("fsdp") * share, share, 0)


def local(features, land_mask, cotangent, kernel, norm_gain, norm_shift, in_proj, in_bias, out_proj, out_bias):
    feats, cot = features[0, 0], cotangent[0, 0]
    height, width, channels = feats.shape
    hidden = in_proj.shape[1]
    shares = lax.axis_size("fsdp")
    padded = round_up(channels + 1, LANES)
    hidden_pad = round_up(hidden + 1, 2 * LANES)
    blocks = -(-channels // HALF)
    pairs = height // 2
    planes_in = (FINE + 2 * SPAN) // 2
    row_pairs = pairs + PASSES - 1
    cells = height * FINE * PAD
    block_rows = pairs * (FINE // 2) * PAD
    stage_rows = round_up(BASE + SPAN + FINE * PAD, 8)
    tile_count = len(tiles_of(channels))
    tap_rows = round_up(TAPS, 8)
    real = width // FINE
    layout = Packing(channels, hidden, shares)

    tile_index = lax.axis_index("dp") % TILES
    land = lax.dynamic_slice_in_dim(land_mask, tile_index * height, height, 0)
    low_mask = land.astype(BF16)[:, :, None]
    top, bottom = rims_of(feats[:SPAN] * low_mask[:SPAN], feats[-SPAN:] * low_mask[-SPAN:])
    shards = gathered(jnp.pad(kernel, ((0, layout.in_pad - layout.in_rows), (0, LANES - TAPS))), "fsdp")
    (packed,) = call(
        functools.partial(pack_kernel, layout),
        [((layout.rows, LANES), BF16)],
        (in_proj, in_bias[None], out_proj, norm_gain[None], norm_shift[None], out_bias[None]),
        [WHOLE] * 6,
        [pltpu.VMEM((layout.in_pad, hidden_pad), F32), pltpu.VMEM((layout.out_pad, padded), F32)],
        name="pack",
    )
    packed = gathered(packed, "fsdp")

    paired_shape = (blocks, row_pairs, planes_in, PAD, 4 * HALF)
    rims_shape = (blocks, RIM_PAIRS, planes_in, PAD, 4 * HALF)
    plane_shape = (height, FINE, PAD, padded)
    mask_shape = (height, FINE, PAD, LANES)
    natural_shape = (height, width, channels)
    stage = pltpu.VMEM((2, tile_count, 2, stage_rows, LANES), F32)
    paired, gbranch, mask, masked, upstream = call(
        prepare_kernel,
        [(paired_shape, BF16), (plane_shape, BF16), (mask_shape, F32), (natural_shape, BF16), (natural_shape, BF16)],
        (feats, cot, land),
        [WHOLE] * 3,
        [
            stage,
            pltpu.VMEM((2, 1 + tile_count, stage_rows, LANES), F32),
            pltpu.VMEM((round_up(height, LANES), round_up(width, LANES)), F32),
        ],
        moved=20 * MIB,
        limit=32,
        name="prepare",
    )

    accs = pltpu.VMEM((2, block_rows, 4 * HALF), F32)
    weights = pltpu.VMEM((PASSES * PASSES * 4 * HALF, 4 * HALF), BF16)
    conv, stats, rims, taps = call(
        functools.partial(forward_kernel, channels),
        [(plane_shape, F32), ((8, padded), F32), (rims_shape, BF16), ((blocks, tap_rows, LANES), F32)],
        (paired, top, bottom, shards, mask),
        [WHOLE] * 5,
        [weights, accs, stage, pltpu.VMEM((blocks * HALF, LANES), F32)],
        flops=9 * 10**9,
        limit=28,
        name="forward",
    )
    w_in, w_out, vectors = call(
        functools.partial(assemble_kernel, layout),
        [((padded, hidden_pad), BF16), ((hidden_pad, padded), BF16), ((8, padded), F32)],
        (packed,),
        [WHOLE],
        [pltpu.VMEM((padded, hidden_pad), F32), pltpu.VMEM((hidden_pad, padded), F32)],
        name="assemble",
    )

    stats = butterfly(stats[:3], merge_stats)
    count = jnp.maximum(stats[2], 1.0)
    mean = stats[0]
    inverse = lax.rsqrt(stats[1] / count + EPSILON)
    gain, shift = vectors[0], vectors[1]
    zero = jnp.zeros_like(mean)
    vec = jnp.stack([mean, inverse, gain, shift, zero, zero, zero, zero])

    rows = 3 if height % 3 == 0 else height
    steps = height // rows
    part = rows * FINE * PAD
    by_row = lambda *rest: pl.BlockSpec((rows, *rest), lambda i: (i,) + (0,) * len(rest))
    by_cell = lambda lanes: pl.BlockSpec((part, lanes), lambda i: (i, 0))
    fixed = lambda *shape: pl.BlockSpec(shape, lambda i: (0,) * len(shape))
    output, act, ghid, gz, zvals, sums = call(
        functools.partial(pointwise_kernel, channels, hidden),
        [
            (natural_shape, BF16),
            ((cells, hidden_pad), BF16),
            ((cells, hidden_pad), BF16),
            (plane_shape, F32),
            ((cells, padded), BF16),
            ((8, padded), F32),
        ],
        (conv, gbranch, masked, mask, vec, w_in, w_out),
        [
            by_row(FINE, PAD, padded),
            by_row(FINE, PAD, padded),
            by_row(width, channels),
            by_row(FINE, PAD, LANES),
            fixed(8, padded),
            fixed(padded, hidden_pad),
            fixed(hidden_pad, padded),
        ],
        [pltpu.VMEM((rows, tile_count, round_up(FINE * PAD, 8), LANES), F32)],
        flops=14 * 10**9,
        grid=(steps,),
        out_specs=[
            by_row(width, channels),
            by_cell(hidden_pad),
            by_cell(hidden_pad),
            by_row(FINE, PAD, padded),
            by_cell(padded),
            fixed(8, padded),
        ],
        limit=32,
        name="pointwise",
    )

    grad_rows = round_up(channels + 1, 16)
    (grad_out,) = call(
        out_grads_kernel,
        [((grad_rows, hidden_pad), F32)],
        (gbranch.reshape(cells, padded), act),
        [WHOLE] * 2,
        flops=3 * 10**9,
        limit=28,
        name="out_grads",
    )
    (packed_grads,) = call(
        functools.partial(in_grads_kernel, channels, hidden),
        [((shares, layout.rows, LANES), BF16)],
        (zvals, ghid, grad_out),
        [WHOLE] * 3,
        [pltpu.VMEM((grad_rows, hidden_pad), F32)],
        flops=3 * 10**9,
        limit=32,
        name="in_grads",
    )
    sums = butterfly(sums[:2], add)
    grad_gain, grad_shift = sums[0], sums[1]
    scaled = inverse * gain
    gvec = jnp.stack([mean, inverse, scaled, scaled * grad_shift / count, scaled * grad_gain / count, zero, zero, zero])
    edges, gpaired, grad_taps = call(
        functools.partial(gradient_kernel, channels, real),
        [
            ((2, SPAN, FINE, PAD, padded), BF16),
            (paired_shape, BF16),
            ((tile_count, tap_rows, LANES), F32),
        ],
        (gz, conv, mask, gvec, paired, rims, jnp.asarray(tap_selectors(tap_rows))),
        [WHOLE] * 7,
        [pltpu.VMEM((blocks, block_rows, 4 * HALF), BF16)],
        flops=9 * 10**9,
        limit=36,
        name="gradient",
    )
    gtop, gbottom = rims_of(edges[0], edges[1])
    result = None
    for t in range(tile_count):
        column = pl.BlockSpec((height, width, LANES), lambda i, t=t: (0, 0, t))
        operands = (gpaired, gtop, gbottom, taps, upstream, mask)
        specs = [WHOLE] * 4 + [column, WHOLE]
        if result is not None:
            operands, specs = operands + (result,), specs + [HBM]
        result = pl.pallas_call(
            functools.partial(backward_kernel, t, real),
            out_shape=jax.ShapeDtypeStruct(natural_shape, BF16),
            grid=(1,),
            in_specs=specs,
            out_specs=column,
            scratch_shapes=[
                pltpu.VMEM((2, RIM_PAIRS, planes_in, PAD, 4 * HALF), BF16),
                weights,
                accs,
                pltpu.VMEM((2, round_up(FINE * PAD, 8), LANES), F32),
            ],
            input_output_aliases={} if result is None else {6: 0},
            compiler_params=pltpu.CompilerParams(vmem_limit_bytes=24 * MIB),
            cost_estimate=pl.CostEstimate(flops=4 * 10**9, bytes_accessed=10 * MIB, transcendentals=0),
            name="backward",
        )(*operands)

    share = summed_share(packed_grads)
    grad_in, grad_in_bias, grad_out, grad_out_bias = call(
        functools.partial(finish_kernel, channels, hidden),
        [
            ((layout.in_rows, hidden), F32),
            ((1, layout.out_rows), F32),
            ((layout.out_rows, channels), F32),
            ((1, layout.in_rows), F32),
        ],
        (share,),
        [WHOLE],
        name="finish",
    )
    grad_taps = butterfly(grad_taps, add)
    grad_taps = jnp.swapaxes(grad_taps[:, :TAPS], 1, 2).reshape(-1, TAPS)[:channels]
    return (
        output[None, None],
        result[None, None],
        own_share(grad_taps),
        own_share(grad_gain[:channels]),
        own_share(grad_shift[:channels]),
        grad_in,
        grad_in_bias[0],
        grad_out,
        grad_out_bias[0],
    )


def solution(mesh):
    spread = P("dp", "fsdp", None, None, None)
    split = P("fsdp", None)
    line = P("fsdp")
    return jax.shard_map(
        local,
        mesh=mesh,
        in_specs=(spread, P(), spread, split, line, line, split, line, split, line),
        out_specs=(spread, spread, split, line, line, split, line, split, line),
        check_vma=False,
    )
```

```python
import functools

import jax
import jax.numpy as jnp
import numpy as np
from jax import lax
from jax.experimental import pallas as pl
from jax.experimental.pallas import tpu as pltpu
from jax.sharding import PartitionSpec as P

KW = 7
SPAN = KW // 2
TILES = 8
EPSILON = 1e-05

LANES = 128
HALF = 64
FINE = 12
PAD = 16
PASSES = (KW + 1) // 2
TAPS = KW * KW
RIM_PAIRS = 4
BASE = 8

F32 = jnp.float32
BF16 = jnp.bfloat16
MIB = 2**20
WHOLE = pl.BlockSpec(memory_space=pltpu.VMEM)
HBM = pl.BlockSpec(memory_space=pl.ANY)


def round_up(value, step):
    return -(-value // step) * step


def call(kernel, outs, operands, in_specs, scratch=(), flops=0, moved=0, grid=None, out_specs=None, limit=10, aliases=None, name=None):
    extra = {} if grid is None else {"grid": grid}
    return pl.pallas_call(
        kernel,
        out_shape=[jax.ShapeDtypeStruct(shape, dtype) for shape, dtype in outs],
        in_specs=in_specs,
        out_specs=[WHOLE] * len(outs) if out_specs is None else out_specs,
        scratch_shapes=list(scratch),
        input_output_aliases=aliases or {},
        compiler_params=pltpu.CompilerParams(vmem_limit_bytes=limit * MIB),
        cost_estimate=pl.CostEstimate(flops=flops, bytes_accessed=moved, transcendentals=0),
        name=name,
        **extra,
    )(*operands)


def low_half(rows):
    return lax.broadcasted_iota(jnp.int32, (rows, LANES), 1) < HALF


def swap(value):
    return pltpu.roll(value, HALF, 1)


def tiles_of(channels):
    return [(t, min(LANES, channels - t * LANES)) for t in range(-(-channels // LANES))]


def mask_of_row(turned, row):
    chosen = lax.broadcasted_iota(jnp.int32, (LANES, LANES), 0) == row
    return jnp.dot(turned, jnp.where(chosen, 1.0, 0.0).astype(BF16), preferred_element_type=F32)


def stage_row(stage, values, width):
    lanes = values.shape[1]
    stage[0, BASE : BASE + width, :lanes] = values
    stage[0, BASE - SPAN : BASE, :lanes] = values[width - SPAN :]
    stage[0, BASE + width : BASE + width + SPAN, :lanes] = values[:SPAN]
    stage[1] = swap(stage[0])


def plane(stage, which, start):
    return stage[which, pl.ds(start, PAD, stride=FINE), :]


def place_row(paired, stage, tile, blocks, pair, side):
    low = low_half(PAD)
    lanes = pl.ds(side * LANES, LANES)
    for k in range((FINE + 2 * SPAN) // 2):
        start = BASE - SPAN + 2 * k
        paired[2 * tile, pair, k, :, lanes] = jnp.where(
            low, plane(stage, 0, start), plane(stage, 1, start + 1)
        ).astype(BF16)
        if 2 * tile + 1 < blocks:
            paired[2 * tile + 1, pair, k, :, lanes] = jnp.where(
                low, plane(stage, 1, start), plane(stage, 0, start + 1)
            ).astype(BF16)


def place_natural(paired, stage, source, channels, width, blocks, pair, side, factor=None):
    for t, lanes in tiles_of(channels):
        values = source(t * LANES, t * LANES + lanes).astype(F32)
        if factor is not None:
            values = values * factor[:, :lanes]
        buffer = stage.at[side, t]
        stage_row(buffer, values, width)
        place_row(paired, buffer, t, blocks, pair, side)


def rim_rows(height):
    inner = (height + 2 * SPAN) // 2 - RIM_PAIRS // 2
    for index in range(SPAN):
        yield 0, index, index // 2, index % 2
    for index in range(SPAN):
        row = SPAN + height + index
        yield 1, index, row // 2 - inner + RIM_PAIRS // 2, row % 2


def build_weights(weights, taps, block, flip):
    lane = lax.broadcasted_iota(jnp.int32, (HALF, LANES), 1)
    sub = lax.broadcasted_iota(jnp.int32, (HALF, LANES), 0)
    diagonal = lax.rem(lane, HALF) == sub
    low = low_half(1)
    zero = jnp.zeros((1, LANES), F32)

    def tap_row(a, b):
        if not (0 <= a < KW and 0 <= b < KW):
            return zero
        index = (KW - 1 - a) * KW + KW - 1 - b if flip else a * KW + b
        return taps[block, index : index + 1, :]

    for m in range(PASSES):
        for s in range(PASSES):
            for place in range(4):
                pr, pj = divmod(place, 2)
                for qr in range(2):
                    a, b = 2 * m + pr - qr, 2 * s + pj
                    row = jnp.where(low, tap_row(a, b), tap_row(a, b - 1))
                    weights[
                        (m * PASSES + s) * 4 * HALF + place * HALF : (m * PASSES + s) * 4 * HALF + (place + 1) * HALF,
                        qr * LANES : (qr + 1) * LANES,
                    ] = jnp.where(diagonal, row, 0.0).astype(BF16)


def pass_rows(paired, rims, block, m, s, pairs):
    places = pl.ds(s, FINE // 2)
    inner = (RIM_PAIRS // 2, pairs + PASSES - 1 - RIM_PAIRS // 2)
    pieces = [rims[block, i, places] for i in range(m, inner[0])]
    pieces.append(paired[block, max(m, inner[0]) : min(m + pairs, inner[1]), places])
    pieces += [rims[block, i - inner[1] + RIM_PAIRS // 2, places] for i in range(inner[1], m + pairs)]
    return jnp.concatenate([piece.reshape(-1, 4 * HALF) for piece in pieces], axis=0)


def convolve_block(paired, rims, weights, block, pairs):
    rows = jnp.concatenate(
        [pass_rows(paired, rims, block, m, s, pairs) for m in range(PASSES) for s in range(PASSES)], axis=1
    )
    return jnp.dot(rows, weights[...], preferred_element_type=F32)


def split_blocks(lower, upper, start, side):
    low = low_half(PAD)
    rows, lanes = pl.ds(start, PAD), pl.ds(side * LANES, LANES)
    first = lower[rows, lanes]
    if upper is None:
        return first, swap(first)
    second = upper[rows, lanes]
    return jnp.where(low, first, swap(second)), jnp.where(low, swap(first), second)


def begin_kernel(
    layout, first, last, land_mask, kernel, in_proj, in_bias, out_proj, gain, shift, out_bias,
    top, bottom, land, shard, packed, table, wide, tall,
):
    count, width, channels = first.shape
    height = land.shape[0]
    tile_index = lax.axis_index("dp") % TILES
    spots = (height, land_mask.shape[0])
    wanted = lax.broadcasted_iota(jnp.int32, spots, 0) + tile_index * height
    chosen = jnp.where(lax.broadcasted_iota(jnp.int32, spots, 1) == wanted, 1.0, 0.0).astype(BF16)
    ocean = land_mask[...].astype(F32).astype(BF16)
    land[...] = jnp.dot(chosen, ocean, preferred_element_type=F32)
    table[...] = jnp.zeros_like(table)
    table[:height, :width] = land[...]
    turned = table[...].T[:width].astype(BF16)
    for source, out, start in ((first, top, 0), (last, bottom, height - count)):
        for i in range(count):
            factor = mask_of_row(turned, start + i)
            for t, lanes in tiles_of(channels):
                piece = pl.ds(t * LANES, lanes)
                out[i, :, piece] = (source[i, :, piece].astype(F32) * factor[:, :lanes]).astype(BF16)
    wide[...] = jnp.zeros_like(wide)
    wide[: kernel.shape[0], : kernel.shape[1]] = kernel[...].astype(F32)
    shard[...] = wide[:, :LANES].astype(BF16)
    pack_parameters(layout, in_proj, in_bias, out_proj, gain, shift, out_bias, packed, wide, tall)


def prepare_kernel(feats, cot, land, paired, gbranch, mask, masked, upstream, stage, plain, table):
    height, width = land.shape
    channels = feats.shape[-1]
    blocks = paired.shape[0]
    step = pl.program_id(0)

    @pl.when(step == 0)
    def _():
        stage[...] = jnp.zeros_like(stage)
        plain[...] = jnp.zeros_like(plain)
        table[...] = jnp.zeros_like(table)
        table[:height, :width] = land[...]

    turned = table[...].T[:width].astype(BF16)
    for side in range(2):
        row = 2 * step + side
        factor = mask_of_row(turned, row)
        rows = pl.ds(BASE, width)
        plain[side, 0, rows, :] = factor
        for t, lanes in tiles_of(channels):
            piece = pl.ds(t * LANES, lanes)
            values = feats[side, :, piece].astype(F32) * factor[:, :lanes]
            masked[row, :, piece] = values.astype(BF16)
            buffer = stage.at[side, t]
            stage_row(buffer, values, width)
            place_row(paired, buffer, t, blocks, step + (SPAN + side) // 2, (SPAN + side) % 2)
            values = cot[side, :, piece].astype(F32) * factor[:, :lanes]
            upstream[row, :, piece] = values.astype(BF16)
            plain[side, 1 + t, rows, :lanes] = values
        for r in range(FINE):
            mask[row, r] = plain[side, 0, pl.ds(BASE + r, PAD, stride=FINE), :]
            for t, _unused in tiles_of(channels):
                gbranch[row, r, :, t * LANES : (t + 1) * LANES] = plain[
                    side, 1 + t, pl.ds(BASE + r, PAD, stride=FINE), :
                ].astype(BF16)


def forward_kernel(channels, paired, top, bottom, shards, mask, conv, stats, rims, taps, weights, accs, stage, table):
    height = conv.shape[0]
    blocks, pairs = paired.shape[0], height // 2
    width = top.shape[1]
    share = channels // shards.shape[0]
    stage[...] = jnp.zeros_like(stage)
    table[...] = jnp.zeros_like(table)
    for f in range(shards.shape[0]):
        table[f * share : (f + 1) * share] = shards[f].astype(F32)[:share]
    for block in range(blocks):
        piece = table[block * HALF : (block + 1) * HALF]
        taps[block] = jnp.concatenate([piece, piece], axis=0).T[: taps.shape[1]]
    last = pairs + PASSES - 1
    first_half = (SPAN % 2) * LANES
    last_half = ((SPAN + height - 1) % 2) * LANES
    rims[:, 1, :, :, first_half : first_half + LANES] = paired[:, 1, :, :, first_half : first_half + LANES]
    rims[:, 2, :, :, last_half : last_half + LANES] = paired[:, last - 2, :, :, last_half : last_half + LANES]
    for below, index, pair, side in rim_rows(height):
        source = bottom if below else top
        place_natural(
            rims, stage, lambda a, b, source=source, index=index: source[index, :, a:b], channels, width, blocks, pair, side
        )
    for t, _ in tiles_of(channels):
        lanes = pl.ds(t * LANES, LANES)
        has_upper = 2 * t + 1 < blocks
        for half in range(1 + has_upper):
            build_weights(weights, taps, 2 * t + half, False)
            accs[half] = convolve_block(paired, rims, weights, 2 * t + half, pairs)

        def planes(h, k, side, has_upper=has_upper):
            return split_blocks(accs.at[0], accs.at[1] if has_upper else None, (h * (FINE // 2) + k) * PAD, side)

        zero = jnp.zeros((PAD, LANES), F32)
        total, count = zero, zero
        for k in range(FINE // 2):
            even, odd = planes(0, k, 0)
            total = total + (mask[0, 2 * k] * even + mask[0, 2 * k + 1] * odd)
            count = count + (mask[0, 2 * k] + mask[0, 2 * k + 1])
        near = jnp.sum(total, axis=0, keepdims=True) / jnp.maximum(jnp.sum(count, axis=0, keepdims=True), 1.0)

        def spread(h, sums, lanes=lanes, planes=planes, near=near):
            sums = list(sums)
            for k in range(FINE // 2):
                for side in range(2):
                    row = 2 * h + side
                    for odd, value in enumerate(planes(h, k, side)):
                        r = 2 * k + odd
                        conv[row, r, :, lanes] = value
                        weight = mask[row, r]
                        away = value - near
                        part = weight * away
                        at = 3 * (2 * side + odd)
                        sums[at] = sums[at] + part
                        sums[at + 1] = sums[at + 1] + part * away
                        sums[at + 2] = sums[at + 2] + weight
            return tuple(sums)

        sums = lax.fori_loop(0, pairs, spread, (zero,) * 12)
        total, square, count = (
            jnp.sum(sums[i] + sums[i + 3] + sums[i + 6] + sums[i + 9], axis=0, keepdims=True) for i in range(3)
        )
        shift = total / jnp.maximum(count, 1.0)
        stats[0:1, lanes] = near + shift
        stats[1:2, lanes] = jnp.maximum(square - total * shift, 0.0)
        stats[2:3, lanes] = count


def pointwise_kernel(
    channels, real_units, conv, gbranch, feats, mask, vec, w_in, w_out,
    output, act_out, ghid_out, gz_out, z_out, sums, stage,
):
    rows, width = feats.shape[0], feats.shape[1]
    padded = conv.shape[-1]
    cells = rows * FINE * PAD
    hidden_units = act_out.shape[1]
    step = pl.program_id(0)

    @pl.when(step == 0)
    def _():
        sums[...] = jnp.zeros_like(sums)

    one_lane = lax.broadcasted_iota(jnp.int32, (1, padded), 1) == channels
    mean, inverse, gain, shift = (vec[i : i + 1, :] for i in range(4))
    normed = (conv[...].reshape(cells, padded) - mean) * inverse
    zvals = jnp.where(one_lane, 1.0, gain * normed + shift).astype(BF16)
    z_out[...] = zvals
    upstream = gbranch[...].reshape(cells, padded)
    branch = jnp.zeros((cells, padded), F32)
    gz = jnp.zeros((cells, padded), F32)
    chunk = 2 * LANES
    across = (((1,), (1,)), ((), ()))
    c0 = 0.7978845608028654
    c1 = 0.044715 * c0
    for start in range(0, hidden_units, chunk):
        span = pl.ds(start, chunk)
        hidden = jnp.dot(zvals, w_in[:, span], preferred_element_type=F32)
        gact = lax.dot_general(upstream, w_out[span, :], across, preferred_element_type=F32)
        square = hidden * hidden
        bent = jnp.tanh(hidden * (c0 + c1 * square))
        half = 0.5 * hidden
        act = half + half * bent
        slope = (0.5 + 0.5 * bent) + half * (1.0 - bent * bent) * (c0 + (3.0 * c1) * square)
        ghid = (gact * slope).astype(BF16)
        act = act.astype(BF16)
        if start + chunk > real_units:
            lane = lax.broadcasted_iota(jnp.int32, (1, chunk), 1)
            act = jnp.where(lane == real_units - start, jnp.ones((), BF16), act)
        act_out[:, span] = act
        ghid_out[:, span] = ghid
        branch = branch + jnp.dot(act, w_out[span, :], preferred_element_type=F32)
        gz = gz + lax.dot_general(ghid, w_in[:, span], across, preferred_element_type=F32)
    gz_out[...] = gz.reshape(gz_out.shape)
    sums[0:1, :] += jnp.sum(gz * normed, axis=0, keepdims=True)
    sums[1:2, :] += jnp.sum(gz, axis=0, keepdims=True)
    for row in range(rows):
        for t, lanes in tiles_of(channels):
            for r in range(FINE):
                start = (row * FINE + r) * PAD
                values = branch[start : start + PAD, t * LANES : (t + 1) * LANES] * mask[row, r]
                stage[row, t, pl.ds(r, PAD, stride=FINE), :] = values
            piece = pl.ds(t * LANES, lanes)
            values = feats[row, :, piece].astype(F32) + stage[row, t, 0:width, :lanes]
            output[row, :, piece] = values.astype(BF16)


def out_grads_kernel(gbranch, act, grad):
    grad[...] = turned_product(gbranch, act, grad.shape[0])


def turned_product(left, right, rows):
    return lax.dot_general(left[:, :rows], right[...], (((0,), (0,)), ((), ())), preferred_element_type=F32)


def in_grads_kernel(channels, hidden, zvals, ghid, grad_out, packed, grad_in):
    grad_in[...] = turned_product(zvals, ghid, grad_in.shape[0])
    shares, _, _ = packed.shape
    layout = Packing(channels, hidden, shares)
    last = layout.in_tiles - 1
    lane = lax.broadcasted_iota(jnp.int32, (1, LANES), 1)
    for j in range(shares):
        rows = slice(j * layout.in_rows, (j + 1) * layout.in_rows)
        fill = jnp.zeros((layout.in_pad - layout.in_rows, LANES), F32)
        for t in range(layout.in_tiles):
            lanes = slice(t * LANES, (t + 1) * LANES)
            tile = grad_in[rows, lanes]
            if t == last:
                tile = jnp.where(lane == hidden - t * LANES, grad_out[rows, lanes], tile)
            packed[j, t * layout.in_pad : (t + 1) * layout.in_pad] = jnp.concatenate([tile, fill], axis=0)
        start = j * layout.out_rows
        aligned = start // LANES * LANES
        stop = min(aligned + (layout.out_tiles + 1) * LANES, grad_out.shape[1])
        spot = lax.broadcasted_iota(jnp.int32, (layout.out_pad, 1), 0)
        part = jnp.where(
            spot == channels, grad_in[: layout.out_pad, aligned:stop], grad_out[: layout.out_pad, aligned:stop]
        )
        if start != aligned:
            part = pltpu.roll(part, stop - start, 1)
        for u in range(layout.out_tiles):
            base = layout.out_base + u * layout.out_pad
            packed[j, base : base + layout.out_pad] = part[:, u * LANES : (u + 1) * LANES]
        packed[j, layout.small_base :] = jnp.zeros((layout.rows - layout.small_base, LANES), F32)


def finish_kernel(channels, hidden, packed, grad_in, grad_in_bias, grad_out, grad_out_bias):
    layout = Packing(channels, hidden, channels // grad_in.shape[0])
    for t in range(layout.in_tiles):
        stop = min((t + 1) * LANES, hidden)
        tile = packed[t * layout.in_pad : (t + 1) * layout.in_pad].astype(F32)
        grad_in[:, t * LANES : stop] = tile[: layout.in_rows, : stop - t * LANES]
    tall = jnp.concatenate([tile, jnp.zeros((LANES - layout.in_pad, LANES), F32)], axis=0).T
    at = hidden - (layout.in_tiles - 1) * LANES
    grad_out_bias[...] = tall[at : at + 1, : layout.in_rows]
    for u in range(layout.out_tiles):
        base = layout.out_base + u * layout.out_pad
        tile = packed[base : base + layout.out_pad].astype(F32)
        stop = min((u + 1) * LANES, layout.out_rows)
        count = stop - u * LANES
        grad_in_bias[:, u * LANES : stop] = tile[channels : channels + 1, :count]
        fill = jnp.zeros((round_up(layout.out_pad, LANES) - layout.out_pad, LANES), F32)
        grad_out[u * LANES : stop, :] = jnp.concatenate([tile, fill], axis=0).T[:count, :channels]


class Packing:
    def __init__(self, channels, hidden, shares):
        self.in_rows = channels // shares
        self.in_pad = round_up(self.in_rows, 16)
        self.in_tiles = -(-(hidden + 1) // LANES)
        self.out_rows = hidden // shares
        self.out_tiles = -(-self.out_rows // LANES)
        self.out_pad = round_up(max(channels + 1, self.out_rows), 16)
        self.out_base = self.in_pad * self.in_tiles
        self.small_base = self.out_base + self.out_pad * self.out_tiles
        self.small = self.out_tiles + 3
        self.rows = round_up(self.small_base + self.small, 32)


def pack_parameters(layout, in_proj, in_bias, out_proj, gain, shift, out_bias, packed, wide, tall):
    wide[...] = jnp.zeros_like(wide)
    tall[...] = jnp.zeros_like(tall)
    wide[: layout.in_rows, : in_proj.shape[1]] = in_proj[...].astype(F32)
    for t in range(layout.in_tiles):
        packed[t * layout.in_pad : (t + 1) * layout.in_pad] = wide[:, t * LANES : (t + 1) * LANES].astype(BF16)
    tall[: layout.out_rows, : out_proj.shape[1]] = out_proj[...].astype(F32)
    for u in range(layout.out_tiles):
        base = layout.out_base + u * layout.out_pad
        packed[base : base + layout.out_pad] = tall[:, u * LANES : (u + 1) * LANES].astype(BF16)
    wide[...] = jnp.zeros_like(wide)
    wide[0:1, : in_bias.shape[1]] = in_bias[...].astype(F32)
    for i, small in enumerate((gain, shift, out_bias)):
        wide[i + 1 : i + 2, : small.shape[1]] = small[...].astype(F32)
    rows = [wide[0:1, u * LANES : (u + 1) * LANES] for u in range(layout.out_tiles)]
    rows += [wide[i + 1 : i + 2, :LANES] for i in range(3)]
    rows.append(jnp.zeros((layout.rows - layout.small_base - layout.small, LANES), F32))
    packed[layout.small_base :] = jnp.concatenate(rows, axis=0).astype(BF16)


def assemble_kernel(layout, packed, w_in, w_out, vectors, wide, tall):
    wide[...] = jnp.zeros_like(wide)
    tall[...] = jnp.zeros_like(tall)
    shares = packed.shape[0]
    channels, hidden = layout.in_rows * shares, layout.out_rows * shares
    in_bias = jnp.zeros((8, wide.shape[1]), F32)
    smalls = [jnp.zeros((8, tall.shape[1]), F32)] * 3
    for f in range(shares):
        for t in range(layout.in_tiles):
            tile = packed[f, t * layout.in_pad : (t + 1) * layout.in_pad].astype(F32)
            wide[f * layout.in_rows : (f + 1) * layout.in_rows, t * LANES : (t + 1) * LANES] = tile[: layout.in_rows]
        for u in range(layout.out_tiles):
            base = layout.out_base + u * layout.out_pad
            tile = packed[f, base : base + layout.out_pad].astype(F32)
            tall[f * layout.out_rows : (f + 1) * layout.out_rows, u * LANES : (u + 1) * LANES] = tile[: layout.out_rows]
        small = packed[f, layout.small_base :].astype(F32)

        def spread(first, count, lanes, turn):
            pieces = [small[first + u : first + u + 1] for u in range(count)]
            pieces.append(jnp.zeros((1, lanes - count * LANES), F32))
            row = jnp.broadcast_to(jnp.concatenate(pieces, axis=1), (8, lanes))
            return pltpu.roll(row, turn, 1) if turn else row

        in_bias = in_bias + spread(0, layout.out_tiles, wide.shape[1], f * layout.out_rows)
        smalls = [
            total + spread(layout.out_tiles + i, 1, tall.shape[1], f * layout.in_rows)
            for i, total in enumerate(smalls)
        ]
    wide[channels : channels + 1] = in_bias[:1]
    tall[hidden : hidden + 1] = smalls[2][:1]
    w_in[...] = wide[...].astype(BF16)
    w_out[...] = tall[...].astype(BF16)
    vectors[...] = jnp.concatenate([smalls[0][:1], smalls[1][:1], jnp.zeros((6, tall.shape[1]), F32)], axis=0)


def shifted_planes(values, real):
    out = []
    for r in range(-SPAN, FINE + SPAN):
        value = values[r % FINE]
        if r < 0:
            value = jnp.concatenate([value[real - 1 : real], value[: PAD - 1]], axis=0)
        elif r >= FINE:
            value = jnp.concatenate([value[1:real], value[:1], value[: PAD - real]], axis=0)
        out.append(value)
    return out


def join_planes(first, second):
    low = low_half(PAD)
    return (
        jnp.where(low, first, swap(second)).astype(BF16),
        jnp.where(low, swap(first), second).astype(BF16),
    )


def place_planes(paired, planes, tile, blocks, pair, side):
    out_lanes = pl.ds(side * LANES, LANES)
    for k in range(len(planes) // 2):
        for half, value in enumerate(join_planes(planes[2 * k], planes[2 * k + 1])):
            if 2 * tile + half < blocks:
                paired[2 * tile + half, pair, k, :, out_lanes] = value


def arrange_kernel(channels, real, gz, conv, mask, vec, edges, gpaired, own):
    height = gz.shape[0]
    blocks, pairs = own.shape[0], height // 2

    def arrange(h, _):
        for t, _unused in tiles_of(channels):
            lanes = pl.ds(t * LANES, LANES)
            mean, inverse, scaled, bias, slope = (vec[i : i + 1, lanes] for i in range(5))
            for side in range(2):
                row = 2 * h + side
                values = []
                for r in range(FINE):
                    normed = (conv[row, r, :, lanes] - mean) * inverse
                    values.append(scaled * gz[row, r, :, lanes] - mask[row, r] * (bias + normed * slope))
                out_lanes = pl.ds(side * LANES, LANES)
                for k in range(FINE // 2):
                    rows = pl.ds((h * (FINE // 2) + k) * PAD, PAD)
                    for half, value in enumerate(join_planes(values[2 * k], values[2 * k + 1])):
                        if 2 * t + half < blocks:
                            own[2 * t + half, rows, out_lanes] = value
                place_planes(
                    gpaired, shifted_planes(values, real), t, blocks, h + (SPAN + side) // 2, (SPAN + side) % 2
                )
                for edge, near in ((0, row < SPAN), (1, row >= height - SPAN)):

                    @pl.when(near)
                    def _(edge=edge, row=row, values=values, lanes=lanes):
                        place = row - (height - SPAN) * edge
                        for r in range(FINE):
                            edges[edge, place, r, :, lanes] = values[r].astype(BF16)

        return 0

    lax.fori_loop(0, pairs, arrange, 0)


def taps_kernel(tile, own, paired, rims, select, grad_taps):
    blocks, pairs = own.shape[0], paired.shape[1] - PASSES + 1
    lane = lax.broadcasted_iota(jnp.int32, (HALF, 2 * LANES), 1)
    sub = lax.broadcasted_iota(jnp.int32, (HALF, 2 * LANES), 0)
    diagonal = lax.rem(lane, HALF) == sub
    low = low_half(grad_taps.shape[0])
    totals = []
    for block in range(2 * tile, min(2 * tile + 2, blocks)):
        turned = own[block].T
        found = []
        for m in range(PASSES):
            for s in range(PASSES):
                product = jnp.dot(turned, pass_rows(paired, rims, block, m, s, pairs), preferred_element_type=F32)
                for q in range(4):
                    part = product[q * HALF : (q + 1) * HALF]
                    found.append(jnp.sum(jnp.where(diagonal, part, 0.0), axis=0, keepdims=True))
        found = jnp.concatenate(found, axis=0)
        total = None
        for place in range(4):
            group = jnp.dot(select[place], found, preferred_element_type=F32, precision=lax.Precision.HIGHEST)
            group = group[:, (place // 2) * LANES : (place // 2 + 1) * LANES]
            if place % 2:
                group = swap(group)
            total = group if total is None else total + group
        totals.append(total)
    second = swap(totals[1]) if len(totals) > 1 else jnp.zeros_like(totals[0])
    grad_taps[...] = jnp.where(low, totals[0], second)


def backward_kernel(tile, real, gpaired, top, bottom, taps, cot, mask, *rest):
    result, rims, weights, accs, stage = rest[-5:]
    height, width = cot.shape[0], cot.shape[1]
    blocks, pairs = gpaired.shape[0], height // 2
    last = pairs + PASSES - 1
    first_half = (SPAN % 2) * LANES
    last_half = ((SPAN + height - 1) % 2) * LANES
    has_upper = 2 * tile + 1 < blocks
    for half in range(1 + has_upper):
        source = gpaired.at[2 * tile + half]
        rims[half, 1, :, :, first_half : first_half + LANES] = source[1, :, :, first_half : first_half + LANES]
        rims[half, 2, :, :, last_half : last_half + LANES] = source[last - 2, :, :, last_half : last_half + LANES]
    for below, index, pair, side in rim_rows(height):
        source = bottom if below else top
        values = [source[index, r, :, tile * LANES : (tile + 1) * LANES].astype(F32) for r in range(FINE)]
        place_planes(rims, shifted_planes(values, real), 0, 1 + has_upper, pair, side)
    for half in range(1 + has_upper):
        block = 2 * tile + half
        build_weights(weights, taps, block, True)
        accs[half] = convolve_block(gpaired.at[block : block + 1], rims.at[half : half + 1], weights, 0, pairs)

    def spread(h, _):
        for side in range(2):
            row = 2 * h + side
            for k in range(FINE // 2):
                even, odd = split_blocks(
                    accs.at[0], accs.at[1] if has_upper else None, (h * (FINE // 2) + k) * PAD, side
                )
                stage[side, pl.ds(2 * k, PAD, stride=FINE), :] = even * mask[row, 2 * k]
                stage[side, pl.ds(2 * k + 1, PAD, stride=FINE), :] = odd * mask[row, 2 * k + 1]
            values = cot[row].astype(F32) + stage[side, 0:width]
            result[row] = values.astype(BF16)
        return 0

    lax.fori_loop(0, pairs, spread, 0)


def bits(size):
    bit = 1
    while bit < size:
        yield bit
        bit *= 2


def swapped(value, axis, bit):
    size = lax.axis_size(axis)
    return lax.ppermute(value, axis, [(i, i ^ bit) for i in range(size)])


def side_of(axis, bit):
    return lax.axis_index(axis) // bit % 2


def ring_bits(*axes):
    return [(axis, bit) for axis in axes for bit in bits(lax.axis_size(axis))]


def tied(*values):
    return lax.optimization_barrier(values)


def add(mine, other):
    return (mine.astype(F32) + other.astype(F32)).astype(mine.dtype)


def merge_stats(mine, other):
    count = mine[2:3] + other[2:3]
    safe = jnp.maximum(count, 1.0)
    mean = (mine[0:1] * mine[2:3] + other[0:1] * other[2:3]) / safe
    away = mine[0:1] - other[0:1]
    spread = mine[1:2] + other[1:2] + away * away * (mine[2:3] * other[2:3] / safe)
    return jnp.concatenate([mean, spread, count], axis=0)


def joined(value, other, axis, bit):
    first = side_of(axis, bit) == 0
    pair = [jnp.where(first, value, other), jnp.where(first, other, value)]
    return jnp.stack(pair, axis=1).reshape(-1, *value.shape[1:])


def keep_and_send(value, axis, bit, dim):
    side = side_of(axis, bit)
    return (
        lax.dynamic_index_in_dim(value, side, dim, keepdims=False),
        lax.dynamic_index_in_dim(value, 1 - side, dim, keepdims=False),
    )


class Summing:
    def __init__(self, value):
        self.value = value
        self.moves = []
        self.moves += [("share", axis, bit) for axis, bit in ring_bits("fsdp")]
        over = ring_bits("dp")
        self.moves += [("half", axis, bit) for axis, bit in over]
        self.moves += [("join", axis, bit) for axis, bit in reversed(over)]

    def start(self):
        kind, axis, bit = self.moves.pop(0)
        if kind == "join":
            if self.value.dtype == F32:
                self.value = self.value.astype(BF16)
            self.kept, sent = self.value, self.value
        elif kind == "share":
            value = self.value.reshape(-1, 2, *self.value.shape[-2:])
            self.kept, sent = keep_and_send(value, axis, bit, 1)
        else:
            value = self.value.reshape(2, -1, self.value.shape[-1])
            self.kept, sent = keep_and_send(value, axis, bit, 0)
        if kind != "join" and not (kind == "share" and bit == 1):
            sent = sent.astype(BF16)
        self.move = (kind, axis, bit)
        return swapped(sent, axis, bit)

    def finish(self, other):
        kind, axis, bit = self.move
        if kind == "join":
            first = side_of(axis, bit) == 0
            self.value = jnp.concatenate(
                [jnp.where(first, self.kept, other), jnp.where(first, other, self.kept)], axis=0
            )
        else:
            self.value = self.kept + other.astype(F32)


class Adding:
    def __init__(self, value, merge=add):
        self.value, self.merge = value, merge
        self.moves = ring_bits("fsdp", "dp")

    def start(self):
        return swapped(self.value, *self.moves.pop(0))

    def finish(self, other):
        self.value = self.merge(self.value, other)


def beside(work, *sums):
    running = [each for each in sums if each.moves]
    arriving = [each.start() for each in running]
    done = work() if work else ()
    arriving, done = lax.optimization_barrier((arriving, done))
    for each, other in zip(running, arriving):
        each.finish(other)
    return done


def rims_of(top_rows, bottom_rows):
    size = lax.axis_size("dp")
    down = [(i, i + 1) for i in range(size - 1) if (i + 1) % TILES]
    up = [(j, i) for i, j in down]
    return lax.ppermute(bottom_rows, "dp", down), lax.ppermute(top_rows, "dp", up)


def tap_selectors(rows):
    out = np.zeros((4, rows, PASSES * PASSES * 4), np.float32)
    for m in range(PASSES):
        for s in range(PASSES):
            for q in range(4):
                for p in range(4):
                    a = 2 * m + p // 2 - q // 2
                    b = 2 * s + p % 2 - q % 2
                    if 0 <= a < KW and 0 <= b < KW:
                        out[p, a * KW + b, (m * PASSES + s) * 4 + q] = 1.0
    return out


def own_share(value):
    share = value.shape[0] // lax.axis_size("fsdp")
    return lax.dynamic_slice_in_dim(value, lax.axis_index("fsdp") * share, share, 0)


def local(features, land_mask, cotangent, kernel, norm_gain, norm_shift, in_proj, in_bias, out_proj, out_bias):
    feats, cot = features[0, 0], cotangent[0, 0]
    height, width, channels = feats.shape
    hidden = in_proj.shape[1]
    shares = lax.axis_size("fsdp")
    padded = round_up(channels + 1, LANES)
    hidden_pad = round_up(hidden + 1, 2 * LANES)
    blocks = -(-channels // HALF)
    pairs = height // 2
    planes_in = (FINE + 2 * SPAN) // 2
    row_pairs = pairs + PASSES - 1
    cells = height * FINE * PAD
    block_rows = pairs * (FINE // 2) * PAD
    stage_rows = round_up(BASE + SPAN + FINE * PAD, 8)
    tile_count = len(tiles_of(channels))
    tap_rows = round_up(TAPS, 8)
    real = width // FINE
    layout = Packing(channels, hidden, shares)

    edge = lambda at: pl.BlockSpec((SPAN, width, channels), lambda i: (at, 0, 0))
    whole = lambda array: pl.BlockSpec(array.shape, lambda i: (0,) * array.ndim)
    natural_shape = (height, width, channels)
    edge_shape = (SPAN, width, channels)
    small = (kernel, in_proj, in_bias[None], out_proj, norm_gain[None], norm_shift[None], out_bias[None])
    first_rows, last_rows, land, shards, packed = call(
        functools.partial(begin_kernel, layout),
        [
            (edge_shape, BF16),
            (edge_shape, BF16),
            ((height, width), F32),
            ((layout.in_pad, LANES), BF16),
            ((layout.rows, LANES), BF16),
        ],
        (feats, feats, land_mask, *small),
        [edge(0), edge(height // SPAN - 1), whole(land_mask)] + [whole(v) for v in small],
        [
            pltpu.VMEM((round_up(height, LANES), round_up(width, LANES)), F32),
            pltpu.VMEM((layout.in_pad, hidden_pad), F32),
            pltpu.VMEM((layout.out_pad, padded), F32),
        ],
        grid=(1,),
        out_specs=[WHOLE] * 5,
        name="begin",
    )
    shards, packed = shards[None], packed[None]
    far = list(reversed(ring_bits("fsdp")))
    top, bottom = rims_of(first_rows, last_rows)
    shards_there, packed_there = swapped(shards, *far[0]), swapped(packed, *far[0])

    paired_shape = (blocks, row_pairs, planes_in, PAD, 4 * HALF)
    rims_shape = (blocks, RIM_PAIRS, planes_in, PAD, 4 * HALF)
    plane_shape = (height, FINE, PAD, padded)
    mask_shape = (height, FINE, PAD, LANES)
    stage = pltpu.VMEM((2, tile_count, 2, stage_rows, LANES), F32)
    paired, gbranch, mask, masked, upstream = call(
        prepare_kernel,
        [(paired_shape, BF16), (plane_shape, BF16), (mask_shape, F32), (natural_shape, BF16), (natural_shape, BF16)],
        (feats, cot, land),
        [pl.BlockSpec((2, width, channels), lambda i: (i, 0, 0))] * 2 + [whole(land)],
        [
            stage,
            pltpu.VMEM((2, 1 + tile_count, stage_rows, LANES), F32),
            pltpu.VMEM((round_up(height, LANES), round_up(width, LANES)), F32),
        ],
        moved=20 * MIB,
        limit=12,
        grid=(pairs,),
        out_specs=[WHOLE] * 5,
        name="prepare",
    )
    shards_there, packed_there, paired = tied(shards_there, packed_there, paired)
    shards, packed = joined(shards, shards_there, *far[0]), joined(packed, packed_there, *far[0])
    for axis, bit in far[1:]:
        shards = joined(shards, swapped(shards, axis, bit), axis, bit)
    packed_there = [swapped(packed, *far[1])] if far[1:] else []

    accs = pltpu.VMEM((2, block_rows, 4 * HALF), F32)
    weights = pltpu.VMEM((PASSES * PASSES * 4 * HALF, 4 * HALF), BF16)
    conv, stats, rims, taps = call(
        functools.partial(forward_kernel, channels),
        [(plane_shape, F32), ((8, padded), F32), (rims_shape, BF16), ((blocks, tap_rows, LANES), F32)],
        (paired, top, bottom, shards, mask),
        [WHOLE] * 5,
        [weights, accs, stage, pltpu.VMEM((blocks * HALF, LANES), F32)],
        flops=9 * 10**9,
        limit=12,
        name="forward",
    )
    packed_there, stats = tied(packed_there, stats)
    if far[1:]:
        packed = joined(packed, packed_there[0], *far[1])
    for axis, bit in far[2:]:
        packed = joined(packed, swapped(packed, axis, bit), axis, bit)
    assemble = lambda: call(
        functools.partial(assemble_kernel, layout),
        [((padded, hidden_pad), BF16), ((hidden_pad, padded), BF16), ((8, padded), F32)],
        (packed,),
        [WHOLE],
        [pltpu.VMEM((padded, hidden_pad), F32), pltpu.VMEM((hidden_pad, padded), F32)],
        name="assemble",
    )
    norm = Adding(stats[:3], merge_stats)
    w_in, w_out, vectors = beside(assemble, norm)
    while norm.moves:
        beside(None, norm)
    stats = norm.value
    count = jnp.maximum(stats[2], 1.0)
    mean = stats[0]
    inverse = lax.rsqrt(stats[1] / count + EPSILON)
    gain, shift = vectors[0], vectors[1]
    zero = jnp.zeros_like(mean)
    vec = jnp.stack([mean, inverse, gain, shift, zero, zero, zero, zero])

    rows = 3 if height % 3 == 0 else height
    steps = height // rows
    part = rows * FINE * PAD
    by_row = lambda *rest: pl.BlockSpec((rows, *rest), lambda i: (i,) + (0,) * len(rest))
    by_cell = lambda lanes: pl.BlockSpec((part, lanes), lambda i: (i, 0))
    fixed = lambda *shape: pl.BlockSpec(shape, lambda i: (0,) * len(shape))
    output, act, ghid, gz, zvals, sums = call(
        functools.partial(pointwise_kernel, channels, hidden),
        [
            (natural_shape, BF16),
            ((cells, hidden_pad), BF16),
            ((cells, hidden_pad), BF16),
            (plane_shape, F32),
            ((cells, padded), BF16),
            ((8, padded), F32),
        ],
        (conv, gbranch, masked, mask, vec, w_in, w_out),
        [
            by_row(FINE, PAD, padded),
            by_row(FINE, PAD, padded),
            by_row(width, channels),
            by_row(FINE, PAD, LANES),
            fixed(8, padded),
            fixed(padded, hidden_pad),
            fixed(hidden_pad, padded),
        ],
        [pltpu.VMEM((rows, tile_count, round_up(FINE * PAD, 8), LANES), F32)],
        flops=14 * 10**9,
        grid=(steps,),
        out_specs=[
            by_row(width, channels),
            by_cell(hidden_pad),
            by_cell(hidden_pad),
            by_row(FINE, PAD, padded),
            by_cell(padded),
            fixed(8, padded),
        ],
        limit=26,
        name="pointwise",
    )

    grad_rows = round_up(channels + 1, 16)
    norm = Adding(sums[:2])
    (grad_out,) = beside(
        lambda: call(
            out_grads_kernel,
            [((grad_rows, hidden_pad), F32)],
            (gbranch.reshape(cells, padded), act),
            [WHOLE] * 2,
            flops=3 * 10**9,
            limit=4,
            name="out_grads",
        ),
        norm,
    )
    (packed_grads,) = beside(
        lambda: call(
            functools.partial(in_grads_kernel, channels, hidden),
            [((shares, layout.rows, LANES), F32)],
            (zvals, ghid, grad_out),
            [WHOLE] * 3,
            [pltpu.VMEM((grad_rows, hidden_pad), F32)],
            flops=3 * 10**9,
            limit=8,
            name="in_grads",
        ),
        norm,
    )
    summing = Summing(packed_grads)
    beside(None, norm, summing)
    while norm.moves:
        beside(None, norm)
    grad_gain, grad_shift = norm.value[0], norm.value[1]
    scaled = inverse * gain
    gvec = jnp.stack([mean, inverse, scaled, scaled * grad_shift / count, scaled * grad_gain / count, zero, zero, zero])
    edges, gpaired, own = beside(
        lambda: call(
            functools.partial(arrange_kernel, channels, real),
            [
                ((2, SPAN, FINE, PAD, padded), BF16),
                (paired_shape, BF16),
                ((blocks, block_rows, 4 * HALF), BF16),
            ],
            (gz, conv, mask, gvec),
            [WHOLE] * 4,
            flops=10**8,
            moved=10 * MIB,
            limit=6,
            name="arrange",
        ),
        summing,
    )
    select = jnp.asarray(tap_selectors(tap_rows))
    gtop, gbottom = rims_of(edges[0], edges[1])
    grad_taps = []
    for t in range(tile_count):
        grad_taps += beside(
            lambda: call(
                functools.partial(taps_kernel, t),
                [((tap_rows, LANES), F32)],
                (own, paired, rims, select),
                [WHOLE] * 4,
                flops=4 * 10**9,
                limit=6,
                name="taps",
            ),
            summing,
        )
    gtop, gbottom, *grad_taps = tied(gtop, gbottom, *grad_taps)
    turn = Adding(jnp.stack(grad_taps))
    result = ()
    for t in range(tile_count):
        column = pl.BlockSpec((height, width, LANES), lambda i, t=t: (0, 0, t))
        result = beside(
            lambda: call(
                functools.partial(backward_kernel, t, real),
                [(natural_shape, BF16)],
                (gpaired, gtop, gbottom, taps, upstream, mask, *result),
                [WHOLE] * 4 + [column, WHOLE] + [HBM] * len(result),
                [
                    pltpu.VMEM((2, RIM_PAIRS, planes_in, PAD, 4 * HALF), BF16),
                    weights,
                    accs,
                    pltpu.VMEM((2, round_up(FINE * PAD, 8), LANES), F32),
                ],
                flops=4 * 10**9,
                limit=12,
                grid=(1,),
                out_specs=[column],
                aliases={6: 0} if result else {},
                name="backward",
            ),
            turn,
            summing,
        )
    while turn.moves or summing.moves:
        beside(None, turn, summing)
    (result,) = result
    grad_in, grad_in_bias, grad_out, grad_out_bias = call(
        functools.partial(finish_kernel, channels, hidden),
        [
            ((layout.in_rows, hidden), F32),
            ((1, layout.out_rows), F32),
            ((layout.out_rows, channels), F32),
            ((1, layout.in_rows), F32),
        ],
        (summing.value,),
        [WHOLE],
        name="finish",
    )
    grad_taps = jnp.swapaxes(turn.value[:, :TAPS], 1, 2).reshape(-1, TAPS)[:channels]
    return (
        output[None, None],
        result[None, None],
        own_share(grad_taps),
        own_share(grad_gain[:channels]),
        own_share(grad_shift[:channels]),
        grad_in,
        grad_in_bias[0],
        grad_out,
        grad_out_bias[0],
    )


def solution(mesh):
    spread = P("dp", "fsdp", None, None, None)
    split = P("fsdp", None)
    line = P("fsdp")
    return jax.shard_map(
        local,
        mesh=mesh,
        in_specs=(spread, P(), spread, split, line, line, split, line, split, line),
        out_specs=(spread, spread, split, line, line, split, line, split, line),
        check_vma=False,
    )
```

```python
import functools

import jax
import jax.numpy as jnp
import numpy as np
from jax import lax
from jax.experimental import pallas as pl
from jax.experimental.pallas import tpu as pltpu
from jax.sharding import PartitionSpec as P

KW = 7
SPAN = KW // 2
TILES = 8
EPSILON = 1e-05

LANES = 128
HALF = 64
FINE = 12
PAD = 16
PASSES = (KW + 1) // 2
TAPS = KW * KW
RIM_PAIRS = 4
BASE = 8

F32 = jnp.float32
BF16 = jnp.bfloat16
MIB = 2**20
WHOLE = pl.BlockSpec(memory_space=pltpu.VMEM)
HBM = pl.BlockSpec(memory_space=pl.ANY)


def fast(value):
    return pltpu.with_memory_space_constraint(value, pltpu.VMEM)


def slow(value):
    return pltpu.with_memory_space_constraint(value, pltpu.HBM)


def anywhere(shape, dtype):
    return jax.ShapeDtypeStruct(shape, dtype)


def round_up(value, step):
    return -(-value // step) * step


def call(kernel, outs, operands, in_specs, scratch=(), flops=0, moved=0, grid=None, out_specs=None, limit=10, aliases=None, name=None):
    extra = {} if grid is None else {"grid": grid}
    return pl.pallas_call(
        kernel,
        out_shape=outs,
        in_specs=in_specs,
        out_specs=[WHOLE] * len(outs) if out_specs is None else out_specs,
        scratch_shapes=list(scratch),
        input_output_aliases=aliases or {},
        compiler_params=pltpu.CompilerParams(vmem_limit_bytes=limit * MIB),
        cost_estimate=pl.CostEstimate(flops=flops, bytes_accessed=moved, transcendentals=0),
        name=name,
        **extra,
    )(*operands)


def low_half(rows):
    return lax.broadcasted_iota(jnp.int32, (rows, LANES), 1) < HALF


def swap(value):
    return pltpu.roll(value, HALF, 1)


def tiles_of(channels):
    return [(t, min(LANES, channels - t * LANES)) for t in range(-(-channels // LANES))]


def mask_of_row(turned, row):
    chosen = lax.broadcasted_iota(jnp.int32, (LANES, LANES), 0) == row
    return jnp.dot(turned, jnp.where(chosen, 1.0, 0.0).astype(BF16), preferred_element_type=F32)


def stage_row(stage, values, width):
    lanes = values.shape[1]
    stage[0, BASE : BASE + width, :lanes] = values
    stage[0, BASE - SPAN : BASE, :lanes] = values[width - SPAN :]
    stage[0, BASE + width : BASE + width + SPAN, :lanes] = values[:SPAN]
    stage[1] = swap(stage[0])


def plane(stage, which, start):
    return stage[which, pl.ds(start, PAD, stride=FINE), :]


def place_row(paired, stage, tile, blocks, pair, side):
    low = low_half(PAD)
    lanes = pl.ds(side * LANES, LANES)
    for k in range((FINE + 2 * SPAN) // 2):
        start = BASE - SPAN + 2 * k
        paired[2 * tile, pair, k, :, lanes] = jnp.where(
            low, plane(stage, 0, start), plane(stage, 1, start + 1)
        ).astype(BF16)
        if 2 * tile + 1 < blocks:
            paired[2 * tile + 1, pair, k, :, lanes] = jnp.where(
                low, plane(stage, 1, start), plane(stage, 0, start + 1)
            ).astype(BF16)


def place_natural(paired, stage, source, channels, width, blocks, pair, side, factor=None):
    for t, lanes in tiles_of(channels):
        values = source(t * LANES, t * LANES + lanes).astype(F32)
        if factor is not None:
            values = values * factor[:, :lanes]
        buffer = stage.at[side, t]
        stage_row(buffer, values, width)
        place_row(paired, buffer, t, blocks, pair, side)


def rim_rows(height):
    inner = (height + 2 * SPAN) // 2 - RIM_PAIRS // 2
    for index in range(SPAN):
        yield 0, index, index // 2, index % 2
    for index in range(SPAN):
        row = SPAN + height + index
        yield 1, index, row // 2 - inner + RIM_PAIRS // 2, row % 2


def build_weights(weights, taps, block, flip):
    lane = lax.broadcasted_iota(jnp.int32, (HALF, LANES), 1)
    sub = lax.broadcasted_iota(jnp.int32, (HALF, LANES), 0)
    diagonal = lax.rem(lane, HALF) == sub
    low = low_half(1)
    zero = jnp.zeros((1, LANES), F32)

    def tap_row(a, b):
        if not (0 <= a < KW and 0 <= b < KW):
            return zero
        index = (KW - 1 - a) * KW + KW - 1 - b if flip else a * KW + b
        return taps[block, index : index + 1, :]

    for m in range(PASSES):
        for s in range(PASSES):
            for place in range(4):
                pr, pj = divmod(place, 2)
                for qr in range(2):
                    a, b = 2 * m + pr - qr, 2 * s + pj
                    row = jnp.where(low, tap_row(a, b), tap_row(a, b - 1))
                    weights[
                        (m * PASSES + s) * 4 * HALF + place * HALF : (m * PASSES + s) * 4 * HALF + (place + 1) * HALF,
                        qr * LANES : (qr + 1) * LANES,
                    ] = jnp.where(diagonal, row, 0.0).astype(BF16)


def pass_rows(paired, rims, block, m, s, pairs):
    places = pl.ds(s, FINE // 2)
    inner = (RIM_PAIRS // 2, pairs + PASSES - 1 - RIM_PAIRS // 2)
    pieces = [rims[block, i, places] for i in range(m, inner[0])]
    pieces.append(paired[block, max(m, inner[0]) : min(m + pairs, inner[1]), places])
    pieces += [rims[block, i - inner[1] + RIM_PAIRS // 2, places] for i in range(inner[1], m + pairs)]
    return jnp.concatenate([piece.reshape(-1, 4 * HALF) for piece in pieces], axis=0)


def convolve_block(paired, rims, weights, block, pairs):
    rows = jnp.concatenate(
        [pass_rows(paired, rims, block, m, s, pairs) for m in range(PASSES) for s in range(PASSES)], axis=1
    )
    return jnp.dot(rows, weights[...], preferred_element_type=F32)


def split_blocks(lower, upper, start, side):
    low = low_half(PAD)
    rows, lanes = pl.ds(start, PAD), pl.ds(side * LANES, LANES)
    first = lower[rows, lanes]
    if upper is None:
        return first, swap(first)
    second = upper[rows, lanes]
    return jnp.where(low, first, swap(second)), jnp.where(low, swap(first), second)


def begin_kernel(
    layout, first, last, land_mask, kernel, in_proj, in_bias, out_proj, gain, shift, out_bias,
    top, bottom, land, shard, packed, table, wide, tall,
):
    count, width, channels = first.shape
    height = land.shape[0]
    tile_index = lax.axis_index("dp") % TILES
    spots = (height, land_mask.shape[0])
    wanted = lax.broadcasted_iota(jnp.int32, spots, 0) + tile_index * height
    chosen = jnp.where(lax.broadcasted_iota(jnp.int32, spots, 1) == wanted, 1.0, 0.0).astype(BF16)
    ocean = land_mask[...].astype(F32).astype(BF16)
    land[...] = jnp.dot(chosen, ocean, preferred_element_type=F32)
    table[...] = jnp.zeros_like(table)
    table[:height, :width] = land[...]
    turned = table[...].T[:width].astype(BF16)
    for source, out, start in ((first, top, 0), (last, bottom, height - count)):
        for i in range(count):
            factor = mask_of_row(turned, start + i)
            for t, lanes in tiles_of(channels):
                piece = pl.ds(t * LANES, lanes)
                out[i, :, piece] = (source[i, :, piece].astype(F32) * factor[:, :lanes]).astype(BF16)
    wide[...] = jnp.zeros_like(wide)
    wide[: kernel.shape[0], : kernel.shape[1]] = kernel[...].astype(F32)
    shard[...] = wide[:LANES, :LANES].T[: shard.shape[0]].astype(BF16)
    pack_parameters(layout, in_proj, in_bias, out_proj, gain, shift, out_bias, packed, wide, tall)


def prepare_kernel(feats, cot, land, paired, gbranch, mask, masked, upstream, stage, plain, table):
    height, width = land.shape
    channels = feats.shape[-1]
    blocks = paired.shape[0]
    step = pl.program_id(0)

    @pl.when(step == 0)
    def _():
        stage[...] = jnp.zeros_like(stage)
        plain[...] = jnp.zeros_like(plain)
        table[...] = jnp.zeros_like(table)
        table[:height, :width] = land[...]

    turned = table[...].T[:width].astype(BF16)
    for side in range(2):
        row = 2 * step + side
        factor = mask_of_row(turned, row)
        rows = pl.ds(BASE, width)
        plain[side, 0, rows, :] = factor
        for t, lanes in tiles_of(channels):
            piece = pl.ds(t * LANES, lanes)
            values = feats[side, :, piece].astype(F32) * factor[:, :lanes]
            masked[side, :, piece] = values.astype(BF16)
            buffer = stage.at[side, t]
            stage_row(buffer, values, width)
            place_row(paired, buffer, t, blocks, step + (SPAN + side) // 2, (SPAN + side) % 2)
            values = cot[side, :, piece].astype(F32) * factor[:, :lanes]
            upstream[side, :, piece] = values.astype(BF16)
            plain[side, 1 + t, rows, :lanes] = values
        for r in range(FINE):
            mask[row, r] = plain[side, 0, pl.ds(BASE + r, PAD, stride=FINE), :]
            for t, _unused in tiles_of(channels):
                gbranch[row, r, :, t * LANES : (t + 1) * LANES] = plain[
                    side, 1 + t, pl.ds(BASE + r, PAD, stride=FINE), :
                ].astype(BF16)


def forward_kernel(channels, paired, top, bottom, shards, mask, conv, stats, rims, taps, weights, accs, stage, table):
    height = conv.shape[0]
    blocks, pairs = paired.shape[0], height // 2
    width = top.shape[1]
    share = channels // shards.shape[0]
    stage[...] = jnp.zeros_like(stage)
    table[...] = jnp.zeros_like(table)
    for f in range(shards.shape[0]):
        table[f * share : (f + 1) * share] = shards[f].astype(F32)[:share]
    for block in range(blocks):
        piece = table[block * HALF : (block + 1) * HALF]
        taps[block] = jnp.concatenate([piece, piece], axis=0).T[: taps.shape[1]]
    last = pairs + PASSES - 1
    first_half = (SPAN % 2) * LANES
    last_half = ((SPAN + height - 1) % 2) * LANES
    rims[:, 1, :, :, first_half : first_half + LANES] = paired[:, 1, :, :, first_half : first_half + LANES]
    rims[:, 2, :, :, last_half : last_half + LANES] = paired[:, last - 2, :, :, last_half : last_half + LANES]
    for below, index, pair, side in rim_rows(height):
        source = bottom if below else top
        place_natural(
            rims, stage, lambda a, b, source=source, index=index: source[index, :, a:b], channels, width, blocks, pair, side
        )
    for t, _ in tiles_of(channels):
        lanes = pl.ds(t * LANES, LANES)
        has_upper = 2 * t + 1 < blocks
        for half in range(1 + has_upper):
            build_weights(weights, taps, 2 * t + half, False)
            accs[half] = convolve_block(paired, rims, weights, 2 * t + half, pairs)

        def planes(h, k, side, has_upper=has_upper):
            return split_blocks(accs.at[0], accs.at[1] if has_upper else None, (h * (FINE // 2) + k) * PAD, side)

        zero = jnp.zeros((PAD, LANES), F32)
        total, count = zero, zero
        for k in range(FINE // 2):
            even, odd = planes(0, k, 0)
            total = total + (mask[0, 2 * k] * even + mask[0, 2 * k + 1] * odd)
            count = count + (mask[0, 2 * k] + mask[0, 2 * k + 1])
        near = jnp.sum(total, axis=0, keepdims=True) / jnp.maximum(jnp.sum(count, axis=0, keepdims=True), 1.0)

        def spread(h, sums, lanes=lanes, planes=planes, near=near):
            sums = list(sums)
            for k in range(FINE // 2):
                for side in range(2):
                    row = 2 * h + side
                    for odd, value in enumerate(planes(h, k, side)):
                        r = 2 * k + odd
                        conv[row, r, :, lanes] = value
                        weight = mask[row, r]
                        away = value - near
                        part = weight * away
                        at = 3 * (2 * side + odd)
                        sums[at] = sums[at] + part
                        sums[at + 1] = sums[at + 1] + part * away
                        sums[at + 2] = sums[at + 2] + weight
            return tuple(sums)

        sums = lax.fori_loop(0, pairs, spread, (zero,) * 12)
        total, square, count = (
            jnp.sum(sums[i] + sums[i + 3] + sums[i + 6] + sums[i + 9], axis=0, keepdims=True) for i in range(3)
        )
        shift = total / jnp.maximum(count, 1.0)
        stats[0:1, lanes] = near + shift
        stats[1:2, lanes] = jnp.maximum(square - total * shift, 0.0)
        stats[2:3, lanes] = count


def pointwise_kernel(
    channels, real_units, conv, gbranch, feats, mask, vec, w_in, w_out,
    output, act_out, ghid_out, gz_out, z_out, sums, stage,
):
    rows, width = feats.shape[0], feats.shape[1]
    padded = conv.shape[-1]
    cells = rows * FINE * PAD
    hidden_units = act_out.shape[1]
    step = pl.program_id(0)

    @pl.when(step == 0)
    def _():
        sums[...] = jnp.zeros_like(sums)

    one_lane = lax.broadcasted_iota(jnp.int32, (1, padded), 1) == channels
    mean, inverse, gain, shift = (vec[i : i + 1, :] for i in range(4))
    mine = pl.ds(step * rows, rows)
    here = pl.ds(pl.multiple_of(step * cells, cells), cells)
    normed = (conv[mine].reshape(cells, padded) - mean) * inverse
    zvals = jnp.where(one_lane, 1.0, gain * normed + shift).astype(BF16)
    z_out[here, :] = zvals
    upstream = gbranch[mine].reshape(cells, padded)
    branch = jnp.zeros((cells, padded), F32)
    gz = jnp.zeros((cells, padded), F32)
    chunk = 2 * LANES
    across = (((1,), (1,)), ((), ()))
    c0 = 0.7978845608028654
    c1 = 0.044715 * c0
    for start in range(0, hidden_units, chunk):
        span = pl.ds(start, chunk)
        hidden = jnp.dot(zvals, w_in[:, span], preferred_element_type=F32)
        gact = lax.dot_general(upstream, w_out[span, :], across, preferred_element_type=F32)
        square = hidden * hidden
        bent = jnp.tanh(hidden * (c0 + c1 * square))
        half = 0.5 * hidden
        act = half + half * bent
        slope = (0.5 + 0.5 * bent) + half * (1.0 - bent * bent) * (c0 + (3.0 * c1) * square)
        ghid = (gact * slope).astype(BF16)
        act = act.astype(BF16)
        if start + chunk > real_units:
            lane = lax.broadcasted_iota(jnp.int32, (1, chunk), 1)
            act = jnp.where(lane == real_units - start, jnp.ones((), BF16), act)
        act_out[here, span] = act
        ghid_out[here, span] = ghid
        branch = branch + jnp.dot(act, w_out[span, :], preferred_element_type=F32)
        gz = gz + lax.dot_general(ghid, w_in[:, span], across, preferred_element_type=F32)
    gz_out[mine] = gz.reshape(rows, *gz_out.shape[1:])
    sums[0:1, :] += jnp.sum(gz * normed, axis=0, keepdims=True)
    sums[1:2, :] += jnp.sum(gz, axis=0, keepdims=True)
    for row in range(rows):
        for t, lanes in tiles_of(channels):
            for r in range(FINE):
                start = (row * FINE + r) * PAD
                values = branch[start : start + PAD, t * LANES : (t + 1) * LANES] * mask[step * rows + row, r]
                stage[row, t, pl.ds(r, PAD, stride=FINE), :] = values
            piece = pl.ds(t * LANES, lanes)
            values = feats[row, :, piece].astype(F32) + stage[row, t, 0:width, :lanes]
            output[row, :, piece] = values.astype(BF16)


def out_grads_kernel(gbranch, act, grad):
    grad[...] = turned_product(gbranch, act, grad.shape[0])


def turned_product(left, right, rows):
    return lax.dot_general(left[:, :rows], right[...], (((0,), (0,)), ((), ())), preferred_element_type=F32)


def in_grads_kernel(channels, hidden, zvals, ghid, grad_out, kept, sent, grad_in):
    grad_in[...] = turned_product(zvals, ghid, grad_in.shape[0])
    shares = lax.axis_size("fsdp")
    layout = Packing(channels, hidden, shares)
    last = layout.in_tiles - 1
    lane = lax.broadcasted_iota(jnp.int32, (1, LANES), 1)
    spot = lax.broadcasted_iota(jnp.int32, (layout.out_pad, 1), 0)
    fill = jnp.zeros((layout.in_pad - layout.in_rows, LANES), F32)

    def write(out, place, j):
        rows = slice(j * layout.in_rows, (j + 1) * layout.in_rows)
        for t in range(layout.in_tiles):
            lanes = slice(t * LANES, (t + 1) * LANES)
            tile = grad_in[rows, lanes]
            if t == last:
                tile = jnp.where(lane == hidden - t * LANES, grad_out[rows, lanes], tile)
            tile = jnp.concatenate([tile, fill], axis=0)
            out[place, t * layout.in_pad : (t + 1) * layout.in_pad] = tile.astype(out.dtype)
        start = j * layout.out_rows
        aligned = start // LANES * LANES
        stop = min(aligned + (layout.out_tiles + 1) * LANES, grad_out.shape[1])
        part = jnp.where(
            spot == channels, grad_in[: layout.out_pad, aligned:stop], grad_out[: layout.out_pad, aligned:stop]
        )
        if start != aligned:
            part = pltpu.roll(part, stop - start, 1)
        for u in range(layout.out_tiles):
            base = layout.out_base + u * layout.out_pad
            out[place, base : base + layout.out_pad] = part[:, u * LANES : (u + 1) * LANES].astype(out.dtype)
        out[place, layout.small_base :] = jnp.zeros((layout.rows - layout.small_base, LANES), out.dtype)

    side = lax.axis_index("fsdp") % 2
    for mine in range(2):

        @pl.when(side == mine)
        def _(mine=mine):
            for j in range(shares):
                write(kept if j % 2 == mine else sent, j // 2, j)


def finish_kernel(channels, hidden, packed, grad_in, grad_in_bias, grad_out, grad_out_bias):
    layout = Packing(channels, hidden, channels // grad_in.shape[0])
    for t in range(layout.in_tiles):
        stop = min((t + 1) * LANES, hidden)
        tile = packed[t * layout.in_pad : (t + 1) * layout.in_pad].astype(F32)
        grad_in[:, t * LANES : stop] = tile[: layout.in_rows, : stop - t * LANES]
    tall = jnp.concatenate([tile, jnp.zeros((LANES - layout.in_pad, LANES), F32)], axis=0).T
    at = hidden - (layout.in_tiles - 1) * LANES
    grad_out_bias[...] = tall[at : at + 1, : layout.in_rows]
    for u in range(layout.out_tiles):
        base = layout.out_base + u * layout.out_pad
        tile = packed[base : base + layout.out_pad].astype(F32)
        stop = min((u + 1) * LANES, layout.out_rows)
        count = stop - u * LANES
        grad_in_bias[:, u * LANES : stop] = tile[channels : channels + 1, :count]
        fill = jnp.zeros((round_up(layout.out_pad, LANES) - layout.out_pad, LANES), F32)
        grad_out[u * LANES : stop, :] = jnp.concatenate([tile, fill], axis=0).T[:count, :channels]


class Packing:
    def __init__(self, channels, hidden, shares):
        self.in_rows = channels // shares
        self.in_pad = round_up(self.in_rows, 16)
        self.in_tiles = -(-(hidden + 1) // LANES)
        self.out_rows = hidden // shares
        self.out_tiles = -(-self.out_rows // LANES)
        self.out_pad = round_up(max(channels + 1, self.out_rows), 16)
        self.out_base = self.in_pad * self.in_tiles
        self.small_base = self.out_base + self.out_pad * self.out_tiles
        self.small = self.out_tiles + 3
        self.rows = round_up(self.small_base + self.small, 32)


def pack_parameters(layout, in_proj, in_bias, out_proj, gain, shift, out_bias, packed, wide, tall):
    wide[...] = jnp.zeros_like(wide)
    tall[...] = jnp.zeros_like(tall)
    wide[: layout.in_rows, : in_proj.shape[1]] = in_proj[...].astype(F32)
    for t in range(layout.in_tiles):
        packed[t * layout.in_pad : (t + 1) * layout.in_pad] = wide[: layout.in_pad, t * LANES : (t + 1) * LANES].astype(BF16)
    tall[: layout.out_rows, : out_proj.shape[1]] = out_proj[...].astype(F32)
    for u in range(layout.out_tiles):
        base = layout.out_base + u * layout.out_pad
        packed[base : base + layout.out_pad] = tall[:, u * LANES : (u + 1) * LANES].astype(BF16)
    wide[...] = jnp.zeros_like(wide)
    wide[0:1, : in_bias.shape[1]] = in_bias[...].astype(F32)
    for i, small in enumerate((gain, shift, out_bias)):
        wide[i + 1 : i + 2, : small.shape[1]] = small[...].astype(F32)
    rows = [wide[0:1, u * LANES : (u + 1) * LANES] for u in range(layout.out_tiles)]
    rows += [wide[i + 1 : i + 2, :LANES] for i in range(3)]
    rows.append(jnp.zeros((layout.rows - layout.small_base - layout.small, LANES), F32))
    packed[layout.small_base :] = jnp.concatenate(rows, axis=0).astype(BF16)


def assemble_kernel(layout, packed, w_in, w_out, vectors, wide, tall):
    wide[...] = jnp.zeros_like(wide)
    tall[...] = jnp.zeros_like(tall)
    shares = packed.shape[0]
    channels, hidden = layout.in_rows * shares, layout.out_rows * shares
    in_bias = jnp.zeros((8, wide.shape[1]), F32)
    smalls = [jnp.zeros((8, tall.shape[1]), F32)] * 3
    for f in range(shares):
        for t in range(layout.in_tiles):
            tile = packed[f, t * layout.in_pad : (t + 1) * layout.in_pad].astype(F32)
            wide[f * layout.in_rows : (f + 1) * layout.in_rows, t * LANES : (t + 1) * LANES] = tile[: layout.in_rows]
        for u in range(layout.out_tiles):
            base = layout.out_base + u * layout.out_pad
            tile = packed[f, base : base + layout.out_pad].astype(F32)
            tall[f * layout.out_rows : (f + 1) * layout.out_rows, u * LANES : (u + 1) * LANES] = tile[: layout.out_rows]
        small = packed[f, layout.small_base :].astype(F32)

        def spread(first, count, lanes, turn):
            pieces = [small[first + u : first + u + 1] for u in range(count)]
            pieces.append(jnp.zeros((1, lanes - count * LANES), F32))
            row = jnp.broadcast_to(jnp.concatenate(pieces, axis=1), (8, lanes))
            return pltpu.roll(row, turn, 1) if turn else row

        in_bias = in_bias + spread(0, layout.out_tiles, wide.shape[1], f * layout.out_rows)
        smalls = [
            total + spread(layout.out_tiles + i, 1, tall.shape[1], f * layout.in_rows)
            for i, total in enumerate(smalls)
        ]
    wide[channels : channels + 1] = in_bias[:1]
    tall[hidden : hidden + 1] = smalls[2][:1]
    w_in[...] = wide[...].astype(BF16)
    w_out[...] = tall[...].astype(BF16)
    vectors[...] = jnp.concatenate([smalls[0][:1], smalls[1][:1], jnp.zeros((6, tall.shape[1]), F32)], axis=0)


def shifted_planes(values, real):
    out = []
    for r in range(-SPAN, FINE + SPAN):
        value = values[r % FINE]
        if r < 0:
            value = jnp.concatenate([value[real - 1 : real], value[: PAD - 1]], axis=0)
        elif r >= FINE:
            value = jnp.concatenate([value[1:real], value[:1], value[: PAD - real]], axis=0)
        out.append(value)
    return out


def join_planes(first, second):
    low = low_half(PAD)
    return (
        jnp.where(low, first, swap(second)).astype(BF16),
        jnp.where(low, swap(first), second).astype(BF16),
    )


def place_planes(paired, planes, tile, blocks, pair, side):
    out_lanes = pl.ds(side * LANES, LANES)
    for k in range(len(planes) // 2):
        for half, value in enumerate(join_planes(planes[2 * k], planes[2 * k + 1])):
            if 2 * tile + half < blocks:
                paired[2 * tile + half, pair, k, :, out_lanes] = value


def arrange_kernel(channels, real, gz, conv, mask, vec, edges, gpaired, own):
    height = gz.shape[0]
    blocks, pairs = own.shape[0], height // 2

    def arrange(h, _):
        for t, _unused in tiles_of(channels):
            lanes = pl.ds(t * LANES, LANES)
            mean, inverse, scaled, bias, slope = (vec[i : i + 1, lanes] for i in range(5))
            for side in range(2):
                row = 2 * h + side
                values = []
                for r in range(FINE):
                    normed = (conv[row, r, :, lanes] - mean) * inverse
                    values.append(scaled * gz[row, r, :, lanes] - mask[row, r] * (bias + normed * slope))
                out_lanes = pl.ds(side * LANES, LANES)
                for k in range(FINE // 2):
                    rows = pl.ds((h * (FINE // 2) + k) * PAD, PAD)
                    for half, value in enumerate(join_planes(values[2 * k], values[2 * k + 1])):
                        if 2 * t + half < blocks:
                            own[2 * t + half, rows, out_lanes] = value
                place_planes(
                    gpaired, shifted_planes(values, real), t, blocks, h + (SPAN + side) // 2, (SPAN + side) % 2
                )
                for edge, near in ((0, row < SPAN), (1, row >= height - SPAN)):

                    @pl.when(near)
                    def _(edge=edge, row=row, values=values, lanes=lanes):
                        place = row - (height - SPAN) * edge
                        for r in range(FINE):
                            edges[edge, place, r, :, lanes] = values[r].astype(BF16)

        return 0

    lax.fori_loop(0, pairs, arrange, 0)


def taps_kernel(tile, own, paired, rims, select, grad_taps):
    blocks, pairs = own.shape[0], paired.shape[1] - PASSES + 1
    lane = lax.broadcasted_iota(jnp.int32, (HALF, 2 * LANES), 1)
    sub = lax.broadcasted_iota(jnp.int32, (HALF, 2 * LANES), 0)
    diagonal = lax.rem(lane, HALF) == sub
    low = low_half(grad_taps.shape[0])
    totals = []
    for block in range(2 * tile, min(2 * tile + 2, blocks)):
        turned = own[block].T
        found = []
        for m in range(PASSES):
            for s in range(PASSES):
                product = jnp.dot(turned, pass_rows(paired, rims, block, m, s, pairs), preferred_element_type=F32)
                for q in range(4):
                    part = product[q * HALF : (q + 1) * HALF]
                    found.append(jnp.sum(jnp.where(diagonal, part, 0.0), axis=0, keepdims=True))
        found = jnp.concatenate(found, axis=0)
        total = None
        for place in range(4):
            group = jnp.dot(select[place], found, preferred_element_type=F32, precision=lax.Precision.HIGHEST)
            group = group[:, (place // 2) * LANES : (place // 2 + 1) * LANES]
            if place % 2:
                group = swap(group)
            total = group if total is None else total + group
        totals.append(total)
    second = swap(totals[1]) if len(totals) > 1 else jnp.zeros_like(totals[0])
    grad_taps[...] = jnp.where(low, totals[0], second)


def backward_kernel(tile, real, gpaired, top, bottom, taps, cot, mask, *rest):
    result, rims, weights, accs, stage = rest[-5:]
    height, width = cot.shape[0], cot.shape[1]
    blocks, pairs = gpaired.shape[0], height // 2
    last = pairs + PASSES - 1
    first_half = (SPAN % 2) * LANES
    last_half = ((SPAN + height - 1) % 2) * LANES
    has_upper = 2 * tile + 1 < blocks
    for half in range(1 + has_upper):
        source = gpaired.at[2 * tile + half]
        rims[half, 1, :, :, first_half : first_half + LANES] = source[1, :, :, first_half : first_half + LANES]
        rims[half, 2, :, :, last_half : last_half + LANES] = source[last - 2, :, :, last_half : last_half + LANES]
    for below, index, pair, side in rim_rows(height):
        source = bottom if below else top
        values = [source[index, r, :, tile * LANES : (tile + 1) * LANES].astype(F32) for r in range(FINE)]
        place_planes(rims, shifted_planes(values, real), 0, 1 + has_upper, pair, side)
    for half in range(1 + has_upper):
        block = 2 * tile + half
        build_weights(weights, taps, block, True)
        accs[half] = convolve_block(gpaired.at[block : block + 1], rims.at[half : half + 1], weights, 0, pairs)

    def spread(h, _):
        for side in range(2):
            row = 2 * h + side
            for k in range(FINE // 2):
                even, odd = split_blocks(
                    accs.at[0], accs.at[1] if has_upper else None, (h * (FINE // 2) + k) * PAD, side
                )
                stage[side, pl.ds(2 * k, PAD, stride=FINE), :] = even * mask[row, 2 * k]
                stage[side, pl.ds(2 * k + 1, PAD, stride=FINE), :] = odd * mask[row, 2 * k + 1]
            values = cot[row].astype(F32) + stage[side, 0:width]
            result[row] = values.astype(BF16)
        return 0

    lax.fori_loop(0, pairs, spread, 0)


def bits(size):
    bit = 1
    while bit < size:
        yield bit
        bit *= 2


def swapped(value, axis, bit):
    size = lax.axis_size(axis)
    return lax.ppermute(value, axis, [(i, i ^ bit) for i in range(size)])


def side_of(axis, bit):
    return lax.axis_index(axis) // bit % 2


def ring_bits(*axes):
    return [(axis, bit) for axis in axes for bit in bits(lax.axis_size(axis))]


def tied(*values):
    return lax.optimization_barrier(values)


def add(mine, other):
    return (mine.astype(F32) + other.astype(F32)).astype(mine.dtype)


def merge_stats(mine, other):
    count = mine[2:3] + other[2:3]
    safe = jnp.maximum(count, 1.0)
    mean = (mine[0:1] * mine[2:3] + other[0:1] * other[2:3]) / safe
    away = mine[0:1] - other[0:1]
    spread = mine[1:2] + other[1:2] + away * away * (mine[2:3] * other[2:3] / safe)
    return jnp.concatenate([mean, spread, count], axis=0)


def joined(value, other, axis, bit):
    first = side_of(axis, bit) == 0
    pair = [jnp.where(first, value, other), jnp.where(first, other, value)]
    return jnp.stack(pair, axis=1).reshape(-1, *value.shape[1:])


def keep_and_send(value, axis, bit, dim):
    side = side_of(axis, bit)
    return (
        lax.dynamic_index_in_dim(value, side, dim, keepdims=False),
        lax.dynamic_index_in_dim(value, 1 - side, dim, keepdims=False),
    )


class Summing:
    def __init__(self, kept, sent):
        self.kept, self.sent = kept, sent
        self.moves = ring_bits("fsdp")
        over = ring_bits("dp")
        self.moves += over[:1] + over[1:] + over[:1]
        self.counts = (len(ring_bits("fsdp")), len(over))
        self.done = 0

    def start(self):
        axis, bit = self.moves.pop(0)
        fsdp_count, dp_count = self.counts
        self.kind = "share" if self.done < fsdp_count else "half" if self.done == fsdp_count else "whole"
        if self.done == fsdp_count + dp_count:
            self.kind = "join"
        if self.kind == "share" and self.done:
            value = self.value.reshape(-1, 2, *self.value.shape[-2:])
            self.kept, self.sent = keep_and_send(value, axis, bit, 1)
        elif self.kind == "half":
            value = self.value.reshape(2, -1, self.value.shape[-1])
            self.kept, self.sent = keep_and_send(value, axis, bit, 0)
        elif self.kind in ("whole", "join"):
            self.kept = self.sent = self.value.astype(BF16)
        self.done += 1
        self.move = axis, bit
        return swapped(self.sent.astype(BF16), axis, bit)

    def finish(self, other):
        if self.kind == "join":
            first = side_of(*self.move) == 0
            self.value = jnp.concatenate(
                [jnp.where(first, self.kept, other), jnp.where(first, other, self.kept)], axis=0
            )
        else:
            self.value = self.kept.astype(F32) + other.astype(F32)


class Adding:
    def __init__(self, value, merge=add):
        self.value, self.merge = value, merge
        self.moves = ring_bits("fsdp", "dp")

    def start(self):
        return swapped(self.value, *self.moves.pop(0))

    def finish(self, other):
        self.value = self.merge(self.value, other)


def beside(work, *sums):
    running = [each for each in sums if each.moves]
    arriving = [each.start() for each in running]
    done = work() if work else ()
    arriving, done = lax.optimization_barrier((arriving, done))
    for each, other in zip(running, arriving):
        each.finish(other)
    return done


def rims_of(top_rows, bottom_rows):
    size = lax.axis_size("dp")
    down = [(i, i + 1) for i in range(size - 1) if (i + 1) % TILES]
    up = [(j, i) for i, j in down]
    return lax.ppermute(bottom_rows, "dp", down), lax.ppermute(top_rows, "dp", up)


def tap_selectors(rows):
    out = np.zeros((4, rows, PASSES * PASSES * 4), np.float32)
    for m in range(PASSES):
        for s in range(PASSES):
            for q in range(4):
                for p in range(4):
                    a = 2 * m + p // 2 - q // 2
                    b = 2 * s + p % 2 - q % 2
                    if 0 <= a < KW and 0 <= b < KW:
                        out[p, a * KW + b, (m * PASSES + s) * 4 + q] = 1.0
    return out


def own_share(value):
    share = value.shape[0] // lax.axis_size("fsdp")
    return lax.dynamic_slice_in_dim(value, lax.axis_index("fsdp") * share, share, 0)


def local(features, land_mask, cotangent, kernel, norm_gain, norm_shift, in_proj, in_bias, out_proj, out_bias):
    feats, cot = features[0, 0], cotangent[0, 0]
    height, width, channels = feats.shape
    hidden = in_proj.shape[1]
    shares = lax.axis_size("fsdp")
    padded = round_up(channels + 1, LANES)
    hidden_pad = round_up(hidden + 1, 2 * LANES)
    blocks = -(-channels // HALF)
    pairs = height // 2
    planes_in = (FINE + 2 * SPAN) // 2
    row_pairs = pairs + PASSES - 1
    cells = height * FINE * PAD
    block_rows = pairs * (FINE // 2) * PAD
    stage_rows = round_up(BASE + SPAN + FINE * PAD, 8)
    tile_count = len(tiles_of(channels))
    tap_rows = round_up(TAPS, 8)
    real = width // FINE
    layout = Packing(channels, hidden, shares)

    edge = lambda at: pl.BlockSpec((SPAN, width, channels), lambda i: (at, 0, 0))
    whole = lambda array: pl.BlockSpec(array.shape, lambda i: (0,) * array.ndim)
    natural_shape = (height, width, channels)
    edge_shape = (SPAN, width, channels)
    small = (kernel.T, in_proj, in_bias[None], out_proj, norm_gain[None], norm_shift[None], out_bias[None])
    first_rows, last_rows, land, shards, packed = call(
        functools.partial(begin_kernel, layout),
        [
            anywhere(edge_shape, BF16),
            anywhere(edge_shape, BF16),
            anywhere((height, width), F32),
            anywhere((layout.in_pad, LANES), BF16),
            anywhere((layout.rows, LANES), BF16),
        ],
        (slow(feats), slow(feats), slow(land_mask), *(slow(v) for v in small)),
        [edge(0), edge(height // SPAN - 1), whole(land_mask)] + [whole(v) for v in small],
        [
            pltpu.VMEM((round_up(height, LANES), round_up(width, LANES)), F32),
            pltpu.VMEM((round_up(layout.in_pad, LANES), hidden_pad), F32),
            pltpu.VMEM((layout.out_pad, padded), F32),
        ],
        grid=(1,),
        out_specs=[WHOLE] * 5,
        name="begin",
    )
    shards, packed = shards[None], packed[None]
    far = list(reversed(ring_bits("fsdp")))
    top, bottom = rims_of(first_rows, last_rows)
    shards_there, packed_there = swapped(shards, *far[0]), swapped(packed, *far[0])

    paired_shape = (blocks, row_pairs, planes_in, PAD, 4 * HALF)
    rims_shape = (blocks, RIM_PAIRS, planes_in, PAD, 4 * HALF)
    plane_shape = (height, FINE, PAD, padded)
    mask_shape = (height, FINE, PAD, LANES)
    stage = pltpu.VMEM((2, tile_count, 2, stage_rows, LANES), F32)
    paired, gbranch, mask, masked, upstream = call(
        prepare_kernel,
        [
            pltpu.VMEM(paired_shape, BF16),
            pltpu.VMEM(plane_shape, BF16),
            pltpu.VMEM(mask_shape, F32),
            pltpu.HBM(natural_shape, BF16),
            pltpu.HBM(natural_shape, BF16),
        ],
        (slow(feats), slow(cot), land),
        [pl.BlockSpec((2, width, channels), lambda i: (i, 0, 0))] * 2 + [whole(land)],
        [
            stage,
            pltpu.VMEM((2, 1 + tile_count, stage_rows, LANES), F32),
            pltpu.VMEM((round_up(height, LANES), round_up(width, LANES)), F32),
        ],
        moved=20 * MIB,
        limit=12,
        grid=(pairs,),
        out_specs=[WHOLE] * 3 + [pl.BlockSpec((2, width, channels), lambda i: (i, 0, 0))] * 2,
        name="prepare",
    )
    shards_there, packed_there, paired = tied(shards_there, packed_there, paired)
    shards, packed = joined(shards, shards_there, *far[0]), joined(packed, packed_there, *far[0])
    for axis, bit in far[1:]:
        shards = joined(shards, swapped(shards, axis, bit), axis, bit)
    packed_there = [swapped(packed, *far[1])] if far[1:] else []

    accs = pltpu.VMEM((2, block_rows, 4 * HALF), F32)
    weights = pltpu.VMEM((PASSES * PASSES * 4 * HALF, 4 * HALF), BF16)
    conv, stats, rims, taps = call(
        functools.partial(forward_kernel, channels),
        [
            pltpu.VMEM(plane_shape, F32),
            anywhere((8, padded), F32),
            pltpu.VMEM(rims_shape, BF16),
            anywhere((blocks, tap_rows, LANES), F32),
        ],
        (fast(paired), top, bottom, shards, fast(mask)),
        [WHOLE] * 5,
        [weights, accs, stage, pltpu.VMEM((blocks * HALF, LANES), F32)],
        flops=9 * 10**9,
        limit=12,
        name="forward",
    )
    packed_there, stats = tied(packed_there, stats)
    if far[1:]:
        packed = joined(packed, packed_there[0], *far[1])
    for axis, bit in far[2:]:
        packed = joined(packed, swapped(packed, axis, bit), axis, bit)
    assemble = lambda: call(
        functools.partial(assemble_kernel, layout),
        [
            anywhere((padded, hidden_pad), BF16),
            anywhere((hidden_pad, padded), BF16),
            anywhere((8, padded), F32),
        ],
        (packed,),
        [WHOLE],
        [pltpu.VMEM((padded, hidden_pad), F32), pltpu.VMEM((hidden_pad, padded), F32)],
        name="assemble",
    )
    norm = Adding(stats[:3], merge_stats)
    w_in, w_out, vectors = beside(assemble, norm)
    while norm.moves:
        beside(None, norm)
    stats = norm.value
    count = jnp.maximum(stats[2], 1.0)
    mean = stats[0]
    inverse = lax.rsqrt(stats[1] / count + EPSILON)
    gain, shift = vectors[0], vectors[1]
    zero = jnp.zeros_like(mean)
    vec = jnp.stack([mean, inverse, gain, shift, zero, zero, zero, zero])

    rows = 3 if height % 3 == 0 else height
    steps = height // rows
    part = rows * FINE * PAD
    by_row = lambda *rest: pl.BlockSpec((rows, *rest), lambda i: (i,) + (0,) * len(rest))
    output, act, ghid, gz, zvals, sums = call(
        functools.partial(pointwise_kernel, channels, hidden),
        [
            anywhere(natural_shape, BF16),
            pltpu.VMEM((cells, hidden_pad), BF16),
            pltpu.VMEM((cells, hidden_pad), BF16),
            pltpu.VMEM(plane_shape, F32),
            pltpu.VMEM((cells, padded), BF16),
            anywhere((8, padded), F32),
        ],
        (fast(conv), fast(gbranch), slow(masked), fast(mask), vec, w_in, w_out),
        [WHOLE, WHOLE, by_row(width, channels)] + [WHOLE] * 4,
        [pltpu.VMEM((rows, tile_count, round_up(FINE * PAD, 8), LANES), F32)],
        flops=14 * 10**9,
        grid=(steps,),
        out_specs=[by_row(width, channels)] + [WHOLE] * 5,
        limit=14,
        name="pointwise",
    )

    grad_rows = round_up(channels + 1, 16)
    norm = Adding(sums[:2])
    (grad_out,) = beside(
        lambda: call(
            out_grads_kernel,
            [pltpu.VMEM((grad_rows, hidden_pad), F32)],
            (fast(gbranch.reshape(cells, padded)), fast(act)),
            [WHOLE] * 2,
            flops=3 * 10**9,
            limit=4,
            name="out_grads",
        ),
        norm,
    )
    kept, sent = beside(
        lambda: call(
            functools.partial(in_grads_kernel, channels, hidden),
            [
                pltpu.VMEM((-(-shares // 2), layout.rows, LANES), F32),
                pltpu.VMEM((-(-shares // 2), layout.rows, LANES), BF16),
            ],
            (fast(zvals), fast(ghid), fast(grad_out)),
            [WHOLE] * 3,
            [pltpu.VMEM((grad_rows, hidden_pad), F32)],
            flops=3 * 10**9,
            limit=8,
            name="in_grads",
        ),
        norm,
    )
    summing = Summing(kept, sent)
    beside(None, norm, summing)
    beside(None, norm)
    beside(None, norm, summing)
    grad_gain, grad_shift = norm.value[0], norm.value[1]
    scaled = inverse * gain
    gvec = jnp.stack([mean, inverse, scaled, scaled * grad_shift / count, scaled * grad_gain / count, zero, zero, zero])
    edges, gpaired, own = beside(
        lambda: call(
            functools.partial(arrange_kernel, channels, real),
            [
                anywhere((2, SPAN, FINE, PAD, padded), BF16),
                pltpu.VMEM(paired_shape, BF16),
                pltpu.VMEM((blocks, block_rows, 4 * HALF), BF16),
            ],
            (fast(gz), fast(conv), fast(mask), gvec),
            [WHOLE] * 4,
            flops=10**8,
            moved=10 * MIB,
            limit=6,
            name="arrange",
        ),
        summing,
    )
    select = jnp.asarray(tap_selectors(tap_rows))
    gtop, gbottom = rims_of(edges[0], edges[1])
    grad_taps = []
    for t in range(tile_count):
        grad_taps += beside(
            lambda: call(
                functools.partial(taps_kernel, t),
                [anywhere((tap_rows, LANES), F32)],
                (fast(own), fast(paired), fast(rims), select),
                [WHOLE] * 4,
                flops=4 * 10**9,
                limit=6,
                name="taps",
            ),
            summing,
        )
    gtop, gbottom, *grad_taps = tied(gtop, gbottom, *grad_taps)
    turn = Adding(jnp.stack(grad_taps))
    result = ()
    for t in range(tile_count):
        column = pl.BlockSpec((height, width, LANES), lambda i, t=t: (0, 0, t))
        result = beside(
            lambda: call(
                functools.partial(backward_kernel, t, real),
                [anywhere(natural_shape, BF16)],
                (fast(gpaired), gtop, gbottom, taps, slow(upstream), fast(mask), *result),
                [WHOLE] * 4 + [column, WHOLE] + [HBM] * len(result),
                [
                    pltpu.VMEM((2, RIM_PAIRS, planes_in, PAD, 4 * HALF), BF16),
                    weights,
                    accs,
                    pltpu.VMEM((2, round_up(FINE * PAD, 8), LANES), F32),
                ],
                flops=4 * 10**9,
                limit=12,
                grid=(1,),
                out_specs=[column],
                aliases={6: 0} if result else {},
                name="backward",
            ),
            turn,
            summing,
        )
    while turn.moves or summing.moves:
        beside(None, turn, summing)
    (result,) = result
    grad_in, grad_in_bias, grad_out, grad_out_bias = call(
        functools.partial(finish_kernel, channels, hidden),
        [
            anywhere((layout.in_rows, hidden), F32),
            anywhere((1, layout.out_rows), F32),
            anywhere((layout.out_rows, channels), F32),
            anywhere((1, layout.in_rows), F32),
        ],
        (summing.value,),
        [WHOLE],
        name="finish",
    )
    grad_taps = jnp.swapaxes(turn.value[:, :TAPS], 1, 2).reshape(-1, TAPS)[:channels]
    return (
        output[None, None],
        result[None, None],
        own_share(grad_taps),
        own_share(grad_gain[:channels]),
        own_share(grad_shift[:channels]),
        grad_in,
        grad_in_bias[0],
        grad_out,
        grad_out_bias[0],
    )


def solution(mesh):
    spread = P("dp", "fsdp", None, None, None)
    split = P("fsdp", None)
    line = P("fsdp")
    return jax.shard_map(
        local,
        mesh=mesh,
        in_specs=(spread, P(), spread, split, line, line, split, line, split, line),
        out_specs=(spread, spread, split, line, line, split, line, split, line),
        check_vma=False,
    )
```

```python
import functools

import jax
import jax.numpy as jnp
import numpy as np
from jax import lax
from jax.experimental import pallas as pl
from jax.experimental.pallas import tpu as pltpu
from jax.sharding import PartitionSpec as P

KW = 7
SPAN = KW // 2
TILES = 8
EPSILON = 1e-05

LANES = 128
HALF = 64
FINE = 12
PAD = 16
PASSES = (KW + 1) // 2
TAPS = KW * KW
RIM_PAIRS = 4
BASE = 8

F32 = jnp.float32
BF16 = jnp.bfloat16
MIB = 2**20
WHOLE = pl.BlockSpec(memory_space=pltpu.VMEM)
HBM = pl.BlockSpec(memory_space=pl.ANY)


def fast(value):
    return pltpu.with_memory_space_constraint(value, pltpu.VMEM)


def slow(value):
    return pltpu.with_memory_space_constraint(value, pltpu.HBM)


def anywhere(shape, dtype):
    return jax.ShapeDtypeStruct(shape, dtype)


def round_up(value, step):
    return -(-value // step) * step


def call(kernel, outs, operands, in_specs, scratch=(), flops=0, moved=0, grid=None, out_specs=None, limit=10, aliases=None, name=None):
    extra = {} if grid is None else {"grid": grid}
    return pl.pallas_call(
        kernel,
        out_shape=outs,
        in_specs=in_specs,
        out_specs=[WHOLE] * len(outs) if out_specs is None else out_specs,
        scratch_shapes=list(scratch),
        input_output_aliases=aliases or {},
        compiler_params=pltpu.CompilerParams(vmem_limit_bytes=limit * MIB),
        cost_estimate=pl.CostEstimate(flops=flops, bytes_accessed=moved, transcendentals=0),
        name=name,
        **extra,
    )(*operands)


def low_half(rows):
    return lax.broadcasted_iota(jnp.int32, (rows, LANES), 1) < HALF


def swap(value):
    return pltpu.roll(value, HALF, 1)


def tiles_of(channels):
    return [(t, min(LANES, channels - t * LANES)) for t in range(-(-channels // LANES))]


def mask_of_row(turned, row):
    chosen = lax.broadcasted_iota(jnp.int32, (turned.shape[1], LANES), 0) == row
    return jnp.dot(turned, jnp.where(chosen, 1.0, 0.0).astype(BF16), preferred_element_type=F32)


def stage_row(stage, values, width):
    lanes = values.shape[1]
    stage[0, BASE : BASE + width, :lanes] = values
    stage[0, BASE - SPAN : BASE, :lanes] = values[width - SPAN :]
    stage[0, BASE + width : BASE + width + SPAN, :lanes] = values[:SPAN]
    stage[1] = swap(stage[0])


def plane(stage, which, start):
    return stage[which, pl.ds(start, PAD, stride=FINE), :]


def place_row(paired, stage, tile, blocks, pair, side):
    low = low_half(PAD)
    lanes = pl.ds(side * LANES, LANES)
    for k in range((FINE + 2 * SPAN) // 2):
        start = BASE - SPAN + 2 * k
        paired[2 * tile, pair, k, :, lanes] = jnp.where(
            low, plane(stage, 0, start), plane(stage, 1, start + 1)
        ).astype(BF16)
        if 2 * tile + 1 < blocks:
            paired[2 * tile + 1, pair, k, :, lanes] = jnp.where(
                low, plane(stage, 1, start), plane(stage, 0, start + 1)
            ).astype(BF16)


def place_natural(paired, stage, source, channels, width, blocks, pair, side, factor=None):
    for t, lanes in tiles_of(channels):
        values = source(t * LANES, t * LANES + lanes).astype(F32)
        if factor is not None:
            values = values * factor[:, :lanes]
        buffer = stage.at[side, t]
        stage_row(buffer, values, width)
        place_row(paired, buffer, t, blocks, pair, side)


def rim_rows(height):
    inner = (height + 2 * SPAN) // 2 - RIM_PAIRS // 2
    for index in range(SPAN):
        yield 0, index, index // 2, index % 2
    for index in range(SPAN):
        row = SPAN + height + index
        yield 1, index, row // 2 - inner + RIM_PAIRS // 2, row % 2


def build_weights(weights, taps, block, flip):
    lane = lax.broadcasted_iota(jnp.int32, (HALF, LANES), 1)
    sub = lax.broadcasted_iota(jnp.int32, (HALF, LANES), 0)
    diagonal = lax.rem(lane, HALF) == sub
    low = low_half(1)
    zero = jnp.zeros((1, LANES), F32)

    def tap_row(a, b):
        if not (0 <= a < KW and 0 <= b < KW):
            return zero
        index = (KW - 1 - a) * KW + KW - 1 - b if flip else a * KW + b
        return taps[block, index : index + 1, :]

    for m in range(PASSES):
        for s in range(PASSES):
            for place in range(4):
                pr, pj = divmod(place, 2)
                for qr in range(2):
                    a, b = 2 * m + pr - qr, 2 * s + pj
                    row = jnp.where(low, tap_row(a, b), tap_row(a, b - 1))
                    weights[
                        (m * PASSES + s) * 4 * HALF + place * HALF : (m * PASSES + s) * 4 * HALF + (place + 1) * HALF,
                        qr * LANES : (qr + 1) * LANES,
                    ] = jnp.where(diagonal, row, 0.0).astype(BF16)


def pass_rows(paired, rims, block, m, s, pairs):
    places = pl.ds(s, FINE // 2)
    inner = (RIM_PAIRS // 2, pairs + PASSES - 1 - RIM_PAIRS // 2)
    pieces = [rims[block, i, places] for i in range(m, inner[0])]
    pieces.append(paired[block, max(m, inner[0]) : min(m + pairs, inner[1]), places])
    pieces += [rims[block, i - inner[1] + RIM_PAIRS // 2, places] for i in range(inner[1], m + pairs)]
    return jnp.concatenate([piece.reshape(-1, 4 * HALF) for piece in pieces], axis=0)


def convolve_block(paired, rims, weights, block, pairs):
    rows = jnp.concatenate(
        [pass_rows(paired, rims, block, m, s, pairs) for m in range(PASSES) for s in range(PASSES)], axis=1
    )
    return jnp.dot(rows, weights[...], preferred_element_type=F32)


def split_blocks(lower, upper, start, side):
    low = low_half(PAD)
    rows, lanes = pl.ds(start, PAD), pl.ds(side * LANES, LANES)
    first = lower[rows, lanes]
    if upper is None:
        return first, swap(first)
    second = upper[rows, lanes]
    return jnp.where(low, first, swap(second)), jnp.where(low, swap(first), second)


def begin_kernel(
    layout, first, last, land_mask, kernel, in_proj, in_bias, out_proj, gain, shift, out_bias,
    top, bottom, turned_out, shard, packed, table, wide, tall,
):
    count, width, channels = first.shape
    height = turned_out.shape[1]
    tile_index = lax.axis_index("dp") % TILES
    spots = (height, land_mask.shape[0])
    wanted = lax.broadcasted_iota(jnp.int32, spots, 0) + tile_index * height
    chosen = jnp.where(lax.broadcasted_iota(jnp.int32, spots, 1) == wanted, 1.0, 0.0).astype(BF16)
    ocean = land_mask[...].astype(F32).astype(BF16)
    table[...] = jnp.zeros_like(table)
    table[:height, :width] = jnp.dot(chosen, ocean, preferred_element_type=F32)
    turned = table[...].T[:width].astype(BF16)
    turned_out[...] = turned[:, :height]
    for source, out, start in ((first, top, 0), (last, bottom, height - count)):
        for i in range(count):
            factor = mask_of_row(turned, start + i)
            for t, lanes in tiles_of(channels):
                piece = pl.ds(t * LANES, lanes)
                out[i, :, piece] = (source[i, :, piece].astype(F32) * factor[:, :lanes]).astype(BF16)
    wide[...] = jnp.zeros_like(wide)
    wide[: kernel.shape[0], : kernel.shape[1]] = kernel[...].astype(F32)
    shard[...] = wide[:LANES, :LANES].T[: shard.shape[0]].astype(BF16)
    pack_parameters(layout, in_proj, in_bias, out_proj, gain, shift, out_bias, packed, wide, tall)


def prepare_kernel(feats, cot, turned, paired, gbranch, mask, stage, plain):
    width, channels = feats.shape[1:]
    blocks = paired.shape[0]
    step = pl.program_id(0)

    @pl.when(step == 0)
    def _():
        stage[...] = jnp.zeros_like(stage)
        plain[...] = jnp.zeros_like(plain)

    for local_row in range(feats.shape[0]):
        side = local_row % 2
        row = feats.shape[0] * step + local_row
        factor = mask_of_row(turned[...], row)
        rows = pl.ds(BASE, width)
        plain[side, 0, rows, :] = factor
        for t, lanes in tiles_of(channels):
            piece = pl.ds(t * LANES, lanes)
            buffer = stage.at[side, t]
            stage_row(buffer, feats[local_row, :, piece].astype(F32) * factor[:, :lanes], width)
            place_row(paired, buffer, t, blocks, step * (feats.shape[0] // 2) + (SPAN + local_row) // 2, (SPAN + local_row) % 2)
            plain[side, 1 + t, rows, :lanes] = cot[local_row, :, piece].astype(F32) * factor[:, :lanes]
        for r in range(FINE):
            mask[row, r] = plain[side, 0, pl.ds(BASE + r, PAD, stride=FINE), :]
            for t, _unused in tiles_of(channels):
                gbranch[row, r, :, t * LANES : (t + 1) * LANES] = plain[
                    side, 1 + t, pl.ds(BASE + r, PAD, stride=FINE), :
                ].astype(BF16)


def in_place(mine, parts, place):
    value = parts[0]
    for i, part in enumerate(parts[1:], 1):
        value = jnp.where(mine ^ i == place, part, value)
    return value


def forward_kernel(channels, shares, paired, top, bottom, mask, *rest):
    shards, (conv, stats, rims, taps, weights, accs, stage, table) = rest[:shares], rest[shares:]
    height = conv.shape[0]
    blocks, pairs = paired.shape[0], height // 2
    width = top.shape[1]
    share = channels // shares
    mine = lax.axis_index("fsdp")
    stage[...] = jnp.zeros_like(stage)
    table[...] = jnp.zeros_like(table)
    parts = [shard[...].astype(F32) for shard in shards]
    for f in range(shares):
        table[f * share : (f + 1) * share] = in_place(mine, parts, f)[:share]
    for block in range(blocks):
        piece = table[block * HALF : (block + 1) * HALF]
        taps[block] = jnp.concatenate([piece, piece], axis=0).T[: taps.shape[1]]
    last = pairs + PASSES - 1
    first_half = (SPAN % 2) * LANES
    last_half = ((SPAN + height - 1) % 2) * LANES
    rims[:, 1, :, :, first_half : first_half + LANES] = paired[:, 1, :, :, first_half : first_half + LANES]
    rims[:, 2, :, :, last_half : last_half + LANES] = paired[:, last - 2, :, :, last_half : last_half + LANES]
    for below, index, pair, side in rim_rows(height):
        source = bottom if below else top
        place_natural(
            rims, stage, lambda a, b, source=source, index=index: source[index, :, a:b], channels, width, blocks, pair, side
        )
    def counted(row, sums):
        return tuple(total + (mask[row, 2 * k] + mask[row, 2 * k + 1]) for k, total in enumerate(sums))

    count = sum(lax.fori_loop(0, height, counted, (jnp.zeros((PAD, LANES), F32),) * (FINE // 2)))
    count = jnp.sum(count, axis=0, keepdims=True)
    for t, _ in tiles_of(channels):
        lanes = pl.ds(t * LANES, LANES)
        has_upper = 2 * t + 1 < blocks
        for half in range(1 + has_upper):
            build_weights(weights, taps, 2 * t + half, False)
            accs[half] = convolve_block(paired, rims, weights, 2 * t + half, pairs)

        def planes(h, k, side, has_upper=has_upper):
            return split_blocks(accs.at[0], accs.at[1] if has_upper else None, (h * (FINE // 2) + k) * PAD, side)

        zero = jnp.zeros((PAD, LANES), F32)
        total, here = zero, zero
        for k in range(FINE // 2):
            even, odd = planes(0, k, 0)
            total = total + (mask[0, 2 * k] * even + mask[0, 2 * k + 1] * odd)
            here = here + (mask[0, 2 * k] + mask[0, 2 * k + 1])
        near = jnp.sum(total, axis=0, keepdims=True) / jnp.maximum(jnp.sum(here, axis=0, keepdims=True), 1.0)

        def spread(h, sums, lanes=lanes, planes=planes, near=near):
            sums = list(sums)
            for k in range(FINE // 2):
                for side in range(2):
                    row = 2 * h + side
                    for odd, value in enumerate(planes(h, k, side)):
                        r = 2 * k + odd
                        conv[row, r, :, lanes] = value
                        weight = mask[row, r]
                        away = value - near
                        part = weight * away
                        at = 2 * (2 * side + odd)
                        sums[at] = sums[at] + part
                        sums[at + 1] = sums[at + 1] + part * away
            return tuple(sums)

        sums = (zero,) * 8
        for h in range(pairs):
            sums = spread(h, sums)
        total, square = (
            jnp.sum(sums[i] + sums[i + 2] + sums[i + 4] + sums[i + 6], axis=0, keepdims=True) for i in range(2)
        )
        shift = total / jnp.maximum(count, 1.0)
        stats[0:1, lanes] = near + shift
        stats[1:2, lanes] = jnp.maximum(square - total * shift, 0.0)
        stats[2:3, lanes] = count
        stats[3:8, lanes] = jnp.zeros((5, LANES), F32)


def pointwise_kernel(
    channels, real_units, conv, gbranch, feats, turned, vec, w_in, w_out,
    output, act_out, ghid_out, gz_out, z_out, sums, stage,
):
    rows, width = feats.shape[0], feats.shape[1]
    padded = conv.shape[-1]
    cells = rows * FINE * PAD
    hidden_units = act_out.shape[1]
    step = pl.program_id(0)

    @pl.when(step == 0)
    def _():
        sums[...] = jnp.zeros_like(sums)

    one_lane = lax.broadcasted_iota(jnp.int32, (1, padded), 1) == channels
    mean, inverse, gain, shift = (vec[i : i + 1, :] for i in range(4))
    mine = pl.ds(step * rows, rows)
    here = pl.ds(pl.multiple_of(step * cells, cells), cells)
    normed = (conv[mine].reshape(cells, padded) - mean) * inverse
    zvals = jnp.where(one_lane, 1.0, gain * normed + shift).astype(BF16)
    z_out[here, :] = zvals
    upstream = gbranch[mine].reshape(cells, padded)
    chunk = 2 * LANES
    across = (((1,), (1,)), ((), ()))
    c0 = 0.7978845608028654
    c1 = 0.044715 * c0
    for start in range(0, hidden_units, chunk):
        span = pl.ds(start, chunk)
        hidden = jnp.dot(zvals, w_in[:, span], preferred_element_type=F32)
        gact = lax.dot_general(upstream, w_out[span, :], across, preferred_element_type=F32)
        square = hidden * hidden
        share = 0.5 + 0.5 * jnp.tanh(hidden * (c0 + c1 * square))
        act = hidden * share
        slope = share + (act - act * share) * (2.0 * c0 + (6.0 * c1) * square)
        ghid = (gact * slope).astype(BF16)
        act = act.astype(BF16)
        if start + chunk > real_units:
            lane = lax.broadcasted_iota(jnp.int32, (1, chunk), 1)
            act = jnp.where(lane == real_units - start, jnp.ones((), BF16), act)
        act_out[here, span] = act
        ghid_out[here, span] = ghid
    branch = jnp.dot(act_out[here, :], w_out[...], preferred_element_type=F32)
    gz = lax.dot_general(ghid_out[here, :], w_in[...], across, preferred_element_type=F32)
    gz_out[...] = gz.reshape(gz_out.shape)
    sums[0:1, :] += jnp.sum(gz * normed, axis=0, keepdims=True)
    sums[1:2, :] += jnp.sum(gz, axis=0, keepdims=True)
    for row in range(rows):
        factor = mask_of_row(turned[...], step * rows + row)
        for t, lanes in tiles_of(channels):
            for r in range(FINE):
                start = (row * FINE + r) * PAD
                stage[row, t, pl.ds(r, PAD, stride=FINE), :] = branch[start : start + PAD, t * LANES : (t + 1) * LANES]
            piece = pl.ds(t * LANES, lanes)
            values = feats[row, :, piece].astype(F32) + stage[row, t, 0:width, :lanes]
            output[row, :, piece] = (values * factor[:, :lanes]).astype(BF16)


def out_grads_kernel(gbranch, act, grad):
    grad[...] = turned_product(gbranch, act, grad.shape[0])


def turned_product(left, right, rows):
    return lax.dot_general(left[:, :rows], right[...], (((0,), (0,)), ((), ())), preferred_element_type=F32)


def in_grads_kernel(channels, hidden, zvals, ghid, grad_out, kept, *rest):
    sent, grad_in = rest[:-1], rest[-1]
    grad_in[...] = turned_product(zvals, ghid, grad_in.shape[0])
    shares = lax.axis_size("fsdp")
    layout = Packing(channels, hidden, shares)
    last = layout.in_tiles - 1
    lane = lax.broadcasted_iota(jnp.int32, (1, LANES), 1)
    spot = lax.broadcasted_iota(jnp.int32, (layout.out_pad, 1), 0)
    fill = jnp.zeros((layout.in_pad - layout.in_rows, LANES), F32)

    def write(out, j):
        rows = slice(j * layout.in_rows, (j + 1) * layout.in_rows)
        for t in range(layout.in_tiles):
            lanes = slice(t * LANES, (t + 1) * LANES)
            tile = grad_in[rows, lanes]
            if t == last:
                tile = jnp.where(lane == hidden - t * LANES, grad_out[rows, lanes], tile)
            tile = jnp.concatenate([tile, fill], axis=0)
            out[t * layout.in_pad : (t + 1) * layout.in_pad] = tile.astype(out.dtype)
        start = j * layout.out_rows
        aligned = start // LANES * LANES
        stop = min(aligned + (layout.out_tiles + 1) * LANES, grad_out.shape[1])
        part = jnp.where(
            spot == channels, grad_in[: layout.out_pad, aligned:stop], grad_out[: layout.out_pad, aligned:stop]
        )
        if start != aligned:
            part = pltpu.roll(part, stop - start, 1)
        for u in range(layout.out_tiles):
            base = layout.out_base + u * layout.out_pad
            out[base : base + layout.out_pad] = part[:, u * LANES : (u + 1) * LANES].astype(out.dtype)
        out[layout.small_base :] = jnp.zeros((layout.rows - layout.small_base, LANES), out.dtype)

    for mine in range(shares):

        @pl.when(lax.axis_index("fsdp") == mine)
        def _(mine=mine):
            write(kept, mine)
            for i, out in enumerate(sent, 1):
                write(out, mine ^ i)


def finish_kernel(channels, hidden, packed, grad_in, grad_in_bias, grad_out, grad_out_bias):
    layout = Packing(channels, hidden, channels // grad_in.shape[0])
    for t in range(layout.in_tiles):
        stop = min((t + 1) * LANES, hidden)
        tile = packed[t * layout.in_pad : (t + 1) * layout.in_pad].astype(F32)
        grad_in[:, t * LANES : stop] = tile[: layout.in_rows, : stop - t * LANES]
    tall = jnp.concatenate([tile, jnp.zeros((LANES - layout.in_pad, LANES), F32)], axis=0).T
    at = hidden - (layout.in_tiles - 1) * LANES
    grad_out_bias[...] = tall[at : at + 1, : layout.in_rows]
    for u in range(layout.out_tiles):
        base = layout.out_base + u * layout.out_pad
        tile = packed[base : base + layout.out_pad].astype(F32)
        stop = min((u + 1) * LANES, layout.out_rows)
        count = stop - u * LANES
        grad_in_bias[:, u * LANES : stop] = tile[channels : channels + 1, :count]
        fill = jnp.zeros((round_up(layout.out_pad, LANES) - layout.out_pad, LANES), F32)
        grad_out[u * LANES : stop, :] = jnp.concatenate([tile, fill], axis=0).T[:count, :channels]


def finish_taps_kernel(share, *refs):
    grad = refs[-1]
    total = tree([ref[...] for ref in refs[:-1]], lambda a, b: a + b)
    wide = jnp.concatenate([total[t] for t in range(total.shape[0])], axis=1)
    for f in range(lax.axis_size("fsdp")):

        @pl.when(lax.axis_index("fsdp") == f)
        def _(f=f):
            start = f * share
            turned = pltpu.roll(wide, wide.shape[1] - start, 1) if start else wide
            grad[...] = turned[: grad.shape[0], :share]


def tree(values, merge):
    while len(values) > 1:
        values = [merge(values[i], values[i + 1]) for i in range(0, len(values), 2)]
    return values[0]


def merge_stats(mine, other):
    count = mine[2:3] + other[2:3]
    safe = jnp.maximum(count, 1.0)
    mean = (mine[0:1] * mine[2:3] + other[0:1] * other[2:3]) / safe
    away = mine[0:1] - other[0:1]
    spread = mine[1:2] + other[1:2] + away * away * (mine[2:3] * other[2:3] / safe)
    return jnp.concatenate([mean, spread, count, jnp.zeros_like(mine[3:8])], axis=0)


def stats_kernel(*refs):
    refs[-1][...] = tree([ref[...] for ref in refs[:-1]], merge_stats)


def norm_kernel(vectors, *refs):
    stats = tree([ref[...] for ref in refs[:-1]], merge_stats)
    count = jnp.maximum(stats[2:3], 1.0)
    inverse = lax.rsqrt(stats[1:2] / count + EPSILON)
    refs[-1][...] = jnp.concatenate(
        [stats[0:1], inverse, vectors[0:2, :], count, jnp.zeros((3, stats.shape[1]), F32)], axis=0
    )


def sums_kernel(*refs):
    refs[-1][...] = tree([ref[...] for ref in refs[:-1]], lambda a, b: a + b)


def slopes_kernel(vec, *refs):
    sums = tree([ref[...] for ref in refs[:-1]], lambda a, b: a + b)
    scaled = vec[1:2, :] * vec[2:3, :]
    count = vec[4:5, :]
    refs[-1][...] = jnp.concatenate(
        [vec[0:2, :], scaled, scaled * sums[1:2] / count, scaled * sums[0:1] / count, sums[0:2], sums[2:3]], axis=0
    )


class Packing:
    def __init__(self, channels, hidden, shares):
        self.in_rows = channels // shares
        self.in_pad = round_up(self.in_rows, 16)
        self.in_tiles = -(-(hidden + 1) // LANES)
        self.out_rows = hidden // shares
        self.out_tiles = -(-self.out_rows // LANES)
        self.out_pad = round_up(max(channels + 1, self.out_rows), 16)
        self.out_base = self.in_pad * self.in_tiles
        self.small_base = self.out_base + self.out_pad * self.out_tiles
        self.small = self.out_tiles + 3
        self.rows = round_up(self.small_base + self.small, 32)


def pack_parameters(layout, in_proj, in_bias, out_proj, gain, shift, out_bias, packed, wide, tall):
    wide[...] = jnp.zeros_like(wide)
    tall[...] = jnp.zeros_like(tall)
    wide[: layout.in_rows, : in_proj.shape[1]] = in_proj[...].astype(F32)
    for t in range(layout.in_tiles):
        packed[t * layout.in_pad : (t + 1) * layout.in_pad] = wide[: layout.in_pad, t * LANES : (t + 1) * LANES].astype(BF16)
    tall[: layout.out_rows, : out_proj.shape[1]] = out_proj[...].astype(F32)
    for u in range(layout.out_tiles):
        base = layout.out_base + u * layout.out_pad
        packed[base : base + layout.out_pad] = tall[:, u * LANES : (u + 1) * LANES].astype(BF16)
    wide[...] = jnp.zeros_like(wide)
    for i, small in enumerate((in_bias, gain, shift, out_bias)):
        wide[i : i + 1, : small.shape[0]] = small[...].reshape(1, -1).astype(F32)
    rows = [wide[0:1, u * LANES : (u + 1) * LANES] for u in range(layout.out_tiles)]
    rows += [wide[i + 1 : i + 2, :LANES] for i in range(3)]
    rows.append(jnp.zeros((layout.rows - layout.small_base - layout.small, LANES), F32))
    packed[layout.small_base :] = jnp.concatenate(rows, axis=0).astype(BF16)


def assemble_kernel(layout, shares, *refs):
    packed, (w_in, w_out, vectors, wide, tall) = refs[:shares], refs[shares:]
    mine = lax.axis_index("fsdp")

    def rows_of(f, start, stop):
        return in_place(mine, [part[start:stop].astype(F32) for part in packed], f)

    wide[...] = jnp.zeros_like(wide)
    tall[...] = jnp.zeros_like(tall)
    channels, hidden = layout.in_rows * shares, layout.out_rows * shares
    in_bias = jnp.zeros((8, wide.shape[1]), F32)
    smalls = [jnp.zeros((8, tall.shape[1]), F32)] * 3
    for f in range(shares):
        for t in range(layout.in_tiles):
            tile = rows_of(f, t * layout.in_pad, (t + 1) * layout.in_pad)
            wide[f * layout.in_rows : (f + 1) * layout.in_rows, t * LANES : (t + 1) * LANES] = tile[: layout.in_rows]
        for u in range(layout.out_tiles):
            base = layout.out_base + u * layout.out_pad
            tile = rows_of(f, base, base + layout.out_pad)
            tall[f * layout.out_rows : (f + 1) * layout.out_rows, u * LANES : (u + 1) * LANES] = tile[: layout.out_rows]
        small = rows_of(f, layout.small_base, layout.rows)

        def spread(first, count, lanes, turn):
            pieces = [small[first + u : first + u + 1] for u in range(count)]
            pieces.append(jnp.zeros((1, lanes - count * LANES), F32))
            row = jnp.broadcast_to(jnp.concatenate(pieces, axis=1), (8, lanes))
            return pltpu.roll(row, turn, 1) if turn else row

        in_bias = in_bias + spread(0, layout.out_tiles, wide.shape[1], f * layout.out_rows)
        smalls = [
            total + spread(layout.out_tiles + i, 1, tall.shape[1], f * layout.in_rows)
            for i, total in enumerate(smalls)
        ]
    wide[channels : channels + 1] = in_bias[:1]
    tall[hidden : hidden + 1] = smalls[2][:1]
    w_in[...] = wide[...].astype(BF16)
    w_out[...] = tall[...].astype(BF16)
    vectors[...] = jnp.concatenate([smalls[0][:1], smalls[1][:1], jnp.zeros((6, tall.shape[1]), F32)], axis=0)


def shifted_planes(values, real):
    out = []
    for r in range(-SPAN, FINE + SPAN):
        value = values[r % FINE]
        if r < 0:
            value = jnp.concatenate([value[real - 1 : real], value[: PAD - 1]], axis=0)
        elif r >= FINE:
            value = jnp.concatenate([value[1:real], value[:1], value[: PAD - real]], axis=0)
        out.append(value)
    return out


def join_planes(first, second):
    low = low_half(PAD)
    return (
        jnp.where(low, first, swap(second)).astype(BF16),
        jnp.where(low, swap(first), second).astype(BF16),
    )


def place_planes(paired, planes, tile, blocks, pair, side):
    out_lanes = pl.ds(side * LANES, LANES)
    for k in range(len(planes) // 2):
        for half, value in enumerate(join_planes(planes[2 * k], planes[2 * k + 1])):
            if 2 * tile + half < blocks:
                paired[2 * tile + half, pair, k, :, out_lanes] = value


def arrange_kernel(channels, real, gz, conv, mask, vec, edges, gpaired, own):
    height = conv.shape[0]
    blocks = own.shape[0]
    count = gz.shape[0] // 2
    for local_pair in range(count):
        h = pl.program_id(0) * count + local_pair
        for t, _unused in tiles_of(channels):
            lanes = pl.ds(t * LANES, LANES)
            mean, inverse, scaled, bias, slope = (vec[i : i + 1, lanes] for i in range(5))
            for side in range(2):
                row = 2 * h + side
                values = []
                for r in range(FINE):
                    normed = (conv[row, r, :, lanes] - mean) * inverse
                    values.append(scaled * gz[2 * local_pair + side, r, :, lanes] - mask[row, r] * (bias + normed * slope))
                out_lanes = pl.ds(side * LANES, LANES)
                for k in range(FINE // 2):
                    rows = pl.ds((h * (FINE // 2) + k) * PAD, PAD)
                    for half, value in enumerate(join_planes(values[2 * k], values[2 * k + 1])):
                        if 2 * t + half < blocks:
                            own[2 * t + half, rows, out_lanes] = value
                place_planes(
                    gpaired, shifted_planes(values, real), t, blocks, h + (SPAN + side) // 2, (SPAN + side) % 2
                )
                for edge, near in ((0, row < SPAN), (1, row >= height - SPAN)):

                    @pl.when(near)
                    def _(edge=edge, row=row, values=values, lanes=lanes):
                        place = row - (height - SPAN) * edge
                        for r in range(FINE):
                            edges[edge, place, r, :, lanes] = values[r].astype(BF16)


def taps_kernel(tile, own, paired, rims, select, grad_taps):
    blocks, pairs = own.shape[0], paired.shape[1] - PASSES + 1
    lane = lax.broadcasted_iota(jnp.int32, (HALF, 2 * LANES), 1)
    sub = lax.broadcasted_iota(jnp.int32, (HALF, 2 * LANES), 0)
    diagonal = lax.rem(lane, HALF) == sub
    low = low_half(grad_taps.shape[0])
    totals = []
    for block in range(2 * tile, min(2 * tile + 2, blocks)):
        turned = own[block].T
        found = []
        for m in range(PASSES):
            for s in range(PASSES):
                product = jnp.dot(turned, pass_rows(paired, rims, block, m, s, pairs), preferred_element_type=F32)
                for q in range(4):
                    part = product[q * HALF : (q + 1) * HALF]
                    found.append(jnp.sum(jnp.where(diagonal, part, 0.0), axis=0, keepdims=True))
        found = jnp.concatenate(found, axis=0)
        total = None
        for place in range(4):
            group = jnp.dot(select[place], found, preferred_element_type=F32, precision=lax.Precision.HIGHEST)
            group = group[:, (place // 2) * LANES : (place // 2 + 1) * LANES]
            if place % 2:
                group = swap(group)
            total = group if total is None else total + group
        totals.append(total)
    second = swap(totals[1]) if len(totals) > 1 else jnp.zeros_like(totals[0])
    grad_taps[...] = jnp.where(low, totals[0], second)


def backward_kernel(tile, real, gpaired, top, bottom, taps, cot, turned, *rest):
    result, rims, weights, accs, stage = rest[-5:]
    height, width = cot.shape[0], cot.shape[1]
    blocks, pairs = gpaired.shape[0], height // 2
    last = pairs + PASSES - 1
    first_half = (SPAN % 2) * LANES
    last_half = ((SPAN + height - 1) % 2) * LANES
    has_upper = 2 * tile + 1 < blocks
    for half in range(1 + has_upper):
        source = gpaired.at[2 * tile + half]
        rims[half, 1, :, :, first_half : first_half + LANES] = source[1, :, :, first_half : first_half + LANES]
        rims[half, 2, :, :, last_half : last_half + LANES] = source[last - 2, :, :, last_half : last_half + LANES]
    for below, index, pair, side in rim_rows(height):
        source = bottom if below else top
        values = [source[index, r, :, tile * LANES : (tile + 1) * LANES].astype(F32) for r in range(FINE)]
        place_planes(rims, shifted_planes(values, real), 0, 1 + has_upper, pair, side)
    for half in range(1 + has_upper):
        block = 2 * tile + half
        build_weights(weights, taps, block, True)
        accs[half] = convolve_block(gpaired.at[block : block + 1], rims.at[half : half + 1], weights, 0, pairs)

    def spread(h, _):
        for side in range(2):
            row = 2 * h + side
            for k in range(FINE // 2):
                even, odd = split_blocks(
                    accs.at[0], accs.at[1] if has_upper else None, (h * (FINE // 2) + k) * PAD, side
                )
                stage[side, pl.ds(2 * k, PAD, stride=FINE), :] = even
                stage[side, pl.ds(2 * k + 1, PAD, stride=FINE), :] = odd
            values = cot[row].astype(F32) + stage[side, 0:width]
            result[row] = (values * mask_of_row(turned[...], row)).astype(BF16)
        return 0

    for h in range(pairs):
        spread(h, 0)


def bits(size):
    bit = 1
    while bit < size:
        yield bit
        bit *= 2


def swapped(value, axis, flip):
    size = lax.axis_size(axis)
    return lax.ppermute(value, axis, [(i, i ^ flip) for i in range(size)])


def side_of(axis, bit):
    return lax.axis_index(axis) // bit % 2


def phases(*axes):
    out = []
    for axis in axes:
        left = list(bits(lax.axis_size(axis)))
        while left:
            near, left = left[:2], left[2:]
            out.append((axis, near if len(near) < 2 else [near[0], near[1], near[0] | near[1]]))
    return out


def tied(*values):
    return lax.optimization_barrier(values)


def keep_and_send(value, axis, bit, dim):
    side = side_of(axis, bit)
    return (
        lax.dynamic_index_in_dim(value, side, dim, keepdims=False),
        lax.dynamic_index_in_dim(value, 1 - side, dim, keepdims=False),
    )


def beside(work, *values):
    done = work() if work else ()
    return lax.optimization_barrier((done, values))


class Spreading:
    def __init__(self, value):
        self.value = value
        over = list(bits(lax.axis_size("dp")))
        over = over[1:] + over[:1]
        self.moves = [("half", bit) for bit in over[:1]] + [("whole", bit) for bit in over[1:]]
        self.moves += [("join", bit) for bit in over[:1]]

    def start(self):
        if not self.moves:
            return ()
        self.kind, self.bit = self.moves.pop(0)
        if self.kind == "half":
            self.kept, sent = keep_and_send(self.value.reshape(2, -1, self.value.shape[-1]), "dp", self.bit, 0)
            sent = sent.astype(BF16)
        else:
            self.kept = sent = self.value.astype(BF16)
        self.running = True
        return swapped(sent, "dp", self.bit)

    def finish(self, other):
        if isinstance(other, tuple):
            return
        if self.kind == "join":
            first = side_of("dp", self.bit) == 0
            self.value = jnp.concatenate(
                [jnp.where(first, self.kept, other), jnp.where(first, other, self.kept)], axis=0
            )
        else:
            self.value = self.kept.astype(F32) + other.astype(F32)


def rims_of(top_rows, bottom_rows):
    size = lax.axis_size("dp")
    down = [(i, i + 1) for i in range(size - 1) if (i + 1) % TILES]
    up = [(j, i) for i, j in down]
    return lax.ppermute(bottom_rows, "dp", down), lax.ppermute(top_rows, "dp", up)


def tap_selectors(rows):
    out = np.zeros((4, rows, PASSES * PASSES * 4), np.float32)
    for m in range(PASSES):
        for s in range(PASSES):
            for q in range(4):
                for p in range(4):
                    a = 2 * m + p // 2 - q // 2
                    b = 2 * s + p % 2 - q % 2
                    if 0 <= a < KW and 0 <= b < KW:
                        out[p, a * KW + b, (m * PASSES + s) * 4 + q] = 1.0
    return out


def own_share(value):
    share = value.shape[0] // lax.axis_size("fsdp")
    return lax.dynamic_slice_in_dim(value, lax.axis_index("fsdp") * share, share, 0)


def local(features, land_mask, cotangent, kernel, norm_gain, norm_shift, in_proj, in_bias, out_proj, out_bias):
    feats, cot = features[0, 0], cotangent[0, 0]
    height, width, channels = feats.shape
    hidden = in_proj.shape[1]
    shares = lax.axis_size("fsdp")
    padded = round_up(channels + 1, LANES)
    hidden_pad = round_up(hidden + 1, 2 * LANES)
    blocks = -(-channels // HALF)
    pairs = height // 2
    planes_in = (FINE + 2 * SPAN) // 2
    row_pairs = pairs + PASSES - 1
    cells = height * FINE * PAD
    block_rows = pairs * (FINE // 2) * PAD
    stage_rows = round_up(BASE + SPAN + FINE * PAD, 8)
    tile_count = len(tiles_of(channels))
    tap_rows = round_up(TAPS, 8)
    real = width // FINE
    layout = Packing(channels, hidden, shares)

    edge = lambda at: pl.BlockSpec((SPAN, width, channels), lambda i: (at, 0, 0))
    whole = lambda array: pl.BlockSpec(array.shape, lambda i: (0,) * array.ndim)
    natural_shape = (height, width, channels)
    edge_shape = (SPAN, width, channels)
    paired_shape = (blocks, row_pairs, planes_in, PAD, 4 * HALF)
    rims_shape = (blocks, RIM_PAIRS, planes_in, PAD, 4 * HALF)
    plane_shape = (height, FINE, PAD, padded)
    mask_shape = (height, FINE, PAD, LANES)
    small = (kernel.T, in_proj, in_bias, out_proj, norm_gain, norm_shift, out_bias)
    first_rows, last_rows, turned, shard, packed = call(
        functools.partial(begin_kernel, layout),
        [
            anywhere(edge_shape, BF16),
            anywhere(edge_shape, BF16),
            anywhere((width, height), BF16),
            anywhere((layout.in_pad, LANES), BF16),
            anywhere((layout.rows, LANES), BF16),
        ],
        (slow(feats), slow(feats), slow(land_mask), *(slow(v) for v in small)),
        [edge(0), edge(height // SPAN - 1), whole(land_mask)] + [whole(v) for v in small],
        [
            pltpu.VMEM((round_up(height, LANES), round_up(width, LANES)), F32),
            pltpu.VMEM((round_up(layout.in_pad, LANES), hidden_pad), F32),
            pltpu.VMEM((layout.out_pad, padded), F32),
        ],
        grid=(1,),
        out_specs=[WHOLE] * 5,
        name="begin",
    )
    others = list(range(1, shares))
    six = 6 if height % 6 == 0 else 2
    stage = pltpu.VMEM((2, tile_count, 2, stage_rows, LANES), F32)
    top, bottom = rims_of(first_rows, last_rows)
    shards = [swapped(shard, "fsdp", i) for i in others]
    (paired, gbranch, mask), (packed, *shards) = beside(
        lambda: call(
            prepare_kernel,
            [pltpu.VMEM(paired_shape, BF16), pltpu.VMEM(plane_shape, BF16), pltpu.VMEM(mask_shape, F32)],
            (slow(feats), slow(cot), turned),
            [pl.BlockSpec((six, width, channels), lambda i: (i, 0, 0))] * 2 + [WHOLE],
            [stage, pltpu.VMEM((2, 1 + tile_count, stage_rows, LANES), F32)],
            flops=10**8,
            moved=10 * MIB,
            grid=(height // six,),
            name="prepare",
        ),
        packed,
        shard,
        *shards,
    )

    accs = pltpu.VMEM((2, block_rows, 4 * HALF), F32)
    weights = pltpu.VMEM((PASSES * PASSES * 4 * HALF, 4 * HALF), BF16)
    (conv, stats, rims, taps), packed = beside(
        lambda: call(
            functools.partial(forward_kernel, channels, shares),
            [
                pltpu.VMEM(plane_shape, F32),
                anywhere((8, padded), F32),
                pltpu.VMEM(rims_shape, BF16),
                anywhere((blocks, tap_rows, LANES), F32),
            ],
            (fast(paired), top, bottom, fast(mask), *shards),
            [WHOLE] * (4 + shares),
            [weights, accs, stage, pltpu.VMEM((blocks * HALF, LANES), F32)],
            flops=9 * 10**9,
            limit=12,
            name="forward",
        ),
        packed,
        *(swapped(packed, "fsdp", i) for i in others),
    )
    assemble = lambda: call(
        functools.partial(assemble_kernel, layout, shares),
        [
            anywhere((padded, hidden_pad), BF16),
            anywhere((hidden_pad, padded), BF16),
            anywhere((8, padded), F32),
        ],
        packed,
        [WHOLE] * shares,
        [pltpu.VMEM((padded, hidden_pad), F32), pltpu.VMEM((hidden_pad, padded), F32)],
        name="assemble",
    )
    row_sums = anywhere((8, padded), F32)
    combine = lambda kernel, *values: call(kernel, [row_sums], values, [WHOLE] * len(values), limit=4, name="combine")[0]
    rounds = phases("fsdp", "dp")
    work = assemble
    for n, (axis, flips) in enumerate(rounds):
        done, values = beside(work, stats, *(swapped(stats, axis, i) for i in flips))
        if n == 0:
            w_in, w_out, vectors = done
        if n + 1 < len(rounds):
            stats = combine(stats_kernel, *values)
        work = None
    vec = combine(norm_kernel, vectors, *values)

    rows = 2
    steps = height // rows
    by_row = lambda *rest: pl.BlockSpec((rows, *rest), lambda i: (i,) + (0,) * len(rest))
    output, act, ghid, gz, zvals, sums = call(
        functools.partial(pointwise_kernel, channels, hidden),
        [
            anywhere(natural_shape, BF16),
            pltpu.VMEM((cells, hidden_pad), BF16),
            pltpu.VMEM((cells, hidden_pad), BF16),
            pltpu.HBM(plane_shape, F32),
            pltpu.VMEM((cells, padded), BF16),
            row_sums,
        ],
        (fast(conv), fast(gbranch), slow(feats), turned, vec, w_in, w_out),
        [WHOLE, WHOLE, by_row(width, channels)] + [WHOLE] * 4,
        [pltpu.VMEM((rows, tile_count, round_up(FINE * PAD, 8), LANES), F32)],
        flops=14 * 10**9,
        grid=(steps,),
        out_specs=[by_row(width, channels), WHOLE, WHOLE, by_row(FINE, PAD, padded), WHOLE, WHOLE],
        limit=14,
        name="pointwise",
    )

    grad_rows = round_up(channels + 1, 16)

    def weight_grads():
        (grad_out,) = call(
            out_grads_kernel,
            [pltpu.VMEM((grad_rows, hidden_pad), F32)],
            (fast(gbranch.reshape(cells, padded)), fast(act)),
            [WHOLE] * 2,
            flops=3 * 10**9,
            limit=4,
            name="out_grads",
        )
        return call(
            functools.partial(in_grads_kernel, channels, hidden),
            [pltpu.VMEM((layout.rows, LANES), F32)] + [anywhere((layout.rows, LANES), BF16)] * len(others),
            (fast(zvals), fast(ghid), fast(grad_out)),
            [WHOLE] * 3,
            [pltpu.VMEM((grad_rows, hidden_pad), F32)],
            flops=3 * 10**9,
            limit=8,
            name="in_grads",
        )

    work = weight_grads
    for n, (axis, flips) in enumerate(rounds):
        done, values = beside(work, sums, *(swapped(sums, axis, i) for i in flips))
        if n == 0:
            kept, *sent = done
            sent = [swapped(v, "fsdp", i) for i, v in zip(others, sent)]
        if n + 1 < len(rounds):
            sums = combine(sums_kernel, *values)
        work = None
    gvec = combine(slopes_kernel, vec, *values)
    edges, gpaired, own = call(
        functools.partial(arrange_kernel, channels, real),
        [
            anywhere((2, SPAN, FINE, PAD, padded), BF16),
            pltpu.VMEM(paired_shape, BF16),
            pltpu.VMEM((blocks, block_rows, 4 * HALF), BF16),
        ],
        (slow(gz), fast(conv), fast(mask), gvec),
        [pl.BlockSpec(plane_shape, lambda i: (0, 0, 0, 0))] + [WHOLE] * 3,
        flops=10**8,
        moved=10 * MIB,
        grid=(1,),
        out_specs=[WHOLE] * 3,
        limit=14,
        name="arrange",
    )
    select = jnp.asarray(tap_selectors(tap_rows))
    gtop, gbottom = rims_of(edges[0], edges[1])

    def taps_of(t):
        return lambda: call(
            functools.partial(taps_kernel, t),
            [anywhere((tap_rows, LANES), F32)],
            (fast(own), fast(paired), fast(rims), select),
            [WHOLE] * 4,
            flops=4 * 10**9,
            limit=6,
            name="taps",
        )

    (grad_taps,), sent = beside(taps_of(0), *sent)
    grad_taps = [grad_taps]
    spreading = Spreading(sum((v.astype(F32) for v in sent), kept))
    for t in range(1, tile_count):
        (more,), (there,) = beside(taps_of(t), spreading.start())
        spreading.finish(there)
        grad_taps.append(more)
    gtop, gbottom, *grad_taps = tied(gtop, gbottom, *grad_taps)
    grad_taps = jnp.stack(grad_taps)

    def backward_of(t, *before):
        column = pl.BlockSpec((height, width, LANES), lambda i: (0, 0, t))
        return lambda: call(
            functools.partial(backward_kernel, t, real),
            [anywhere(natural_shape, BF16)],
            (fast(gpaired), gtop, gbottom, taps, slow(cot), turned, *before),
            [WHOLE] * 4 + [column, WHOLE] + [HBM] * len(before),
            [
                pltpu.VMEM((2, RIM_PAIRS, planes_in, PAD, 4 * HALF), BF16),
                weights,
                accs,
                pltpu.VMEM((2, round_up(FINE * PAD, 8), LANES), F32),
            ],
            flops=4 * 10**9,
            limit=12,
            grid=(1,),
            out_specs=[column],
            aliases={6: 0} if before else {},
            name="backward",
        )

    result = ()
    for n in range(max(tile_count, len(rounds))):
        axis, flips = rounds[n] if n < len(rounds) else (None, ())
        work = backward_of(n, *result) if n < tile_count else None
        done, (there, *values) = beside(
            work, spreading.start(), grad_taps, *(swapped(grad_taps, axis, i) for i in flips)
        )
        result = done or result
        spreading.finish(there)
        if n + 1 < len(rounds):
            grad_taps = tree(list(values), jnp.add)
        elif n + 1 == len(rounds):
            last_taps = values
    while spreading.moves:
        spreading.finish(spreading.start())
    (result,) = result
    (grad_kernel,) = call(
        functools.partial(finish_taps_kernel, layout.in_rows),
        [anywhere((TAPS, layout.in_rows), F32)],
        last_taps,
        [WHOLE] * len(last_taps),
        limit=4,
        name="finish_taps",
    )
    grad_in, grad_in_bias, grad_out, grad_out_bias = call(
        functools.partial(finish_kernel, channels, hidden),
        [
            anywhere((layout.in_rows, hidden), F32),
            anywhere((1, layout.out_rows), F32),
            anywhere((layout.out_rows, channels), F32),
            anywhere((1, layout.in_rows), F32),
        ],
        (spreading.value,),
        [WHOLE],
        name="finish",
    )
    return (
        output[None, None],
        result[None, None],
        grad_kernel.T,
        own_share(gvec[5, :channels]),
        own_share(gvec[6, :channels]),
        grad_in,
        grad_in_bias[0],
        grad_out,
        grad_out_bias[0],
    )


def solution(mesh):
    spread = P("dp", "fsdp", None, None, None)
    split = P("fsdp", None)
    line = P("fsdp")
    return jax.shard_map(
        local,
        mesh=mesh,
        in_specs=(spread, P(), spread, split, line, line, split, line, split, line),
        out_specs=(spread, spread, split, line, line, split, line, split, line),
        check_vma=False,
    )
```

```python
import functools

import jax
import jax.numpy as jnp
import numpy as np
from jax import lax
from jax.experimental import pallas as pl
from jax.experimental.pallas import tpu as pltpu
from jax.sharding import PartitionSpec as P

KW = 7
SPAN = KW // 2
TILES = 8
EPSILON = 1e-05

LANES = 128
HALF = 64
FINE = 12
PAD = 16
PASSES = (KW + 1) // 2
TAPS = KW * KW
RIM_PAIRS = 4
BASE = 8

F32 = jnp.float32
BF16 = jnp.bfloat16
MIB = 2**20
WHOLE = pl.BlockSpec(memory_space=pltpu.VMEM)
HBM = pl.BlockSpec(memory_space=pl.ANY)


def fast(value):
    return pltpu.with_memory_space_constraint(value, pltpu.VMEM)


def slow(value):
    return pltpu.with_memory_space_constraint(value, pltpu.HBM)


def anywhere(shape, dtype):
    return jax.ShapeDtypeStruct(shape, dtype)


def round_up(value, step):
    return -(-value // step) * step


def call(kernel, outs, operands, in_specs, scratch=(), flops=0, moved=0, grid=None, out_specs=None, limit=10, aliases=None, name=None):
    extra = {} if grid is None else {"grid": grid}
    return pl.pallas_call(
        kernel,
        out_shape=outs,
        in_specs=in_specs,
        out_specs=[WHOLE] * len(outs) if out_specs is None else out_specs,
        scratch_shapes=list(scratch),
        input_output_aliases=aliases or {},
        compiler_params=pltpu.CompilerParams(vmem_limit_bytes=limit * MIB),
        cost_estimate=pl.CostEstimate(flops=flops, bytes_accessed=moved, transcendentals=0),
        name=name,
        **extra,
    )(*operands)


def low_half(rows):
    return lax.broadcasted_iota(jnp.int32, (rows, LANES), 1) < HALF


def swap(value):
    return pltpu.roll(value, HALF, 1)


def tiles_of(channels):
    return [(t, min(LANES, channels - t * LANES)) for t in range(-(-channels // LANES))]


def mask_of_row(turned, row):
    chosen = lax.broadcasted_iota(jnp.int32, (turned.shape[1], LANES), 0) == row
    return jnp.dot(turned, jnp.where(chosen, 1.0, 0.0).astype(BF16), preferred_element_type=F32)


def stage_row(stage, values, width):
    lanes = values.shape[1]
    stage[0, BASE : BASE + width, :lanes] = values
    stage[0, BASE - SPAN : BASE, :lanes] = values[width - SPAN :]
    stage[0, BASE + width : BASE + width + SPAN, :lanes] = values[:SPAN]
    stage[1] = swap(stage[0])


def plane(stage, which, start):
    return stage[which, pl.ds(start, PAD, stride=FINE), :]


def place_row(paired, stage, tile, blocks, pair, side):
    low = low_half(PAD)
    lanes = pl.ds(side * LANES, LANES)
    for k in range((FINE + 2 * SPAN) // 2):
        start = BASE - SPAN + 2 * k
        paired[2 * tile, pair, k, :, lanes] = jnp.where(
            low, plane(stage, 0, start), plane(stage, 1, start + 1)
        ).astype(BF16)
        if 2 * tile + 1 < blocks:
            paired[2 * tile + 1, pair, k, :, lanes] = jnp.where(
                low, plane(stage, 1, start), plane(stage, 0, start + 1)
            ).astype(BF16)


def place_natural(paired, stage, source, channels, width, blocks, pair, side, factor=None):
    for t, lanes in tiles_of(channels):
        values = source(t * LANES, t * LANES + lanes).astype(F32)
        if factor is not None:
            values = values * factor[:, :lanes]
        buffer = stage.at[side, t]
        stage_row(buffer, values, width)
        place_row(paired, buffer, t, blocks, pair, side)


def rim_rows(height):
    inner = (height + 2 * SPAN) // 2 - RIM_PAIRS // 2
    for index in range(SPAN):
        yield 0, index, index // 2, index % 2
    for index in range(SPAN):
        row = SPAN + height + index
        yield 1, index, row // 2 - inner + RIM_PAIRS // 2, row % 2


def build_weights(weights, taps, block, flip):
    lane = lax.broadcasted_iota(jnp.int32, (HALF, LANES), 1)
    sub = lax.broadcasted_iota(jnp.int32, (HALF, LANES), 0)
    diagonal = lax.rem(lane, HALF) == sub
    low = low_half(1)
    zero = jnp.zeros((1, LANES), F32)

    def tap_row(a, b):
        if not (0 <= a < KW and 0 <= b < KW):
            return zero
        index = (KW - 1 - a) * KW + KW - 1 - b if flip else a * KW + b
        return taps[block, index : index + 1, :]

    for m in range(PASSES):
        for s in range(PASSES):
            for place in range(4):
                pr, pj = divmod(place, 2)
                for qr in range(2):
                    a, b = 2 * m + pr - qr, 2 * s + pj
                    row = jnp.where(low, tap_row(a, b), tap_row(a, b - 1))
                    weights[
                        (m * PASSES + s) * 4 * HALF + place * HALF : (m * PASSES + s) * 4 * HALF + (place + 1) * HALF,
                        qr * LANES : (qr + 1) * LANES,
                    ] = jnp.where(diagonal, row, 0.0).astype(BF16)


def pass_rows(paired, rims, block, m, s, runs):
    places = pl.ds(s, FINE // 2)
    side = RIM_PAIRS // 2
    inner = paired.shape[1] - side
    pieces = []
    for start, stop in runs:
        start, stop = start + m, stop + m
        pieces += [rims[block, i, places] for i in range(start, min(stop, side))]
        if max(start, side) < min(stop, inner):
            pieces.append(paired[block, max(start, side) : min(stop, inner), places])
        pieces += [rims[block, i - inner + side, places] for i in range(max(start, inner), stop)]
    return jnp.concatenate([piece.reshape(-1, 4 * HALF) for piece in pieces], axis=0)


def convolve_block(paired, rims, weights, block, runs):
    rows = jnp.concatenate(
        [pass_rows(paired, rims, block, m, s, runs) for m in range(PASSES) for s in range(PASSES)], axis=1
    )
    return jnp.dot(rows, weights[...], preferred_element_type=F32)


def inner_runs(pairs):
    side = RIM_PAIRS // 2
    return [(side, pairs - side)], [(0, side), (pairs - side, pairs)]


def pairs_of(runs):
    return [h for start, stop in runs for h in range(start, stop)]


def split_blocks(lower, upper, start, side):
    low = low_half(PAD)
    rows, lanes = pl.ds(start, PAD), pl.ds(side * LANES, LANES)
    first = lower[rows, lanes]
    if upper is None:
        return first, swap(first)
    second = upper[rows, lanes]
    return jnp.where(low, first, swap(second)), jnp.where(low, swap(first), second)


def begin_kernel(
    layout, first, last, land_mask, kernel, in_proj, in_bias, out_proj, gain, shift, out_bias,
    top, bottom, turned_out, shard, packed, table, wide, tall,
):
    count, width, channels = first.shape
    height = turned_out.shape[1]
    tile_index = lax.axis_index("dp") % TILES
    spots = (height, land_mask.shape[0])
    wanted = lax.broadcasted_iota(jnp.int32, spots, 0) + tile_index * height
    chosen = jnp.where(lax.broadcasted_iota(jnp.int32, spots, 1) == wanted, 1.0, 0.0).astype(BF16)
    ocean = land_mask[...].astype(F32).astype(BF16)
    table[...] = jnp.zeros_like(table)
    table[:height, :width] = jnp.dot(chosen, ocean, preferred_element_type=F32)
    turned = table[...].T[:width].astype(BF16)
    turned_out[...] = turned[:, :height]
    for source, out, start in ((first, top, 0), (last, bottom, height - count)):
        for i in range(count):
            factor = mask_of_row(turned, start + i)
            for t, lanes in tiles_of(channels):
                piece = pl.ds(t * LANES, lanes)
                out[i, :, piece] = (source[i, :, piece].astype(F32) * factor[:, :lanes]).astype(BF16)
    wide[...] = jnp.zeros_like(wide)
    wide[: kernel.shape[0], : kernel.shape[1]] = kernel[...].astype(F32)
    shard[...] = wide[:LANES, :LANES].T[: shard.shape[0]].astype(BF16)
    pack_parameters(layout, in_proj, in_bias, out_proj, gain, shift, out_bias, packed, wide, tall)


def prepare_kernel(feats, cot, turned, paired, gbranch, mask, stage, plain):
    width, channels = feats.shape[1:]
    blocks = paired.shape[0]
    step = pl.program_id(0)

    @pl.when(step == 0)
    def _():
        stage[...] = jnp.zeros_like(stage)
        plain[...] = jnp.zeros_like(plain)

    for local_row in range(feats.shape[0]):
        side = local_row % 2
        row = feats.shape[0] * step + local_row
        factor = mask_of_row(turned[...], row)
        rows = pl.ds(BASE, width)
        plain[side, 0, rows, :] = factor
        for t, lanes in tiles_of(channels):
            piece = pl.ds(t * LANES, lanes)
            buffer = stage.at[side, t]
            stage_row(buffer, feats[local_row, :, piece].astype(F32) * factor[:, :lanes], width)
            place_row(paired, buffer, t, blocks, step * (feats.shape[0] // 2) + (SPAN + local_row) // 2, (SPAN + local_row) % 2)
            plain[side, 1 + t, rows, :lanes] = cot[local_row, :, piece].astype(F32) * factor[:, :lanes]
        for r in range(FINE):
            mask[row, r] = plain[side, 0, pl.ds(BASE + r, PAD, stride=FINE), :]
            for t, _unused in tiles_of(channels):
                gbranch[row, r, :, t * LANES : (t + 1) * LANES] = plain[
                    side, 1 + t, pl.ds(BASE + r, PAD, stride=FINE), :
                ].astype(BF16)


def in_place(mine, parts, place):
    value = parts[0]
    for i, part in enumerate(parts[1:], 1):
        value = jnp.where(mine ^ i == place, part, value)
    return value


def inner_kernel(channels, shares, paired, mask, *rest):
    shards, (conv, sums, taps, weights, accs, table) = rest[:shares], rest[shares:]
    share = channels // shares
    mine = lax.axis_index("fsdp")
    table[...] = jnp.zeros_like(table)
    parts = [shard[...].astype(F32) for shard in shards]
    for f in range(shares):
        table[f * share : (f + 1) * share] = in_place(mine, parts, f)[:share]
    blocks = paired.shape[0]
    for block in range(blocks):
        piece = table[block * HALF : (block + 1) * HALF]
        taps[block] = jnp.concatenate([piece, piece], axis=0).T[: taps.shape[1]]
        build_weights(weights.at[block], taps, block, False)
    runs = inner_runs(mask.shape[0] // 2)[0]
    for t, _ in tiles_of(channels):
        lanes = pl.ds(t * LANES, LANES)
        planes = products(paired, None, weights, accs, t, runs)
        row, total, count = 2 * runs[0][0], 0.0, 0.0
        for k in range(FINE // 2):
            for odd, value in enumerate(planes(0, k, 0)):
                total = total + mask[row, 2 * k + odd] * value
                count = count + mask[row, 2 * k + odd]
        near = jnp.sum(total, axis=0, keepdims=True) / jnp.maximum(jnp.sum(count, axis=0, keepdims=True), 1.0)
        total, square = settle(planes, conv, mask, runs, lanes, near)
        sums[0:1, lanes] = near
        sums[1:2, lanes] = total
        sums[2:3, lanes] = square


def outer_kernel(channels, paired, top, bottom, mask, weights, sums, conv, stats, rims, accs, stage):
    height = mask.shape[0]
    blocks, pairs = paired.shape[0], height // 2
    width = top.shape[1]
    stage[...] = jnp.zeros_like(stage)
    last = pairs + PASSES - 1
    first_half = (SPAN % 2) * LANES
    last_half = ((SPAN + height - 1) % 2) * LANES
    rims[:, 1, :, :, first_half : first_half + LANES] = paired[:, 1, :, :, first_half : first_half + LANES]
    rims[:, 2, :, :, last_half : last_half + LANES] = paired[:, last - 2, :, :, last_half : last_half + LANES]
    for below, index, pair, side in rim_rows(height):
        source = bottom if below else top
        place_natural(
            rims, stage, lambda a, b, source=source, index=index: source[index, :, a:b], channels, width, blocks, pair, side
        )
    runs = inner_runs(pairs)[1]
    count = 0.0
    for row in range(height):
        for r in range(FINE):
            count = count + mask[row, r]
    count = jnp.sum(count, axis=0, keepdims=True)
    for t, _ in tiles_of(channels):
        lanes = pl.ds(t * LANES, LANES)
        planes = products(paired, rims, weights, accs, t, runs)
        near = sums[0:1, lanes]
        total, square = settle(planes, conv, mask, runs, lanes, near)
        total, square = total + sums[1:2, lanes], square + sums[2:3, lanes]
        shift = total / jnp.maximum(count, 1.0)
        stats[0:1, lanes] = near + shift
        stats[1:2, lanes] = jnp.maximum(square - total * shift, 0.0)
        stats[2:3, lanes] = count
        stats[3:8, lanes] = jnp.zeros((5, LANES), F32)


def products(paired, rims, weights, accs, tile, runs):
    has_upper = 2 * tile + 1 < paired.shape[0]
    for half in range(1 + has_upper):
        block = 2 * tile + half
        accs[half] = convolve_block(paired, rims, weights.at[block], block, runs)

    def planes(place, k, side):
        start = (place * (FINE // 2) + k) * PAD
        return split_blocks(accs.at[0], accs.at[1] if has_upper else None, start, side)

    return planes


def settle(planes, conv, mask, runs, lanes, near):
    sums = [jnp.zeros((PAD, LANES), F32)] * 8
    for place, h in enumerate(pairs_of(runs)):
        for k in range(FINE // 2):
            for side in range(2):
                for odd, value in enumerate(planes(place, k, side)):
                    conv[2 * place + side, 2 * k + odd, :, lanes] = value
                    away = value - near
                    part = mask[2 * h + side, 2 * k + odd] * away
                    at = 2 * (2 * side + odd)
                    sums[at] = sums[at] + part
                    sums[at + 1] = sums[at + 1] + part * away
    return (jnp.sum(sums[i] + sums[i + 2] + sums[i + 4] + sums[i + 6], axis=0, keepdims=True) for i in range(2))


def pointwise_kernel(
    channels, real_units, inner, outer, gbranch, feats, turned, vec, w_in, w_out,
    output, act_out, ghid_out, gz_out, z_out, sums, stage, conv,
):
    rows, width = feats.shape[0], feats.shape[1]
    padded = conv.shape[-1]
    cells = rows * FINE * PAD
    hidden_units = act_out.shape[1]
    step = pl.program_id(0)

    @pl.when(step == 0)
    def _():
        sums[...] = jnp.zeros_like(sums)

    one_lane = lax.broadcasted_iota(jnp.int32, (1, padded), 1) == channels
    mean, inverse, gain, shift = (vec[i : i + 1, :] for i in range(4))
    side = RIM_PAIRS // 2
    is_inner = jnp.logical_and(step >= side, step < pl.num_programs(0) - side)

    @pl.when(is_inner)
    def _():
        conv[...] = inner[pl.ds((step - side) * rows, rows)]

    @pl.when(jnp.logical_not(is_inner))
    def _():
        place = jnp.where(step < side, step, step + 2 * side - pl.num_programs(0))
        conv[...] = outer[pl.ds(place * rows, rows)]

    here = pl.ds(pl.multiple_of(step * cells, cells), cells)
    normed = (conv[...].reshape(cells, padded) - mean) * inverse
    zvals = jnp.where(one_lane, 1.0, gain * normed + shift).astype(BF16)
    z_out[here, :] = zvals
    mine = pl.ds(step * rows, rows)
    upstream = gbranch[mine].reshape(cells, padded)
    chunk = 2 * LANES
    across = (((1,), (1,)), ((), ()))
    c0 = 0.7978845608028654
    c1 = 0.044715 * c0
    for start in range(0, hidden_units, chunk):
        span = pl.ds(start, chunk)
        hidden = jnp.dot(zvals, w_in[:, span], preferred_element_type=F32)
        gact = lax.dot_general(upstream, w_out[span, :], across, preferred_element_type=F32)
        square = hidden * hidden
        share = 0.5 + 0.5 * jnp.tanh(hidden * (c0 + c1 * square))
        act = hidden * share
        slope = share + (act - act * share) * (2.0 * c0 + (6.0 * c1) * square)
        ghid = (gact * slope).astype(BF16)
        act = act.astype(BF16)
        if start + chunk > real_units:
            lane = lax.broadcasted_iota(jnp.int32, (1, chunk), 1)
            act = jnp.where(lane == real_units - start, jnp.ones((), BF16), act)
        act_out[here, span] = act
        ghid_out[here, span] = ghid
    branch = jnp.dot(act_out[here, :], w_out[...], preferred_element_type=F32)
    gz = lax.dot_general(ghid_out[here, :], w_in[...], across, preferred_element_type=F32)
    gz_out[mine] = gz.reshape(rows, *gz_out.shape[1:])
    sums[0:1, :] += jnp.sum(gz * normed, axis=0, keepdims=True)
    sums[1:2, :] += jnp.sum(gz, axis=0, keepdims=True)
    for row in range(rows):
        factor = mask_of_row(turned[...], step * rows + row)
        for t, lanes in tiles_of(channels):
            for r in range(FINE):
                start = (row * FINE + r) * PAD
                stage[row, t, pl.ds(r, PAD, stride=FINE), :] = branch[start : start + PAD, t * LANES : (t + 1) * LANES]
            piece = pl.ds(t * LANES, lanes)
            values = feats[row, :, piece].astype(F32) + stage[row, t, 0:width, :lanes]
            output[row, :, piece] = (values * factor[:, :lanes]).astype(BF16)


def out_grads_kernel(gbranch, act, grad):
    grad[...] = turned_product(gbranch, act, grad.shape[0])


def turned_product(left, right, rows):
    return lax.dot_general(left[:, :rows], right[...], (((0,), (0,)), ((), ())), preferred_element_type=F32)


def in_grads_kernel(channels, hidden, zvals, ghid, grad_out, kept, sent, grad_in):
    grad_in[...] = turned_product(zvals, ghid, grad_in.shape[0])
    shares = lax.axis_size("fsdp")
    layout = Packing(channels, hidden, shares)
    last = layout.in_tiles - 1
    lane = lax.broadcasted_iota(jnp.int32, (1, LANES), 1)
    spot = lax.broadcasted_iota(jnp.int32, (layout.out_pad, 1), 0)
    fill = jnp.zeros((layout.in_pad - layout.in_rows, LANES), F32)

    def write(out, j):
        rows = slice(j * layout.in_rows, (j + 1) * layout.in_rows)
        for t in range(layout.in_tiles):
            lanes = slice(t * LANES, (t + 1) * LANES)
            tile = grad_in[rows, lanes]
            if t == last:
                tile = jnp.where(lane == hidden - t * LANES, grad_out[rows, lanes], tile)
            tile = jnp.concatenate([tile, fill], axis=0)
            out[t * layout.in_pad : (t + 1) * layout.in_pad] = tile.astype(out.dtype)
        start = j * layout.out_rows
        aligned = start // LANES * LANES
        stop = min(aligned + (layout.out_tiles + 1) * LANES, grad_out.shape[1])
        part = jnp.where(
            spot == channels, grad_in[: layout.out_pad, aligned:stop], grad_out[: layout.out_pad, aligned:stop]
        )
        if start != aligned:
            part = pltpu.roll(part, stop - start, 1)
        for u in range(layout.out_tiles):
            base = layout.out_base + u * layout.out_pad
            out[base : base + layout.out_pad] = part[:, u * LANES : (u + 1) * LANES].astype(out.dtype)
        out[layout.small_base :] = jnp.zeros((layout.rows - layout.small_base, LANES), out.dtype)

    for mine in range(shares):

        @pl.when(lax.axis_index("fsdp") == mine)
        def _(mine=mine):
            for i in range(shares):
                rows = pl.ds(i // 2 * layout.rows, layout.rows)
                write((sent if i % 2 else kept).at[rows], mine ^ i)


def near_sum_kernel(kept, arrived, own, sent):
    rows = own.shape[0]
    own[...] = kept[:rows] + arrived[:rows].astype(F32)
    sent[...] = (kept[rows:] + arrived[rows:].astype(F32)).astype(BF16)


def finish_kernel(channels, hidden, slopes, *refs):
    parts, refs = refs[:-8], refs[-8:]
    grad_in, grad_in_bias, grad_out, grad_out_bias, grad_taps, grad_gain, grad_shift, packed = refs
    place = piece_of(lax.axis_index("dp"))
    rows = packed.shape[0] // len(parts)
    values = [part[:rows] for part in parts]
    for i in range(len(parts)):
        packed[i * rows : (i + 1) * rows] = in_place(place, values, i)
    low = (parts[0].shape[0] - rows) // 2
    exact = [part[rows : rows + low].astype(F32) + part[rows + low :].astype(F32) for part in parts]
    share = grad_in.shape[0]
    grad_taps[...] = tree(exact, lambda a, b: a + b)[: grad_taps.shape[0], :share]
    for mine in range(channels // share):

        @pl.when(lax.axis_index("fsdp") == mine)
        def _(start=mine * share):
            turned = pltpu.roll(slopes[...], slopes.shape[1] - start, 1) if start else slopes[...]
            grad_gain[...] = turned[5, :share]
            grad_shift[...] = turned[6, :share]

    layout = Packing(channels, hidden, channels // grad_in.shape[0])
    for t in range(layout.in_tiles):
        stop = min((t + 1) * LANES, hidden)
        tile = packed[t * layout.in_pad : (t + 1) * layout.in_pad].astype(F32)
        grad_in[:, t * LANES : stop] = tile[: layout.in_rows, : stop - t * LANES]
    tall = jnp.concatenate([tile, jnp.zeros((LANES - layout.in_pad, LANES), F32)], axis=0).T
    at = hidden - (layout.in_tiles - 1) * LANES
    grad_out_bias[...] = tall[at, : layout.in_rows]
    bias = []
    for u in range(layout.out_tiles):
        base = layout.out_base + u * layout.out_pad
        tile = packed[base : base + layout.out_pad].astype(F32)
        stop = min((u + 1) * LANES, layout.out_rows)
        count = stop - u * LANES
        bias.append(tile[channels : channels + 1, :])
        fill = jnp.zeros((round_up(layout.out_pad, LANES) - layout.out_pad, LANES), F32)
        grad_out[u * LANES : stop, :] = jnp.concatenate([tile, fill], axis=0).T[:count, :channels]
    grad_in_bias[...] = jnp.concatenate(bias, axis=1)[0, : layout.out_rows]


def share_taps_kernel(share, *refs):
    shares = lax.axis_size("fsdp")
    tiles, outs = refs[:-shares], refs[-shares:]
    wide = jnp.concatenate([tile[...] for tile in tiles], axis=1)
    for mine in range(shares):

        @pl.when(lax.axis_index("fsdp") == mine)
        def _(mine=mine):
            for i, out in enumerate(outs):
                start = (mine ^ i) * share
                turned = pltpu.roll(wide, wide.shape[1] - start, 1) if start else wide
                out[...] = turned[:, :LANES]


def tree(values, merge):
    while len(values) > 1:
        values = [merge(values[i], values[i + 1]) for i in range(0, len(values), 2)]
    return values[0]


def merge_stats(mine, other):
    count = mine[2:3] + other[2:3]
    safe = jnp.maximum(count, 1.0)
    mean = (mine[0:1] * mine[2:3] + other[0:1] * other[2:3]) / safe
    away = mine[0:1] - other[0:1]
    spread = mine[1:2] + other[1:2] + away * away * (mine[2:3] * other[2:3] / safe)
    return jnp.concatenate([mean, spread, count, jnp.zeros_like(mine[3:8])], axis=0)


def stats_kernel(*refs):
    refs[-1][...] = tree([ref[...] for ref in refs[:-1]], merge_stats)


def norm_kernel(vectors, *refs):
    stats = tree([ref[...] for ref in refs[:-1]], merge_stats)
    count = jnp.maximum(stats[2:3], 1.0)
    inverse = lax.rsqrt(stats[1:2] / count + EPSILON)
    refs[-1][...] = jnp.concatenate(
        [stats[0:1], inverse, vectors[0:2, :], count, jnp.zeros((3, stats.shape[1]), F32)], axis=0
    )


def sums_kernel(*refs):
    refs[-1][...] = tree([ref[...] for ref in refs[:-1]], lambda a, b: a + b)


def slopes_kernel(vec, *refs):
    sums = tree([ref[...] for ref in refs[:-1]], lambda a, b: a + b)
    scaled = vec[1:2, :] * vec[2:3, :]
    count = vec[4:5, :]
    refs[-1][...] = jnp.concatenate(
        [vec[0:2, :], scaled, scaled * sums[1:2] / count, scaled * sums[0:1] / count, sums[0:2], sums[2:3]], axis=0
    )


class Packing:
    def __init__(self, channels, hidden, shares):
        self.in_rows = channels // shares
        self.in_pad = round_up(self.in_rows, 16)
        self.in_tiles = -(-(hidden + 1) // LANES)
        self.out_rows = hidden // shares
        self.out_tiles = -(-self.out_rows // LANES)
        self.out_pad = round_up(max(channels + 1, self.out_rows), 16)
        self.out_base = self.in_pad * self.in_tiles
        self.small_base = self.out_base + self.out_pad * self.out_tiles
        self.small = self.out_tiles + 3
        self.rows = round_up(self.small_base + self.small, 32)


def pack_parameters(layout, in_proj, in_bias, out_proj, gain, shift, out_bias, packed, wide, tall):
    wide[...] = jnp.zeros_like(wide)
    tall[...] = jnp.zeros_like(tall)
    wide[: layout.in_rows, : in_proj.shape[1]] = in_proj[...].astype(F32)
    for t in range(layout.in_tiles):
        packed[t * layout.in_pad : (t + 1) * layout.in_pad] = wide[: layout.in_pad, t * LANES : (t + 1) * LANES].astype(BF16)
    tall[: layout.out_rows, : out_proj.shape[1]] = out_proj[...].astype(F32)
    for u in range(layout.out_tiles):
        base = layout.out_base + u * layout.out_pad
        packed[base : base + layout.out_pad] = tall[:, u * LANES : (u + 1) * LANES].astype(BF16)
    wide[...] = jnp.zeros_like(wide)
    for i, small in enumerate((in_bias, gain, shift, out_bias)):
        wide[i : i + 1, : small.shape[0]] = small[...].reshape(1, -1).astype(F32)
    rows = [wide[0:1, u * LANES : (u + 1) * LANES] for u in range(layout.out_tiles)]
    rows += [wide[i + 1 : i + 2, :LANES] for i in range(3)]
    rows.append(jnp.zeros((layout.rows - layout.small_base - layout.small, LANES), F32))
    packed[layout.small_base :] = jnp.concatenate(rows, axis=0).astype(BF16)


def assemble_kernel(layout, shares, *refs):
    packed, (w_in, w_out, vectors, wide, tall) = refs[:shares], refs[shares:]
    mine = lax.axis_index("fsdp")

    def rows_of(f, start, stop):
        return in_place(mine, [part[start:stop].astype(F32) for part in packed], f)

    wide[...] = jnp.zeros_like(wide)
    tall[...] = jnp.zeros_like(tall)
    channels, hidden = layout.in_rows * shares, layout.out_rows * shares
    in_bias = jnp.zeros((8, wide.shape[1]), F32)
    smalls = [jnp.zeros((8, tall.shape[1]), F32)] * 3
    for f in range(shares):
        for t in range(layout.in_tiles):
            tile = rows_of(f, t * layout.in_pad, (t + 1) * layout.in_pad)
            wide[f * layout.in_rows : (f + 1) * layout.in_rows, t * LANES : (t + 1) * LANES] = tile[: layout.in_rows]
        for u in range(layout.out_tiles):
            base = layout.out_base + u * layout.out_pad
            tile = rows_of(f, base, base + layout.out_pad)
            tall[f * layout.out_rows : (f + 1) * layout.out_rows, u * LANES : (u + 1) * LANES] = tile[: layout.out_rows]
        small = rows_of(f, layout.small_base, layout.rows)

        def spread(first, count, lanes, turn):
            pieces = [small[first + u : first + u + 1] for u in range(count)]
            pieces.append(jnp.zeros((1, lanes - count * LANES), F32))
            row = jnp.broadcast_to(jnp.concatenate(pieces, axis=1), (8, lanes))
            return pltpu.roll(row, turn, 1) if turn else row

        in_bias = in_bias + spread(0, layout.out_tiles, wide.shape[1], f * layout.out_rows)
        smalls = [
            total + spread(layout.out_tiles + i, 1, tall.shape[1], f * layout.in_rows)
            for i, total in enumerate(smalls)
        ]
    wide[channels : channels + 1] = in_bias[:1]
    tall[hidden : hidden + 1] = smalls[2][:1]
    w_in[...] = wide[...].astype(BF16)
    w_out[...] = tall[...].astype(BF16)
    vectors[...] = jnp.concatenate([smalls[0][:1], smalls[1][:1], jnp.zeros((6, tall.shape[1]), F32)], axis=0)


def shifted_planes(values, real):
    out = []
    for r in range(-SPAN, FINE + SPAN):
        value = values[r % FINE]
        if r < 0:
            value = jnp.concatenate([value[real - 1 : real], value[: PAD - 1]], axis=0)
        elif r >= FINE:
            value = jnp.concatenate([value[1:real], value[:1], value[: PAD - real]], axis=0)
        out.append(value)
    return out


def join_planes(first, second):
    low = low_half(PAD)
    return (
        jnp.where(low, first, swap(second)).astype(BF16),
        jnp.where(low, swap(first), second).astype(BF16),
    )


def place_planes(paired, planes, tile, blocks, pair, side):
    out_lanes = pl.ds(side * LANES, LANES)
    for k in range(len(planes) // 2):
        for half, value in enumerate(join_planes(planes[2 * k], planes[2 * k + 1])):
            if 2 * tile + half < blocks:
                paired[2 * tile + half, pair, k, :, out_lanes] = value


def arrange_kernel(
    channels, real, gz, inner, outer, mask, vec, edges, gpaired, own,
):
    height = gz.shape[0]
    blocks = own.shape[0]
    for t, _ in tiles_of(channels):
        lanes = pl.ds(t * LANES, LANES)
        mean, inverse, scaled, bias, slope = (vec[i : i + 1, lanes] for i in range(5))
        for row in range(height):
            h, side = row // 2, row % 2
            values = []
            for r in range(FINE):
                normed = (conv_at(inner, outer, row, r, lanes) - mean) * inverse
                values.append(scaled * gz[row, r, :, lanes] - mask[row, r] * (bias + normed * slope))
            out_lanes = pl.ds(side * LANES, LANES)
            for k in range(FINE // 2):
                rows = pl.ds((h * (FINE // 2) + k) * PAD, PAD)
                for half, value in enumerate(join_planes(values[2 * k], values[2 * k + 1])):
                    if 2 * t + half < blocks:
                        own[2 * t + half, rows, out_lanes] = value
            place_planes(gpaired, shifted_planes(values, real), t, blocks, (SPAN + row) // 2, (SPAN + row) % 2)
            for edge, near in ((0, row < SPAN), (1, row >= height - SPAN)):
                if near:
                    place = row - (height - SPAN) * edge
                    for r in range(FINE):
                        edges[edge, place, r, :, lanes] = values[r].astype(BF16)


def conv_at(inner, outer, row, r, lanes):
    start = RIM_PAIRS
    stop = start + inner.shape[0]
    if start <= row < stop:
        return inner[row - start, r, :, lanes]
    return outer[row if row < start else row - stop + start, r, :, lanes]


def taps_kernel(tile, own, paired, rims, select, grad_taps):
    blocks, pairs = own.shape[0], paired.shape[1] - PASSES + 1
    lane = lax.broadcasted_iota(jnp.int32, (HALF, 2 * LANES), 1)
    sub = lax.broadcasted_iota(jnp.int32, (HALF, 2 * LANES), 0)
    diagonal = lax.rem(lane, HALF) == sub
    low = low_half(grad_taps.shape[0])
    totals = []
    for block in range(2 * tile, min(2 * tile + 2, blocks)):
        turned = own[block].T
        found = []
        for m in range(PASSES):
            for s in range(PASSES):
                product = jnp.dot(turned, pass_rows(paired, rims, block, m, s, [(0, pairs)]), preferred_element_type=F32)
                for q in range(4):
                    part = product[q * HALF : (q + 1) * HALF]
                    found.append(jnp.sum(jnp.where(diagonal, part, 0.0), axis=0, keepdims=True))
        found = jnp.concatenate(found, axis=0)
        total = None
        for place in range(4):
            group = jnp.dot(select[place], found, preferred_element_type=F32, precision=lax.Precision.HIGHEST)
            group = group[:, (place // 2) * LANES : (place // 2 + 1) * LANES]
            if place % 2:
                group = swap(group)
            total = group if total is None else total + group
        totals.append(total)
    second = swap(totals[1]) if len(totals) > 1 else jnp.zeros_like(totals[0])
    grad_taps[...] = jnp.where(low, totals[0], second)


def backward_kernel(tile, real, gpaired, top, bottom, taps, cot, turned, *rest):
    result, rims, weights, accs, stage = rest[-5:]
    height, width = cot.shape[0], cot.shape[1]
    blocks, pairs = gpaired.shape[0], height // 2
    last = pairs + PASSES - 1
    first_half = (SPAN % 2) * LANES
    last_half = ((SPAN + height - 1) % 2) * LANES
    has_upper = 2 * tile + 1 < blocks
    for half in range(1 + has_upper):
        source = gpaired.at[2 * tile + half]
        rims[half, 1, :, :, first_half : first_half + LANES] = source[1, :, :, first_half : first_half + LANES]
        rims[half, 2, :, :, last_half : last_half + LANES] = source[last - 2, :, :, last_half : last_half + LANES]
    for below, index, pair, side in rim_rows(height):
        source = bottom if below else top
        values = [source[index, r, :, tile * LANES : (tile + 1) * LANES].astype(F32) for r in range(FINE)]
        place_planes(rims, shifted_planes(values, real), 0, 1 + has_upper, pair, side)
    for half in range(1 + has_upper):
        block = 2 * tile + half
        build_weights(weights, taps, block, True)
        accs[half] = convolve_block(
            gpaired.at[block : block + 1], rims.at[half : half + 1], weights, 0, [(0, pairs)]
        )

    def spread(h, _):
        for side in range(2):
            row = 2 * h + side
            for k in range(FINE // 2):
                even, odd = split_blocks(
                    accs.at[0], accs.at[1] if has_upper else None, (h * (FINE // 2) + k) * PAD, side
                )
                stage[side, pl.ds(2 * k, PAD, stride=FINE), :] = even
                stage[side, pl.ds(2 * k + 1, PAD, stride=FINE), :] = odd
            values = cot[row].astype(F32) + stage[side, 0:width]
            result[row] = (values * mask_of_row(turned[...], row)).astype(BF16)
        return 0

    for h in range(pairs):
        spread(h, 0)


def bits(size):
    bit = 1
    while bit < size:
        yield bit
        bit *= 2


def swapped(value, axis, flip):
    size = lax.axis_size(axis)
    return lax.ppermute(value, axis, [(i, i ^ flip) for i in range(size)])


def phases(*axes):
    out = []
    for axis in axes:
        left = list(bits(lax.axis_size(axis)))
        while left:
            near, left = left[:2], left[2:]
            out.append((axis, near if len(near) < 2 else [near[0], near[1], near[0] | near[1]]))
    return out


def tied(*values):
    return lax.optimization_barrier(values)


def halves_kernel(bit, *refs):
    parts, (keep, send) = refs[:-2], refs[-2:]
    rows = keep.shape[0]
    halves = [sum((part[a : a + rows].astype(F32) for part in parts[1:]), parts[0][a : a + rows]) for a in (0, rows)]
    first = lax.axis_index("dp") // bit % 2 == 0
    keep[...] = jnp.where(first, halves[0], halves[1])
    send[...] = jnp.where(first, halves[1], halves[0]).astype(send.dtype)


def whole_kernel(count, *refs):
    parts, extra, out = refs[:count], refs[count:-1], refs[-1]
    rows = parts[0].shape[0]
    out[:rows] = sum((part[...].astype(F32) for part in parts[1:]), parts[0][...])
    if extra:
        out[rows:] = sum((part[...] for part in extra[1:]), extra[0][...])


def last_kernel(rows, mine, other, out):
    total = mine[...] + other[...]
    rest = total.shape[0] - rows
    high = total[rows:].astype(BF16)
    out[:rows] = total[:rows].astype(BF16)
    out[rows : rows + rest] = high
    out[rows + rest :] = (total[rows:] - high.astype(F32)).astype(BF16)


def beside(work, *values):
    done = work() if work else ()
    return lax.optimization_barrier((done, values))


def far_bits():
    return list(bits(lax.axis_size("dp")))[1:3]


def piece_of(place):
    piece = 0
    for bit in far_bits():
        piece = 2 * piece + place // bit % 2
    return piece


class Spreading:
    def __init__(self, *parts):
        self.parts, self.extra = parts, ()
        cuts = far_bits()
        self.moves = [("half", [bit]) for bit in cuts]
        self.moves += [("whole", [bit]) for bit in bits(lax.axis_size("dp")) if bit not in cuts]
        flips = [0]
        for bit in reversed(cuts):
            flips += [flip | bit for flip in flips]
        self.moves.append(("gather", flips[1:]))

    def start(self):
        kind, flips = self.moves.pop(0)
        rows, lanes = self.parts[0].shape
        operands = (*self.parts, *self.extra)
        run = lambda kernel, *outs: call(
            kernel, outs, operands, [WHOLE] * len(operands), limit=10, name="sum_weights"
        )
        if kind == "half":
            kept, sent = run(
                functools.partial(halves_kernel, flips[0]),
                anywhere((rows // 2, lanes), F32),
                anywhere((rows // 2, lanes), BF16),
            )
        elif kind == "whole":
            low = self.extra[0].shape[0] if self.extra else 0
            if self.extra:
                self.rows = rows
            (kept,) = (sent,) = run(
                functools.partial(whole_kernel, len(self.parts)), anywhere((rows + low, lanes), F32)
            )
            self.extra = ()
        else:
            (kept,) = (sent,) = run(
                functools.partial(last_kernel, self.rows), anywhere((2 * rows - self.rows, lanes), BF16)
            )
        self.parts = (kept,)
        return [swapped(sent, "dp", flip) for flip in flips]

    def finish(self, others):
        self.parts = (*self.parts, *others)


def rims_of(top_rows, bottom_rows):
    size = lax.axis_size("dp")
    down = [(i, i + 1) for i in range(size - 1) if (i + 1) % TILES]
    up = [(j, i) for i, j in down]
    return lax.ppermute(bottom_rows, "dp", down), lax.ppermute(top_rows, "dp", up)


def tap_selectors(rows):
    out = np.zeros((4, rows, PASSES * PASSES * 4), np.float32)
    for m in range(PASSES):
        for s in range(PASSES):
            for q in range(4):
                for p in range(4):
                    a = 2 * m + p // 2 - q // 2
                    b = 2 * s + p % 2 - q % 2
                    if 0 <= a < KW and 0 <= b < KW:
                        out[p, a * KW + b, (m * PASSES + s) * 4 + q] = 1.0
    return out


def local(features, land_mask, cotangent, kernel, norm_gain, norm_shift, in_proj, in_bias, out_proj, out_bias):
    feats, cot = features[0, 0], cotangent[0, 0]
    height, width, channels = feats.shape
    hidden = in_proj.shape[1]
    shares = lax.axis_size("fsdp")
    padded = round_up(channels + 1, LANES)
    hidden_pad = round_up(hidden + 1, 2 * LANES)
    blocks = -(-channels // HALF)
    pairs = height // 2
    planes_in = (FINE + 2 * SPAN) // 2
    row_pairs = pairs + PASSES - 1
    cells = height * FINE * PAD
    block_rows = pairs * (FINE // 2) * PAD
    stage_rows = round_up(BASE + SPAN + FINE * PAD, 8)
    tile_count = len(tiles_of(channels))
    tap_rows = round_up(TAPS, 8)
    real = width // FINE
    layout = Packing(channels, hidden, shares)

    edge = lambda at: pl.BlockSpec((SPAN, width, channels), lambda i: (at, 0, 0))
    whole = lambda array: pl.BlockSpec(array.shape, lambda i: (0,) * array.ndim)
    natural_shape = (height, width, channels)
    edge_shape = (SPAN, width, channels)
    paired_shape = (blocks, row_pairs, planes_in, PAD, 4 * HALF)
    rims_shape = (blocks, RIM_PAIRS, planes_in, PAD, 4 * HALF)
    plane_shape = (height, FINE, PAD, padded)
    mask_shape = (height, FINE, PAD, LANES)
    small = (kernel.T, in_proj, in_bias, out_proj, norm_gain, norm_shift, out_bias)
    first_rows, last_rows, turned, shard, packed = call(
        functools.partial(begin_kernel, layout),
        [
            anywhere(edge_shape, BF16),
            anywhere(edge_shape, BF16),
            anywhere((width, height), BF16),
            anywhere((layout.in_pad, LANES), BF16),
            anywhere((layout.rows, LANES), BF16),
        ],
        (slow(feats), slow(feats), slow(land_mask), *(slow(v) for v in small)),
        [edge(0), edge(height // SPAN - 1), whole(land_mask)] + [whole(v) for v in small],
        [
            pltpu.VMEM((round_up(height, LANES), round_up(width, LANES)), F32),
            pltpu.VMEM((round_up(layout.in_pad, LANES), hidden_pad), F32),
            pltpu.VMEM((layout.out_pad, padded), F32),
        ],
        grid=(1,),
        out_specs=[WHOLE] * 5,
        name="begin",
    )
    others = list(range(1, shares))
    six = 6 if height % 6 == 0 else 2
    stage = pltpu.VMEM((2, tile_count, 2, stage_rows, LANES), F32)
    top, bottom = rims_of(first_rows, last_rows)
    shards = [swapped(shard, "fsdp", i) for i in others]
    (paired, gbranch, mask), (packed, shards) = beside(
        lambda: call(
            prepare_kernel,
            [pltpu.VMEM(paired_shape, BF16), pltpu.VMEM(plane_shape, BF16), pltpu.VMEM(mask_shape, F32)],
            (slow(feats), slow(cot), turned),
            [pl.BlockSpec((six, width, channels), lambda i: (i, 0, 0))] * 2 + [WHOLE],
            [stage, pltpu.VMEM((2, 1 + tile_count, stage_rows, LANES), F32)],
            grid=(height // six,),
            name="prepare",
        ),
        packed,
        [shard, *shards],
    )
    cuts = list(bits(shares))
    direct = [swapped(packed, "fsdp", bit) for bit in cuts]
    inner, outer = inner_runs(pairs)
    run_rows = lambda runs: 2 * len(pairs_of(runs))
    run_accs = lambda runs: pltpu.VMEM((2, run_rows(runs) * (FINE // 2) * PAD // 2, 4 * HALF), F32)
    weights_shape = (PASSES * PASSES * 4 * HALF, 4 * HALF)
    (conv_inner, sums, taps, weights), (top, bottom) = beside(
        lambda: call(
            functools.partial(inner_kernel, channels, shares),
            [
                pltpu.VMEM((run_rows(inner), FINE, PAD, padded), F32),
                anywhere((8, padded), F32),
                anywhere((blocks, tap_rows, LANES), F32),
                pltpu.VMEM((blocks, *weights_shape), BF16),
            ],
            (fast(paired), fast(mask), *shards),
            [WHOLE] * (2 + shares),
            [run_accs(inner), pltpu.VMEM((blocks * HALF, LANES), F32)],
            limit=10,
            name="inner",
        ),
        top,
        bottom,
    )
    (conv_outer, stats, rims), (packed, direct) = beside(
        lambda: call(
            functools.partial(outer_kernel, channels),
            [
                pltpu.VMEM((run_rows(outer), FINE, PAD, padded), F32),
                anywhere((8, padded), F32),
                pltpu.VMEM(rims_shape, BF16),
            ],
            (fast(paired), top, bottom, fast(mask), fast(weights), sums),
            [WHOLE] * 6,
            [run_accs(outer), stage],
            flops=4 * 10**9,
            limit=10,
            name="outer",
        ),
        packed,
        direct,
    )
    packed = {0: packed, **dict(zip(cuts, direct))}
    for flip in others:
        if flip not in packed:
            packed[flip] = swapped(packed[flip & (flip - 1)], "fsdp", flip & -flip)
    packed = [packed[flip] for flip in range(shares)]
    assemble = lambda: call(
        functools.partial(assemble_kernel, layout, shares),
        [
            anywhere((padded, hidden_pad), BF16),
            anywhere((hidden_pad, padded), BF16),
            anywhere((8, padded), F32),
        ],
        packed,
        [WHOLE] * shares,
        [pltpu.VMEM((padded, hidden_pad), F32), pltpu.VMEM((hidden_pad, padded), F32)],
        name="assemble",
    )
    row_sums = anywhere((8, padded), F32)
    combine = lambda kernel, *values: call(kernel, [row_sums], values, [WHOLE] * len(values), limit=4, name="combine")[0]
    rounds = phases("fsdp", "dp")
    for n, (axis, flips) in enumerate(rounds):
        work = assemble if n == 1 else None
        values = [stats, *(swapped(stats, axis, i) for i in flips)]
        if n == 0:
            values += packed
        done, values = beside(work, *values)
        if n == 0:
            packed, values = values[-shares:], values[:-shares]
        if n == 1:
            w_in, w_out, vectors = done
        if n + 1 < len(rounds):
            stats = combine(stats_kernel, *values)
    vec = combine(norm_kernel, vectors, *values)

    rows = 2
    steps = height // rows
    by_row = lambda *rest: pl.BlockSpec((rows, *rest), lambda i: (i,) + (0,) * len(rest))
    output, act, ghid, gz, zvals, sums = call(
        functools.partial(pointwise_kernel, channels, hidden),
        [
            anywhere(natural_shape, BF16),
            pltpu.VMEM((cells, hidden_pad), BF16),
            pltpu.VMEM((cells, hidden_pad), BF16),
            pltpu.VMEM(plane_shape, F32),
            pltpu.VMEM((cells, padded), BF16),
            row_sums,
        ],
        (fast(conv_inner), fast(conv_outer), fast(gbranch), slow(feats), turned, vec, w_in, w_out),
        [WHOLE] * 3 + [by_row(width, channels)] + [WHOLE] * 4,
        [
            pltpu.VMEM((rows, tile_count, round_up(FINE * PAD, 8), LANES), F32),
            pltpu.VMEM((rows, FINE, PAD, padded), F32),
        ],
        flops=14 * 10**9,
        grid=(steps,),
        out_specs=[by_row(width, channels)] + [WHOLE] * 5,
        limit=9,
        name="pointwise",
    )

    grad_rows = round_up(channels + 1, 16)

    def out_grads():
        return call(
            out_grads_kernel,
            [pltpu.VMEM((grad_rows, hidden_pad), F32)],
            (fast(gbranch.reshape(cells, padded)), fast(act)),
            [WHOLE] * 2,
            flops=3 * 10**9,
            limit=4,
            name="out_grads",
        )

    def in_grads():
        return call(
            functools.partial(in_grads_kernel, channels, hidden),
            [pltpu.VMEM((shares // 2 * layout.rows, LANES), dtype) for dtype in (F32, BF16)],
            (fast(zvals), fast(ghid), fast(grad_out)),
            [WHOLE] * 3,
            [pltpu.VMEM((grad_rows, hidden_pad), F32)],
            flops=3 * 10**9,
            limit=6,
            name="in_grads",
        )

    work = out_grads
    for n, (axis, flips) in enumerate(rounds):
        values = [sums, *(swapped(sums, axis, i) for i in flips)]
        if n == 2:
            values.append(sent)
        done, values = beside(work, *values)
        if n == 2:
            *values, sent = values
        work = None
        if n == 0:
            (grad_out,) = done
            work = in_grads
        if n == 1:
            kept, sent = done
            sent = swapped(sent, "fsdp", 1)
        if n + 1 < len(rounds):
            sums = combine(sums_kernel, *values)
    gvec = combine(slopes_kernel, vec, *values)
    kept, sent = call(
        near_sum_kernel,
        [anywhere((layout.rows, LANES), F32), anywhere((layout.rows, LANES), BF16)],
        (kept, sent),
        [WHOLE] * 2,
        limit=10,
        name="near_sum",
    )
    sent = swapped(sent, "fsdp", 2)
    edges, gpaired, own = call(
        functools.partial(arrange_kernel, channels, real),
        [
            anywhere((2, SPAN, FINE, PAD, padded), BF16),
            pltpu.VMEM(paired_shape, BF16),
            pltpu.VMEM((blocks, block_rows, 4 * HALF), BF16),
        ],
        (fast(gz), fast(conv_inner), fast(conv_outer), fast(mask), gvec),
        [WHOLE] * 5,
        flops=10**8,
        moved=10 * MIB,
        limit=6,
        name="arrange",
    )
    select = jnp.asarray(tap_selectors(tap_rows))
    gtop, gbottom = rims_of(edges[0], edges[1])

    def taps_of(t):
        return lambda: call(
            functools.partial(taps_kernel, t),
            [anywhere((tap_rows, LANES), F32)],
            (fast(own), fast(paired), fast(rims), select),
            [WHOLE] * 4,
            flops=4 * 10**9,
            limit=6,
            name="taps",
        )

    (first,) = taps_of(0)()
    (second,), (sent,) = beside(taps_of(1), sent)
    spreading = Spreading(kept, sent)
    rest = lambda: [taps_of(t)()[0] for t in range(2, tile_count)]
    more, (there,) = beside(rest, spreading.start())
    spreading.finish(there)
    gtop, gbottom, *tiles = tied(gtop, gbottom, first, second, *more)
    own_taps, *sent_taps = call(
        functools.partial(share_taps_kernel, layout.in_rows),
        [anywhere((tap_rows, LANES), F32)] * shares,
        tiles,
        [WHOLE] * tile_count,
        limit=4,
        name="share_taps",
    )
    sent_taps = [swapped(v, "fsdp", i) for i, v in zip(others, sent_taps)]
    accs = pltpu.VMEM((2, block_rows, 4 * HALF), F32)
    weights = pltpu.VMEM(weights_shape, BF16)

    def backward_of(t, *before):
        column = pl.BlockSpec((height, width, LANES), lambda i: (0, 0, t))
        return lambda: call(
            functools.partial(backward_kernel, t, real),
            [anywhere(natural_shape, BF16)],
            (fast(gpaired), gtop, gbottom, taps, slow(cot), turned, *before),
            [WHOLE] * 4 + [column, WHOLE] + [HBM] * len(before),
            [
                pltpu.VMEM((2, RIM_PAIRS, planes_in, PAD, 4 * HALF), BF16),
                weights,
                accs,
                pltpu.VMEM((2, round_up(FINE * PAD, 8), LANES), F32),
            ],
            flops=4 * 10**9,
            limit=12,
            grid=(1,),
            out_specs=[column],
            aliases={6: 0} if before else {},
            name="backward",
        )

    result = ()
    for n in range(max(tile_count, len(spreading.moves))):
        work = backward_of(tile_count - 1 - n, *result) if n < tile_count else None
        values = [spreading.start()] if spreading.moves else []
        if n == 0:
            values += sent_taps
        done, values = beside(work, *values)
        result = done or result
        if values:
            spreading.finish(values[0])
        if n == 0:
            spreading.extra = (own_taps, *values[1:])
    (result,) = result
    pieces = spreading.parts
    grad_in, grad_in_bias, grad_out, grad_out_bias, grad_taps, grad_gain, grad_shift = call(
        functools.partial(finish_kernel, channels, hidden),
        [
            anywhere((layout.in_rows, hidden), F32),
            anywhere((layout.out_rows,), F32),
            anywhere((layout.out_rows, channels), F32),
            anywhere((layout.in_rows,), F32),
            anywhere((TAPS, layout.in_rows), F32),
            anywhere((layout.in_rows,), F32),
            anywhere((layout.in_rows,), F32),
        ],
        (gvec, *pieces),
        [WHOLE] * (1 + len(pieces)),
        [pltpu.VMEM((layout.rows, LANES), BF16)],
        name="finish",
    )
    return (
        output[None, None],
        result[None, None],
        grad_taps.T,
        grad_gain,
        grad_shift,
        grad_in,
        grad_in_bias,
        grad_out,
        grad_out_bias,
    )


def solution(mesh):
    spread = P("dp", "fsdp", None, None, None)
    split = P("fsdp", None)
    line = P("fsdp")
    return jax.shard_map(
        local,
        mesh=mesh,
        in_specs=(spread, P(), spread, split, line, line, split, line, split, line),
        out_specs=(spread, spread, split, line, line, split, line, split, line),
        check_vma=False,
    )
```

```python
import functools

import jax
import jax.numpy as jnp
import numpy as np
from jax import lax
from jax.experimental import pallas as pl
from jax.experimental.pallas import tpu as pltpu
from jax.sharding import PartitionSpec as P

KW = 7
SPAN = KW // 2
TILES = 8
EPSILON = 1e-05

LANES = 128
HALF = 64
FINE = 12
PAD = 16
PASSES = (KW + 1) // 2
TAPS = KW * KW
RIM_PAIRS = 4
BASE = 8

F32 = jnp.float32
BF16 = jnp.bfloat16
MIB = 2**20
WHOLE = pl.BlockSpec(memory_space=pltpu.VMEM)
HBM = pl.BlockSpec(memory_space=pl.ANY)


def fast(value):
    return pltpu.with_memory_space_constraint(value, pltpu.VMEM)


def slow(value):
    return pltpu.with_memory_space_constraint(value, pltpu.HBM)


def anywhere(shape, dtype):
    return jax.ShapeDtypeStruct(shape, dtype)


def round_up(value, step):
    return -(-value // step) * step


def call(kernel, outs, operands, in_specs, scratch=(), flops=0, moved=0, grid=None, out_specs=None, limit=10, aliases=None, name=None):
    extra = {} if grid is None else {"grid": grid}
    return pl.pallas_call(
        kernel,
        out_shape=outs,
        in_specs=in_specs,
        out_specs=[WHOLE] * len(outs) if out_specs is None else out_specs,
        scratch_shapes=list(scratch),
        input_output_aliases=aliases or {},
        compiler_params=pltpu.CompilerParams(vmem_limit_bytes=limit * MIB),
        cost_estimate=pl.CostEstimate(flops=flops, bytes_accessed=moved, transcendentals=0),
        name=name,
        **extra,
    )(*operands)


def low_half(rows):
    return lax.broadcasted_iota(jnp.int32, (rows, LANES), 1) < HALF


def swap(value):
    return pltpu.roll(value, HALF, 1)


def tiles_of(channels):
    return [(t, min(LANES, channels - t * LANES)) for t in range(-(-channels // LANES))]


def mask_of_row(turned, row):
    chosen = lax.broadcasted_iota(jnp.int32, (turned.shape[1], LANES), 0) == row
    return jnp.dot(turned, jnp.where(chosen, 1.0, 0.0).astype(BF16), preferred_element_type=F32)


def stage_row(stage, values, width):
    lanes = values.shape[1]
    stage[0, BASE : BASE + width, :lanes] = values
    stage[0, BASE - SPAN : BASE, :lanes] = values[width - SPAN :]
    stage[0, BASE + width : BASE + width + SPAN, :lanes] = values[:SPAN]
    stage[1] = swap(stage[0])


def plane(stage, which, start):
    return stage[which, pl.ds(start, PAD, stride=FINE), :]


def place_row(paired, stage, tile, blocks, pair, side):
    low = low_half(PAD)
    lanes = pl.ds(side * LANES, LANES)
    for k in range((FINE + 2 * SPAN) // 2):
        start = BASE - SPAN + 2 * k
        paired[2 * tile, pair, k, :, lanes] = jnp.where(
            low, plane(stage, 0, start), plane(stage, 1, start + 1)
        ).astype(BF16)
        if 2 * tile + 1 < blocks:
            paired[2 * tile + 1, pair, k, :, lanes] = jnp.where(
                low, plane(stage, 1, start), plane(stage, 0, start + 1)
            ).astype(BF16)


def place_natural(paired, stage, source, channels, width, blocks, pair, side, factor=None):
    for t, lanes in tiles_of(channels):
        values = source(t * LANES, t * LANES + lanes).astype(F32)
        if factor is not None:
            values = values * factor[:, :lanes]
        buffer = stage.at[side, t]
        stage_row(buffer, values, width)
        place_row(paired, buffer, t, blocks, pair, side)


def rim_rows(height):
    inner = (height + 2 * SPAN) // 2 - RIM_PAIRS // 2
    for index in range(SPAN):
        yield 0, index, index // 2, index % 2
    for index in range(SPAN):
        row = SPAN + height + index
        yield 1, index, row // 2 - inner + RIM_PAIRS // 2, row % 2


def build_weights(weights, taps, block, flip):
    lane = lax.broadcasted_iota(jnp.int32, (HALF, LANES), 1)
    sub = lax.broadcasted_iota(jnp.int32, (HALF, LANES), 0)
    diagonal = lax.rem(lane, HALF) == sub
    low = low_half(1)
    zero = jnp.zeros((1, LANES), F32)

    def tap_row(a, b):
        if not (0 <= a < KW and 0 <= b < KW):
            return zero
        index = (KW - 1 - a) * KW + KW - 1 - b if flip else a * KW + b
        return taps[block, index : index + 1, :]

    for m in range(PASSES):
        for s in range(PASSES):
            for place in range(4):
                pr, pj = divmod(place, 2)
                for qr in range(2):
                    a, b = 2 * m + pr - qr, 2 * s + pj
                    row = jnp.where(low, tap_row(a, b), tap_row(a, b - 1))
                    weights[
                        (m * PASSES + s) * 4 * HALF + place * HALF : (m * PASSES + s) * 4 * HALF + (place + 1) * HALF,
                        qr * LANES : (qr + 1) * LANES,
                    ] = jnp.where(diagonal, row, 0.0).astype(BF16)


def pass_rows(paired, rims, block, m, s, runs):
    places = pl.ds(s, FINE // 2)
    side = RIM_PAIRS // 2
    inner = paired.shape[1] - side
    pieces = []
    for start, stop in runs:
        start, stop = start + m, stop + m
        pieces += [rims[block, i, places] for i in range(start, min(stop, side))]
        if max(start, side) < min(stop, inner):
            pieces.append(paired[block, max(start, side) : min(stop, inner), places])
        pieces += [rims[block, i - inner + side, places] for i in range(max(start, inner), stop)]
    return jnp.concatenate([piece.reshape(-1, 4 * HALF) for piece in pieces], axis=0)


def convolve_block(paired, rims, weights, block, runs):
    rows = jnp.concatenate(
        [pass_rows(paired, rims, block, m, s, runs) for m in range(PASSES) for s in range(PASSES)], axis=1
    )
    return jnp.dot(rows, weights[...], preferred_element_type=F32)


def inner_runs(pairs):
    side = RIM_PAIRS // 2
    return [(side, pairs - side)], [(0, side), (pairs - side, pairs)]


def pairs_of(runs):
    return [h for start, stop in runs for h in range(start, stop)]


def split_blocks(lower, upper, start, side):
    low = low_half(PAD)
    rows, lanes = pl.ds(start, PAD), pl.ds(side * LANES, LANES)
    first = lower[rows, lanes]
    if upper is None:
        return first, swap(first)
    second = upper[rows, lanes]
    return jnp.where(low, first, swap(second)), jnp.where(low, swap(first), second)


def begin_kernel(
    layout, first, last, land_mask, kernel, in_proj, in_bias, out_proj, gain, shift, out_bias,
    near, far, turned_out, shard, packed, table, wide, tall,
):
    count, width, channels = first.shape
    height = turned_out.shape[1]
    tile_index = lax.axis_index("dp") % TILES
    spots = (height, land_mask.shape[0])
    wanted = lax.broadcasted_iota(jnp.int32, spots, 0) + tile_index * height
    chosen = jnp.where(lax.broadcasted_iota(jnp.int32, spots, 1) == wanted, 1.0, 0.0).astype(BF16)
    ocean = land_mask[...].astype(F32).astype(BF16)
    table[...] = jnp.zeros_like(table)
    table[:height, :width] = jnp.dot(chosen, ocean, preferred_element_type=F32)
    turned = table[...].T[:width].astype(BF16)
    turned_out[...] = turned[:, :height]
    for i in range(count):
        factors = mask_of_row(turned, i), mask_of_row(turned, height - count + i)
        for t, lanes in tiles_of(channels):
            piece = pl.ds(t * LANES, lanes)
            rows = [v[i, :, piece].astype(F32) * f[:, :lanes] for v, f in zip((first, last), factors)]
            near[i, :, piece], far[i, :, piece] = (v.astype(BF16) for v in by_partner(*rows))
    wide[...] = jnp.zeros_like(wide)
    wide[: kernel.shape[0], : kernel.shape[1]] = kernel[...].astype(F32)
    shard[...] = wide[:LANES, :LANES].T[: shard.shape[0]].astype(BF16)
    pack_parameters(layout, in_proj, in_bias, out_proj, gain, shift, out_bias, packed, wide, tall)


def by_partner(top, bottom):
    odd = lax.axis_index("dp") % 2 == 1
    return jnp.where(odd, top, bottom), jnp.where(odd, bottom, top)


def prepare_kernel(feats, cot, turned, paired, gbranch, mask, stage, plain):
    width, channels = feats.shape[1:]
    blocks = paired.shape[0]
    step = pl.program_id(0)

    @pl.when(step == 0)
    def _():
        stage[...] = jnp.zeros_like(stage)
        plain[...] = jnp.zeros_like(plain)

    for local_row in range(feats.shape[0]):
        side = local_row % 2
        row = feats.shape[0] * step + local_row
        factor = mask_of_row(turned[...], row)
        rows = pl.ds(BASE, width)
        plain[side, 0, rows, :] = factor
        for t, lanes in tiles_of(channels):
            piece = pl.ds(t * LANES, lanes)
            buffer = stage.at[side, t]
            stage_row(buffer, feats[local_row, :, piece].astype(F32) * factor[:, :lanes], width)
            place_row(paired, buffer, t, blocks, step * (feats.shape[0] // 2) + (SPAN + local_row) // 2, (SPAN + local_row) % 2)
            plain[side, 1 + t, rows, :lanes] = cot[local_row, :, piece].astype(F32) * factor[:, :lanes]
        for r in range(FINE):
            mask[row, r] = plain[side, 0, pl.ds(BASE + r, PAD, stride=FINE), :]
            for t, _unused in tiles_of(channels):
                gbranch[row, r, :, t * LANES : (t + 1) * LANES] = plain[
                    side, 1 + t, pl.ds(BASE + r, PAD, stride=FINE), :
                ].astype(BF16)


def in_place(mine, parts, place):
    value = parts[0]
    for i, part in enumerate(parts[1:], 1):
        value = jnp.where(mine ^ i == place, part, value)
    return value


def inner_kernel(channels, shares, paired, mask, *rest):
    shards, (conv, sums, taps, weights, accs, table) = rest[:shares], rest[shares:]
    share = channels // shares
    mine = lax.axis_index("fsdp")
    table[...] = jnp.zeros_like(table)
    parts = [shard[...].astype(F32) for shard in shards]
    for f in range(shares):
        table[f * share : (f + 1) * share] = in_place(mine, parts, f)[:share]
    blocks = paired.shape[0]
    for block in range(blocks):
        piece = table[block * HALF : (block + 1) * HALF]
        taps[block] = jnp.concatenate([piece, piece], axis=0).T[: taps.shape[1]]
        build_weights(weights.at[block], taps, block, False)
    runs = inner_runs(mask.shape[0] // 2)[0]
    for t, _ in tiles_of(channels):
        lanes = pl.ds(t * LANES, LANES)
        planes = products(paired, None, weights, accs, t, runs)
        row, total, count = 2 * runs[0][0], 0.0, 0.0
        for k in range(FINE // 2):
            for odd, value in enumerate(planes(0, k, 0)):
                total = total + mask[row, 2 * k + odd] * value
                count = count + mask[row, 2 * k + odd]
        near = jnp.sum(total, axis=0, keepdims=True) / jnp.maximum(jnp.sum(count, axis=0, keepdims=True), 1.0)
        total, square = settle(planes, conv, mask, runs, lanes, near)
        sums[0:1, lanes] = near
        sums[1:2, lanes] = total
        sums[2:3, lanes] = square


def outer_kernel(channels, paired, near, far, mask, weights, sums, conv, stats, rims, accs, stage):
    height = mask.shape[0]
    blocks, pairs = paired.shape[0], height // 2
    width = near.shape[1]
    stage[...] = jnp.zeros_like(stage)
    last = pairs + PASSES - 1
    first_half = (SPAN % 2) * LANES
    last_half = ((SPAN + height - 1) % 2) * LANES
    rims[:, 1, :, :, first_half : first_half + LANES] = paired[:, 1, :, :, first_half : first_half + LANES]
    rims[:, 2, :, :, last_half : last_half + LANES] = paired[:, last - 2, :, :, last_half : last_half + LANES]
    for below, index, pair, side in rim_rows(height):

        def source(a, b, below=below, index=index):
            return by_partner(near[index, :, a:b].astype(F32), far[index, :, a:b].astype(F32))[below]

        place_natural(rims, stage, source, channels, width, blocks, pair, side)
    runs = inner_runs(pairs)[1]
    count = 0.0
    for row in range(height):
        for r in range(FINE):
            count = count + mask[row, r]
    count = jnp.sum(count, axis=0, keepdims=True)
    for t, _ in tiles_of(channels):
        lanes = pl.ds(t * LANES, LANES)
        planes = products(paired, rims, weights, accs, t, runs)
        near = sums[0:1, lanes]
        total, square = settle(planes, conv, mask, runs, lanes, near)
        total, square = total + sums[1:2, lanes], square + sums[2:3, lanes]
        shift = total / jnp.maximum(count, 1.0)
        stats[0:1, lanes] = near + shift
        stats[1:2, lanes] = jnp.maximum(square - total * shift, 0.0)
        stats[2:3, lanes] = count
        stats[3:8, lanes] = jnp.zeros((5, LANES), F32)


def products(paired, rims, weights, accs, tile, runs):
    has_upper = 2 * tile + 1 < paired.shape[0]
    for half in range(1 + has_upper):
        block = 2 * tile + half
        accs[half] = convolve_block(paired, rims, weights.at[block], block, runs)

    def planes(place, k, side):
        start = (place * (FINE // 2) + k) * PAD
        return split_blocks(accs.at[0], accs.at[1] if has_upper else None, start, side)

    return planes


def settle(planes, conv, mask, runs, lanes, near):
    sums = [jnp.zeros((PAD, LANES), F32)] * 8
    for place, h in enumerate(pairs_of(runs)):
        for k in range(FINE // 2):
            for side in range(2):
                for odd, value in enumerate(planes(place, k, side)):
                    conv[2 * place + side, 2 * k + odd, :, lanes] = value
                    away = value - near
                    part = mask[2 * h + side, 2 * k + odd] * away
                    at = 2 * (2 * side + odd)
                    sums[at] = sums[at] + part
                    sums[at + 1] = sums[at + 1] + part * away
    return (jnp.sum(sums[i] + sums[i + 2] + sums[i + 4] + sums[i + 6], axis=0, keepdims=True) for i in range(2))


def pointwise_kernel(
    channels, real_units, inner, outer, gbranch, feats, turned, vec, w_in, w_out,
    output, act_out, ghid_out, gz_out, z_out, sums, stage, conv,
):
    rows, width = feats.shape[0], feats.shape[1]
    padded = conv.shape[-1]
    cells = rows * FINE * PAD
    hidden_units = act_out.shape[1]
    step = pl.program_id(0)

    @pl.when(step == 0)
    def _():
        sums[...] = jnp.zeros_like(sums)

    one_lane = lax.broadcasted_iota(jnp.int32, (1, padded), 1) == channels
    mean, inverse, gain, shift = (vec[i : i + 1, :] for i in range(4))
    side = RIM_PAIRS // 2
    is_inner = jnp.logical_and(step >= side, step < pl.num_programs(0) - side)

    @pl.when(is_inner)
    def _():
        conv[...] = inner[pl.ds((step - side) * rows, rows)]

    @pl.when(jnp.logical_not(is_inner))
    def _():
        place = jnp.where(step < side, step, step + 2 * side - pl.num_programs(0))
        conv[...] = outer[pl.ds(place * rows, rows)]

    here = pl.ds(pl.multiple_of(step * cells, cells), cells)
    normed = (conv[...].reshape(cells, padded) - mean) * inverse
    zvals = jnp.where(one_lane, 1.0, gain * normed + shift).astype(BF16)
    z_out[here, :] = zvals
    mine = pl.ds(step * rows, rows)
    upstream = gbranch[mine].reshape(cells, padded)
    chunk = 2 * LANES
    across = (((1,), (1,)), ((), ()))
    c0 = 0.7978845608028654
    c1 = 0.044715 * c0
    for start in range(0, hidden_units, chunk):
        span = pl.ds(start, chunk)
        hidden = jnp.dot(zvals, w_in[:, span], preferred_element_type=F32)
        gact = lax.dot_general(upstream, w_out[span, :], across, preferred_element_type=F32)
        square = hidden * hidden
        share = 0.5 + 0.5 * jnp.tanh(hidden * (c0 + c1 * square))
        act = hidden * share
        slope = share + (act - act * share) * (2.0 * c0 + (6.0 * c1) * square)
        ghid = (gact * slope).astype(BF16)
        act = act.astype(BF16)
        if start + chunk > real_units:
            lane = lax.broadcasted_iota(jnp.int32, (1, chunk), 1)
            act = jnp.where(lane == real_units - start, jnp.ones((), BF16), act)
        act_out[here, span] = act
        ghid_out[here, span] = ghid
    branch = jnp.dot(act_out[here, :], w_out[...], preferred_element_type=F32)
    gz = lax.dot_general(ghid_out[here, :], w_in[...], across, preferred_element_type=F32)
    gz_out[mine] = gz.reshape(rows, *gz_out.shape[1:])
    sums[0:1, :] += jnp.sum(gz * normed, axis=0, keepdims=True)
    sums[1:2, :] += jnp.sum(gz, axis=0, keepdims=True)
    for row in range(rows):
        factor = mask_of_row(turned[...], step * rows + row)
        for t, lanes in tiles_of(channels):
            for r in range(FINE):
                start = (row * FINE + r) * PAD
                stage[row, t, pl.ds(r, PAD, stride=FINE), :] = branch[start : start + PAD, t * LANES : (t + 1) * LANES]
            piece = pl.ds(t * LANES, lanes)
            values = feats[row, :, piece].astype(F32) + stage[row, t, 0:width, :lanes]
            output[row, :, piece] = (values * factor[:, :lanes]).astype(BF16)


def out_grads_kernel(gbranch, act, grad):
    grad[...] = turned_product(gbranch, act, grad.shape[0])


def turned_product(left, right, rows):
    return lax.dot_general(left[:, :rows], right[...], (((0,), (0,)), ((), ())), preferred_element_type=F32)


def in_grads_kernel(channels, hidden, zvals, ghid, grad_out, kept, sent, grad_in):
    grad_in[...] = turned_product(zvals, ghid, grad_in.shape[0])
    shares = lax.axis_size("fsdp")
    layout = Packing(channels, hidden, shares)
    last = layout.in_tiles - 1
    lane = lax.broadcasted_iota(jnp.int32, (1, LANES), 1)
    spot = lax.broadcasted_iota(jnp.int32, (layout.out_pad, 1), 0)
    fill = jnp.zeros((layout.in_pad - layout.in_rows, LANES), F32)

    def write(out, j):
        rows = slice(j * layout.in_rows, (j + 1) * layout.in_rows)
        for t in range(layout.in_tiles):
            lanes = slice(t * LANES, (t + 1) * LANES)
            tile = grad_in[rows, lanes]
            if t == last:
                tile = jnp.where(lane == hidden - t * LANES, grad_out[rows, lanes], tile)
            tile = jnp.concatenate([tile, fill], axis=0)
            out[t * layout.in_pad : (t + 1) * layout.in_pad] = tile.astype(out.dtype)
        start = j * layout.out_rows
        aligned = start // LANES * LANES
        stop = min(aligned + (layout.out_tiles + 1) * LANES, grad_out.shape[1])
        part = jnp.where(
            spot == channels, grad_in[: layout.out_pad, aligned:stop], grad_out[: layout.out_pad, aligned:stop]
        )
        if start != aligned:
            part = pltpu.roll(part, stop - start, 1)
        for u in range(layout.out_tiles):
            base = layout.out_base + u * layout.out_pad
            out[base : base + layout.out_pad] = part[:, u * LANES : (u + 1) * LANES].astype(out.dtype)
        out[layout.small_base :] = jnp.zeros((layout.rows - layout.small_base, LANES), out.dtype)

    for mine in range(shares):

        @pl.when(lax.axis_index("fsdp") == mine)
        def _(mine=mine):
            for i in range(shares):
                rows = pl.ds(i // 2 * layout.rows, layout.rows)
                write((sent if i % 2 else kept).at[rows], mine ^ i)


def near_sum_kernel(kept, arrived, own, sent):
    rows = own.shape[0]
    own[...] = kept[:rows] + arrived[:rows].astype(F32)
    sent[...] = (kept[rows:] + arrived[rows:].astype(F32)).astype(BF16)


def finish_kernel(channels, hidden, slopes, *refs):
    parts, refs = refs[:-8], refs[-8:]
    grad_in, grad_in_bias, grad_out, grad_out_bias, grad_taps, grad_gain, grad_shift, packed = refs
    place = piece_of(lax.axis_index("dp"))
    rows = packed.shape[0] // len(parts)
    values = [part[:rows] for part in parts]
    for i in range(len(parts)):
        packed[i * rows : (i + 1) * rows] = in_place(place, values, i)
    low = (parts[0].shape[0] - rows) // 2
    exact = [part[rows : rows + low].astype(F32) + part[rows + low :].astype(F32) for part in parts]
    share = grad_in.shape[0]
    grad_taps[...] = tree(exact, lambda a, b: a + b)[: grad_taps.shape[0], :share]
    for mine in range(channels // share):

        @pl.when(lax.axis_index("fsdp") == mine)
        def _(start=mine * share):
            turned = pltpu.roll(slopes[...], slopes.shape[1] - start, 1) if start else slopes[...]
            grad_gain[...] = turned[5, :share]
            grad_shift[...] = turned[6, :share]

    layout = Packing(channels, hidden, channels // grad_in.shape[0])
    for t in range(layout.in_tiles):
        stop = min((t + 1) * LANES, hidden)
        tile = packed[t * layout.in_pad : (t + 1) * layout.in_pad].astype(F32)
        grad_in[:, t * LANES : stop] = tile[: layout.in_rows, : stop - t * LANES]
    tall = jnp.concatenate([tile, jnp.zeros((LANES - layout.in_pad, LANES), F32)], axis=0).T
    at = hidden - (layout.in_tiles - 1) * LANES
    grad_out_bias[...] = tall[at, : layout.in_rows]
    bias = []
    for u in range(layout.out_tiles):
        base = layout.out_base + u * layout.out_pad
        tile = packed[base : base + layout.out_pad].astype(F32)
        stop = min((u + 1) * LANES, layout.out_rows)
        count = stop - u * LANES
        bias.append(tile[channels : channels + 1, :])
        fill = jnp.zeros((round_up(layout.out_pad, LANES) - layout.out_pad, LANES), F32)
        grad_out[u * LANES : stop, :] = jnp.concatenate([tile, fill], axis=0).T[:count, :channels]
    grad_in_bias[...] = jnp.concatenate(bias, axis=1)[0, : layout.out_rows]


def share_taps_kernel(share, *refs):
    shares = lax.axis_size("fsdp")
    tiles, outs = refs[:-shares], refs[-shares:]
    wide = jnp.concatenate([tile[...] for tile in tiles], axis=1)
    for mine in range(shares):

        @pl.when(lax.axis_index("fsdp") == mine)
        def _(mine=mine):
            for i, out in enumerate(outs):
                start = (mine ^ i) * share
                turned = pltpu.roll(wide, wide.shape[1] - start, 1) if start else wide
                out[...] = turned[:, :LANES]


def tree(values, merge):
    while len(values) > 1:
        values = [merge(values[i], values[i + 1]) for i in range(0, len(values), 2)]
    return values[0]


def merge_stats(mine, other):
    count = mine[2:3] + other[2:3]
    safe = jnp.maximum(count, 1.0)
    mean = (mine[0:1] * mine[2:3] + other[0:1] * other[2:3]) / safe
    away = mine[0:1] - other[0:1]
    spread = mine[1:2] + other[1:2] + away * away * (mine[2:3] * other[2:3] / safe)
    return jnp.concatenate([mean, spread, count, jnp.zeros_like(mine[3:8])], axis=0)


def stats_kernel(*refs):
    refs[-1][...] = tree([ref[...] for ref in refs[:-1]], merge_stats)


def norm_kernel(vectors, *refs):
    stats = tree([ref[...] for ref in refs[:-1]], merge_stats)
    count = jnp.maximum(stats[2:3], 1.0)
    inverse = lax.rsqrt(stats[1:2] / count + EPSILON)
    refs[-1][...] = jnp.concatenate(
        [stats[0:1], inverse, vectors[0:2, :], count, jnp.zeros((3, stats.shape[1]), F32)], axis=0
    )


def sums_kernel(*refs):
    refs[-1][...] = tree([ref[...] for ref in refs[:-1]], lambda a, b: a + b)


def slopes_kernel(vec, *refs):
    sums = tree([ref[...] for ref in refs[:-1]], lambda a, b: a + b)
    scaled = vec[1:2, :] * vec[2:3, :]
    count = vec[4:5, :]
    refs[-1][...] = jnp.concatenate(
        [vec[0:2, :], scaled, scaled * sums[1:2] / count, scaled * sums[0:1] / count, sums[0:2], sums[2:3]], axis=0
    )


class Packing:
    def __init__(self, channels, hidden, shares):
        self.in_rows = channels // shares
        self.in_pad = round_up(self.in_rows, 16)
        self.in_tiles = -(-(hidden + 1) // LANES)
        self.out_rows = hidden // shares
        self.out_tiles = -(-self.out_rows // LANES)
        self.out_pad = round_up(max(channels + 1, self.out_rows), 16)
        self.out_base = self.in_pad * self.in_tiles
        self.small_base = self.out_base + self.out_pad * self.out_tiles
        self.small = self.out_tiles + 3
        self.rows = round_up(self.small_base + self.small, 32)


def pack_parameters(layout, in_proj, in_bias, out_proj, gain, shift, out_bias, packed, wide, tall):
    wide[...] = jnp.zeros_like(wide)
    tall[...] = jnp.zeros_like(tall)
    wide[: layout.in_rows, : in_proj.shape[1]] = in_proj[...].astype(F32)
    for t in range(layout.in_tiles):
        packed[t * layout.in_pad : (t + 1) * layout.in_pad] = wide[: layout.in_pad, t * LANES : (t + 1) * LANES].astype(BF16)
    tall[: layout.out_rows, : out_proj.shape[1]] = out_proj[...].astype(F32)
    for u in range(layout.out_tiles):
        base = layout.out_base + u * layout.out_pad
        packed[base : base + layout.out_pad] = tall[:, u * LANES : (u + 1) * LANES].astype(BF16)
    wide[...] = jnp.zeros_like(wide)
    for i, small in enumerate((in_bias, gain, shift, out_bias)):
        wide[i : i + 1, : small.shape[0]] = small[...].reshape(1, -1).astype(F32)
    rows = [wide[0:1, u * LANES : (u + 1) * LANES] for u in range(layout.out_tiles)]
    rows += [wide[i + 1 : i + 2, :LANES] for i in range(3)]
    rows.append(jnp.zeros((layout.rows - layout.small_base - layout.small, LANES), F32))
    packed[layout.small_base :] = jnp.concatenate(rows, axis=0).astype(BF16)


def assemble_kernel(layout, shares, *refs):
    packed, (w_in, w_out, vectors, wide, tall) = refs[:shares], refs[shares:]
    mine = lax.axis_index("fsdp")

    def rows_of(f, start, stop):
        return in_place(mine, [part[start:stop].astype(F32) for part in packed], f)

    wide[...] = jnp.zeros_like(wide)
    tall[...] = jnp.zeros_like(tall)
    channels, hidden = layout.in_rows * shares, layout.out_rows * shares
    in_bias = jnp.zeros((8, wide.shape[1]), F32)
    smalls = [jnp.zeros((8, tall.shape[1]), F32)] * 3
    for f in range(shares):
        for t in range(layout.in_tiles):
            tile = rows_of(f, t * layout.in_pad, (t + 1) * layout.in_pad)
            wide[f * layout.in_rows : (f + 1) * layout.in_rows, t * LANES : (t + 1) * LANES] = tile[: layout.in_rows]
        for u in range(layout.out_tiles):
            base = layout.out_base + u * layout.out_pad
            tile = rows_of(f, base, base + layout.out_pad)
            tall[f * layout.out_rows : (f + 1) * layout.out_rows, u * LANES : (u + 1) * LANES] = tile[: layout.out_rows]
        small = rows_of(f, layout.small_base, layout.rows)

        def spread(first, count, lanes, turn):
            pieces = [small[first + u : first + u + 1] for u in range(count)]
            pieces.append(jnp.zeros((1, lanes - count * LANES), F32))
            row = jnp.broadcast_to(jnp.concatenate(pieces, axis=1), (8, lanes))
            return pltpu.roll(row, turn, 1) if turn else row

        in_bias = in_bias + spread(0, layout.out_tiles, wide.shape[1], f * layout.out_rows)
        smalls = [
            total + spread(layout.out_tiles + i, 1, tall.shape[1], f * layout.in_rows)
            for i, total in enumerate(smalls)
        ]
    wide[channels : channels + 1] = in_bias[:1]
    tall[hidden : hidden + 1] = smalls[2][:1]
    w_in[...] = wide[...].astype(BF16)
    w_out[...] = tall[...].astype(BF16)
    vectors[...] = jnp.concatenate([smalls[0][:1], smalls[1][:1], jnp.zeros((6, tall.shape[1]), F32)], axis=0)


def shifted_planes(values, real):
    out = []
    for r in range(-SPAN, FINE + SPAN):
        value = values[r % FINE]
        if r < 0:
            value = jnp.concatenate([value[real - 1 : real], value[: PAD - 1]], axis=0)
        elif r >= FINE:
            value = jnp.concatenate([value[1:real], value[:1], value[: PAD - real]], axis=0)
        out.append(value)
    return out


def join_planes(first, second):
    low = low_half(PAD)
    return (
        jnp.where(low, first, swap(second)).astype(BF16),
        jnp.where(low, swap(first), second).astype(BF16),
    )


def place_planes(paired, planes, tile, blocks, pair, side):
    out_lanes = pl.ds(side * LANES, LANES)
    for k in range(len(planes) // 2):
        for half, value in enumerate(join_planes(planes[2 * k], planes[2 * k + 1])):
            if 2 * tile + half < blocks:
                paired[2 * tile + half, pair, k, :, out_lanes] = value


def arrange_kernel(
    channels, real, gz, inner, outer, mask, vec, near, far, gpaired, own, edges,
):
    height = gz.shape[0]
    blocks = own.shape[0]
    for t, _ in tiles_of(channels):
        lanes = pl.ds(t * LANES, LANES)
        mean, inverse, scaled, bias, slope = (vec[i : i + 1, lanes] for i in range(5))
        for row in range(height):
            h, side = row // 2, row % 2
            values = []
            for r in range(FINE):
                normed = (conv_at(inner, outer, row, r, lanes) - mean) * inverse
                values.append(scaled * gz[row, r, :, lanes] - mask[row, r] * (bias + normed * slope))
            out_lanes = pl.ds(side * LANES, LANES)
            for k in range(FINE // 2):
                rows = pl.ds((h * (FINE // 2) + k) * PAD, PAD)
                for half, value in enumerate(join_planes(values[2 * k], values[2 * k + 1])):
                    if 2 * t + half < blocks:
                        own[2 * t + half, rows, out_lanes] = value
            place_planes(gpaired, shifted_planes(values, real), t, blocks, (SPAN + row) // 2, (SPAN + row) % 2)
            for edge, border in ((0, row < SPAN), (1, row >= height - SPAN)):
                if border:
                    place = row - (height - SPAN) * edge
                    for r in range(FINE):
                        edges[edge, place, r, :, lanes] = values[r].astype(BF16)
    near[...], far[...] = by_partner(edges[0], edges[1])


def conv_at(inner, outer, row, r, lanes):
    start = RIM_PAIRS
    stop = start + inner.shape[0]
    if start <= row < stop:
        return inner[row - start, r, :, lanes]
    return outer[row if row < start else row - stop + start, r, :, lanes]


def taps_kernel(tile, own, paired, rims, select, grad_taps):
    blocks, pairs = own.shape[0], paired.shape[1] - PASSES + 1
    lane = lax.broadcasted_iota(jnp.int32, (HALF, 2 * LANES), 1)
    sub = lax.broadcasted_iota(jnp.int32, (HALF, 2 * LANES), 0)
    diagonal = lax.rem(lane, HALF) == sub
    low = low_half(grad_taps.shape[0])
    totals = []
    for block in range(2 * tile, min(2 * tile + 2, blocks)):
        turned = own[block].T
        found = []
        for m in range(PASSES):
            for s in range(PASSES):
                product = jnp.dot(turned, pass_rows(paired, rims, block, m, s, [(0, pairs)]), preferred_element_type=F32)
                for q in range(4):
                    part = product[q * HALF : (q + 1) * HALF]
                    found.append(jnp.sum(jnp.where(diagonal, part, 0.0), axis=0, keepdims=True))
        found = jnp.concatenate(found, axis=0)
        total = None
        for place in range(4):
            group = jnp.dot(select[place], found, preferred_element_type=F32, precision=lax.Precision.HIGHEST)
            group = group[:, (place // 2) * LANES : (place // 2 + 1) * LANES]
            if place % 2:
                group = swap(group)
            total = group if total is None else total + group
        totals.append(total)
    second = swap(totals[1]) if len(totals) > 1 else jnp.zeros_like(totals[0])
    grad_taps[...] = jnp.where(low, totals[0], second)


def flip_kernel(taps, weights):
    for block in range(weights.shape[0]):
        build_weights(weights.at[block], taps, block, True)


def backward_kernel(tile, real, gpaired, near, far, weights, cot, turned, *rest):
    result, rims, accs, stage = rest[-4:]
    height, width = cot.shape[:2]
    blocks, pairs = gpaired.shape[0], height // 2
    last = pairs + PASSES - 1
    first_half = (SPAN % 2) * LANES
    last_half = ((SPAN + height - 1) % 2) * LANES
    has_upper = 2 * tile + 1 < blocks
    for half in range(1 + has_upper):
        source = gpaired.at[2 * tile + half]
        rims[half, 1, :, :, first_half : first_half + LANES] = source[1, :, :, first_half : first_half + LANES]
        rims[half, 2, :, :, last_half : last_half + LANES] = source[last - 2, :, :, last_half : last_half + LANES]
    for below, index, pair, side in rim_rows(height):
        piece = pl.ds(tile * LANES, LANES)
        values = [
            by_partner(near[index, r, :, piece].astype(F32), far[index, r, :, piece].astype(F32))[below]
            for r in range(FINE)
        ]
        place_planes(rims, shifted_planes(values, real), 0, 1 + has_upper, pair, side)
    for half in range(1 + has_upper):
        block = 2 * tile + half
        accs[half] = convolve_block(
            gpaired.at[block : block + 1], rims.at[half : half + 1], weights.at[block], 0, [(0, pairs)]
        )

    def spread(h, _):
        for side in range(2):
            row = 2 * h + side
            for k in range(FINE // 2):
                even, odd = split_blocks(
                    accs.at[0], accs.at[1] if has_upper else None, (h * (FINE // 2) + k) * PAD, side
                )
                stage[side, pl.ds(2 * k, PAD, stride=FINE), :] = even
                stage[side, pl.ds(2 * k + 1, PAD, stride=FINE), :] = odd
            values = cot[row].astype(F32) + stage[side, 0:width]
            result[row] = (values * mask_of_row(turned[...], row)).astype(BF16)
        return 0

    for h in range(pairs):
        spread(h, 0)


def bits(size):
    bit = 1
    while bit < size:
        yield bit
        bit *= 2


def swapped(value, axis, flip):
    size = lax.axis_size(axis)
    return lax.ppermute(value, axis, [(i, i ^ flip) for i in range(size)])


def phases(*axes):
    out = []
    for axis in axes:
        left = list(bits(lax.axis_size(axis)))
        while left:
            near, left = left[:2], left[2:]
            out.append((axis, near if len(near) < 2 else [near[0], near[1], near[0] | near[1]]))
    return out


def tied(*values):
    return lax.optimization_barrier(values)


def halves_kernel(bit, *refs):
    parts, (keep, send) = refs[:-2], refs[-2:]
    rows = keep.shape[0]
    halves = [sum((part[a : a + rows].astype(F32) for part in parts[1:]), parts[0][a : a + rows]) for a in (0, rows)]
    first = lax.axis_index("dp") // bit % 2 == 0
    keep[...] = jnp.where(first, halves[0], halves[1])
    send[...] = jnp.where(first, halves[1], halves[0]).astype(send.dtype)


def whole_kernel(count, *refs):
    parts, extra, out = refs[:count], refs[count:-1], refs[-1]
    rows = parts[0].shape[0]
    out[:rows] = sum((part[...].astype(F32) for part in parts[1:]), parts[0][...])
    if extra:
        out[rows:] = sum((part[...] for part in extra[1:]), extra[0][...])


def last_kernel(rows, mine, other, out):
    total = mine[...] + other[...]
    rest = total.shape[0] - rows
    high = total[rows:].astype(BF16)
    out[:rows] = total[:rows].astype(BF16)
    out[rows : rows + rest] = high
    out[rows + rest :] = (total[rows:] - high.astype(F32)).astype(BF16)


def beside(work, *values):
    done = work() if work else ()
    return lax.optimization_barrier((done, values))


def far_bits():
    return list(bits(lax.axis_size("dp")))[1:3]


def piece_of(place):
    piece = 0
    for bit in far_bits():
        piece = 2 * piece + place // bit % 2
    return piece


class Spreading:
    def __init__(self, *parts):
        self.parts, self.extra = parts, ()
        cuts = far_bits()
        self.moves = [("half", [bit]) for bit in cuts]
        self.moves += [("whole", [bit]) for bit in bits(lax.axis_size("dp")) if bit not in cuts]
        flips = [0]
        for bit in reversed(cuts):
            flips += [flip | bit for flip in flips]
        self.moves.append(("gather", flips[1:]))

    def start(self):
        kind, flips = self.moves.pop(0)
        rows, lanes = self.parts[0].shape
        operands = (*self.parts, *self.extra)
        run = lambda kernel, *outs: call(
            kernel, outs, operands, [WHOLE] * len(operands), limit=10, name="sum_weights"
        )
        if kind == "half":
            kept, sent = run(
                functools.partial(halves_kernel, flips[0]),
                anywhere((rows // 2, lanes), F32),
                anywhere((rows // 2, lanes), BF16),
            )
        elif kind == "whole":
            low = self.extra[0].shape[0] if self.extra else 0
            if self.extra:
                self.rows = rows
            (kept,) = (sent,) = run(
                functools.partial(whole_kernel, len(self.parts)), anywhere((rows + low, lanes), F32)
            )
            self.extra = ()
        else:
            (kept,) = (sent,) = run(
                functools.partial(last_kernel, self.rows), anywhere((2 * rows - self.rows, lanes), BF16)
            )
        self.parts = (kept,)
        return [swapped(sent, "dp", flip) for flip in flips]

    def finish(self, others):
        self.parts = (*self.parts, *others)


def border_exchange(near, far):
    size = lax.axis_size("dp")
    first = [(i, i ^ 1) for i in range(size)]
    second = [(i, i + 1) for i in range(1, size - 1, 2) if (i + 1) % TILES]
    second += [(j, i) for i, j in second]
    return lax.ppermute(near, "dp", first), lax.ppermute(far, "dp", second)


def tap_selectors(rows):
    out = np.zeros((4, rows, PASSES * PASSES * 4), np.float32)
    for m in range(PASSES):
        for s in range(PASSES):
            for q in range(4):
                for p in range(4):
                    a = 2 * m + p // 2 - q // 2
                    b = 2 * s + p % 2 - q % 2
                    if 0 <= a < KW and 0 <= b < KW:
                        out[p, a * KW + b, (m * PASSES + s) * 4 + q] = 1.0
    return out


def local(features, land_mask, cotangent, kernel, norm_gain, norm_shift, in_proj, in_bias, out_proj, out_bias):
    feats, cot = features[0, 0], cotangent[0, 0]
    height, width, channels = feats.shape
    hidden = in_proj.shape[1]
    shares = lax.axis_size("fsdp")
    padded = round_up(channels + 1, LANES)
    hidden_pad = round_up(hidden + 1, 2 * LANES)
    blocks = -(-channels // HALF)
    pairs = height // 2
    planes_in = (FINE + 2 * SPAN) // 2
    row_pairs = pairs + PASSES - 1
    cells = height * FINE * PAD
    block_rows = pairs * (FINE // 2) * PAD
    stage_rows = round_up(BASE + SPAN + FINE * PAD, 8)
    tile_count = len(tiles_of(channels))
    tap_rows = round_up(TAPS, 8)
    real = width // FINE
    layout = Packing(channels, hidden, shares)

    edge = lambda at: pl.BlockSpec((SPAN, width, channels), lambda i: (at, 0, 0))
    whole = lambda array: pl.BlockSpec(array.shape, lambda i: (0,) * array.ndim)
    natural_shape = (height, width, channels)
    edge_shape = (SPAN, width, channels)
    paired_shape = (blocks, row_pairs, planes_in, PAD, 4 * HALF)
    rims_shape = (blocks, RIM_PAIRS, planes_in, PAD, 4 * HALF)
    plane_shape = (height, FINE, PAD, padded)
    mask_shape = (height, FINE, PAD, LANES)
    small = (kernel.T, in_proj, in_bias, out_proj, norm_gain, norm_shift, out_bias)
    near, far, turned, shard, packed = call(
        functools.partial(begin_kernel, layout),
        [
            anywhere(edge_shape, BF16),
            anywhere(edge_shape, BF16),
            anywhere((width, height), BF16),
            anywhere((layout.in_pad, LANES), BF16),
            anywhere((layout.rows, LANES), BF16),
        ],
        (slow(feats), slow(feats), slow(land_mask), *(slow(v) for v in small)),
        [edge(0), edge(height // SPAN - 1), whole(land_mask)] + [whole(v) for v in small],
        [
            pltpu.VMEM((round_up(height, LANES), round_up(width, LANES)), F32),
            pltpu.VMEM((round_up(layout.in_pad, LANES), hidden_pad), F32),
            pltpu.VMEM((layout.out_pad, padded), F32),
        ],
        grid=(1,),
        out_specs=[WHOLE] * 5,
        name="begin",
    )
    others = list(range(1, shares))
    six = 6 if height % 6 == 0 else 2
    stage = pltpu.VMEM((2, tile_count, 2, stage_rows, LANES), F32)
    near, far = border_exchange(near, far)
    shards = [swapped(shard, "fsdp", i) for i in others]
    (paired, gbranch, mask), (packed, shards) = beside(
        lambda: call(
            prepare_kernel,
            [pltpu.VMEM(paired_shape, BF16), pltpu.VMEM(plane_shape, BF16), pltpu.VMEM(mask_shape, F32)],
            (slow(feats), slow(cot), turned),
            [pl.BlockSpec((six, width, channels), lambda i: (i, 0, 0))] * 2 + [WHOLE],
            [stage, pltpu.VMEM((2, 1 + tile_count, stage_rows, LANES), F32)],
            grid=(height // six,),
            name="prepare",
        ),
        packed,
        [shard, *shards],
    )
    cuts = list(bits(shares))
    direct = [swapped(packed, "fsdp", bit) for bit in cuts]
    inner, outer = inner_runs(pairs)
    run_rows = lambda runs: 2 * len(pairs_of(runs))
    run_accs = lambda runs: pltpu.VMEM((2, run_rows(runs) * (FINE // 2) * PAD // 2, 4 * HALF), F32)
    weights_shape = (PASSES * PASSES * 4 * HALF, 4 * HALF)
    (conv_inner, sums, taps, weights), (near, far) = beside(
        lambda: call(
            functools.partial(inner_kernel, channels, shares),
            [
                pltpu.VMEM((run_rows(inner), FINE, PAD, padded), F32),
                anywhere((8, padded), F32),
                anywhere((blocks, tap_rows, LANES), F32),
                pltpu.VMEM((blocks, *weights_shape), BF16),
            ],
            (fast(paired), fast(mask), *shards),
            [WHOLE] * (2 + shares),
            [run_accs(inner), pltpu.VMEM((blocks * HALF, LANES), F32)],
            limit=10,
            name="inner",
        ),
        near,
        far,
    )
    (conv_outer, stats, rims), (packed, direct) = beside(
        lambda: call(
            functools.partial(outer_kernel, channels),
            [
                pltpu.VMEM((run_rows(outer), FINE, PAD, padded), F32),
                anywhere((8, padded), F32),
                pltpu.VMEM(rims_shape, BF16),
            ],
            (fast(paired), near, far, fast(mask), fast(weights), sums),
            [WHOLE] * 6,
            [run_accs(outer), stage],
            flops=4 * 10**9,
            limit=10,
            name="outer",
        ),
        packed,
        direct,
    )
    packed = {0: packed, **dict(zip(cuts, direct))}
    for flip in others:
        if flip not in packed:
            packed[flip] = swapped(packed[flip & (flip - 1)], "fsdp", flip & -flip)
    packed = [packed[flip] for flip in range(shares)]
    assemble = lambda: call(
        functools.partial(assemble_kernel, layout, shares),
        [
            anywhere((padded, hidden_pad), BF16),
            anywhere((hidden_pad, padded), BF16),
            anywhere((8, padded), F32),
        ],
        packed,
        [WHOLE] * shares,
        [pltpu.VMEM((padded, hidden_pad), F32), pltpu.VMEM((hidden_pad, padded), F32)],
        name="assemble",
    )
    row_sums = anywhere((8, padded), F32)
    combine = lambda kernel, *values: call(kernel, [row_sums], values, [WHOLE] * len(values), limit=4, name="combine")[0]
    rounds = phases("fsdp", "dp")
    for n, (axis, flips) in enumerate(rounds):
        last = n + 1 == len(rounds)
        values = [stats, *(swapped(stats, axis, i) for i in flips)]
        if n + 2 == len(rounds):
            values += packed
        done, values = beside(assemble if last else None, *values)
        if n + 2 == len(rounds):
            packed, values = values[-shares:], values[:-shares]
        if last:
            w_in, w_out, vectors = done
        if n + 1 < len(rounds):
            stats = combine(stats_kernel, *values)
    vec = combine(norm_kernel, vectors, *values)

    rows = 2
    steps = height // rows
    by_row = lambda *rest: pl.BlockSpec((rows, *rest), lambda i: (i,) + (0,) * len(rest))
    output, act, ghid, gz, zvals, sums = call(
        functools.partial(pointwise_kernel, channels, hidden),
        [
            anywhere(natural_shape, BF16),
            pltpu.VMEM((cells, hidden_pad), BF16),
            pltpu.VMEM((cells, hidden_pad), BF16),
            pltpu.VMEM(plane_shape, F32),
            pltpu.VMEM((cells, padded), BF16),
            row_sums,
        ],
        (fast(conv_inner), fast(conv_outer), fast(gbranch), slow(feats), turned, vec, w_in, w_out),
        [WHOLE] * 3 + [by_row(width, channels)] + [WHOLE] * 4,
        [
            pltpu.VMEM((rows, tile_count, round_up(FINE * PAD, 8), LANES), F32),
            pltpu.VMEM((rows, FINE, PAD, padded), F32),
        ],
        flops=14 * 10**9,
        grid=(steps,),
        out_specs=[by_row(width, channels)] + [WHOLE] * 5,
        limit=9,
        name="pointwise",
    )

    grad_rows = round_up(channels + 1, 16)

    def out_grads():
        return call(
            out_grads_kernel,
            [pltpu.VMEM((grad_rows, hidden_pad), F32)],
            (fast(gbranch.reshape(cells, padded)), fast(act)),
            [WHOLE] * 2,
            flops=3 * 10**9,
            limit=4,
            name="out_grads",
        )

    def in_grads():
        return call(
            functools.partial(in_grads_kernel, channels, hidden),
            [pltpu.VMEM((shares // 2 * layout.rows, LANES), dtype) for dtype in (F32, BF16)],
            (fast(zvals), fast(ghid), fast(grad_out)),
            [WHOLE] * 3,
            [pltpu.VMEM((grad_rows, hidden_pad), F32)],
            flops=3 * 10**9,
            limit=6,
            name="in_grads",
        )

    work = out_grads
    for n, (axis, flips) in enumerate(rounds):
        values = [sums, *(swapped(sums, axis, i) for i in flips)]
        if n == 2:
            values.append(sent)
        done, values = beside(work, *values)
        if n == 2:
            *values, sent = values
        work = None
        if n == 0:
            (grad_out,) = done
            work = in_grads
        if n + 1 == len(rounds):
            (flipped,) = done
        if n == 1:
            kept, sent = done
            sent = swapped(sent, "fsdp", 1)
        if n + 2 == len(rounds):
            work = lambda: call(
                flip_kernel,
                [pltpu.VMEM((blocks, *weights_shape), BF16)],
                (taps,),
                [WHOLE],
                limit=4,
                name="flip",
            )
        if n + 1 < len(rounds):
            sums = combine(sums_kernel, *values)
    gvec = combine(slopes_kernel, vec, *values)
    kept, sent = call(
        near_sum_kernel,
        [anywhere((layout.rows, LANES), F32), anywhere((layout.rows, LANES), BF16)],
        (kept, sent),
        [WHOLE] * 2,
        limit=10,
        name="near_sum",
    )
    sent = swapped(sent, "fsdp", 2)
    near, far, gpaired, own = call(
        functools.partial(arrange_kernel, channels, real),
        [
            anywhere((SPAN, FINE, PAD, padded), BF16),
            anywhere((SPAN, FINE, PAD, padded), BF16),
            pltpu.VMEM(paired_shape, BF16),
            pltpu.VMEM((blocks, block_rows, 4 * HALF), BF16),
        ],
        (fast(gz), fast(conv_inner), fast(conv_outer), fast(mask), gvec),
        [WHOLE] * 5,
        [pltpu.VMEM((2, SPAN, FINE, PAD, padded), BF16)],
        flops=10**8,
        moved=10 * MIB,
        limit=6,
        name="arrange",
    )
    select = jnp.asarray(tap_selectors(tap_rows))
    near, far = border_exchange(near, far)

    def taps_of(t):
        return lambda: call(
            functools.partial(taps_kernel, t),
            [anywhere((tap_rows, LANES), F32)],
            (fast(own), fast(paired), fast(rims), select),
            [WHOLE] * 4,
            flops=4 * 10**9,
            limit=6,
            name="taps",
        )

    (first,) = taps_of(0)()
    (second,), (sent,) = beside(taps_of(1), sent)
    spreading = Spreading(kept, sent)
    rest = lambda: [taps_of(t)()[0] for t in range(2, tile_count)]
    more, (there,) = beside(rest, spreading.start())
    spreading.finish(there)
    near, far, *tiles = tied(near, far, first, second, *more)
    own_taps, *sent_taps = call(
        functools.partial(share_taps_kernel, layout.in_rows),
        [anywhere((tap_rows, LANES), F32)] * shares,
        tiles,
        [WHOLE] * tile_count,
        limit=4,
        name="share_taps",
    )
    sent_taps = [swapped(v, "fsdp", i) for i, v in zip(others, sent_taps)]
    accs = pltpu.VMEM((2, block_rows, 4 * HALF), F32)

    def backward_of(t, *before):
        column = pl.BlockSpec((height, width, LANES), lambda i: (0, 0, t))
        return lambda: call(
            functools.partial(backward_kernel, t, real),
            [anywhere(natural_shape, BF16)],
            (fast(gpaired), near, far, fast(flipped), slow(cot), turned, *before),
            [WHOLE] * 4 + [column, WHOLE] + [HBM] * len(before),
            [
                pltpu.VMEM((2, RIM_PAIRS, planes_in, PAD, 4 * HALF), BF16),
                accs,
                pltpu.VMEM((2, round_up(FINE * PAD, 8), LANES), F32),
            ],
            flops=4 * 10**9,
            limit=12,
            grid=(1,),
            out_specs=[column],
            aliases={6: 0} if before else {},
            name="backward",
        )

    result = ()
    for n in range(max(tile_count, len(spreading.moves))):
        work = backward_of(tile_count - 1 - n, *result) if n < tile_count else None
        values = [spreading.start()] if spreading.moves else []
        if n == 0:
            values += sent_taps
        done, values = beside(work, *values)
        result = done or result
        if values:
            spreading.finish(values[0])
        if n == 0:
            spreading.extra = (own_taps, *values[1:])
    (result,) = result
    pieces = spreading.parts
    grad_in, grad_in_bias, grad_out, grad_out_bias, grad_taps, grad_gain, grad_shift = call(
        functools.partial(finish_kernel, channels, hidden),
        [
            anywhere((layout.in_rows, hidden), F32),
            anywhere((layout.out_rows,), F32),
            anywhere((layout.out_rows, channels), F32),
            anywhere((layout.in_rows,), F32),
            anywhere((TAPS, layout.in_rows), F32),
            anywhere((layout.in_rows,), F32),
            anywhere((layout.in_rows,), F32),
        ],
        (gvec, *pieces),
        [WHOLE] * (1 + len(pieces)),
        [pltpu.VMEM((layout.rows, LANES), BF16)],
        name="finish",
    )
    return (
        output[None, None],
        result[None, None],
        grad_taps.T,
        grad_gain,
        grad_shift,
        grad_in,
        grad_in_bias,
        grad_out,
        grad_out_bias,
    )


def solution(mesh):
    spread = P("dp", "fsdp", None, None, None)
    split = P("fsdp", None)
    line = P("fsdp")
    return jax.shard_map(
        local,
        mesh=mesh,
        in_specs=(spread, P(), spread, split, line, line, split, line, split, line),
        out_specs=(spread, spread, split, line, line, split, line, split, line),
        check_vma=False,
    )
```

```python
import functools

import jax
import jax.numpy as jnp
import numpy as np
from jax import lax
from jax.experimental import pallas as pl
from jax.experimental.pallas import tpu as pltpu
from jax.sharding import PartitionSpec as P

KW = 7
SPAN = KW // 2
TILES = 8
EPSILON = 1e-05

LANES = 128
HALF = 64
FINE = 12
PAD = 16
PASSES = (KW + 1) // 2
TAPS = KW * KW
RIM_PAIRS = 4
BASE = 8

F32 = jnp.float32
BF16 = jnp.bfloat16
MIB = 2**20
WHOLE = pl.BlockSpec(memory_space=pltpu.VMEM)
HBM = pl.BlockSpec(memory_space=pl.ANY)


def fast(value):
    return pltpu.with_memory_space_constraint(value, pltpu.VMEM)


def slow(value):
    return pltpu.with_memory_space_constraint(value, pltpu.HBM)


def anywhere(shape, dtype):
    return jax.ShapeDtypeStruct(shape, dtype)


def round_up(value, step):
    return -(-value // step) * step


def call(kernel, outs, operands, in_specs, scratch=(), flops=0, moved=0, grid=None, out_specs=None, limit=10, aliases=None, name=None):
    extra = {} if grid is None else {"grid": grid}
    return pl.pallas_call(
        kernel,
        out_shape=outs,
        in_specs=in_specs,
        out_specs=[WHOLE] * len(outs) if out_specs is None else out_specs,
        scratch_shapes=list(scratch),
        input_output_aliases=aliases or {},
        compiler_params=pltpu.CompilerParams(vmem_limit_bytes=limit * MIB),
        cost_estimate=pl.CostEstimate(flops=flops, bytes_accessed=moved, transcendentals=0),
        name=name,
        **extra,
    )(*operands)


def low_half(rows):
    return lax.broadcasted_iota(jnp.int32, (rows, LANES), 1) < HALF


def swap(value):
    return pltpu.roll(value, HALF, 1)


def tiles_of(channels):
    return [(t, min(LANES, channels - t * LANES)) for t in range(-(-channels // LANES))]


def mask_of_row(turned, row):
    chosen = lax.broadcasted_iota(jnp.int32, (turned.shape[1], LANES), 0) == row
    return jnp.dot(turned, jnp.where(chosen, 1.0, 0.0).astype(BF16), preferred_element_type=F32)


def stage_row(stage, values, width):
    lanes = values.shape[1]
    stage[0, BASE : BASE + width, :lanes] = values
    stage[0, BASE - SPAN : BASE, :lanes] = values[width - SPAN :]
    stage[0, BASE + width : BASE + width + SPAN, :lanes] = values[:SPAN]
    stage[1] = swap(stage[0])


def plane(stage, which, start):
    return stage[which, pl.ds(start, PAD, stride=FINE), :]


def place_row(paired, stage, tile, blocks, pair, side):
    low = low_half(PAD)
    lanes = pl.ds(side * LANES, LANES)
    for k in range((FINE + 2 * SPAN) // 2):
        start = BASE - SPAN + 2 * k
        paired[2 * tile, pair, k, :, lanes] = jnp.where(
            low, plane(stage, 0, start), plane(stage, 1, start + 1)
        ).astype(BF16)
        if 2 * tile + 1 < blocks:
            paired[2 * tile + 1, pair, k, :, lanes] = jnp.where(
                low, plane(stage, 1, start), plane(stage, 0, start + 1)
            ).astype(BF16)


def place_natural(paired, stage, source, channels, width, blocks, pair, side, factor=None):
    for t, lanes in tiles_of(channels):
        values = source(t * LANES, t * LANES + lanes).astype(F32)
        if factor is not None:
            values = values * factor[:, :lanes]
        buffer = stage.at[side, t]
        stage_row(buffer, values, width)
        place_row(paired, buffer, t, blocks, pair, side)


def rim_rows(height):
    inner = (height + 2 * SPAN) // 2 - RIM_PAIRS // 2
    for index in range(SPAN):
        yield 0, index, index // 2, index % 2
    for index in range(SPAN):
        row = SPAN + height + index
        yield 1, index, row // 2 - inner + RIM_PAIRS // 2, row % 2


def build_weights(weights, taps, block, flip):
    lane = lax.broadcasted_iota(jnp.int32, (HALF, LANES), 1)
    sub = lax.broadcasted_iota(jnp.int32, (HALF, LANES), 0)
    diagonal = lax.rem(lane, HALF) == sub
    low = low_half(1)
    zero = jnp.zeros((1, LANES), F32)

    def tap_row(a, b):
        if not (0 <= a < KW and 0 <= b < KW):
            return zero
        index = (KW - 1 - a) * KW + KW - 1 - b if flip else a * KW + b
        return taps[block, index : index + 1, :]

    for m in range(PASSES):
        for s in range(PASSES):
            for place in range(4):
                pr, pj = divmod(place, 2)
                for qr in range(2):
                    a, b = 2 * m + pr - qr, 2 * s + pj
                    row = jnp.where(low, tap_row(a, b), tap_row(a, b - 1))
                    weights[
                        (m * PASSES + s) * 4 * HALF + place * HALF : (m * PASSES + s) * 4 * HALF + (place + 1) * HALF,
                        qr * LANES : (qr + 1) * LANES,
                    ] = jnp.where(diagonal, row, 0.0).astype(BF16)


def pass_rows(paired, rims, block, m, s, runs):
    places = pl.ds(s, FINE // 2)
    side = RIM_PAIRS // 2
    inner = paired.shape[1] - side
    pieces = []
    for start, stop in runs:
        start, stop = start + m, stop + m
        pieces += [rims[block, i, places] for i in range(start, min(stop, side))]
        if max(start, side) < min(stop, inner):
            pieces.append(paired[block, max(start, side) : min(stop, inner), places])
        pieces += [rims[block, i - inner + side, places] for i in range(max(start, inner), stop)]
    return jnp.concatenate([piece.reshape(-1, 4 * HALF) for piece in pieces], axis=0)


def convolve_block(paired, rims, weights, block, runs):
    rows = jnp.concatenate(
        [pass_rows(paired, rims, block, m, s, runs) for m in range(PASSES) for s in range(PASSES)], axis=1
    )
    return jnp.dot(rows, weights[...], preferred_element_type=F32)


def inner_runs(pairs):
    side = RIM_PAIRS // 2
    return [(side, pairs - side)], [(0, side), (pairs - side, pairs)]


def pairs_of(runs):
    return [h for start, stop in runs for h in range(start, stop)]


def split_blocks(lower, upper, start, side):
    low = low_half(PAD)
    rows, lanes = pl.ds(start, PAD), pl.ds(side * LANES, LANES)
    first = lower[rows, lanes]
    if upper is None:
        return first, swap(first)
    second = upper[rows, lanes]
    return jnp.where(low, first, swap(second)), jnp.where(low, swap(first), second)


def begin_kernel(
    layout, first, last, land_mask, kernel, in_proj, in_bias, out_proj, gain, shift, out_bias,
    near, far, turned_out, shard, packed, table, wide, tall, edge, side,
):
    count, width, channels = first.shape
    height = turned_out.shape[1]
    tile_index = lax.axis_index("dp") % TILES
    spots = (height, land_mask.shape[0])
    wanted = lax.broadcasted_iota(jnp.int32, spots, 0) + tile_index * height
    chosen = jnp.where(lax.broadcasted_iota(jnp.int32, spots, 1) == wanted, 1.0, 0.0).astype(BF16)
    ocean = land_mask[...].astype(F32).astype(BF16)
    table[...] = jnp.zeros_like(table)
    table[:height, :width] = jnp.dot(chosen, ocean, preferred_element_type=F32)
    turned = table[...].T[:width].astype(BF16)
    turned_out[...] = turned[:, :height]
    edge[...] = jnp.zeros_like(edge)
    side[...] = jnp.zeros_like(side)
    for i in range(count):
        factors = mask_of_row(turned, i), mask_of_row(turned, height - count + i)
        for t, lanes in tiles_of(channels):
            piece = pl.ds(t * LANES, lanes)
            rows = [v[i, :, piece].astype(F32) * f[:, :lanes] for v, f in zip((first, last), factors)]
            place, turn = border_place(i, t, channels, count)
            for out, row in enumerate(by_partner(*rows)):
                if lanes == LANES:
                    edge[out, place] = row
                else:
                    side[out, :, :lanes] = row
                    value = swap(side[out]) if turn else side[out]
                    edge[out, place] = edge[out, place] + value
    near[...] = edge[0].astype(BF16)
    far[...] = edge[1].astype(BF16)
    wide[...] = jnp.zeros_like(wide)
    wide[: kernel.shape[0], : kernel.shape[1]] = kernel[...].astype(F32)
    shard[...] = wide[:LANES, :LANES].T[: shard.shape[0]].astype(BF16)
    pack_parameters(layout, in_proj, in_bias, out_proj, gain, shift, out_bias, packed, wide, tall)


def border_place(row, tile, channels, rows):
    whole, left = divmod(channels, LANES)
    if tile < whole:
        return row * whole + tile, False
    if left > HALF:
        return rows * whole + row, False
    return rows * whole + row // 2, row % 2 == 1


def by_partner(top, bottom):
    odd = lax.axis_index("dp") % 2 == 1
    return jnp.where(odd, top, bottom), jnp.where(odd, bottom, top)


def prepare_kernel(feats, cot, turned, paired, gbranch, mask, stage, plain):
    width, channels = feats.shape[1:]
    blocks = paired.shape[0]
    step = pl.program_id(0)

    @pl.when(step == 0)
    def _():
        stage[...] = jnp.zeros_like(stage)
        plain[...] = jnp.zeros_like(plain)

    for local_row in range(feats.shape[0]):
        side = local_row % 2
        row = feats.shape[0] * step + local_row
        factor = mask_of_row(turned[...], row)
        rows = pl.ds(BASE, width)
        plain[side, 0, rows, :] = factor
        for t, lanes in tiles_of(channels):
            piece = pl.ds(t * LANES, lanes)
            buffer = stage.at[side, t]
            stage_row(buffer, feats[local_row, :, piece].astype(F32) * factor[:, :lanes], width)
            place_row(paired, buffer, t, blocks, step * (feats.shape[0] // 2) + (SPAN + local_row) // 2, (SPAN + local_row) % 2)
            plain[side, 1 + t, rows, :lanes] = cot[local_row, :, piece].astype(F32) * factor[:, :lanes]
        for r in range(FINE):
            mask[row, r] = plain[side, 0, pl.ds(BASE + r, PAD, stride=FINE), :]
            for t, _unused in tiles_of(channels):
                gbranch[row, r, :, t * LANES : (t + 1) * LANES] = plain[
                    side, 1 + t, pl.ds(BASE + r, PAD, stride=FINE), :
                ].astype(BF16)


def in_place(mine, parts, place):
    value = parts[0]
    for i, part in enumerate(parts[1:], 1):
        value = jnp.where(mine ^ i == place, part, value)
    return value


def inner_kernel(channels, shares, paired, mask, *rest):
    shards, (conv, sums, taps, weights, accs, table) = rest[:shares], rest[shares:]
    share = channels // shares
    mine = lax.axis_index("fsdp")
    table[...] = jnp.zeros_like(table)
    parts = [shard[...].astype(F32) for shard in shards]
    for f in range(shares):
        table[f * share : (f + 1) * share] = in_place(mine, parts, f)[:share]
    blocks = paired.shape[0]
    for block in range(blocks):
        piece = table[block * HALF : (block + 1) * HALF]
        taps[block] = jnp.concatenate([piece, piece], axis=0).T[: taps.shape[1]]
        build_weights(weights.at[block], taps, block, False)
    runs = inner_runs(mask.shape[0] // 2)[0]
    for t, _ in tiles_of(channels):
        lanes = pl.ds(t * LANES, LANES)
        planes = products(paired, None, weights, accs, t, runs)
        row, total, count = 2 * runs[0][0], 0.0, 0.0
        for k in range(FINE // 2):
            for odd, value in enumerate(planes(0, k, 0)):
                total = total + mask[row, 2 * k + odd] * value
                count = count + mask[row, 2 * k + odd]
        near = jnp.sum(total, axis=0, keepdims=True) / jnp.maximum(jnp.sum(count, axis=0, keepdims=True), 1.0)
        total, square = settle(planes, conv, mask, runs, lanes, near)
        sums[0:1, lanes] = near
        sums[1:2, lanes] = total
        sums[2:3, lanes] = square


def outer_kernel(channels, paired, near, far, mask, weights, sums, conv, stats, rims, accs, stage):
    height = mask.shape[0]
    blocks, pairs = paired.shape[0], height // 2
    width = near.shape[1]
    stage[...] = jnp.zeros_like(stage)
    last = pairs + PASSES - 1
    first_half = (SPAN % 2) * LANES
    last_half = ((SPAN + height - 1) % 2) * LANES
    rims[:, 1, :, :, first_half : first_half + LANES] = paired[:, 1, :, :, first_half : first_half + LANES]
    rims[:, 2, :, :, last_half : last_half + LANES] = paired[:, last - 2, :, :, last_half : last_half + LANES]
    for below, index, pair, side in rim_rows(height):

        def source(a, b, below=below, index=index):
            place, turn = border_place(index, a // LANES, channels, SPAN)
            value = by_partner(near[place].astype(F32), far[place].astype(F32))[below]
            return (swap(value) if turn else value)[:, : b - a]

        place_natural(rims, stage, source, channels, width, blocks, pair, side)
    runs = inner_runs(pairs)[1]
    count = 0.0
    for row in range(height):
        for r in range(FINE):
            count = count + mask[row, r]
    count = jnp.sum(count, axis=0, keepdims=True)
    for t, _ in tiles_of(channels):
        lanes = pl.ds(t * LANES, LANES)
        planes = products(paired, rims, weights, accs, t, runs)
        near = sums[0:1, lanes]
        total, square = settle(planes, conv, mask, runs, lanes, near)
        total, square = total + sums[1:2, lanes], square + sums[2:3, lanes]
        shift = total / jnp.maximum(count, 1.0)
        stats[0:1, lanes] = near + shift
        stats[1:2, lanes] = jnp.maximum(square - total * shift, 0.0)
        stats[2:3, lanes] = count
        stats[3:8, lanes] = jnp.zeros((5, LANES), F32)


def products(paired, rims, weights, accs, tile, runs):
    has_upper = 2 * tile + 1 < paired.shape[0]
    for half in range(1 + has_upper):
        block = 2 * tile + half
        accs[half] = convolve_block(paired, rims, weights.at[block], block, runs)

    def planes(place, k, side):
        start = (place * (FINE // 2) + k) * PAD
        return split_blocks(accs.at[0], accs.at[1] if has_upper else None, start, side)

    return planes


def settle(planes, conv, mask, runs, lanes, near):
    sums = [jnp.zeros((PAD, LANES), F32)] * 8
    for place, h in enumerate(pairs_of(runs)):
        for k in range(FINE // 2):
            for side in range(2):
                for odd, value in enumerate(planes(place, k, side)):
                    conv[2 * place + side, 2 * k + odd, :, lanes] = value
                    away = value - near
                    part = mask[2 * h + side, 2 * k + odd] * away
                    at = 2 * (2 * side + odd)
                    sums[at] = sums[at] + part
                    sums[at + 1] = sums[at + 1] + part * away
    return (jnp.sum(sums[i] + sums[i + 2] + sums[i + 4] + sums[i + 6], axis=0, keepdims=True) for i in range(2))


def pointwise_kernel(
    channels, real_units, inner, outer, gbranch, feats, turned, vec, w_in, w_out,
    output, act_out, ghid_out, gz_out, z_out, sums, stage, conv,
):
    rows, width = feats.shape[0], feats.shape[1]
    padded = conv.shape[-1]
    cells = rows * FINE * PAD
    hidden_units = act_out.shape[1]
    step = pl.program_id(0)

    @pl.when(step == 0)
    def _():
        sums[...] = jnp.zeros_like(sums)

    one_lane = lax.broadcasted_iota(jnp.int32, (1, padded), 1) == channels
    mean, inverse, gain, shift = (vec[i : i + 1, :] for i in range(4))
    side = RIM_PAIRS // 2
    is_inner = jnp.logical_and(step >= side, step < pl.num_programs(0) - side)

    @pl.when(is_inner)
    def _():
        conv[...] = inner[pl.ds((step - side) * rows, rows)]

    @pl.when(jnp.logical_not(is_inner))
    def _():
        place = jnp.where(step < side, step, step + 2 * side - pl.num_programs(0))
        conv[...] = outer[pl.ds(place * rows, rows)]

    here = pl.ds(pl.multiple_of(step * cells, cells), cells)
    normed = (conv[...].reshape(cells, padded) - mean) * inverse
    zvals = jnp.where(one_lane, 1.0, gain * normed + shift).astype(BF16)
    z_out[here, :] = zvals
    mine = pl.ds(step * rows, rows)
    upstream = gbranch[mine].reshape(cells, padded)
    chunk = 2 * LANES
    across = (((1,), (1,)), ((), ()))
    c0 = 0.7978845608028654
    c1 = 0.044715 * c0
    for start in range(0, hidden_units, chunk):
        span = pl.ds(start, chunk)
        hidden = jnp.dot(zvals, w_in[:, span], preferred_element_type=F32)
        gact = lax.dot_general(upstream, w_out[span, :], across, preferred_element_type=F32)
        square = hidden * hidden
        share = 0.5 + 0.5 * jnp.tanh(hidden * (c0 + c1 * square))
        act = hidden * share
        slope = share + (act - act * share) * (2.0 * c0 + (6.0 * c1) * square)
        ghid = (gact * slope).astype(BF16)
        act = act.astype(BF16)
        if start + chunk > real_units:
            lane = lax.broadcasted_iota(jnp.int32, (1, chunk), 1)
            act = jnp.where(lane == real_units - start, jnp.ones((), BF16), act)
        act_out[here, span] = act
        ghid_out[here, span] = ghid
    branch = jnp.dot(act_out[here, :], w_out[...], preferred_element_type=F32)
    gz = lax.dot_general(ghid_out[here, :], w_in[...], across, preferred_element_type=F32)
    gz_out[mine] = gz.reshape(rows, *gz_out.shape[1:])
    sums[0:1, :] += jnp.sum(gz * normed, axis=0, keepdims=True)
    sums[1:2, :] += jnp.sum(gz, axis=0, keepdims=True)
    for row in range(rows):
        factor = mask_of_row(turned[...], step * rows + row)
        for t, lanes in tiles_of(channels):
            for r in range(FINE):
                start = (row * FINE + r) * PAD
                stage[row, t, pl.ds(r, PAD, stride=FINE), :] = branch[start : start + PAD, t * LANES : (t + 1) * LANES]
            piece = pl.ds(t * LANES, lanes)
            values = feats[row, :, piece].astype(F32) + stage[row, t, 0:width, :lanes]
            output[row, :, piece] = (values * factor[:, :lanes]).astype(BF16)


def out_grads_kernel(gbranch, act, grad):
    grad[...] = turned_product(gbranch, act, grad.shape[0])


def turned_product(left, right, rows):
    return lax.dot_general(left[:, :rows], right[...], (((0,), (0,)), ((), ())), preferred_element_type=F32)


def in_grads_kernel(channels, hidden, zvals, ghid, grad_out, kept, sent, grad_in):
    grad_in[...] = turned_product(zvals, ghid, grad_in.shape[0])
    shares = lax.axis_size("fsdp")
    layout = Packing(channels, hidden, shares)
    last = layout.in_tiles - 1
    lane = lax.broadcasted_iota(jnp.int32, (1, LANES), 1)
    spot = lax.broadcasted_iota(jnp.int32, (layout.out_pad, 1), 0)
    fill = jnp.zeros((layout.in_pad - layout.in_rows, LANES), F32)

    def write(out, j):
        rows = slice(j * layout.in_rows, (j + 1) * layout.in_rows)
        for t in range(layout.in_tiles):
            lanes = slice(t * LANES, (t + 1) * LANES)
            tile = grad_in[rows, lanes]
            if t == last:
                tile = jnp.where(lane == hidden - t * LANES, grad_out[rows, lanes], tile)
            tile = jnp.concatenate([tile, fill], axis=0)
            out[t * layout.in_pad : (t + 1) * layout.in_pad] = tile.astype(out.dtype)
        start = j * layout.out_rows
        aligned = start // LANES * LANES
        stop = min(aligned + (layout.out_tiles + 1) * LANES, grad_out.shape[1])
        part = jnp.where(
            spot == channels, grad_in[: layout.out_pad, aligned:stop], grad_out[: layout.out_pad, aligned:stop]
        )
        if start != aligned:
            part = pltpu.roll(part, stop - start, 1)
        for u in range(layout.out_tiles):
            base = layout.out_base + u * layout.out_pad
            out[base : base + layout.out_pad] = part[:, u * LANES : (u + 1) * LANES].astype(out.dtype)
        out[layout.small_base :] = jnp.zeros((layout.rows - layout.small_base, LANES), out.dtype)

    for mine in range(shares):

        @pl.when(lax.axis_index("fsdp") == mine)
        def _(mine=mine):
            for i in range(shares):
                rows = pl.ds(i // 2 * layout.rows, layout.rows)
                write((sent if i % 2 else kept).at[rows], mine ^ i)


def near_sum_kernel(kept, arrived, own, sent):
    rows = own.shape[0]
    own[...] = kept[:rows] + arrived[:rows].astype(F32)
    sent[...] = (kept[rows:] + arrived[rows:].astype(F32)).astype(BF16)


def finish_kernel(channels, hidden, slopes, *refs):
    parts, refs = refs[:-8], refs[-8:]
    grad_in, grad_in_bias, grad_out, grad_out_bias, grad_taps, grad_gain, grad_shift, packed = refs
    place = piece_of(lax.axis_index("dp"))
    rows = packed.shape[0] // len(parts)
    values = [part[:rows] for part in parts]
    for i in range(len(parts)):
        packed[i * rows : (i + 1) * rows] = in_place(place, values, i)
    low = (parts[0].shape[0] - rows) // 2
    exact = [part[rows : rows + low].astype(F32) + part[rows + low :].astype(F32) for part in parts]
    share = grad_in.shape[0]
    grad_taps[...] = tree(exact, lambda a, b: a + b)[: grad_taps.shape[0], :share]
    for mine in range(channels // share):

        @pl.when(lax.axis_index("fsdp") == mine)
        def _(start=mine * share):
            turned = pltpu.roll(slopes[...], slopes.shape[1] - start, 1) if start else slopes[...]
            grad_gain[...] = turned[5, :share]
            grad_shift[...] = turned[6, :share]

    layout = Packing(channels, hidden, channels // grad_in.shape[0])
    for t in range(layout.in_tiles):
        stop = min((t + 1) * LANES, hidden)
        tile = packed[t * layout.in_pad : (t + 1) * layout.in_pad].astype(F32)
        grad_in[:, t * LANES : stop] = tile[: layout.in_rows, : stop - t * LANES]
    tall = jnp.concatenate([tile, jnp.zeros((LANES - layout.in_pad, LANES), F32)], axis=0).T
    at = hidden - (layout.in_tiles - 1) * LANES
    grad_out_bias[...] = tall[at, : layout.in_rows]
    bias = []
    for u in range(layout.out_tiles):
        base = layout.out_base + u * layout.out_pad
        tile = packed[base : base + layout.out_pad].astype(F32)
        stop = min((u + 1) * LANES, layout.out_rows)
        count = stop - u * LANES
        bias.append(tile[channels : channels + 1, :])
        fill = jnp.zeros((round_up(layout.out_pad, LANES) - layout.out_pad, LANES), F32)
        grad_out[u * LANES : stop, :] = jnp.concatenate([tile, fill], axis=0).T[:count, :channels]
    grad_in_bias[...] = jnp.concatenate(bias, axis=1)[0, : layout.out_rows]


def share_taps_kernel(share, *refs):
    shares = lax.axis_size("fsdp")
    tiles, outs = refs[:-shares], refs[-shares:]
    wide = jnp.concatenate([tile[...] for tile in tiles], axis=1)
    for mine in range(shares):

        @pl.when(lax.axis_index("fsdp") == mine)
        def _(mine=mine):
            for i, out in enumerate(outs):
                start = (mine ^ i) * share
                turned = pltpu.roll(wide, wide.shape[1] - start, 1) if start else wide
                out[...] = turned[:, :LANES]


def tree(values, merge):
    while len(values) > 1:
        values = [merge(values[i], values[i + 1]) for i in range(0, len(values), 2)]
    return values[0]


def merge_stats(mine, other):
    count = mine[2:3] + other[2:3]
    safe = jnp.maximum(count, 1.0)
    mean = (mine[0:1] * mine[2:3] + other[0:1] * other[2:3]) / safe
    away = mine[0:1] - other[0:1]
    spread = mine[1:2] + other[1:2] + away * away * (mine[2:3] * other[2:3] / safe)
    return jnp.concatenate([mean, spread, count, jnp.zeros_like(mine[3:8])], axis=0)


def stats_kernel(*refs):
    refs[-1][...] = tree([ref[...] for ref in refs[:-1]], merge_stats)


def norm_kernel(vectors, *refs):
    stats = tree([ref[...] for ref in refs[:-1]], merge_stats)
    count = jnp.maximum(stats[2:3], 1.0)
    inverse = lax.rsqrt(stats[1:2] / count + EPSILON)
    refs[-1][...] = jnp.concatenate(
        [stats[0:1], inverse, vectors[0:2, :], count, jnp.zeros((3, stats.shape[1]), F32)], axis=0
    )


def sums_kernel(*refs):
    refs[-1][...] = tree([ref[...] for ref in refs[:-1]], lambda a, b: a + b)


def slopes_kernel(vec, *refs):
    sums = tree([ref[...] for ref in refs[:-1]], lambda a, b: a + b)
    scaled = vec[1:2, :] * vec[2:3, :]
    count = vec[4:5, :]
    refs[-1][...] = jnp.concatenate(
        [vec[0:2, :], scaled, scaled * sums[1:2] / count, scaled * sums[0:1] / count, sums[0:2], sums[2:3]], axis=0
    )


class Packing:
    def __init__(self, channels, hidden, shares):
        self.in_rows = channels // shares
        self.in_pad = round_up(self.in_rows, 16)
        self.in_tiles = -(-(hidden + 1) // LANES)
        self.out_rows = hidden // shares
        self.out_tiles = -(-self.out_rows // LANES)
        self.out_pad = round_up(max(channels + 1, self.out_rows), 16)
        self.out_base = self.in_pad * self.in_tiles
        self.small_base = self.out_base + self.out_pad * self.out_tiles
        self.small = self.out_tiles + 3
        self.rows = round_up(self.small_base + self.small, 32)


def pack_parameters(layout, in_proj, in_bias, out_proj, gain, shift, out_bias, packed, wide, tall):
    wide[...] = jnp.zeros_like(wide)
    tall[...] = jnp.zeros_like(tall)
    wide[: layout.in_rows, : in_proj.shape[1]] = in_proj[...].astype(F32)
    for t in range(layout.in_tiles):
        packed[t * layout.in_pad : (t + 1) * layout.in_pad] = wide[: layout.in_pad, t * LANES : (t + 1) * LANES].astype(BF16)
    tall[: layout.out_rows, : out_proj.shape[1]] = out_proj[...].astype(F32)
    for u in range(layout.out_tiles):
        base = layout.out_base + u * layout.out_pad
        packed[base : base + layout.out_pad] = tall[:, u * LANES : (u + 1) * LANES].astype(BF16)
    wide[...] = jnp.zeros_like(wide)
    for i, small in enumerate((in_bias, gain, shift, out_bias)):
        wide[i : i + 1, : small.shape[0]] = small[...].reshape(1, -1).astype(F32)
    rows = [wide[0:1, u * LANES : (u + 1) * LANES] for u in range(layout.out_tiles)]
    rows += [wide[i + 1 : i + 2, :LANES] for i in range(3)]
    rows.append(jnp.zeros((layout.rows - layout.small_base - layout.small, LANES), F32))
    packed[layout.small_base :] = jnp.concatenate(rows, axis=0).astype(BF16)


def assemble_kernel(layout, shares, *refs):
    packed, (w_in, w_out, vectors, wide, tall) = refs[:shares], refs[shares:]
    mine = lax.axis_index("fsdp")

    def rows_of(f, start, stop):
        return in_place(mine, [part[start:stop].astype(F32) for part in packed], f)

    wide[...] = jnp.zeros_like(wide)
    tall[...] = jnp.zeros_like(tall)
    channels, hidden = layout.in_rows * shares, layout.out_rows * shares
    in_bias = jnp.zeros((8, wide.shape[1]), F32)
    smalls = [jnp.zeros((8, tall.shape[1]), F32)] * 3
    for f in range(shares):
        for t in range(layout.in_tiles):
            tile = rows_of(f, t * layout.in_pad, (t + 1) * layout.in_pad)
            wide[f * layout.in_rows : (f + 1) * layout.in_rows, t * LANES : (t + 1) * LANES] = tile[: layout.in_rows]
        for u in range(layout.out_tiles):
            base = layout.out_base + u * layout.out_pad
            tile = rows_of(f, base, base + layout.out_pad)
            tall[f * layout.out_rows : (f + 1) * layout.out_rows, u * LANES : (u + 1) * LANES] = tile[: layout.out_rows]
        small = rows_of(f, layout.small_base, layout.rows)

        def spread(first, count, lanes, turn):
            pieces = [small[first + u : first + u + 1] for u in range(count)]
            pieces.append(jnp.zeros((1, lanes - count * LANES), F32))
            row = jnp.broadcast_to(jnp.concatenate(pieces, axis=1), (8, lanes))
            return pltpu.roll(row, turn, 1) if turn else row

        in_bias = in_bias + spread(0, layout.out_tiles, wide.shape[1], f * layout.out_rows)
        smalls = [
            total + spread(layout.out_tiles + i, 1, tall.shape[1], f * layout.in_rows)
            for i, total in enumerate(smalls)
        ]
    wide[channels : channels + 1] = in_bias[:1]
    tall[hidden : hidden + 1] = smalls[2][:1]
    w_in[...] = wide[...].astype(BF16)
    w_out[...] = tall[...].astype(BF16)
    vectors[...] = jnp.concatenate([smalls[0][:1], smalls[1][:1], jnp.zeros((6, tall.shape[1]), F32)], axis=0)


def shifted_planes(values, real):
    out = []
    for r in range(-SPAN, FINE + SPAN):
        value = values[r % FINE]
        if r < 0:
            value = jnp.concatenate([value[real - 1 : real], value[: PAD - 1]], axis=0)
        elif r >= FINE:
            value = jnp.concatenate([value[1:real], value[:1], value[: PAD - real]], axis=0)
        out.append(value)
    return out


def join_planes(first, second):
    low = low_half(PAD)
    return (
        jnp.where(low, first, swap(second)).astype(BF16),
        jnp.where(low, swap(first), second).astype(BF16),
    )


def place_planes(paired, planes, tile, blocks, pair, side):
    out_lanes = pl.ds(side * LANES, LANES)
    for k in range(len(planes) // 2):
        for half, value in enumerate(join_planes(planes[2 * k], planes[2 * k + 1])):
            if 2 * tile + half < blocks:
                paired[2 * tile + half, pair, k, :, out_lanes] = value


def arrange_kernel(
    channels, real, gz, inner, outer, mask, vec, near, far, gpaired, own, edges,
):
    height = gz.shape[0]
    blocks = own.shape[0]
    for t, _ in tiles_of(channels):
        lanes = pl.ds(t * LANES, LANES)
        mean, inverse, scaled, bias, slope = (vec[i : i + 1, lanes] for i in range(5))
        for row in range(height):
            h, side = row // 2, row % 2
            values = []
            for r in range(FINE):
                normed = (conv_at(inner, outer, row, r, lanes) - mean) * inverse
                values.append(scaled * gz[row, r, :, lanes] - mask[row, r] * (bias + normed * slope))
            out_lanes = pl.ds(side * LANES, LANES)
            for k in range(FINE // 2):
                rows = pl.ds((h * (FINE // 2) + k) * PAD, PAD)
                for half, value in enumerate(join_planes(values[2 * k], values[2 * k + 1])):
                    if 2 * t + half < blocks:
                        own[2 * t + half, rows, out_lanes] = value
            place_planes(gpaired, shifted_planes(values, real), t, blocks, (SPAN + row) // 2, (SPAN + row) % 2)
            for edge, border in ((0, row < SPAN), (1, row >= height - SPAN)):
                if border:
                    place = row - (height - SPAN) * edge
                    for r in range(FINE):
                        edges[edge, place, r, :, lanes] = values[r].astype(BF16)
    near[...], far[...] = by_partner(edges[0], edges[1])


def conv_at(inner, outer, row, r, lanes):
    start = RIM_PAIRS
    stop = start + inner.shape[0]
    if start <= row < stop:
        return inner[row - start, r, :, lanes]
    return outer[row if row < start else row - stop + start, r, :, lanes]


def taps_kernel(tile, own, paired, rims, select, grad_taps):
    blocks, pairs = own.shape[0], paired.shape[1] - PASSES + 1
    lane = lax.broadcasted_iota(jnp.int32, (HALF, 2 * LANES), 1)
    sub = lax.broadcasted_iota(jnp.int32, (HALF, 2 * LANES), 0)
    diagonal = lax.rem(lane, HALF) == sub
    low = low_half(grad_taps.shape[0])
    totals = []
    for block in range(2 * tile, min(2 * tile + 2, blocks)):
        turned = own[block].T
        found = []
        for m in range(PASSES):
            for s in range(PASSES):
                product = jnp.dot(turned, pass_rows(paired, rims, block, m, s, [(0, pairs)]), preferred_element_type=F32)
                for q in range(4):
                    part = product[q * HALF : (q + 1) * HALF]
                    found.append(jnp.sum(jnp.where(diagonal, part, 0.0), axis=0, keepdims=True))
        found = jnp.concatenate(found, axis=0)
        total = None
        for place in range(4):
            group = jnp.dot(select[place], found, preferred_element_type=F32, precision=lax.Precision.HIGHEST)
            group = group[:, (place // 2) * LANES : (place // 2 + 1) * LANES]
            if place % 2:
                group = swap(group)
            total = group if total is None else total + group
        totals.append(total)
    second = swap(totals[1]) if len(totals) > 1 else jnp.zeros_like(totals[0])
    grad_taps[...] = jnp.where(low, totals[0], second)


def flip_kernel(taps, weights):
    for block in range(weights.shape[0]):
        build_weights(weights.at[block], taps, block, True)


def backward_kernel(tile, real, gpaired, near, far, weights, cot, turned, *rest):
    result, rims, accs, stage = rest[-4:]
    height, width = cot.shape[:2]
    blocks, pairs = gpaired.shape[0], height // 2
    last = pairs + PASSES - 1
    first_half = (SPAN % 2) * LANES
    last_half = ((SPAN + height - 1) % 2) * LANES
    has_upper = 2 * tile + 1 < blocks
    for half in range(1 + has_upper):
        source = gpaired.at[2 * tile + half]
        rims[half, 1, :, :, first_half : first_half + LANES] = source[1, :, :, first_half : first_half + LANES]
        rims[half, 2, :, :, last_half : last_half + LANES] = source[last - 2, :, :, last_half : last_half + LANES]
    for below, index, pair, side in rim_rows(height):
        piece = pl.ds(tile * LANES, LANES)
        values = [
            by_partner(near[index, r, :, piece].astype(F32), far[index, r, :, piece].astype(F32))[below]
            for r in range(FINE)
        ]
        place_planes(rims, shifted_planes(values, real), 0, 1 + has_upper, pair, side)
    for half in range(1 + has_upper):
        block = 2 * tile + half
        accs[half] = convolve_block(
            gpaired.at[block : block + 1], rims.at[half : half + 1], weights.at[block], 0, [(0, pairs)]
        )

    def spread(h, _):
        for side in range(2):
            row = 2 * h + side
            for k in range(FINE // 2):
                even, odd = split_blocks(
                    accs.at[0], accs.at[1] if has_upper else None, (h * (FINE // 2) + k) * PAD, side
                )
                stage[side, pl.ds(2 * k, PAD, stride=FINE), :] = even
                stage[side, pl.ds(2 * k + 1, PAD, stride=FINE), :] = odd
            values = cot[row].astype(F32) + stage[side, 0:width]
            result[row] = (values * mask_of_row(turned[...], row)).astype(BF16)
        return 0

    for h in range(pairs):
        spread(h, 0)


def bits(size):
    bit = 1
    while bit < size:
        yield bit
        bit *= 2


def swapped(value, axis, flip):
    size = lax.axis_size(axis)
    return lax.ppermute(value, axis, [(i, i ^ flip) for i in range(size)])


def phases(*axes):
    out = []
    for axis in axes:
        left = list(bits(lax.axis_size(axis)))
        while left:
            near, left = left[:2], left[2:]
            out.append((axis, near if len(near) < 2 else [near[0], near[1], near[0] | near[1]]))
    return out


def tied(*values):
    return lax.optimization_barrier(values)


def halves_kernel(bit, *refs):
    parts, (keep, send) = refs[:-2], refs[-2:]
    rows = keep.shape[0]
    halves = [sum((part[a : a + rows].astype(F32) for part in parts[1:]), parts[0][a : a + rows]) for a in (0, rows)]
    first = lax.axis_index("dp") // bit % 2 == 0
    keep[...] = jnp.where(first, halves[0], halves[1])
    send[...] = jnp.where(first, halves[1], halves[0]).astype(send.dtype)


def whole_kernel(count, *refs):
    parts, extra, out = refs[:count], refs[count:-1], refs[-1]
    rows = parts[0].shape[0]
    out[:rows] = sum((part[...].astype(F32) for part in parts[1:]), parts[0][...])
    if extra:
        out[rows:] = sum((part[...] for part in extra[1:]), extra[0][...])


def last_kernel(rows, mine, other, out):
    total = mine[...] + other[...]
    rest = total.shape[0] - rows
    high = total[rows:].astype(BF16)
    out[:rows] = total[:rows].astype(BF16)
    out[rows : rows + rest] = high
    out[rows + rest :] = (total[rows:] - high.astype(F32)).astype(BF16)


def beside(work, *values):
    done = work() if work else ()
    return lax.optimization_barrier((done, values))


def far_bits():
    return list(bits(lax.axis_size("dp")))[1:3]


def piece_of(place):
    piece = 0
    for bit in far_bits():
        piece = 2 * piece + place // bit % 2
    return piece


class Spreading:
    def __init__(self, *parts):
        self.parts, self.extra = parts, ()
        cuts = far_bits()
        self.moves = [("half", [bit]) for bit in cuts]
        self.moves += [("whole", [bit]) for bit in bits(lax.axis_size("dp")) if bit not in cuts]
        flips = [0]
        for bit in reversed(cuts):
            flips += [flip | bit for flip in flips]
        self.moves.append(("gather", flips[1:]))

    def start(self):
        kind, flips = self.moves.pop(0)
        rows, lanes = self.parts[0].shape
        operands = (*self.parts, *self.extra)
        run = lambda kernel, *outs: call(
            kernel, outs, operands, [WHOLE] * len(operands), limit=10, name="sum_weights"
        )
        if kind == "half":
            kept, sent = run(
                functools.partial(halves_kernel, flips[0]),
                anywhere((rows // 2, lanes), F32),
                anywhere((rows // 2, lanes), BF16),
            )
        elif kind == "whole":
            low = self.extra[0].shape[0] if self.extra else 0
            if self.extra:
                self.rows = rows
            (kept,) = (sent,) = run(
                functools.partial(whole_kernel, len(self.parts)), anywhere((rows + low, lanes), F32)
            )
            self.extra = ()
        else:
            (kept,) = (sent,) = run(
                functools.partial(last_kernel, self.rows), anywhere((2 * rows - self.rows, lanes), BF16)
            )
        self.parts = (kept,)
        return [swapped(sent, "dp", flip) for flip in flips]

    def finish(self, others):
        self.parts = (*self.parts, *others)


def border_exchange(near, far):
    size = lax.axis_size("dp")
    first = [(i, i ^ 1) for i in range(size)]
    second = [(i, i + 1) for i in range(1, size - 1, 2) if (i + 1) % TILES]
    second += [(j, i) for i, j in second]
    return lax.ppermute(near, "dp", first), lax.ppermute(far, "dp", second)


def tap_selectors(rows):
    out = np.zeros((4, rows, PASSES * PASSES * 4), np.float32)
    for m in range(PASSES):
        for s in range(PASSES):
            for q in range(4):
                for p in range(4):
                    a = 2 * m + p // 2 - q // 2
                    b = 2 * s + p % 2 - q % 2
                    if 0 <= a < KW and 0 <= b < KW:
                        out[p, a * KW + b, (m * PASSES + s) * 4 + q] = 1.0
    return out


def local(features, land_mask, cotangent, kernel, norm_gain, norm_shift, in_proj, in_bias, out_proj, out_bias):
    feats, cot = features[0, 0], cotangent[0, 0]
    height, width, channels = feats.shape
    hidden = in_proj.shape[1]
    shares = lax.axis_size("fsdp")
    padded = round_up(channels + 1, LANES)
    hidden_pad = round_up(hidden + 1, 2 * LANES)
    blocks = -(-channels // HALF)
    pairs = height // 2
    planes_in = (FINE + 2 * SPAN) // 2
    row_pairs = pairs + PASSES - 1
    cells = height * FINE * PAD
    block_rows = pairs * (FINE // 2) * PAD
    stage_rows = round_up(BASE + SPAN + FINE * PAD, 8)
    tile_count = len(tiles_of(channels))
    tap_rows = round_up(TAPS, 16)
    real = width // FINE
    layout = Packing(channels, hidden, shares)

    edge = lambda at: pl.BlockSpec((SPAN, width, channels), lambda i: (at, 0, 0))
    whole = lambda array: pl.BlockSpec(array.shape, lambda i: (0,) * array.ndim)
    natural_shape = (height, width, channels)
    edge_shape = (1 + max(border_place(SPAN - 1, t, channels, SPAN)[0] for t in range(tile_count)), width, LANES)
    paired_shape = (blocks, row_pairs, planes_in, PAD, 4 * HALF)
    rims_shape = (blocks, RIM_PAIRS, planes_in, PAD, 4 * HALF)
    plane_shape = (height, FINE, PAD, padded)
    mask_shape = (height, FINE, PAD, LANES)
    small = (kernel.T, in_proj, in_bias, out_proj, norm_gain, norm_shift, out_bias)
    near, far, turned, shard, packed = call(
        functools.partial(begin_kernel, layout),
        [
            anywhere(edge_shape, BF16),
            anywhere(edge_shape, BF16),
            anywhere((width, height), BF16),
            anywhere((layout.in_pad, LANES), BF16),
            anywhere((layout.rows, LANES), BF16),
        ],
        (slow(feats), slow(feats), slow(land_mask), *(slow(v) for v in small)),
        [edge(0), edge(height // SPAN - 1), whole(land_mask)] + [whole(v) for v in small],
        [
            pltpu.VMEM((round_up(height, LANES), round_up(width, LANES)), F32),
            pltpu.VMEM((round_up(layout.in_pad, LANES), hidden_pad), F32),
            pltpu.VMEM((layout.out_pad, padded), F32),
            pltpu.VMEM((2, *edge_shape), F32),
            pltpu.VMEM((2, width, LANES), F32),
        ],
        grid=(1,),
        out_specs=[WHOLE] * 5,
        name="begin",
    )
    others = list(range(1, shares))
    six = 6 if height % 6 == 0 else 2
    stage = pltpu.VMEM((2, tile_count, 2, stage_rows, LANES), F32)
    near, far = border_exchange(near, far)
    shards = [swapped(shard, "fsdp", i) for i in others]
    (paired, gbranch, mask), (packed, shards) = beside(
        lambda: call(
            prepare_kernel,
            [pltpu.VMEM(paired_shape, BF16), pltpu.VMEM(plane_shape, BF16), pltpu.VMEM(mask_shape, F32)],
            (slow(feats), slow(cot), turned),
            [pl.BlockSpec((six, width, channels), lambda i: (i, 0, 0))] * 2 + [WHOLE],
            [stage, pltpu.VMEM((2, 1 + tile_count, stage_rows, LANES), F32)],
            grid=(height // six,),
            name="prepare",
        ),
        packed,
        [shard, *shards],
    )
    cuts = list(bits(shares))
    direct = [swapped(packed, "fsdp", bit) for bit in cuts]
    inner, outer = inner_runs(pairs)
    run_rows = lambda runs: 2 * len(pairs_of(runs))
    run_accs = lambda runs: pltpu.VMEM((2, run_rows(runs) * (FINE // 2) * PAD // 2, 4 * HALF), F32)
    weights_shape = (PASSES * PASSES * 4 * HALF, 4 * HALF)
    (conv_inner, sums, taps, weights), (near, far) = beside(
        lambda: call(
            functools.partial(inner_kernel, channels, shares),
            [
                pltpu.VMEM((run_rows(inner), FINE, PAD, padded), F32),
                anywhere((8, padded), F32),
                anywhere((blocks, tap_rows, LANES), F32),
                pltpu.VMEM((blocks, *weights_shape), BF16),
            ],
            (fast(paired), fast(mask), *shards),
            [WHOLE] * (2 + shares),
            [run_accs(inner), pltpu.VMEM((blocks * HALF, LANES), F32)],
            limit=10,
            name="inner",
        ),
        near,
        far,
    )
    (conv_outer, stats, rims), (packed, direct) = beside(
        lambda: call(
            functools.partial(outer_kernel, channels),
            [
                pltpu.VMEM((run_rows(outer), FINE, PAD, padded), F32),
                anywhere((8, padded), F32),
                pltpu.VMEM(rims_shape, BF16),
            ],
            (fast(paired), near, far, fast(mask), fast(weights), sums),
            [WHOLE] * 6,
            [run_accs(outer), stage],
            flops=4 * 10**9,
            limit=10,
            name="outer",
        ),
        packed,
        direct,
    )
    packed = {0: packed, **dict(zip(cuts, direct))}
    for flip in others:
        if flip not in packed:
            packed[flip] = swapped(packed[flip & (flip - 1)], "fsdp", flip & -flip)
    packed = [packed[flip] for flip in range(shares)]
    assemble = lambda: call(
        functools.partial(assemble_kernel, layout, shares),
        [
            anywhere((padded, hidden_pad), BF16),
            anywhere((hidden_pad, padded), BF16),
            anywhere((8, padded), F32),
        ],
        packed,
        [WHOLE] * shares,
        [pltpu.VMEM((padded, hidden_pad), F32), pltpu.VMEM((hidden_pad, padded), F32)],
        name="assemble",
    )
    row_sums = anywhere((8, padded), F32)
    combine = lambda kernel, *values: call(kernel, [row_sums], values, [WHOLE] * len(values), limit=4, name="combine")[0]
    rounds = phases("fsdp", "dp")
    for n, (axis, flips) in enumerate(rounds):
        last = n + 1 == len(rounds)
        values = [stats, *(swapped(stats, axis, i) for i in flips)]
        if n + 2 == len(rounds):
            values += packed
        done, values = beside(assemble if last else None, *values)
        if n + 2 == len(rounds):
            packed, values = values[-shares:], values[:-shares]
        if last:
            w_in, w_out, vectors = done
        if n + 1 < len(rounds):
            stats = combine(stats_kernel, *values)
    vec = combine(norm_kernel, vectors, *values)

    rows = 2
    steps = height // rows
    by_row = lambda *rest: pl.BlockSpec((rows, *rest), lambda i: (i,) + (0,) * len(rest))
    output, act, ghid, gz, zvals, sums = call(
        functools.partial(pointwise_kernel, channels, hidden),
        [
            anywhere(natural_shape, BF16),
            pltpu.VMEM((cells, hidden_pad), BF16),
            pltpu.VMEM((cells, hidden_pad), BF16),
            pltpu.VMEM(plane_shape, F32),
            pltpu.VMEM((cells, padded), BF16),
            row_sums,
        ],
        (fast(conv_inner), fast(conv_outer), fast(gbranch), slow(feats), turned, vec, w_in, w_out),
        [WHOLE] * 3 + [by_row(width, channels)] + [WHOLE] * 4,
        [
            pltpu.VMEM((rows, tile_count, round_up(FINE * PAD, 8), LANES), F32),
            pltpu.VMEM((rows, FINE, PAD, padded), F32),
        ],
        flops=14 * 10**9,
        grid=(steps,),
        out_specs=[by_row(width, channels)] + [WHOLE] * 5,
        limit=9,
        name="pointwise",
    )

    grad_rows = round_up(channels + 1, 16)

    def out_grads():
        return call(
            out_grads_kernel,
            [pltpu.VMEM((grad_rows, hidden_pad), F32)],
            (fast(gbranch.reshape(cells, padded)), fast(act)),
            [WHOLE] * 2,
            flops=3 * 10**9,
            limit=4,
            name="out_grads",
        )

    def in_grads():
        return call(
            functools.partial(in_grads_kernel, channels, hidden),
            [pltpu.VMEM((shares // 2 * layout.rows, LANES), dtype) for dtype in (F32, BF16)],
            (fast(zvals), fast(ghid), fast(grad_out)),
            [WHOLE] * 3,
            [pltpu.VMEM((grad_rows, hidden_pad), F32)],
            flops=3 * 10**9,
            limit=6,
            name="in_grads",
        )

    work = out_grads
    for n, (axis, flips) in enumerate(rounds):
        values = [sums, *(swapped(sums, axis, i) for i in flips)]
        if n == 2:
            values.append(sent)
        done, values = beside(work, *values)
        if n == 2:
            *values, sent = values
        work = None
        if n == 0:
            (grad_out,) = done
            work = in_grads
        if n + 1 == len(rounds):
            (flipped,) = done
        if n == 1:
            kept, sent = done
            sent = swapped(sent, "fsdp", 1)
        if n + 2 == len(rounds):
            work = lambda: call(
                flip_kernel,
                [pltpu.VMEM((blocks, *weights_shape), BF16)],
                (taps,),
                [WHOLE],
                limit=4,
                name="flip",
            )
        if n + 1 < len(rounds):
            sums = combine(sums_kernel, *values)
    gvec = combine(slopes_kernel, vec, *values)
    kept, sent = call(
        near_sum_kernel,
        [anywhere((layout.rows, LANES), F32), anywhere((layout.rows, LANES), BF16)],
        (kept, sent),
        [WHOLE] * 2,
        limit=10,
        name="near_sum",
    )
    sent = swapped(sent, "fsdp", 2)
    near, far, gpaired, own = call(
        functools.partial(arrange_kernel, channels, real),
        [
            anywhere((SPAN, FINE, PAD, padded), BF16),
            anywhere((SPAN, FINE, PAD, padded), BF16),
            pltpu.VMEM(paired_shape, BF16),
            pltpu.VMEM((blocks, block_rows, 4 * HALF), BF16),
        ],
        (fast(gz), fast(conv_inner), fast(conv_outer), fast(mask), gvec),
        [WHOLE] * 5,
        [pltpu.VMEM((2, SPAN, FINE, PAD, padded), BF16)],
        flops=10**8,
        moved=10 * MIB,
        limit=6,
        name="arrange",
    )
    select = jnp.asarray(tap_selectors(tap_rows))
    near, far = border_exchange(near, far)

    def taps_of(t):
        return lambda: call(
            functools.partial(taps_kernel, t),
            [anywhere((tap_rows, LANES), F32)],
            (fast(own), fast(paired), fast(rims), select),
            [WHOLE] * 4,
            flops=4 * 10**9,
            limit=6,
            name="taps",
        )

    (first,) = taps_of(0)()
    (second,), (sent,) = beside(taps_of(1), sent)
    spreading = Spreading(kept, sent)
    rest = lambda: [taps_of(t)()[0] for t in range(2, tile_count)]
    more, (there,) = beside(rest, spreading.start())
    spreading.finish(there)
    near, far, *tiles = tied(near, far, first, second, *more)
    own_taps, *sent_taps = call(
        functools.partial(share_taps_kernel, layout.in_rows),
        [anywhere((tap_rows, LANES), F32)] * shares,
        tiles,
        [WHOLE] * tile_count,
        limit=4,
        name="share_taps",
    )
    sent_taps = [swapped(v, "fsdp", i) for i, v in zip(others, sent_taps)]
    accs = pltpu.VMEM((2, block_rows, 4 * HALF), F32)

    def backward_of(t, *before):
        column = pl.BlockSpec((height, width, LANES), lambda i: (0, 0, t))
        return lambda: call(
            functools.partial(backward_kernel, t, real),
            [anywhere(natural_shape, BF16)],
            (fast(gpaired), near, far, fast(flipped), slow(cot), turned, *before),
            [WHOLE] * 4 + [column, WHOLE] + [HBM] * len(before),
            [
                pltpu.VMEM((2, RIM_PAIRS, planes_in, PAD, 4 * HALF), BF16),
                accs,
                pltpu.VMEM((2, round_up(FINE * PAD, 8), LANES), F32),
            ],
            flops=4 * 10**9,
            limit=12,
            grid=(1,),
            out_specs=[column],
            aliases={6: 0} if before else {},
            name="backward",
        )

    result = ()
    for n in range(max(tile_count, len(spreading.moves))):
        work = backward_of(tile_count - 1 - n, *result) if n < tile_count else None
        values = [spreading.start()] if spreading.moves else []
        if n == 0:
            values += sent_taps
        done, values = beside(work, *values)
        result = done or result
        if values:
            spreading.finish(values[0])
        if n == 0:
            spreading.extra = (own_taps, *values[1:])
    (result,) = result
    pieces = spreading.parts
    grad_in, grad_in_bias, grad_out, grad_out_bias, grad_taps, grad_gain, grad_shift = call(
        functools.partial(finish_kernel, channels, hidden),
        [
            anywhere((layout.in_rows, hidden), F32),
            anywhere((layout.out_rows,), F32),
            anywhere((layout.out_rows, channels), F32),
            anywhere((layout.in_rows,), F32),
            anywhere((TAPS, layout.in_rows), F32),
            anywhere((layout.in_rows,), F32),
            anywhere((layout.in_rows,), F32),
        ],
        (gvec, *pieces),
        [WHOLE] * (1 + len(pieces)),
        [pltpu.VMEM((layout.rows, LANES), BF16)],
        name="finish",
    )
    return (
        output[None, None],
        result[None, None],
        grad_taps.T,
        grad_gain,
        grad_shift,
        grad_in,
        grad_in_bias,
        grad_out,
        grad_out_bias,
    )


def solution(mesh):
    spread = P("dp", "fsdp", None, None, None)
    split = P("fsdp", None)
    line = P("fsdp")
    return jax.shard_map(
        local,
        mesh=mesh,
        in_specs=(spread, P(), spread, split, line, line, split, line, split, line),
        out_specs=(spread, spread, split, line, line, split, line, split, line),
        check_vma=False,
    )
```

```python
import functools

import jax
import jax.numpy as jnp
import numpy as np
from jax import lax
from jax.experimental import pallas as pl
from jax.experimental.pallas import tpu as pltpu
from jax.sharding import PartitionSpec as P

KW = 7
SPAN = KW // 2
TILES = 8
EPSILON = 1e-05

LANES = 128
HALF = 64
FINE = 12
PAD = 16
PASSES = (KW + 1) // 2
TAPS = KW * KW
RIM_PAIRS = 4
BASE = 8

F32 = jnp.float32
BF16 = jnp.bfloat16
MIB = 2**20
WHOLE = pl.BlockSpec(memory_space=pltpu.VMEM)
HBM = pl.BlockSpec(memory_space=pl.ANY)


def fast(value):
    return pltpu.with_memory_space_constraint(value, pltpu.VMEM)


def slow(value):
    return pltpu.with_memory_space_constraint(value, pltpu.HBM)


def anywhere(shape, dtype):
    return jax.ShapeDtypeStruct(shape, dtype)


def round_up(value, step):
    return -(-value // step) * step


def call(kernel, outs, operands, in_specs, scratch=(), flops=0, moved=0, grid=None, out_specs=None, limit=10, aliases=None, name=None):
    extra = {} if grid is None else {"grid": grid}
    return pl.pallas_call(
        kernel,
        out_shape=outs,
        in_specs=in_specs,
        out_specs=[WHOLE] * len(outs) if out_specs is None else out_specs,
        scratch_shapes=list(scratch),
        input_output_aliases=aliases or {},
        compiler_params=pltpu.CompilerParams(vmem_limit_bytes=limit * MIB),
        cost_estimate=pl.CostEstimate(flops=flops, bytes_accessed=moved, transcendentals=0),
        name=name,
        **extra,
    )(*operands)


def low_half(rows):
    return lax.broadcasted_iota(jnp.int32, (rows, LANES), 1) < HALF


def swap(value):
    return pltpu.roll(value, HALF, 1)


def tiles_of(channels):
    return [(t, min(LANES, channels - t * LANES)) for t in range(-(-channels // LANES))]


def mask_of_row(turned, row):
    chosen = lax.broadcasted_iota(jnp.int32, (turned.shape[1], LANES), 0) == row
    return jnp.dot(turned, jnp.where(chosen, 1.0, 0.0).astype(BF16), preferred_element_type=F32)


def stage_row(stage, values, width):
    lanes = values.shape[1]
    stage[0, BASE : BASE + width, :lanes] = values
    stage[0, BASE - SPAN : BASE, :lanes] = values[width - SPAN :]
    stage[0, BASE + width : BASE + width + SPAN, :lanes] = values[:SPAN]
    stage[1] = swap(stage[0])


def plane(stage, which, start):
    return stage[which, pl.ds(start, PAD, stride=FINE), :]


def place_row(paired, stage, tile, blocks, pair, side):
    low = low_half(PAD)
    lanes = pl.ds(side * LANES, LANES)
    for k in range((FINE + 2 * SPAN) // 2):
        start = BASE - SPAN + 2 * k
        paired[2 * tile, pair, k, :, lanes] = jnp.where(
            low, plane(stage, 0, start), plane(stage, 1, start + 1)
        ).astype(BF16)
        if 2 * tile + 1 < blocks:
            paired[2 * tile + 1, pair, k, :, lanes] = jnp.where(
                low, plane(stage, 1, start), plane(stage, 0, start + 1)
            ).astype(BF16)


def place_natural(paired, stage, source, channels, width, blocks, pair, side, factor=None):
    for t, lanes in tiles_of(channels):
        values = source(t * LANES, t * LANES + lanes).astype(F32)
        if factor is not None:
            values = values * factor[:, :lanes]
        buffer = stage.at[side, t]
        stage_row(buffer, values, width)
        place_row(paired, buffer, t, blocks, pair, side)


def rim_rows(height):
    inner = (height + 2 * SPAN) // 2 - RIM_PAIRS // 2
    for index in range(SPAN):
        yield 0, index, index // 2, index % 2
    for index in range(SPAN):
        row = SPAN + height + index
        yield 1, index, row // 2 - inner + RIM_PAIRS // 2, row % 2


def build_weights(weights, taps, block, flip):
    lane = lax.broadcasted_iota(jnp.int32, (HALF, LANES), 1)
    sub = lax.broadcasted_iota(jnp.int32, (HALF, LANES), 0)
    diagonal = lax.rem(lane, HALF) == sub
    low = low_half(1)
    zero = jnp.zeros((1, LANES), F32)

    def tap_row(a, b):
        if not (0 <= a < KW and 0 <= b < KW):
            return zero
        index = (KW - 1 - a) * KW + KW - 1 - b if flip else a * KW + b
        return taps[block, index : index + 1, :]

    for m in range(PASSES):
        for s in range(PASSES):
            for place in range(4):
                pr, pj = divmod(place, 2)
                for qr in range(2):
                    a, b = 2 * m + pr - qr, 2 * s + pj
                    row = jnp.where(low, tap_row(a, b), tap_row(a, b - 1))
                    weights[
                        (m * PASSES + s) * 4 * HALF + place * HALF : (m * PASSES + s) * 4 * HALF + (place + 1) * HALF,
                        qr * LANES : (qr + 1) * LANES,
                    ] = jnp.where(diagonal, row, 0.0).astype(BF16)


def pass_rows(paired, rims, block, m, s, runs):
    places = pl.ds(s, FINE // 2)
    side = RIM_PAIRS // 2
    inner = paired.shape[1] - side
    pieces = []
    for start, stop in runs:
        start, stop = start + m, stop + m
        pieces += [rims[block, i, places] for i in range(start, min(stop, side))]
        if max(start, side) < min(stop, inner):
            pieces.append(paired[block, max(start, side) : min(stop, inner), places])
        pieces += [rims[block, i - inner + side, places] for i in range(max(start, inner), stop)]
    return jnp.concatenate([piece.reshape(-1, 4 * HALF) for piece in pieces], axis=0)


def convolve_block(paired, rims, weights, block, runs):
    rows = jnp.concatenate(
        [pass_rows(paired, rims, block, m, s, runs) for m in range(PASSES) for s in range(PASSES)], axis=1
    )
    return jnp.dot(rows, weights[...], preferred_element_type=F32)


def inner_runs(pairs):
    side = RIM_PAIRS // 2
    return [(side, pairs - side)], [(0, side), (pairs - side, pairs)]


def pairs_of(runs):
    return [h for start, stop in runs for h in range(start, stop)]


def split_blocks(lower, upper, start, side):
    low = low_half(PAD)
    rows, lanes = pl.ds(start, PAD), pl.ds(side * LANES, LANES)
    first = lower[rows, lanes]
    if upper is None:
        return first, swap(first)
    second = upper[rows, lanes]
    return jnp.where(low, first, swap(second)), jnp.where(low, swap(first), second)


def begin_kernel(
    layout, first, last, land_mask, kernel, in_proj, in_bias, out_proj, gain, shift, out_bias,
    near, far, turned_out, shard, packed, table, wide, tall, edge, side,
):
    count, width, channels = first.shape
    height = turned_out.shape[1]
    tile_index = lax.axis_index("dp") % TILES
    spots = (height, land_mask.shape[0])
    wanted = lax.broadcasted_iota(jnp.int32, spots, 0) + tile_index * height
    chosen = jnp.where(lax.broadcasted_iota(jnp.int32, spots, 1) == wanted, 1.0, 0.0).astype(BF16)
    ocean = land_mask[...].astype(F32).astype(BF16)
    table[...] = jnp.zeros_like(table)
    table[:height, :width] = jnp.dot(chosen, ocean, preferred_element_type=F32)
    turned = table[...].T[:width].astype(BF16)
    turned_out[...] = turned[:, :height]
    edge[...] = jnp.zeros_like(edge)
    side[...] = jnp.zeros_like(side)
    for i in range(count):
        factors = mask_of_row(turned, i), mask_of_row(turned, height - count + i)
        for t, lanes in tiles_of(channels):
            piece = pl.ds(t * LANES, lanes)
            rows = [v[i, :, piece].astype(F32) * f[:, :lanes] for v, f in zip((first, last), factors)]
            place, turn = border_place(i, t, channels, count)
            for out, row in enumerate(by_partner(*rows)):
                if lanes == LANES:
                    edge[out, place] = row
                else:
                    side[out, :, :lanes] = row
                    value = swap(side[out]) if turn else side[out]
                    edge[out, place] = edge[out, place] + value
    near[...] = edge[0].astype(BF16)
    far[...] = edge[1].astype(BF16)
    wide[...] = jnp.zeros_like(wide)
    wide[: kernel.shape[0], : kernel.shape[1]] = kernel[...].astype(F32)
    shard[...] = wide[:LANES, :LANES].T[: shard.shape[0]].astype(BF16)
    pack_parameters(layout, in_proj, in_bias, out_proj, gain, shift, out_bias, packed, wide, tall)


def border_place(row, tile, channels, rows):
    whole, left = divmod(channels, LANES)
    if tile < whole:
        return row * whole + tile, False
    if left > HALF:
        return rows * whole + row, False
    return rows * whole + row // 2, row % 2 == 1


def by_partner(top, bottom):
    odd = lax.axis_index("dp") % 2 == 1
    return jnp.where(odd, top, bottom), jnp.where(odd, bottom, top)


def prepare_kernel(feats, cot, turned, paired, gbranch, mask, stage, plain):
    width, channels = feats.shape[1:]
    blocks = paired.shape[0]
    step = pl.program_id(0)

    @pl.when(step == 0)
    def _():
        stage[...] = jnp.zeros_like(stage)
        plain[...] = jnp.zeros_like(plain)

    for local_row in range(feats.shape[0]):
        side = local_row % 2
        row = feats.shape[0] * step + local_row
        factor = mask_of_row(turned[...], row)
        rows = pl.ds(BASE, width)
        plain[side, 0, rows, :] = factor
        for t, lanes in tiles_of(channels):
            piece = pl.ds(t * LANES, lanes)
            buffer = stage.at[side, t]
            stage_row(buffer, feats[local_row, :, piece].astype(F32) * factor[:, :lanes], width)
            place_row(paired, buffer, t, blocks, step * (feats.shape[0] // 2) + (SPAN + local_row) // 2, (SPAN + local_row) % 2)
            plain[side, 1 + t, rows, :lanes] = cot[local_row, :, piece].astype(F32) * factor[:, :lanes]
        for r in range(FINE):
            mask[row, r] = plain[side, 0, pl.ds(BASE + r, PAD, stride=FINE), :]
            for t, _unused in tiles_of(channels):
                gbranch[row, r, :, t * LANES : (t + 1) * LANES] = plain[
                    side, 1 + t, pl.ds(BASE + r, PAD, stride=FINE), :
                ].astype(BF16)


def in_place(mine, parts, place):
    value = parts[0]
    for i, part in enumerate(parts[1:], 1):
        value = jnp.where(mine ^ i == place, part, value)
    return value


def inner_kernel(channels, shares, paired, mask, *rest):
    shards, (conv, sums, taps, weights, accs, table) = rest[:shares], rest[shares:]
    share = channels // shares
    mine = lax.axis_index("fsdp")
    table[...] = jnp.zeros_like(table)
    parts = [shard[...].astype(F32) for shard in shards]
    for f in range(shares):
        table[f * share : (f + 1) * share] = in_place(mine, parts, f)[:share]
    blocks = paired.shape[0]
    for block in range(blocks):
        piece = table[block * HALF : (block + 1) * HALF]
        taps[block] = jnp.concatenate([piece, piece], axis=0).T[: taps.shape[1]]
        build_weights(weights.at[block], taps, block, False)
    runs = inner_runs(mask.shape[0] // 2)[0]
    for t, _ in tiles_of(channels):
        lanes = pl.ds(t * LANES, LANES)
        planes = products(paired, None, weights, accs, t, runs)
        row, total, count = 2 * runs[0][0], 0.0, 0.0
        for k in range(FINE // 2):
            for odd, value in enumerate(planes(0, k, 0)):
                total = total + mask[row, 2 * k + odd] * value
                count = count + mask[row, 2 * k + odd]
        near = jnp.sum(total, axis=0, keepdims=True) / jnp.maximum(jnp.sum(count, axis=0, keepdims=True), 1.0)
        total, square = settle(planes, conv, mask, runs, lanes, near)
        sums[0:1, lanes] = near
        sums[1:2, lanes] = total
        sums[2:3, lanes] = square


def outer_kernel(channels, paired, near, far, mask, weights, sums, conv, stats, rims, accs, stage):
    height = mask.shape[0]
    blocks, pairs = paired.shape[0], height // 2
    width = near.shape[1]
    stage[...] = jnp.zeros_like(stage)
    last = pairs + PASSES - 1
    first_half = (SPAN % 2) * LANES
    last_half = ((SPAN + height - 1) % 2) * LANES
    rims[:, 1, :, :, first_half : first_half + LANES] = paired[:, 1, :, :, first_half : first_half + LANES]
    rims[:, 2, :, :, last_half : last_half + LANES] = paired[:, last - 2, :, :, last_half : last_half + LANES]
    for below, index, pair, side in rim_rows(height):

        def source(a, b, below=below, index=index):
            place, turn = border_place(index, a // LANES, channels, SPAN)
            value = by_partner(near[place].astype(F32), far[place].astype(F32))[below]
            return (swap(value) if turn else value)[:, : b - a]

        place_natural(rims, stage, source, channels, width, blocks, pair, side)
    runs = inner_runs(pairs)[1]
    count = 0.0
    for row in range(height):
        for r in range(FINE):
            count = count + mask[row, r]
    count = jnp.sum(count, axis=0, keepdims=True)
    for t, _ in tiles_of(channels):
        lanes = pl.ds(t * LANES, LANES)
        planes = products(paired, rims, weights, accs, t, runs)
        near = sums[0:1, lanes]
        total, square = settle(planes, conv, mask, runs, lanes, near)
        total, square = total + sums[1:2, lanes], square + sums[2:3, lanes]
        shift = total / jnp.maximum(count, 1.0)
        stats[0:1, lanes] = near + shift
        stats[1:2, lanes] = jnp.maximum(square - total * shift, 0.0)
        stats[2:3, lanes] = count
        stats[3:8, lanes] = jnp.zeros((5, LANES), F32)


def products(paired, rims, weights, accs, tile, runs):
    has_upper = 2 * tile + 1 < paired.shape[0]
    for half in range(1 + has_upper):
        block = 2 * tile + half
        accs[half] = convolve_block(paired, rims, weights.at[block], block, runs)

    def planes(place, k, side):
        start = (place * (FINE // 2) + k) * PAD
        return split_blocks(accs.at[0], accs.at[1] if has_upper else None, start, side)

    return planes


def settle(planes, conv, mask, runs, lanes, near):
    sums = [jnp.zeros((PAD, LANES), F32)] * 8
    for place, h in enumerate(pairs_of(runs)):
        for k in range(FINE // 2):
            for side in range(2):
                for odd, value in enumerate(planes(place, k, side)):
                    conv[2 * place + side, 2 * k + odd, :, lanes] = value
                    away = value - near
                    part = mask[2 * h + side, 2 * k + odd] * away
                    at = 2 * (2 * side + odd)
                    sums[at] = sums[at] + part
                    sums[at + 1] = sums[at + 1] + part * away
    return (jnp.sum(sums[i] + sums[i + 2] + sums[i + 4] + sums[i + 6], axis=0, keepdims=True) for i in range(2))


def pointwise_kernel(
    channels, real_units, inner, outer, gbranch, feats, turned, vec, w_in, w_out,
    output, act_out, ghid_out, gz_out, z_out, sums, stage, conv,
):
    rows, width = feats.shape[0], feats.shape[1]
    padded = conv.shape[-1]
    cells = rows * FINE * PAD
    hidden_units = act_out.shape[1]
    step = pl.program_id(0)

    @pl.when(step == 0)
    def _():
        sums[...] = jnp.zeros_like(sums)

    one_lane = lax.broadcasted_iota(jnp.int32, (1, padded), 1) == channels
    mean, inverse, gain, shift = (vec[i : i + 1, :] for i in range(4))
    side = RIM_PAIRS // 2
    is_inner = jnp.logical_and(step >= side, step < pl.num_programs(0) - side)

    @pl.when(is_inner)
    def _():
        conv[...] = inner[pl.ds((step - side) * rows, rows)]

    @pl.when(jnp.logical_not(is_inner))
    def _():
        place = jnp.where(step < side, step, step + 2 * side - pl.num_programs(0))
        conv[...] = outer[pl.ds(place * rows, rows)]

    here = pl.ds(pl.multiple_of(step * cells, cells), cells)
    normed = (conv[...].reshape(cells, padded) - mean) * inverse
    zvals = jnp.where(one_lane, 1.0, gain * normed + shift).astype(BF16)
    z_out[here, :] = zvals
    mine = pl.ds(step * rows, rows)
    upstream = gbranch[mine].reshape(cells, padded)
    chunk = 2 * LANES
    across = (((1,), (1,)), ((), ()))
    c0 = 0.7978845608028654
    c1 = 0.044715 * c0
    for start in range(0, hidden_units, chunk):
        span = pl.ds(start, chunk)
        hidden = jnp.dot(zvals, w_in[:, span], preferred_element_type=F32)
        gact = lax.dot_general(upstream, w_out[span, :], across, preferred_element_type=F32)
        square = hidden * hidden
        share = 0.5 + 0.5 * jnp.tanh(hidden * (c0 + c1 * square))
        act = hidden * share
        slope = share + (act - act * share) * (2.0 * c0 + (6.0 * c1) * square)
        ghid = (gact * slope).astype(BF16)
        act = act.astype(BF16)
        if start + chunk > real_units:
            lane = lax.broadcasted_iota(jnp.int32, (1, chunk), 1)
            act = jnp.where(lane == real_units - start, jnp.ones((), BF16), act)
        act_out[here, span] = act
        ghid_out[here, span] = ghid
    branch = jnp.dot(act_out[here, :], w_out[...], preferred_element_type=F32)
    gz = lax.dot_general(ghid_out[here, :], w_in[...], across, preferred_element_type=F32)
    gz_out[mine] = gz.reshape(rows, *gz_out.shape[1:])
    sums[0:1, :] += jnp.sum(gz * normed, axis=0, keepdims=True)
    sums[1:2, :] += jnp.sum(gz, axis=0, keepdims=True)
    for row in range(rows):
        factor = mask_of_row(turned[...], step * rows + row)
        for t, lanes in tiles_of(channels):
            for r in range(FINE):
                start = (row * FINE + r) * PAD
                stage[row, t, pl.ds(r, PAD, stride=FINE), :] = branch[start : start + PAD, t * LANES : (t + 1) * LANES]
            piece = pl.ds(t * LANES, lanes)
            values = feats[row, :, piece].astype(F32) + stage[row, t, 0:width, :lanes]
            output[row, :, piece] = (values * factor[:, :lanes]).astype(BF16)


def out_grads_kernel(gbranch, act, grad):
    grad[...] = turned_product(gbranch, act, grad.shape[0])


def turned_product(left, right, rows):
    return lax.dot_general(left[:, :rows], right[...], (((0,), (0,)), ((), ())), preferred_element_type=F32)


def in_grads_kernel(channels, hidden, zvals, ghid, grad_out, kept, sent, grad_in):
    grad_in[...] = turned_product(zvals, ghid, grad_in.shape[0])
    shares = lax.axis_size("fsdp")
    layout = Packing(channels, hidden, shares)
    last = layout.in_tiles - 1
    lane = lax.broadcasted_iota(jnp.int32, (1, LANES), 1)
    spot = lax.broadcasted_iota(jnp.int32, (layout.out_pad, 1), 0)
    fill = jnp.zeros((layout.in_pad - layout.in_rows, LANES), F32)

    def write(out, j):
        rows = slice(j * layout.in_rows, (j + 1) * layout.in_rows)
        for t in range(layout.in_tiles):
            lanes = slice(t * LANES, (t + 1) * LANES)
            tile = grad_in[rows, lanes]
            if t == last:
                tile = jnp.where(lane == hidden - t * LANES, grad_out[rows, lanes], tile)
            tile = jnp.concatenate([tile, fill], axis=0)
            out[t * layout.in_pad : (t + 1) * layout.in_pad] = tile.astype(out.dtype)
        start = j * layout.out_rows
        aligned = start // LANES * LANES
        stop = min(aligned + (layout.out_tiles + 1) * LANES, grad_out.shape[1])
        part = jnp.where(
            spot == channels, grad_in[: layout.out_pad, aligned:stop], grad_out[: layout.out_pad, aligned:stop]
        )
        if start != aligned:
            part = pltpu.roll(part, stop - start, 1)
        for u in range(layout.out_tiles):
            base = layout.out_base + u * layout.out_pad
            out[base : base + layout.out_pad] = part[:, u * LANES : (u + 1) * LANES].astype(out.dtype)
        out[layout.small_base :] = jnp.zeros((layout.rows - layout.small_base, LANES), out.dtype)

    for mine in range(shares):

        @pl.when(lax.axis_index("fsdp") == mine)
        def _(mine=mine):
            for i in range(shares):
                rows = pl.ds(i // 2 * layout.rows, layout.rows)
                write((sent if i % 2 else kept).at[rows], mine ^ i)


def near_sum_kernel(kept, arrived, own, sent):
    rows = own.shape[0]
    own[...] = kept[:rows] + arrived[:rows].astype(F32)
    sent[...] = (kept[rows:] + arrived[rows:].astype(F32)).astype(BF16)


def finish_kernel(channels, hidden, slopes, *refs):
    parts, refs = refs[:-8], refs[-8:]
    grad_in, grad_in_bias, grad_out, grad_out_bias, grad_taps, grad_gain, grad_shift, packed = refs
    place = piece_of(lax.axis_index("dp"))
    rows = packed.shape[0] // len(parts)
    values = [part[:rows] for part in parts]
    for i in range(len(parts)):
        packed[i * rows : (i + 1) * rows] = in_place(place, values, i)
    low = (parts[0].shape[0] - rows) // 2
    exact = [part[rows : rows + low].astype(F32) + part[rows + low :].astype(F32) for part in parts]
    share = grad_in.shape[0]
    grad_taps[...] = tree(exact, lambda a, b: a + b)[: grad_taps.shape[0], :share]
    for mine in range(channels // share):

        @pl.when(lax.axis_index("fsdp") == mine)
        def _(start=mine * share):
            turned = pltpu.roll(slopes[...], slopes.shape[1] - start, 1) if start else slopes[...]
            grad_gain[...] = turned[5, :share]
            grad_shift[...] = turned[6, :share]

    layout = Packing(channels, hidden, channels // grad_in.shape[0])
    for t in range(layout.in_tiles):
        stop = min((t + 1) * LANES, hidden)
        tile = packed[t * layout.in_pad : (t + 1) * layout.in_pad].astype(F32)
        grad_in[:, t * LANES : stop] = tile[: layout.in_rows, : stop - t * LANES]
    tall = jnp.concatenate([tile, jnp.zeros((LANES - layout.in_pad, LANES), F32)], axis=0).T
    at = hidden - (layout.in_tiles - 1) * LANES
    grad_out_bias[...] = tall[at, : layout.in_rows]
    bias = []
    for u in range(layout.out_tiles):
        base = layout.out_base + u * layout.out_pad
        tile = packed[base : base + layout.out_pad].astype(F32)
        stop = min((u + 1) * LANES, layout.out_rows)
        count = stop - u * LANES
        bias.append(tile[channels : channels + 1, :])
        fill = jnp.zeros((round_up(layout.out_pad, LANES) - layout.out_pad, LANES), F32)
        grad_out[u * LANES : stop, :] = jnp.concatenate([tile, fill], axis=0).T[:count, :channels]
    grad_in_bias[...] = jnp.concatenate(bias, axis=1)[0, : layout.out_rows]


def share_taps_kernel(share, *refs):
    shares = lax.axis_size("fsdp")
    tiles, outs = refs[:-shares], refs[-shares:]
    wide = jnp.concatenate([tile[...] for tile in tiles], axis=1)
    for mine in range(shares):

        @pl.when(lax.axis_index("fsdp") == mine)
        def _(mine=mine):
            for i, out in enumerate(outs):
                start = (mine ^ i) * share
                turned = pltpu.roll(wide, wide.shape[1] - start, 1) if start else wide
                out[...] = turned[:, :LANES]


def tree(values, merge):
    while len(values) > 1:
        values = [merge(values[i], values[i + 1]) for i in range(0, len(values), 2)]
    return values[0]


def merge_stats(mine, other):
    count = mine[2:3] + other[2:3]
    safe = jnp.maximum(count, 1.0)
    mean = (mine[0:1] * mine[2:3] + other[0:1] * other[2:3]) / safe
    away = mine[0:1] - other[0:1]
    spread = mine[1:2] + other[1:2] + away * away * (mine[2:3] * other[2:3] / safe)
    return jnp.concatenate([mean, spread, count, jnp.zeros_like(mine[3:8])], axis=0)


def stats_kernel(*refs):
    refs[-1][...] = tree([ref[...] for ref in refs[:-1]], merge_stats)


def norm_kernel(vectors, *refs):
    stats = tree([ref[...] for ref in refs[:-1]], merge_stats)
    count = jnp.maximum(stats[2:3], 1.0)
    inverse = lax.rsqrt(stats[1:2] / count + EPSILON)
    refs[-1][...] = jnp.concatenate(
        [stats[0:1], inverse, vectors[0:2, :], count, jnp.zeros((3, stats.shape[1]), F32)], axis=0
    )


def sums_kernel(*refs):
    refs[-1][...] = tree([ref[...] for ref in refs[:-1]], lambda a, b: a + b)


def slopes_kernel(vec, *refs):
    sums = tree([ref[...] for ref in refs[:-1]], lambda a, b: a + b)
    scaled = vec[1:2, :] * vec[2:3, :]
    count = vec[4:5, :]
    refs[-1][...] = jnp.concatenate(
        [vec[0:2, :], scaled, scaled * sums[1:2] / count, scaled * sums[0:1] / count, sums[0:2], sums[2:3]], axis=0
    )


class Packing:
    def __init__(self, channels, hidden, shares):
        self.in_rows = channels // shares
        self.in_pad = round_up(self.in_rows, 16)
        self.in_tiles = -(-(hidden + 1) // LANES)
        self.out_rows = hidden // shares
        self.out_tiles = -(-self.out_rows // LANES)
        self.out_pad = round_up(max(channels + 1, self.out_rows), 16)
        self.out_base = self.in_pad * self.in_tiles
        self.small_base = self.out_base + self.out_pad * self.out_tiles
        self.small = self.out_tiles + 3
        self.rows = round_up(self.small_base + self.small, 32)


def pack_parameters(layout, in_proj, in_bias, out_proj, gain, shift, out_bias, packed, wide, tall):
    wide[...] = jnp.zeros_like(wide)
    tall[...] = jnp.zeros_like(tall)
    wide[: layout.in_rows, : in_proj.shape[1]] = in_proj[...].astype(F32)
    for t in range(layout.in_tiles):
        packed[t * layout.in_pad : (t + 1) * layout.in_pad] = wide[: layout.in_pad, t * LANES : (t + 1) * LANES].astype(BF16)
    tall[: layout.out_rows, : out_proj.shape[1]] = out_proj[...].astype(F32)
    for u in range(layout.out_tiles):
        base = layout.out_base + u * layout.out_pad
        packed[base : base + layout.out_pad] = tall[:, u * LANES : (u + 1) * LANES].astype(BF16)
    wide[...] = jnp.zeros_like(wide)
    for i, small in enumerate((in_bias, gain, shift, out_bias)):
        wide[i : i + 1, : small.shape[0]] = small[...].reshape(1, -1).astype(F32)
    rows = [wide[0:1, u * LANES : (u + 1) * LANES] for u in range(layout.out_tiles)]
    rows += [wide[i + 1 : i + 2, :LANES] for i in range(3)]
    rows.append(jnp.zeros((layout.rows - layout.small_base - layout.small, LANES), F32))
    packed[layout.small_base :] = jnp.concatenate(rows, axis=0).astype(BF16)


def assemble_kernel(layout, shares, *refs):
    packed, (w_in, w_out, vectors, wide, tall) = refs[:shares], refs[shares:]
    mine = lax.axis_index("fsdp")

    def rows_of(f, start, stop):
        return in_place(mine, [part[start:stop].astype(F32) for part in packed], f)

    wide[...] = jnp.zeros_like(wide)
    tall[...] = jnp.zeros_like(tall)
    channels, hidden = layout.in_rows * shares, layout.out_rows * shares
    in_bias = jnp.zeros((8, wide.shape[1]), F32)
    smalls = [jnp.zeros((8, tall.shape[1]), F32)] * 3
    for f in range(shares):
        for t in range(layout.in_tiles):
            tile = rows_of(f, t * layout.in_pad, (t + 1) * layout.in_pad)
            wide[f * layout.in_rows : (f + 1) * layout.in_rows, t * LANES : (t + 1) * LANES] = tile[: layout.in_rows]
        for u in range(layout.out_tiles):
            base = layout.out_base + u * layout.out_pad
            tile = rows_of(f, base, base + layout.out_pad)
            tall[f * layout.out_rows : (f + 1) * layout.out_rows, u * LANES : (u + 1) * LANES] = tile[: layout.out_rows]
        small = rows_of(f, layout.small_base, layout.rows)

        def spread(first, count, lanes, turn):
            pieces = [small[first + u : first + u + 1] for u in range(count)]
            pieces.append(jnp.zeros((1, lanes - count * LANES), F32))
            row = jnp.broadcast_to(jnp.concatenate(pieces, axis=1), (8, lanes))
            return pltpu.roll(row, turn, 1) if turn else row

        in_bias = in_bias + spread(0, layout.out_tiles, wide.shape[1], f * layout.out_rows)
        smalls = [
            total + spread(layout.out_tiles + i, 1, tall.shape[1], f * layout.in_rows)
            for i, total in enumerate(smalls)
        ]
    wide[channels : channels + 1] = in_bias[:1]
    tall[hidden : hidden + 1] = smalls[2][:1]
    w_in[...] = wide[...].astype(BF16)
    w_out[...] = tall[...].astype(BF16)
    vectors[...] = jnp.concatenate([smalls[0][:1], smalls[1][:1], jnp.zeros((6, tall.shape[1]), F32)], axis=0)


def shifted_planes(values, real):
    out = []
    for r in range(-SPAN, FINE + SPAN):
        value = values[r % FINE]
        if r < 0:
            value = jnp.concatenate([value[real - 1 : real], value[: PAD - 1]], axis=0)
        elif r >= FINE:
            value = jnp.concatenate([value[1:real], value[:1], value[: PAD - real]], axis=0)
        out.append(value)
    return out


def join_planes(first, second):
    low = low_half(PAD)
    return (
        jnp.where(low, first, swap(second)).astype(BF16),
        jnp.where(low, swap(first), second).astype(BF16),
    )


def place_planes(paired, planes, tile, blocks, pair, side):
    out_lanes = pl.ds(side * LANES, LANES)
    for k in range(len(planes) // 2):
        for half, value in enumerate(join_planes(planes[2 * k], planes[2 * k + 1])):
            if 2 * tile + half < blocks:
                paired[2 * tile + half, pair, k, :, out_lanes] = value


def arrange_kernel(
    channels, real, gz, inner, outer, mask, vec, near, far, gpaired, own, edges,
):
    height = gz.shape[0]
    blocks = own.shape[0]
    for t, _ in tiles_of(channels):
        lanes = pl.ds(t * LANES, LANES)
        mean, inverse, scaled, bias, slope = (vec[i : i + 1, lanes] for i in range(5))
        for row in range(height):
            h, side = row // 2, row % 2
            values = []
            for r in range(FINE):
                normed = (conv_at(inner, outer, row, r, lanes) - mean) * inverse
                values.append(scaled * gz[row, r, :, lanes] - mask[row, r] * (bias + normed * slope))
            out_lanes = pl.ds(side * LANES, LANES)
            for k in range(FINE // 2):
                rows = pl.ds((h * (FINE // 2) + k) * PAD, PAD)
                for half, value in enumerate(join_planes(values[2 * k], values[2 * k + 1])):
                    if 2 * t + half < blocks:
                        own[2 * t + half, rows, out_lanes] = value
            place_planes(gpaired, shifted_planes(values, real), t, blocks, (SPAN + row) // 2, (SPAN + row) % 2)
            for edge, border in ((0, row < SPAN), (1, row >= height - SPAN)):
                if border:
                    place = row - (height - SPAN) * edge
                    for r in range(FINE):
                        edges[edge, place, r, :, lanes] = values[r].astype(BF16)
    near[...], far[...] = by_partner(edges[0], edges[1])


def conv_at(inner, outer, row, r, lanes):
    start = RIM_PAIRS
    stop = start + inner.shape[0]
    if start <= row < stop:
        return inner[row - start, r, :, lanes]
    return outer[row if row < start else row - stop + start, r, :, lanes]


def taps_kernel(tile, own, paired, rims, select, grad_taps):
    blocks, pairs = own.shape[0], paired.shape[1] - PASSES + 1
    lane = lax.broadcasted_iota(jnp.int32, (HALF, 2 * LANES), 1)
    sub = lax.broadcasted_iota(jnp.int32, (HALF, 2 * LANES), 0)
    diagonal = lax.rem(lane, HALF) == sub
    low = low_half(grad_taps.shape[0])
    totals = []
    for block in range(2 * tile, min(2 * tile + 2, blocks)):
        turned = own[block].T
        found = []
        for m in range(PASSES):
            for s in range(PASSES):
                product = jnp.dot(turned, pass_rows(paired, rims, block, m, s, [(0, pairs)]), preferred_element_type=F32)
                for q in range(4):
                    part = product[q * HALF : (q + 1) * HALF]
                    found.append(jnp.sum(jnp.where(diagonal, part, 0.0), axis=0, keepdims=True))
        found = jnp.concatenate(found, axis=0)
        total = None
        for place in range(4):
            group = jnp.dot(select[place], found, preferred_element_type=F32, precision=lax.Precision.HIGHEST)
            group = group[:, (place // 2) * LANES : (place // 2 + 1) * LANES]
            if place % 2:
                group = swap(group)
            total = group if total is None else total + group
        totals.append(total)
    second = swap(totals[1]) if len(totals) > 1 else jnp.zeros_like(totals[0])
    grad_taps[...] = jnp.where(low, totals[0], second)


def flip_kernel(taps, weights):
    for block in range(weights.shape[0]):
        build_weights(weights.at[block], taps, block, True)


def backward_kernel(tile, real, gpaired, near, far, weights, cot, turned, *rest):
    result, rims, accs, stage = rest[-4:]
    height, width = cot.shape[:2]
    blocks, pairs = gpaired.shape[0], height // 2
    last = pairs + PASSES - 1
    first_half = (SPAN % 2) * LANES
    last_half = ((SPAN + height - 1) % 2) * LANES
    has_upper = 2 * tile + 1 < blocks
    for half in range(1 + has_upper):
        source = gpaired.at[2 * tile + half]
        rims[half, 1, :, :, first_half : first_half + LANES] = source[1, :, :, first_half : first_half + LANES]
        rims[half, 2, :, :, last_half : last_half + LANES] = source[last - 2, :, :, last_half : last_half + LANES]
    for below, index, pair, side in rim_rows(height):
        piece = pl.ds(tile * LANES, LANES)
        values = [
            by_partner(near[index, r, :, piece].astype(F32), far[index, r, :, piece].astype(F32))[below]
            for r in range(FINE)
        ]
        place_planes(rims, shifted_planes(values, real), 0, 1 + has_upper, pair, side)
    for half in range(1 + has_upper):
        block = 2 * tile + half
        accs[half] = convolve_block(
            gpaired.at[block : block + 1], rims.at[half : half + 1], weights.at[block], 0, [(0, pairs)]
        )

    def spread(h, _):
        for side in range(2):
            row = 2 * h + side
            for k in range(FINE // 2):
                even, odd = split_blocks(
                    accs.at[0], accs.at[1] if has_upper else None, (h * (FINE // 2) + k) * PAD, side
                )
                stage[side, pl.ds(2 * k, PAD, stride=FINE), :] = even
                stage[side, pl.ds(2 * k + 1, PAD, stride=FINE), :] = odd
            values = cot[row].astype(F32) + stage[side, 0:width]
            result[row] = (values * mask_of_row(turned[...], row)).astype(BF16)
        return 0

    for h in range(pairs):
        spread(h, 0)


def bits(size):
    bit = 1
    while bit < size:
        yield bit
        bit *= 2


def swapped(value, axis, flip):
    size = lax.axis_size(axis)
    return lax.ppermute(value, axis, [(i, i ^ flip) for i in range(size)])


def phases(*axes):
    out = []
    for axis in axes:
        left = list(bits(lax.axis_size(axis)))
        while left:
            near, left = left[:2], left[2:]
            out.append((axis, near if len(near) < 2 else [near[0], near[1], near[0] | near[1]]))
    return out


def tied(*values):
    return lax.optimization_barrier(values)


def halves_kernel(bit, *refs):
    parts, (keep, send) = refs[:-2], refs[-2:]
    rows = keep.shape[0]
    halves = [sum((part[a : a + rows].astype(F32) for part in parts[1:]), parts[0][a : a + rows]) for a in (0, rows)]
    first = lax.axis_index("dp") // bit % 2 == 0
    keep[...] = jnp.where(first, halves[0], halves[1])
    send[...] = jnp.where(first, halves[1], halves[0]).astype(send.dtype)


def whole_kernel(count, *refs):
    parts, extra, out = refs[:count], refs[count:-1], refs[-1]
    rows = parts[0].shape[0]
    out[:rows] = sum((part[...].astype(F32) for part in parts[1:]), parts[0][...])
    if extra:
        out[rows:] = sum((part[...] for part in extra[1:]), extra[0][...])


def last_kernel(rows, mine, other, out):
    total = mine[...] + other[...]
    rest = total.shape[0] - rows
    high = total[rows:].astype(BF16)
    out[:rows] = total[:rows].astype(BF16)
    out[rows : rows + rest] = high
    out[rows + rest :] = (total[rows:] - high.astype(F32)).astype(BF16)


def beside(work, *values):
    done = work() if work else ()
    return lax.optimization_barrier((done, values))


def far_bits():
    return list(bits(lax.axis_size("dp")))[1:3]


def piece_of(place):
    piece = 0
    for bit in far_bits():
        piece = 2 * piece + place // bit % 2
    return piece


class Spreading:
    def __init__(self, *parts):
        self.parts, self.extra = parts, ()
        cuts = far_bits()
        self.moves = [("half", [bit]) for bit in cuts]
        self.moves += [("whole", [bit]) for bit in bits(lax.axis_size("dp")) if bit not in cuts]
        flips = [0]
        for bit in reversed(cuts):
            flips += [flip | bit for flip in flips]
        self.moves.append(("gather", flips[1:]))

    def start(self):
        kind, flips = self.moves.pop(0)
        rows, lanes = self.parts[0].shape
        operands = (*self.parts, *self.extra)
        run = lambda kernel, *outs: call(
            kernel, outs, operands, [WHOLE] * len(operands), limit=10, name="sum_weights"
        )
        if kind == "half":
            kept, sent = run(
                functools.partial(halves_kernel, flips[0]),
                anywhere((rows // 2, lanes), F32),
                anywhere((rows // 2, lanes), BF16),
            )
        elif kind == "whole":
            low = self.extra[0].shape[0] if self.extra else 0
            if self.extra:
                self.rows = rows
            (kept,) = (sent,) = run(
                functools.partial(whole_kernel, len(self.parts)), anywhere((rows + low, lanes), F32)
            )
            self.extra = ()
        else:
            (kept,) = (sent,) = run(
                functools.partial(last_kernel, self.rows), anywhere((2 * rows - self.rows, lanes), BF16)
            )
        self.parts = (kept,)
        return [swapped(sent, "dp", flip) for flip in flips]

    def finish(self, others):
        self.parts = (*self.parts, *others)


def border_exchange(near, far):
    size = lax.axis_size("dp")
    first = [(i, i ^ 1) for i in range(size)]
    second = [(i, i + 1) for i in range(1, size - 1, 2) if (i + 1) % TILES]
    second += [(j, i) for i, j in second]
    return lax.ppermute(near, "dp", first), lax.ppermute(far, "dp", second)


def tap_selectors(rows):
    out = np.zeros((4, rows, PASSES * PASSES * 4), np.float32)
    for m in range(PASSES):
        for s in range(PASSES):
            for q in range(4):
                for p in range(4):
                    a = 2 * m + p // 2 - q // 2
                    b = 2 * s + p % 2 - q % 2
                    if 0 <= a < KW and 0 <= b < KW:
                        out[p, a * KW + b, (m * PASSES + s) * 4 + q] = 1.0
    return out


def local(features, land_mask, cotangent, kernel, norm_gain, norm_shift, in_proj, in_bias, out_proj, out_bias):
    feats, cot = features[0, 0], cotangent[0, 0]
    height, width, channels = feats.shape
    hidden = in_proj.shape[1]
    shares = lax.axis_size("fsdp")
    padded = round_up(channels + 1, LANES)
    hidden_pad = round_up(hidden + 1, 2 * LANES)
    blocks = -(-channels // HALF)
    pairs = height // 2
    planes_in = (FINE + 2 * SPAN) // 2
    row_pairs = pairs + PASSES - 1
    cells = height * FINE * PAD
    block_rows = pairs * (FINE // 2) * PAD
    stage_rows = round_up(BASE + SPAN + FINE * PAD, 8)
    tile_count = len(tiles_of(channels))
    tap_rows = round_up(TAPS, 16)
    real = width // FINE
    layout = Packing(channels, hidden, shares)

    edge = lambda at: pl.BlockSpec((SPAN, width, channels), lambda i: (at, 0, 0))
    whole = lambda array: pl.BlockSpec(array.shape, lambda i: (0,) * array.ndim)
    natural_shape = (height, width, channels)
    edge_shape = (1 + max(border_place(SPAN - 1, t, channels, SPAN)[0] for t in range(tile_count)), width, LANES)
    paired_shape = (blocks, row_pairs, planes_in, PAD, 4 * HALF)
    rims_shape = (blocks, RIM_PAIRS, planes_in, PAD, 4 * HALF)
    plane_shape = (height, FINE, PAD, padded)
    mask_shape = (height, FINE, PAD, LANES)
    small = (kernel.T, in_proj, in_bias, out_proj, norm_gain, norm_shift, out_bias)
    near, far, turned, shard, packed = call(
        functools.partial(begin_kernel, layout),
        [
            anywhere(edge_shape, BF16),
            anywhere(edge_shape, BF16),
            anywhere((width, height), BF16),
            anywhere((layout.in_pad, LANES), BF16),
            anywhere((layout.rows, LANES), BF16),
        ],
        (slow(feats), slow(feats), slow(land_mask), *(slow(v) for v in small)),
        [edge(0), edge(height // SPAN - 1), whole(land_mask)] + [whole(v) for v in small],
        [
            pltpu.VMEM((round_up(height, LANES), round_up(width, LANES)), F32),
            pltpu.VMEM((round_up(layout.in_pad, LANES), hidden_pad), F32),
            pltpu.VMEM((layout.out_pad, padded), F32),
            pltpu.VMEM((2, *edge_shape), F32),
            pltpu.VMEM((2, width, LANES), F32),
        ],
        grid=(1,),
        out_specs=[WHOLE] * 5,
        name="begin",
    )
    others = list(range(1, shares))
    six = 6 if height % 6 == 0 else 2
    stage = pltpu.VMEM((2, tile_count, 2, stage_rows, LANES), F32)
    near, far = border_exchange(near, far)
    shards = [swapped(shard, "fsdp", i) for i in others]
    (paired, gbranch, mask), (packed, shards) = beside(
        lambda: call(
            prepare_kernel,
            [pltpu.VMEM(paired_shape, BF16), pltpu.VMEM(plane_shape, BF16), pltpu.VMEM(mask_shape, F32)],
            (slow(feats), slow(cot), turned),
            [pl.BlockSpec((six, width, channels), lambda i: (i, 0, 0))] * 2 + [WHOLE],
            [stage, pltpu.VMEM((2, 1 + tile_count, stage_rows, LANES), F32)],
            grid=(height // six,),
            name="prepare",
        ),
        packed,
        [shard, *shards],
    )
    cuts = list(bits(shares))
    direct = [swapped(packed, "fsdp", bit) for bit in cuts]
    inner, outer = inner_runs(pairs)
    run_rows = lambda runs: 2 * len(pairs_of(runs))
    run_accs = lambda runs: pltpu.VMEM((2, run_rows(runs) * (FINE // 2) * PAD // 2, 4 * HALF), F32)
    weights_shape = (PASSES * PASSES * 4 * HALF, 4 * HALF)
    (conv_inner, sums, taps, weights), (near, far) = beside(
        lambda: call(
            functools.partial(inner_kernel, channels, shares),
            [
                pltpu.VMEM((run_rows(inner), FINE, PAD, padded), F32),
                anywhere((8, padded), F32),
                anywhere((blocks, tap_rows, LANES), F32),
                pltpu.VMEM((blocks, *weights_shape), BF16),
            ],
            (fast(paired), fast(mask), *shards),
            [WHOLE] * (2 + shares),
            [run_accs(inner), pltpu.VMEM((blocks * HALF, LANES), F32)],
            limit=10,
            name="inner",
        ),
        near,
        far,
    )
    (conv_outer, stats, rims), (packed, direct) = beside(
        lambda: call(
            functools.partial(outer_kernel, channels),
            [
                pltpu.VMEM((run_rows(outer), FINE, PAD, padded), F32),
                anywhere((8, padded), F32),
                pltpu.VMEM(rims_shape, BF16),
            ],
            (fast(paired), near, far, fast(mask), fast(weights), sums),
            [WHOLE] * 6,
            [run_accs(outer), stage],
            flops=4 * 10**9,
            limit=10,
            name="outer",
        ),
        packed,
        direct,
    )
    packed = {0: packed, **dict(zip(cuts, direct))}
    for flip in others:
        if flip not in packed:
            packed[flip] = swapped(packed[flip & (flip - 1)], "fsdp", flip & -flip)
    packed = [packed[flip] for flip in range(shares)]
    assemble = lambda: call(
        functools.partial(assemble_kernel, layout, shares),
        [
            anywhere((padded, hidden_pad), BF16),
            anywhere((hidden_pad, padded), BF16),
            anywhere((8, padded), F32),
        ],
        packed,
        [WHOLE] * shares,
        [pltpu.VMEM((padded, hidden_pad), F32), pltpu.VMEM((hidden_pad, padded), F32)],
        name="assemble",
    )
    row_sums = anywhere((8, padded), F32)
    combine = lambda kernel, *values: call(kernel, [row_sums], values, [WHOLE] * len(values), limit=4, name="combine")[0]
    rounds = phases("fsdp", "dp")
    for n, (axis, flips) in enumerate(rounds):
        last = n + 1 == len(rounds)
        values = [stats, *(swapped(stats, axis, i) for i in flips)]
        if n + 2 == len(rounds):
            values += packed
        done, values = beside(assemble if last else None, *values)
        if n + 2 == len(rounds):
            packed, values = values[-shares:], values[:-shares]
        if last:
            w_in, w_out, vectors = done
        if n + 1 < len(rounds):
            stats = combine(stats_kernel, *values)
    vec = combine(norm_kernel, vectors, *values)

    rows = 2
    steps = height // rows
    by_row = lambda *rest: pl.BlockSpec((rows, *rest), lambda i: (i,) + (0,) * len(rest))
    output, act, ghid, gz, zvals, sums = call(
        functools.partial(pointwise_kernel, channels, hidden),
        [
            anywhere(natural_shape, BF16),
            pltpu.VMEM((cells, hidden_pad), BF16),
            pltpu.VMEM((cells, hidden_pad), BF16),
            pltpu.VMEM(plane_shape, F32),
            pltpu.VMEM((cells, padded), BF16),
            row_sums,
        ],
        (fast(conv_inner), fast(conv_outer), fast(gbranch), slow(feats), turned, vec, w_in, w_out),
        [WHOLE] * 3 + [by_row(width, channels)] + [WHOLE] * 4,
        [
            pltpu.VMEM((rows, tile_count, round_up(FINE * PAD, 8), LANES), F32),
            pltpu.VMEM((rows, FINE, PAD, padded), F32),
        ],
        flops=14 * 10**9,
        grid=(steps,),
        out_specs=[by_row(width, channels)] + [WHOLE] * 5,
        limit=9,
        name="pointwise",
    )

    grad_rows = round_up(channels + 1, 16)

    def out_grads():
        return call(
            out_grads_kernel,
            [pltpu.VMEM((grad_rows, hidden_pad), F32)],
            (fast(gbranch.reshape(cells, padded)), fast(act)),
            [WHOLE] * 2,
            flops=3 * 10**9,
            limit=4,
            name="out_grads",
        )

    def in_grads():
        return call(
            functools.partial(in_grads_kernel, channels, hidden),
            [pltpu.VMEM((shares // 2 * layout.rows, LANES), dtype) for dtype in (F32, BF16)],
            (fast(zvals), fast(ghid), fast(grad_out)),
            [WHOLE] * 3,
            [pltpu.VMEM((grad_rows, hidden_pad), F32)],
            flops=3 * 10**9,
            limit=6,
            name="in_grads",
        )

    work = out_grads
    for n, (axis, flips) in enumerate(rounds):
        values = [sums, *(swapped(sums, axis, i) for i in flips)]
        if n == 2:
            values.append(sent)
        done, values = beside(work, *values)
        if n == 2:
            *values, sent = values
        work = None
        if n == 0:
            (grad_out,) = done
            work = in_grads
        if n + 1 == len(rounds):
            (flipped,) = done
        if n == 1:
            kept, sent = done
            sent = swapped(sent, "fsdp", 1)
        if n + 2 == len(rounds):
            work = lambda: call(
                flip_kernel,
                [pltpu.VMEM((blocks, *weights_shape), BF16)],
                (taps,),
                [WHOLE],
                limit=4,
                name="flip",
            )
        if n + 1 < len(rounds):
            sums = combine(sums_kernel, *values)
    gvec = combine(slopes_kernel, vec, *values)
    kept, sent = call(
        near_sum_kernel,
        [anywhere((layout.rows, LANES), F32), anywhere((layout.rows, LANES), BF16)],
        (kept, sent),
        [WHOLE] * 2,
        limit=10,
        name="near_sum",
    )
    sent = swapped(sent, "fsdp", 2)
    near, far, gpaired, own = call(
        functools.partial(arrange_kernel, channels, real),
        [
            anywhere((SPAN, FINE, PAD, padded), BF16),
            anywhere((SPAN, FINE, PAD, padded), BF16),
            pltpu.VMEM(paired_shape, BF16),
            pltpu.VMEM((blocks, block_rows, 4 * HALF), BF16),
        ],
        (fast(gz), fast(conv_inner), fast(conv_outer), fast(mask), gvec),
        [WHOLE] * 5,
        [pltpu.VMEM((2, SPAN, FINE, PAD, padded), BF16)],
        flops=10**8,
        moved=10 * MIB,
        limit=6,
        name="arrange",
    )
    select = jnp.asarray(tap_selectors(tap_rows))
    near, far = border_exchange(near, far)

    def taps_of(t):
        return lambda: call(
            functools.partial(taps_kernel, t),
            [anywhere((tap_rows, LANES), F32)],
            (fast(own), fast(paired), fast(rims), select),
            [WHOLE] * 4,
            flops=4 * 10**9,
            limit=6,
            name="taps",
        )

    (first,) = taps_of(0)()
    (second,), (sent,) = beside(taps_of(1), sent)
    spreading = Spreading(kept, sent)
    rest = lambda: [taps_of(t)()[0] for t in range(2, tile_count)]
    more, (there,) = beside(rest, spreading.start())
    spreading.finish(there)
    near, far, *tiles = tied(near, far, first, second, *more)
    own_taps, *sent_taps = call(
        functools.partial(share_taps_kernel, layout.in_rows),
        [anywhere((tap_rows, LANES), F32)] * shares,
        tiles,
        [WHOLE] * tile_count,
        limit=4,
        name="share_taps",
    )
    sent_taps = [swapped(v, "fsdp", i) for i, v in zip(others, sent_taps)]
    accs = pltpu.VMEM((2, block_rows, 4 * HALF), F32)

    def backward_of(t, *before):
        column = pl.BlockSpec((height, width, LANES), lambda i: (0, 0, t))
        return lambda: call(
            functools.partial(backward_kernel, t, real),
            [anywhere(natural_shape, BF16)],
            (fast(gpaired), near, far, fast(flipped), slow(cot), turned, *before),
            [WHOLE] * 4 + [column, WHOLE] + [HBM] * len(before),
            [
                pltpu.VMEM((2, RIM_PAIRS, planes_in, PAD, 4 * HALF), BF16),
                accs,
                pltpu.VMEM((2, round_up(FINE * PAD, 8), LANES), F32),
            ],
            flops=4 * 10**9,
            limit=12,
            grid=(1,),
            out_specs=[column],
            aliases={6: 0} if before else {},
            name="backward",
        )

    result = ()
    for n in range(max(tile_count, len(spreading.moves))):
        work = backward_of((n + 1) % tile_count, *result) if n < tile_count else None
        values = [spreading.start()] if spreading.moves else []
        if n == 0:
            values += sent_taps
        done, values = beside(work, *values)
        result = done or result
        if values:
            spreading.finish(values[0])
        if n == 0:
            spreading.extra = (own_taps, *values[1:])
    (result,) = result
    pieces = spreading.parts
    grad_in, grad_in_bias, grad_out, grad_out_bias, grad_taps, grad_gain, grad_shift = call(
        functools.partial(finish_kernel, channels, hidden),
        [
            anywhere((layout.in_rows, hidden), F32),
            anywhere((layout.out_rows,), F32),
            anywhere((layout.out_rows, channels), F32),
            anywhere((layout.in_rows,), F32),
            anywhere((TAPS, layout.in_rows), F32),
            anywhere((layout.in_rows,), F32),
            anywhere((layout.in_rows,), F32),
        ],
        (gvec, *pieces),
        [WHOLE] * (1 + len(pieces)),
        [pltpu.VMEM((layout.rows, LANES), BF16)],
        name="finish",
    )
    return (
        output[None, None],
        result[None, None],
        grad_taps.T,
        grad_gain,
        grad_shift,
        grad_in,
        grad_in_bias,
        grad_out,
        grad_out_bias,
    )


def solution(mesh):
    spread = P("dp", "fsdp", None, None, None)
    split = P("fsdp", None)
    line = P("fsdp")
    return jax.shard_map(
        local,
        mesh=mesh,
        in_specs=(spread, P(), spread, split, line, line, split, line, split, line),
        out_specs=(spread, spread, split, line, line, split, line, split, line),
        check_vma=False,
    )
```
